32 devices in a mesh: rx: 4 (over x, core), ry: 8 (over z, y).
Axes of the slice: x: 2, y: 2, z: 4, core: 2. Of those that a mesh axis runs over, the one named last changes fastest.
Arguments:
- column_features: bfloat16 [4096, 1536], P(('rx', 'ry')), may hold values from -6 to 6
- column_route: int32 [4096], P(('rx', 'ry')), may hold values from 0 to 8191, as said below
- cotangent: bfloat16 [64, 128, 1536], P('rx', 'ry'), may hold values from -6 to 6
- first_weight: bfloat16 [27, 96, 96], replicated, may hold values from -0.125 to 0.125
- second_weight: bfloat16 [27, 96, 96], replicated, may hold values from -0.125 to 0.125
Outputs:
- block_output: bfloat16 [64, 128, 1536], P('rx', 'ry')
- feature_grads: bfloat16 [4096, 1536], P(('rx', 'ry'))
- first_grad: float32 [27, 96, 96], replicated
- second_grad: float32 [27, 96, 96], replicated
The draws below stay inside these ranges and needn't reach their ends.
Inputs may be any that keep to these rules, and one draw needn't show every extreme that they name: `column_route`: entries are distinct; entry o * 256 + q names slot q of owner o, owner o = i * 8 + j being the device at rx index i and ry index j. The columns of one owner are spread over the devices' shards as evenly as possible: each shard holds the floor or the ceiling of that owner's count / 32. An owner holds at most 256 columns, and in every draw one owner holds exactly 256, so that it receives 8 from every shard.
All inputs are finite; a program needn't handle non-finite values.
Results may differ from the reference program's by a relative error of at most 0.0029.
Values may be sent and summed in bfloat16 or wider, within the bound.
No kernel may reach another device: no remote copies, remote signals or barrier semaphores. Data moves between devices by JAX's collectives and lax.ppermute only.
A program may use at most 256 MiB of HBM per device.

```python
import jax
import jax.numpy as jnp
from jax import lax

C = 96
RX = 16
RY = 16
RZ = 16
SLOTS = 256
TILES_DEV = 128
TILES = 4096
NXV = 64
NYV = 128
N_RX = 4
N_RY = 8
DEVICES = 32


def draw_column_route(key, part):
    devices_all = DEVICES
    per_shard = TILES_DEV
    region_slots = SLOTS
    overall = devices_all * per_shard
    keys = jax.random.split(jax.random.fold_in(key, 17), 5)
    halfway = devices_all // 2
    surplus = jax.random.randint(keys[0], (halfway,), 0, per_shard + 1).astype(jnp.int32)
    surplus = surplus.at[0].set(per_shard)
    loads = jnp.concatenate([per_shard + surplus, per_shard - surplus]).astype(jnp.int32)
    owner_order = jax.random.permutation(keys[1], devices_all).astype(jnp.int32)
    ends = jnp.cumsum(loads).astype(jnp.int32)
    position = jnp.arange(overall, dtype=jnp.int32)
    which = jnp.searchsorted(ends, position, side='right').astype(jnp.int32)
    starts = ends[which] - loads[which]
    within = position - starts
    owners = owner_order[which]
    slot_scores = jax.random.randint(keys[2], (devices_all, region_slots), 0, 1 << 14).astype(jnp.int32) * region_slots + jnp.arange(region_slots, dtype=jnp.int32)[None, :]
    slot_perm = jnp.argsort(slot_scores, axis=1).astype(jnp.int32)
    slot_of = slot_perm[owners, within]
    offset = jax.random.randint(keys[3], (), 0, devices_all).astype(jnp.int32)
    source = (position + offset) % devices_all
    ordinal = position // devices_all
    shard_scores = jax.random.randint(keys[4], (devices_all, per_shard), 0, 1 << 14).astype(jnp.int32) * per_shard + jnp.arange(per_shard, dtype=jnp.int32)[None, :]
    shard_perm = jnp.argsort(shard_scores, axis=1).astype(jnp.int32)
    index_in_shard = shard_perm[source, ordinal]
    target = owners * region_slots + slot_of
    result = jnp.zeros((overall,), jnp.int32).at[source * per_shard + index_in_shard].set(target)
    return result.astype(jnp.int32)


def levels(rng, extent, cuts, low, largest):
    gain, own = 1.0, jax.random.fold_in(rng, 6)
    for dim, blocks in cuts:
        steps = jnp.exp(jax.random.uniform(jax.random.fold_in(own, dim), (blocks,), jnp.float32, low / len(cuts), largest / len(cuts)))
        gain = gain * jnp.repeat(steps, extent[dim] // blocks).reshape([-1 if axis == dim else 1 for axis in range(len(extent))])
    return gain


def centred(stream_key, extent, scale, most, shards=(), held_as=jnp.bfloat16):
    array = jax.random.normal(stream_key, extent, jnp.float32) * scale
    if len(shards) > 0:
        array = levels(stream_key, extent, shards, -0.22, 0.18) * array
    return jnp.clip(array, min=-most, max=most).astype(held_as)


def setup_inputs(seed: int = 0) -> dict:
    arg_keys = jax.random.split(jax.random.key(seed), 6)
    return {
        "column_features": centred(arg_keys[0], (TILES, C * RZ), 1.0, 6.0, ((0, 32),)),
        "column_route": draw_column_route(jax.random.fold_in(arg_keys[5], 71), 0),
        "cotangent": centred(arg_keys[2], (NXV, NYV, C * RZ), 1.0, 6.0, ((0, 4), (1, 8))),
        "first_weight": centred(arg_keys[3], (27, C, C), (27 * C) ** -0.5, 0.125),
        "second_weight": centred(arg_keys[4], (27, C, C), (27 * C) ** -0.5, 0.125),
    }


def pad_field(field):
    return jnp.pad(field, ((1, 1), (1, 1), (0, 0), (1, 1)))

def conv_sum(padded, weights):
    size_x = padded.shape[0] - 2
    size_y = padded.shape[1] - 2
    size_z = padded.shape[3] - 2
    result = jnp.zeros((size_x, size_y, weights.shape[1], size_z), jnp.float32)
    for a in range(3):
        for b in range(3):
            for c in range(3):
                piece = padded[a:a + size_x, b:b + size_y, :, c:c + size_z].astype(jnp.float32)
                result = result + jnp.einsum('oi,xyiz->xyoz', weights[9 * a + 3 * b + c].astype(jnp.float32), piece, precision=lax.Precision.HIGHEST)
    return result

def correlate(grads, padded):
    size_x, size_y, _, size_z = grads.shape
    grads_f = grads.astype(jnp.float32)
    terms = []
    for a in range(3):
        for b in range(3):
            for c in range(3):
                piece = padded[a:a + size_x, b:b + size_y, :, c:c + size_z].astype(jnp.float32)
                terms.append(jnp.einsum('xyoz,xyiz->oi', grads_f, piece, precision=lax.Precision.HIGHEST))
    return jnp.stack(terms, axis=0)

def flipped(weights):
    return jnp.transpose(weights[::-1], (0, 2, 1))

def to_grid(rows, width):
    shaped = rows.reshape(N_RX, N_RY, RX, RY, width)
    return jnp.transpose(shaped, (0, 2, 1, 3, 4)).reshape(N_RX * RX, N_RY * RY, width)

def from_grid(field, width):
    shaped = field.reshape(N_RX, RX, N_RY, RY, width)
    return jnp.transpose(shaped, (0, 2, 1, 3, 4)).reshape(N_RX * N_RY * RX * RY, width)

def reference(column_features, column_route, cotangent, first_weight, second_weight):
    devices_all = N_RX * N_RY
    row_width = C * RZ
    columns = jnp.zeros((devices_all * SLOTS, row_width), jnp.bfloat16).at[column_route].set(column_features)
    active = jnp.zeros((devices_all * SLOTS, 1), jnp.float32).at[column_route].set(1.0)
    field = to_grid(columns, row_width).reshape(NXV, NYV, C, RZ)
    mask = to_grid(active, 1).reshape(NXV, NYV, 1, 1)
    padded_x = pad_field(field)
    hidden = mask * conv_sum(padded_x, first_weight)
    act = jax.nn.silu(hidden).astype(jnp.bfloat16)
    padded_a = pad_field(act)
    second = conv_sum(padded_a, second_weight)
    block_output = (field.astype(jnp.float32) + mask * second).astype(jnp.bfloat16).reshape(NXV, NYV, row_width)
    cot_field = cotangent.reshape(NXV, NYV, C, RZ).astype(jnp.float32)
    outer_grad = (mask * cot_field).astype(jnp.bfloat16)
    act_grad = conv_sum(pad_field(outer_grad), flipped(second_weight))
    sigma = jax.nn.sigmoid(hidden)
    hidden_grad = (mask * act_grad * sigma * (1.0 + hidden * (1.0 - sigma))).astype(jnp.bfloat16)
    grid_grad = (mask * cot_field + conv_sum(pad_field(hidden_grad), flipped(first_weight))).astype(jnp.bfloat16)
    back_rows = from_grid(grid_grad.reshape(NXV, NYV, row_width), row_width)
    feature_grads = back_rows[column_route]
    factor = 1.0 / jnp.sqrt(jnp.float32(devices_all * TILES_DEV * RZ))
    second_grad = correlate(outer_grad, padded_a) * factor
    first_grad = correlate(hidden_grad, padded_x) * factor
    return (block_output, feature_grads, first_grad, second_grad)
```

```python
import functools

import jax
import jax.numpy as jnp
import numpy as np
from jax import lax
from jax.experimental import pallas as pl
from jax.experimental.pallas import tpu as pltpu
from jax.sharding import PartitionSpec as P

LANES = 128
PAIR = 256
VMEM = 56 * 1024 * 1024
BF = jnp.bfloat16
F32 = jnp.float32


def call(body, out_shape, flops, moved, grid=None, in_specs=None, out_specs=None, scratch=()):
    extra = {}
    if grid is not None:
        extra = dict(grid=grid, in_specs=in_specs, out_specs=out_specs)
    return pl.pallas_call(
        body,
        out_shape=out_shape,
        scratch_shapes=list(scratch),
        compiler_params=pltpu.CompilerParams(vmem_limit_bytes=VMEM),
        cost_estimate=pl.CostEstimate(flops=int(flops), bytes_accessed=int(moved), transcendentals=0),
        **extra,
    )


def dot(left, right):
    return jnp.dot(left, right, preferred_element_type=F32)


def dot_nt(left, right):
    return lax.dot_general(left, right, (((1,), (1,)), ((), ())), preferred_element_type=F32)


def send_kernel(cap, slots, row_ref, col_ref, feat_ref, out_ref):
    rows = feat_ref.shape[0]
    owner_row = row_ref[...] // slots
    owner_col = col_ref[...] // slots
    first = lax.broadcasted_iota(jnp.int32, (rows, rows), 0)
    second = lax.broadcasted_iota(jnp.int32, (rows, rows), 1)
    same = jnp.where((owner_col == owner_row) & (first < second), 1.0, 0.0)
    rank = jnp.sum(same, axis=0, keepdims=True)
    pos = owner_row.astype(F32) * cap + rank
    place = lax.broadcasted_iota(jnp.int32, (out_ref.shape[0], rows), 0).astype(F32)
    hot = jnp.where(place == pos, 1.0, 0.0).astype(BF)
    out_ref[...] = dot(hot, feat_ref[...]).astype(BF)


def collect_kernel(cap, slots, row_ref, col_ref, back_ref, out_ref):
    rows = out_ref.shape[0]
    owner_row = row_ref[...] // slots
    owner_col = col_ref[...] // slots
    first = lax.broadcasted_iota(jnp.int32, (rows, rows), 0)
    second = lax.broadcasted_iota(jnp.int32, (rows, rows), 1)
    same = jnp.where((owner_col == owner_row) & (second < first), 1.0, 0.0)
    rank = jnp.sum(same, axis=1, keepdims=True)
    pos = owner_col.astype(F32) * cap + rank
    place = lax.broadcasted_iota(jnp.int32, (rows, back_ref.shape[0]), 1).astype(F32)
    hot = jnp.where(place == pos, 1.0, 0.0).astype(BF)
    out_ref[...] = dot(hot, back_ref[...]).astype(BF)


def mask_kernel(cap, slots, route_ref, rel_ref, codes_ref, mask_ref, take_ref, put_ref):
    count, rows = route_ref.shape
    total = mask_ref.shape[0]
    codes = jnp.broadcast_to(codes_ref[...], (total, rows))
    hits = jnp.zeros((total, rows), F32)
    for s in range(count):
        hits = hits + jnp.where(codes == route_ref[s : s + 1, :], 1.0, 0.0)
    mask_ref[...] = jnp.broadcast_to(jnp.sum(hits, axis=1, keepdims=True), (total, LANES))
    rel = rel_ref[...]
    mine = (rel >= 0) & (rel < slots)
    mine_f = jnp.where(mine, 1.0, 0.0)
    slot_f = jnp.where(mine, rel, 0).astype(F32)
    first = lax.broadcasted_iota(jnp.int32, (rows, rows), 0)
    second = lax.broadcasted_iota(jnp.int32, (rows, rows), 1)
    tri = jnp.where(first < second, 1.0, 0.0).astype(BF)
    rank = dot(mine_f.astype(BF), tri)
    lane = lax.broadcasted_iota(jnp.int32, (count, LANES), 1)
    held = jnp.zeros((count, LANES), F32)
    for j in range(cap):
        here = jnp.where(rank == j, mine_f, 0.0)
        number = jnp.sum(here, axis=1, keepdims=True)
        value = jnp.sum(here * slot_f, axis=1, keepdims=True)
        value = value + (1.0 - number) * slots
        held = jnp.where(lane == j, value, held)
    buffers = count * cap
    place = lax.broadcasted_iota(jnp.int32, (buffers, count), 0)
    source = lax.broadcasted_iota(jnp.int32, (buffers, count), 1)
    spread = jnp.where(place // cap == source, 1.0, 0.0).astype(BF)
    wide = dot(spread, held.astype(BF))
    place = lax.broadcasted_iota(jnp.int32, (buffers, LANES), 0)
    lane = lax.broadcasted_iota(jnp.int32, (buffers, LANES), 1)
    slot_col = jnp.sum(jnp.where(place % cap == lane, wide, 0.0), axis=1, keepdims=True)
    slot_id = lax.broadcasted_iota(jnp.int32, (buffers, slots), 1).astype(F32)
    take = jnp.where(slot_col == slot_id, 1.0, 0.0)
    take_ref[...] = take.astype(BF)
    put_ref[...] = take.T.astype(BF)


def to_pairs_kernel(rows_ref, perm_ref, face_ref, out_ref, faces_ref):
    block = dot(rows_ref[...], perm_ref[0]).astype(BF)
    out_ref[0] = block
    faces_ref[0] = dot(face_ref[...], block).astype(BF)


def place_kernel(put_ref, rows_ref, perm_ref, face_ref, out_ref, faces_ref, held_ref):
    @pl.when(pl.program_id(0) == 0)
    def _():
        held_ref[...] = dot(put_ref[...], rows_ref[...]).astype(BF)

    block = dot(held_ref[...], perm_ref[0]).astype(BF)
    out_ref[0] = block
    faces_ref[0] = dot(face_ref[...], block).astype(BF)


def band_kernel(first_ref, second_ref, w1_ref, w2_ref, f1_ref, f2_ref):
    channels = first_ref.shape[1]
    for ref in (w1_ref, w2_ref, f1_ref, f2_ref):
        ref[...] = jnp.zeros_like(ref)
    for a in range(3):
        for b in range(3):
            for c in range(3):
                tap = 9 * a + 3 * b + c
                back = 26 - tap
                parts = (
                    (w1_ref, first_ref[tap].T),
                    (w2_ref, second_ref[tap].T),
                    (f1_ref, first_ref[back]),
                    (f2_ref, second_ref[back]),
                )
                for zo in range(2):
                    row = ((a * 3 + b) * 4 + zo + c) * LANES
                    for ref, value in parts:
                        ref[row : row + channels, zo * LANES : zo * LANES + channels] = value


def widen(ext_ref, f_ref, xlo_ref, xhi_ref, ylo_ref, yhi_ref, mask_ref=None):
    pairs = f_ref.shape[0]
    nx = ext_ref.shape[2] - 2
    ny = ext_ref.shape[3]
    inner = nx * ny
    for b in range(3):
        ext_ref[b, 0, :, :, 0:LANES] = jnp.zeros((nx + 2, ny, LANES), BF)
        ext_ref[b, pairs, :, :, LANES:PAIR] = jnp.zeros((nx + 2, ny, LANES), BF)
    row = lax.broadcasted_iota(jnp.int32, (ny, PAIR), 0)

    def masked(value, start, size):
        if mask_ref is None:
            return value
        m = mask_ref[start : start + size, :]
        return value * jnp.concatenate([m, m], axis=1)

    def body(k, carry):
        low = masked(ylo_ref[k].astype(F32), inner + 2 * ny, nx + 2)
        high = masked(yhi_ref[k].astype(F32), inner + 4 * ny, nx + 2)
        for xp in range(nx + 2):
            if xp == 0:
                mid = masked(xlo_ref[k].astype(F32), inner, ny)
            elif xp == nx + 1:
                mid = masked(xhi_ref[k].astype(F32), inner + ny, ny)
            else:
                mid = masked(f_ref[k, (xp - 1) * ny : xp * ny, :].astype(F32), (xp - 1) * ny, ny)
            up = jnp.where(row == 0, low[xp : xp + 1, :], pltpu.roll(mid, 1, 0))
            down = jnp.where(row == ny - 1, high[xp : xp + 1, :], pltpu.roll(mid, ny - 1, 0))
            for b, value in enumerate((up, mid, down)):
                value = value.astype(BF)
                ext_ref[b, k, xp, :, LANES:PAIR] = value[:, 0:LANES]
                ext_ref[b, k + 1, xp, :, 0:LANES] = value[:, LANES:PAIR]
        return carry

    lax.fori_loop(0, pairs, body, 0)


def conv_block(ext_ref, w_ref, k):
    nx = ext_ref.shape[2] - 2
    ny = ext_ref.shape[3]
    pieces = []
    for a in range(3):
        for b in range(3):
            for j in range(2):
                pieces.append(ext_ref[b, k + j, a : a + nx].reshape(nx * ny, PAIR))
    return dot(jnp.concatenate(pieces, axis=1), w_ref[...])


def wide_mask(mask_ref, rows):
    m = mask_ref[0:rows, :]
    return jnp.concatenate([m, m], axis=1)


def act_grad_kernel(f_ref, xlo_ref, xhi_ref, ylo_ref, yhi_ref, mask_ref, w_ref, out_ref, outer_ref, ext_ref):
    k = pl.program_id(0)

    @pl.when(k == 0)
    def _():
        widen(ext_ref, f_ref, xlo_ref, xhi_ref, ylo_ref, yhi_ref, mask_ref)

    rows = out_ref.shape[1]
    out_ref[0] = conv_block(ext_ref, w_ref, k)
    outer_ref[0] = (f_ref[k].astype(F32) * wide_mask(mask_ref, rows)).astype(BF)


def hidden_kernel(f_ref, xlo_ref, xhi_ref, ylo_ref, yhi_ref, mask_ref, w_ref, grad_ref, face_ref,
                  act_ref, hg_ref, faces_ref, ext_ref):
    k = pl.program_id(0)

    @pl.when(k == 0)
    def _():
        widen(ext_ref, f_ref, xlo_ref, xhi_ref, ylo_ref, yhi_ref)

    rows = act_ref.shape[1]
    m = wide_mask(mask_ref, rows)
    hidden = m * conv_block(ext_ref, w_ref, k)
    sigma = jax.nn.sigmoid(hidden)
    act = (hidden * sigma).astype(BF)
    hg = (m * grad_ref[0] * sigma * (1.0 + hidden * (1.0 - sigma))).astype(BF)
    act_ref[0] = act
    hg_ref[0] = hg
    faces_ref[0, 0] = dot(face_ref[...], act).astype(BF)
    faces_ref[1, 0] = dot(face_ref[...], hg).astype(BF)


def grid_grad_kernel(f_ref, xlo_ref, xhi_ref, ylo_ref, yhi_ref, w_ref, outer_ref, perm_ref, take_ref,
                     out_ref, ext_ref, acc_ref):
    k = pl.program_id(0)

    @pl.when(k == 0)
    def _():
        widen(ext_ref, f_ref, xlo_ref, xhi_ref, ylo_ref, yhi_ref)
        acc_ref[...] = jnp.zeros_like(acc_ref)

    total = (outer_ref[0].astype(F32) + conv_block(ext_ref, w_ref, k)).astype(BF)
    acc_ref[...] += dot_nt(total, perm_ref[0])

    @pl.when(k == pl.num_programs(0) - 1)
    def _():
        out_ref[...] = dot(take_ref[...], acc_ref[...].astype(BF)).astype(BF)


def block_kernel(f_ref, xlo_ref, xhi_ref, ylo_ref, yhi_ref, mask_ref, w_ref, field_ref, perm_ref,
                 out_ref, ext_ref, acc_ref):
    k = pl.program_id(0)

    @pl.when(k == 0)
    def _():
        widen(ext_ref, f_ref, xlo_ref, xhi_ref, ylo_ref, yhi_ref)
        acc_ref[...] = jnp.zeros_like(acc_ref)

    m = wide_mask(mask_ref, f_ref.shape[1])
    total = (field_ref[0].astype(F32) + m * conv_block(ext_ref, w_ref, k)).astype(BF)
    acc_ref[...] += dot_nt(total, perm_ref[0])

    @pl.when(k == pl.num_programs(0) - 1)
    def _():
        out_ref[...] = acc_ref[...].astype(BF)


def corr_kernel(channels, f_ref, xlo_ref, xhi_ref, ylo_ref, yhi_ref, g_ref, out_ref, ext_ref, gt_ref, taps_ref):
    pairs, rows, _ = g_ref.shape
    nx = ext_ref.shape[2] - 2
    widen(ext_ref, f_ref, xlo_ref, xhi_ref, ylo_ref, yhi_ref)
    for k in range(pairs):
        gt_ref[:, k * rows : (k + 1) * rows] = g_ref[k].T
    taps_ref[27] = jnp.zeros((channels, LANES), F32)

    def body(ab, carry):
        a = ab // 3
        b = ab % 3
        left = gt_ref[...]
        near = dot(left, ext_ref[b, 0:pairs, pl.ds(a, nx)].reshape(pairs * rows, PAIR))
        far = dot(left, ext_ref[b, 1 : pairs + 1, pl.ds(a, nx)].reshape(pairs * rows, PAIR))
        low = slice(0, channels)
        high = slice(LANES, LANES + channels)
        taps_ref[3 * ab] = near[low, 0:LANES] + near[high, LANES:PAIR]
        taps_ref[3 * ab + 1] = near[low, LANES:PAIR] + far[high, 0:LANES]
        taps_ref[3 * ab + 2] = far[low, 0:LANES] + far[high, LANES:PAIR]
        return carry

    lax.fori_loop(0, 9, body, 0)
    lane = lax.broadcasted_iota(jnp.int32, (channels, LANES), 1)
    for g in range(7):
        t1 = pltpu.roll(taps_ref[4 * g + 1], 96, 1)
        t2 = pltpu.roll(taps_ref[4 * g + 2], 64, 1)
        t3 = pltpu.roll(taps_ref[4 * g + 3], 32, 1)
        blocks = (
            jnp.where(lane < 96, taps_ref[4 * g], t1),
            jnp.where(lane < 64, t1, t2),
            jnp.where(lane < 32, t2, t3),
        )
        for i, value in enumerate(blocks):
            start = (3 * g + i) * channels
            out_ref[start : start + channels, :] = value.astype(BF)
    rest = out_ref.shape[0] - 21 * channels
    if rest:
        out_ref[21 * channels :, :] = jnp.zeros((rest, LANES), BF)


def chunk_sum_kernel(in_ref, out_ref):
    total = in_ref[0].astype(F32)
    for s in range(1, in_ref.shape[0]):
        total = total + in_ref[s].astype(F32)
    out_ref[...] = total.astype(BF)


def unpack_kernel(factor, packed_ref, out_ref):
    channels = out_ref.shape[1]
    lane = lax.broadcasted_iota(jnp.int32, (channels, LANES), 1)
    for g in range(7):
        v = []
        for i in range(3):
            start = (3 * g + i) * channels
            v.append(packed_ref[start : start + channels, :].astype(F32) * factor)
        taps = (
            v[0],
            pltpu.roll(jnp.where(lane < 64, v[1], v[0]), 32, 1),
            pltpu.roll(jnp.where(lane < 32, v[2], v[1]), 64, 1),
            pltpu.roll(v[2], 96, 1),
        )
        for u in range(4):
            if 4 * g + u < 27:
                out_ref[4 * g + u] = taps[u][:, 0:channels]


def permutation(channels, depth):
    perm = np.zeros((depth // 2, channels * depth, PAIR), np.float32)
    for c in range(channels):
        for z in range(depth):
            perm[z // 2, c * depth + z, (z % 2) * LANES + c] = 1.0
    return perm


def exchange(field, faces, ny):
    axis = field.ndim - 2
    count = lax.axis_size("rx")
    ahead = [(i, i + 1) for i in range(count - 1)]
    behind = [(t, s) for s, t in ahead]
    size = field.shape[axis]

    def cut(value, start, stop):
        return lax.slice_in_dim(value, start, stop, axis=axis)

    xlo = lax.ppermute(cut(field, size - ny, size), "rx", ahead)
    xhi = lax.ppermute(cut(field, 0, ny), "rx", behind)
    nx = faces.shape[axis] // 2
    low = jnp.concatenate([cut(xlo, 0, 1), cut(faces, 0, nx), cut(xhi, 0, 1)], axis=axis)
    high = jnp.concatenate([cut(xlo, ny - 1, ny), cut(faces, nx, 2 * nx), cut(xhi, ny - 1, ny)], axis=axis)
    count = lax.axis_size("ry")
    ahead = [(i, i + 1) for i in range(count - 1)]
    behind = [(t, s) for s, t in ahead]
    ylo = lax.ppermute(high, "ry", ahead)
    yhi = lax.ppermute(low, "ry", behind)
    return xlo, xhi, ylo, yhi


def on_device(column_features, column_route, cotangent, first_weight, second_weight):
    count_x = lax.axis_size("rx")
    count_y = lax.axis_size("ry")
    count_all = count_x * count_y
    shard_rows, row_width = column_features.shape
    nx, ny, _ = cotangent.shape
    channels = first_weight.shape[1]
    depth = row_width // channels
    slots = nx * ny
    pairs = depth // 2
    cap = 2 * shard_rows // count_all
    buffers = count_all * cap
    me_x = lax.axis_index("rx")
    me_y = lax.axis_index("ry")
    conv_flops = 2 * slots * pairs * 36 * LANES * PAIR
    axes = ("rx", "ry")

    shape = jax.ShapeDtypeStruct
    whole = lambda *dims: pl.BlockSpec(dims, lambda k: (0,) * len(dims))
    by_pair = lambda *dims: pl.BlockSpec((1,) + dims, lambda k: (k,) + (0,) * len(dims))
    zeros_like_field = shape((pairs, slots, PAIR), BF)
    ext = pltpu.VMEM((3, pairs + 1, nx + 2, ny, PAIR), BF)

    perm = jnp.asarray(permutation(channels, depth), BF)
    face_np = np.zeros((2 * nx, slots), np.float32)
    for u in range(nx):
        face_np[u, u * ny] = 1.0
        face_np[nx + u, u * ny + ny - 1] = 1.0
    face = jnp.asarray(face_np, BF)

    route_row = column_route.reshape(1, shard_rows)
    route_col = column_route.reshape(shard_rows, 1)
    route_all = lax.all_gather(column_route, axes).reshape(count_all, shard_rows)
    outgoing = call(
        functools.partial(send_kernel, cap, slots), shape((buffers, row_width), BF),
        2 * buffers * shard_rows * row_width, 3 * shard_rows * row_width * 2,
    )(route_row, route_col, column_features)
    incoming = lax.all_to_all(
        outgoing.reshape(count_all, cap, row_width), axes, split_axis=0, concat_axis=0, tiled=True
    ).reshape(buffers, row_width)

    steps, cells = [], []
    for u in range(nx):
        for v in range(ny):
            steps.append((0, 0)), cells.append(u * ny + v)
    for dx, u in ((-1, nx - 1), (1, 0)):
        for v in range(ny):
            steps.append((dx, 0)), cells.append(u * ny + v)
    for dy, v in ((-1, ny - 1), (1, 0)):
        for u in range(-1, nx + 1):
            steps.append((-1 if u < 0 else 1 if u == nx else 0, dy)), cells.append((u % nx) * ny + v)
        for _ in range(2 * ny - nx - 2):
            steps.append((0, 0)), cells.append(-(1 << 30))
    steps_np = np.asarray(steps, np.int32)
    cells_np = np.asarray(cells, np.int32)
    to_x = me_x + steps_np[:, 0]
    to_y = me_y + steps_np[:, 1]
    inside = (to_x >= 0) & (to_x < count_x) & (to_y >= 0) & (to_y < count_y) & (cells_np >= 0)
    codes = jnp.where(inside, (to_x * count_y + to_y) * slots + cells_np, -1).astype(jnp.int32)[:, None]
    spots = codes.shape[0]

    cot, cot_faces = call(
        to_pairs_kernel, (zeros_like_field, shape((pairs, 2 * nx, PAIR), BF)),
        2 * slots * row_width * PAIR * pairs, 10e6, (pairs,),
        [whole(slots, row_width), by_pair(row_width, PAIR), whole(2 * nx, slots)],
        (by_pair(slots, PAIR), by_pair(2 * nx, PAIR)),
    )(cotangent.reshape(slots, row_width), perm, face)
    cot_halo = exchange(cot, cot_faces, ny)

    band = shape((36 * LANES, PAIR), BF)
    w1, w2, f1, f2 = call(band_kernel, (band,) * 4, 1e9, 12e6)(first_weight, second_weight)

    mask, take, put = call(
        functools.partial(mask_kernel, cap, slots),
        (shape((spots, LANES), F32), shape((buffers, slots), BF), shape((slots, buffers), BF)),
        1e8, 1e6,
    )(route_all, route_all - (me_x * count_y + me_y) * slots, codes)

    halo_specs = [
        whole(pairs, slots, PAIR), whole(pairs, ny, PAIR), whole(pairs, ny, PAIR),
        whole(pairs, nx + 2, PAIR), whole(pairs, nx + 2, PAIR),
    ]
    mask_spec = whole(spots, LANES)
    band_spec = whole(36 * LANES, PAIR)
    field_spec = by_pair(slots, PAIR)

    act_grad, outer = call(
        act_grad_kernel, (shape((pairs, slots, PAIR), F32), zeros_like_field),
        conv_flops, 7e6, (pairs,),
        halo_specs + [mask_spec, band_spec], (field_spec, field_spec), (ext,),
    )(cot, *cot_halo, mask, f2)

    field, field_faces = call(
        place_kernel, (zeros_like_field, shape((pairs, 2 * nx, PAIR), BF)),
        2 * slots * row_width * PAIR * pairs, 10e6, (pairs,),
        [whole(slots, buffers), whole(buffers, row_width), by_pair(row_width, PAIR), whole(2 * nx, slots)],
        (by_pair(slots, PAIR), by_pair(2 * nx, PAIR)),
        (pltpu.VMEM((slots, row_width), BF),),
    )(put, incoming, perm, face)
    field_halo = exchange(field, field_faces, ny)

    act, hg, faces = call(
        hidden_kernel,
        (zeros_like_field, zeros_like_field, shape((2, pairs, 2 * nx, PAIR), BF)),
        conv_flops, 10e6, (pairs,),
        halo_specs + [mask_spec, band_spec, field_spec, whole(2 * nx, slots)],
        (field_spec, field_spec, pl.BlockSpec((2, 1, 2 * nx, PAIR), lambda k: (0, k, 0, 0))),
        (ext,),
    )(field, *field_halo, mask, w1, act_grad, face)
    act_halo = exchange(act, faces[0], ny)
    hg_halo = exchange(hg, faces[1], ny)

    unit = 16 * count_all
    packed_rows = -(-21 * channels // unit) * unit
    corr_scratch = (
        ext, pltpu.VMEM((PAIR, pairs * slots), BF), pltpu.VMEM((28, channels, LANES), F32),
    )
    corr = call(
        functools.partial(corr_kernel, channels), shape((packed_rows, LANES), BF), conv_flops, 5e6,
        scratch=corr_scratch,
    )

    def reduce(part):
        got = lax.all_to_all(
            part.reshape(count_all, packed_rows // count_all, LANES), axes, split_axis=0, concat_axis=0, tiled=True
        )
        chunk = call(
            chunk_sum_kernel, shape((packed_rows // count_all, LANES), BF), 1e6, 1e6
        )(got)
        return lax.all_gather(chunk, axes, tiled=True)

    first_packed = reduce(corr(field, *field_halo, hg))
    second_packed = reduce(corr(act, *act_halo, outer))

    rows_acc = pltpu.VMEM((slots, row_width), F32)
    back = call(
        grid_grad_kernel, shape((buffers, row_width), BF), 1.5 * conv_flops, 14e6, (pairs,),
        halo_specs + [band_spec, field_spec, by_pair(row_width, PAIR), whole(buffers, slots)],
        whole(buffers, row_width), (ext, rows_acc),
    )(hg, *hg_halo, f1, outer, perm, take)
    returned = lax.all_to_all(
        back.reshape(count_all, cap, row_width), axes, split_axis=0, concat_axis=0, tiled=True
    ).reshape(buffers, row_width)

    block_output = call(
        block_kernel, shape((slots, row_width), BF), 1.5 * conv_flops, 14e6, (pairs,),
        halo_specs + [mask_spec, band_spec, field_spec, by_pair(row_width, PAIR)],
        whole(slots, row_width), (ext, rows_acc),
    )(act, *act_halo, mask, w2, field, perm)

    feature_grads = call(
        functools.partial(collect_kernel, cap, slots), shape((shard_rows, row_width), BF),
        2 * buffers * shard_rows * row_width, 3 * shard_rows * row_width * 2,
    )(route_row, route_col, returned)

    factor = float(1.0 / np.sqrt(np.float32(count_all * shard_rows * depth)))
    unpack = call(functools.partial(unpack_kernel, factor), shape(first_weight.shape, F32), 1e6, 2e6)
    return (
        block_output.reshape(nx, ny, row_width), feature_grads, unpack(first_packed), unpack(second_packed),
    )


def solution(mesh):
    in_specs = (P(("rx", "ry"), None), P(("rx", "ry")), P("rx", "ry", None), P(), P())
    out_specs = (P("rx", "ry", None), P(("rx", "ry"), None), P(), P())
    return jax.shard_map(
        on_device, mesh=mesh, in_specs=in_specs, out_specs=out_specs, check_vma=False
    )
```

```python
import functools

import jax
import jax.numpy as jnp
import numpy as np
from jax import lax
from jax.experimental import pallas as pl
from jax.experimental.pallas import tpu as pltpu
from jax.sharding import PartitionSpec as P

LANES = 128
PAIR = 256
MIB = 1024 * 1024
BF = jnp.bfloat16
F32 = jnp.float32


def call(body, out_shape, flops, moved, grid=None, in_specs=None, out_specs=None, scratch=(), room=16):
    extra = {}
    if grid is not None:
        extra = dict(grid=grid, in_specs=in_specs, out_specs=out_specs)
    return pl.pallas_call(
        body,
        out_shape=out_shape,
        scratch_shapes=list(scratch),
        compiler_params=pltpu.CompilerParams(vmem_limit_bytes=room * MIB),
        cost_estimate=pl.CostEstimate(flops=int(flops), bytes_accessed=int(moved), transcendentals=0),
        **extra,
    )


def dot(left, right):
    return jnp.dot(left, right, preferred_element_type=F32)


def dot_nt(left, right):
    return lax.dot_general(left, right, (((1,), (1,)), ((), ())), preferred_element_type=F32)


def send_kernel(cap, slots, row_ref, col_ref, feat_ref, out_ref):
    rows = feat_ref.shape[0]
    owner_row = row_ref[...] // slots
    owner_col = col_ref[...] // slots
    first = lax.broadcasted_iota(jnp.int32, (rows, rows), 0)
    second = lax.broadcasted_iota(jnp.int32, (rows, rows), 1)
    same = jnp.where((owner_col == owner_row) & (first < second), 1.0, 0.0)
    rank = jnp.sum(same, axis=0, keepdims=True)
    pos = owner_row.astype(F32) * cap + rank
    place = lax.broadcasted_iota(jnp.int32, (out_ref.shape[0], rows), 0).astype(F32)
    hot = jnp.where(place == pos, 1.0, 0.0).astype(BF)
    out_ref[...] = dot(hot, feat_ref[...]).astype(BF)


def collect_kernel(cap, slots, row_ref, col_ref, back_ref, out_ref):
    rows = out_ref.shape[0]
    owner_row = row_ref[...] // slots
    owner_col = col_ref[...] // slots
    first = lax.broadcasted_iota(jnp.int32, (rows, rows), 0)
    second = lax.broadcasted_iota(jnp.int32, (rows, rows), 1)
    same = jnp.where((owner_col == owner_row) & (second < first), 1.0, 0.0)
    rank = jnp.sum(same, axis=1, keepdims=True)
    pos = owner_col.astype(F32) * cap + rank
    place = lax.broadcasted_iota(jnp.int32, (rows, back_ref.shape[0]), 1).astype(F32)
    hot = jnp.where(place == pos, 1.0, 0.0).astype(BF)
    out_ref[...] = dot(hot, back_ref[...]).astype(BF)


def mask_kernel(cap, slots, route_ref, rel_ref, codes_ref, mask_ref, take_ref, put_ref):
    count, rows = route_ref.shape
    total = mask_ref.shape[0]
    codes = jnp.broadcast_to(codes_ref[...], (total, rows))
    hits = jnp.zeros((total, rows), F32)
    for s in range(count):
        hits = hits + jnp.where(codes == route_ref[s : s + 1, :], 1.0, 0.0)
    mask_ref[...] = jnp.broadcast_to(jnp.sum(hits, axis=1, keepdims=True), (total, LANES))
    rel = rel_ref[...]
    mine = (rel >= 0) & (rel < slots)
    mine_f = jnp.where(mine, 1.0, 0.0)
    slot_f = jnp.where(mine, rel, 0).astype(F32)
    first = lax.broadcasted_iota(jnp.int32, (rows, rows), 0)
    second = lax.broadcasted_iota(jnp.int32, (rows, rows), 1)
    tri = jnp.where(first < second, 1.0, 0.0).astype(BF)
    rank = dot(mine_f.astype(BF), tri)
    lane = lax.broadcasted_iota(jnp.int32, (count, LANES), 1)
    held = jnp.zeros((count, LANES), F32)
    for j in range(cap):
        here = jnp.where(rank == j, mine_f, 0.0)
        number = jnp.sum(here, axis=1, keepdims=True)
        value = jnp.sum(here * slot_f, axis=1, keepdims=True)
        value = value + (1.0 - number) * slots
        held = jnp.where(lane == j, value, held)
    buffers = count * cap
    place = lax.broadcasted_iota(jnp.int32, (buffers, count), 0)
    source = lax.broadcasted_iota(jnp.int32, (buffers, count), 1)
    spread = jnp.where(place // cap == source, 1.0, 0.0).astype(BF)
    wide = dot(spread, held.astype(BF))
    place = lax.broadcasted_iota(jnp.int32, (buffers, LANES), 0)
    lane = lax.broadcasted_iota(jnp.int32, (buffers, LANES), 1)
    slot_col = jnp.sum(jnp.where(place % cap == lane, wide, 0.0), axis=1, keepdims=True)
    slot_id = lax.broadcasted_iota(jnp.int32, (buffers, slots), 1).astype(F32)
    take = jnp.where(slot_col == slot_id, 1.0, 0.0)
    take_ref[...] = take.astype(BF)
    put_ref[...] = take.T.astype(BF)


def to_pairs_kernel(rows_ref, perm_ref, face_ref, out_ref, faces_ref):
    block = dot(rows_ref[...], perm_ref[0]).astype(BF)
    out_ref[0] = block
    faces_ref[0] = dot(face_ref[...], block).astype(BF)


def place_kernel(put_ref, rows_ref, perm_ref, face_ref, out_ref, faces_ref, held_ref):
    @pl.when(pl.program_id(0) == 0)
    def _():
        held_ref[...] = dot(put_ref[...], rows_ref[...]).astype(BF)

    block = dot(held_ref[...], perm_ref[0]).astype(BF)
    out_ref[0] = block
    faces_ref[0] = dot(face_ref[...], block).astype(BF)


def band_kernel(first_ref, second_ref, w1_ref, w2_ref, f1_ref, f2_ref):
    channels = first_ref.shape[1]
    for ref in (w1_ref, w2_ref, f1_ref, f2_ref):
        ref[...] = jnp.zeros_like(ref)
    for a in range(3):
        for b in range(3):
            for c in range(3):
                tap = 9 * a + 3 * b + c
                back = 26 - tap
                parts = (
                    (w1_ref, first_ref[tap].T),
                    (w2_ref, second_ref[tap].T),
                    (f1_ref, first_ref[back]),
                    (f2_ref, second_ref[back]),
                )
                for zo in range(2):
                    row = ((a * 3 + b) * 4 + zo + c) * LANES
                    for ref, value in parts:
                        ref[row : row + channels, zo * LANES : zo * LANES + channels] = value


def widen(ext_ref, f_ref, xlo_ref, xhi_ref, ylo_ref, yhi_ref, mask_ref=None):
    pairs = f_ref.shape[0]
    nx = ext_ref.shape[2] - 2
    ny = ext_ref.shape[3]
    inner = nx * ny
    for b in range(3):
        ext_ref[b, 0, :, :, 0:LANES] = jnp.zeros((nx + 2, ny, LANES), BF)
        ext_ref[b, pairs, :, :, LANES:PAIR] = jnp.zeros((nx + 2, ny, LANES), BF)
    row = lax.broadcasted_iota(jnp.int32, (ny, PAIR), 0)

    def masked(value, start, size):
        if mask_ref is None:
            return value
        m = mask_ref[start : start + size, :]
        return value * jnp.concatenate([m, m], axis=1)

    def body(k, carry):
        low = masked(ylo_ref[k].astype(F32), inner + 2 * ny, nx + 2)
        high = masked(yhi_ref[k].astype(F32), inner + 4 * ny, nx + 2)
        for xp in range(nx + 2):
            if xp == 0:
                mid = masked(xlo_ref[k].astype(F32), inner, ny)
            elif xp == nx + 1:
                mid = masked(xhi_ref[k].astype(F32), inner + ny, ny)
            else:
                mid = masked(f_ref[k, (xp - 1) * ny : xp * ny, :].astype(F32), (xp - 1) * ny, ny)
            up = jnp.where(row == 0, low[xp : xp + 1, :], pltpu.roll(mid, 1, 0))
            down = jnp.where(row == ny - 1, high[xp : xp + 1, :], pltpu.roll(mid, ny - 1, 0))
            for b, value in enumerate((up, mid, down)):
                value = value.astype(BF)
                ext_ref[b, k, xp, :, LANES:PAIR] = value[:, 0:LANES]
                ext_ref[b, k + 1, xp, :, 0:LANES] = value[:, LANES:PAIR]
        return carry

    lax.fori_loop(0, pairs, body, 0)


def conv_block(ext_ref, w_ref, k):
    nx = ext_ref.shape[2] - 2
    ny = ext_ref.shape[3]
    pieces = []
    for a in range(3):
        for b in range(3):
            for j in range(2):
                pieces.append(ext_ref[b, k + j, a : a + nx].reshape(nx * ny, PAIR))
    return dot(jnp.concatenate(pieces, axis=1), w_ref[...])


def wide_mask(mask_ref, rows):
    m = mask_ref[0:rows, :]
    return jnp.concatenate([m, m], axis=1)


def act_grad_kernel(f_ref, xlo_ref, xhi_ref, ylo_ref, yhi_ref, mask_ref, w_ref, out_ref, outer_ref, ext_ref):
    k = pl.program_id(0)

    @pl.when(k == 0)
    def _():
        widen(ext_ref, f_ref, xlo_ref, xhi_ref, ylo_ref, yhi_ref, mask_ref)

    rows = out_ref.shape[1]
    out_ref[0] = conv_block(ext_ref, w_ref, k)
    outer_ref[0] = (f_ref[k].astype(F32) * wide_mask(mask_ref, rows)).astype(BF)


def hidden_kernel(f_ref, xlo_ref, xhi_ref, ylo_ref, yhi_ref, mask_ref, w_ref, grad_ref, face_ref,
                  act_ref, hg_ref, faces_ref, ext_ref):
    k = pl.program_id(0)

    @pl.when(k == 0)
    def _():
        widen(ext_ref, f_ref, xlo_ref, xhi_ref, ylo_ref, yhi_ref)

    rows = act_ref.shape[1]
    m = wide_mask(mask_ref, rows)
    hidden = m * conv_block(ext_ref, w_ref, k)
    sigma = jax.nn.sigmoid(hidden)
    act = (hidden * sigma).astype(BF)
    hg = (m * grad_ref[0] * sigma * (1.0 + hidden * (1.0 - sigma))).astype(BF)
    act_ref[0] = act
    hg_ref[0] = hg
    faces_ref[0, 0] = dot(face_ref[...], act).astype(BF)
    faces_ref[1, 0] = dot(face_ref[...], hg).astype(BF)


def grid_grad_kernel(f_ref, xlo_ref, xhi_ref, ylo_ref, yhi_ref, w_ref, outer_ref, perm_ref, take_ref,
                     out_ref, ext_ref, acc_ref):
    k = pl.program_id(0)

    @pl.when(k == 0)
    def _():
        widen(ext_ref, f_ref, xlo_ref, xhi_ref, ylo_ref, yhi_ref)
        acc_ref[...] = jnp.zeros_like(acc_ref)

    total = (outer_ref[0].astype(F32) + conv_block(ext_ref, w_ref, k)).astype(BF)
    acc_ref[...] += dot_nt(total, perm_ref[0])

    @pl.when(k == pl.num_programs(0) - 1)
    def _():
        out_ref[...] = dot(take_ref[...], acc_ref[...].astype(BF)).astype(BF)


def block_kernel(f_ref, xlo_ref, xhi_ref, ylo_ref, yhi_ref, mask_ref, w_ref, field_ref, perm_ref,
                 out_ref, ext_ref, acc_ref):
    k = pl.program_id(0)

    @pl.when(k == 0)
    def _():
        widen(ext_ref, f_ref, xlo_ref, xhi_ref, ylo_ref, yhi_ref)
        acc_ref[...] = jnp.zeros_like(acc_ref)

    m = wide_mask(mask_ref, f_ref.shape[1])
    total = (field_ref[0].astype(F32) + m * conv_block(ext_ref, w_ref, k)).astype(BF)
    acc_ref[...] += dot_nt(total, perm_ref[0])

    @pl.when(k == pl.num_programs(0) - 1)
    def _():
        out_ref[...] = acc_ref[...].astype(BF)


def corr_kernel(channels, f_ref, xlo_ref, xhi_ref, ylo_ref, yhi_ref, g_ref, out_ref, ext_ref, gt_ref, taps_ref):
    pairs, rows, _ = g_ref.shape
    nx = ext_ref.shape[2] - 2
    widen(ext_ref, f_ref, xlo_ref, xhi_ref, ylo_ref, yhi_ref)
    for k in range(pairs):
        gt_ref[:, k * rows : (k + 1) * rows] = g_ref[k].T
    taps_ref[27] = jnp.zeros((channels, LANES), F32)

    def body(ab, carry):
        a = ab // 3
        b = ab % 3
        left = gt_ref[...]
        near = dot(left, ext_ref[b, 0:pairs, pl.ds(a, nx)].reshape(pairs * rows, PAIR))
        far = dot(left, ext_ref[b, 1 : pairs + 1, pl.ds(a, nx)].reshape(pairs * rows, PAIR))
        low = slice(0, channels)
        high = slice(LANES, LANES + channels)
        taps_ref[3 * ab] = near[low, 0:LANES] + near[high, LANES:PAIR]
        taps_ref[3 * ab + 1] = near[low, LANES:PAIR] + far[high, 0:LANES]
        taps_ref[3 * ab + 2] = far[low, 0:LANES] + far[high, LANES:PAIR]
        return carry

    lax.fori_loop(0, 9, body, 0)
    lane = lax.broadcasted_iota(jnp.int32, (channels, LANES), 1)
    for g in range(7):
        t1 = pltpu.roll(taps_ref[4 * g + 1], 96, 1)
        t2 = pltpu.roll(taps_ref[4 * g + 2], 64, 1)
        t3 = pltpu.roll(taps_ref[4 * g + 3], 32, 1)
        blocks = (
            jnp.where(lane < 96, taps_ref[4 * g], t1),
            jnp.where(lane < 64, t1, t2),
            jnp.where(lane < 32, t2, t3),
        )
        for i, value in enumerate(blocks):
            start = (3 * g + i) * channels
            out_ref[start : start + channels, :] = value.astype(BF)
    rest = out_ref.shape[0] - 21 * channels
    if rest:
        out_ref[21 * channels :, :] = jnp.zeros((rest, LANES), BF)


def chunk_sum_kernel(first_ref, second_ref, out_ref):
    count = first_ref.shape[0]
    for i, ref in enumerate((first_ref, second_ref)):
        total = ref[0].astype(F32)
        for s in range(1, count):
            total = total + ref[s].astype(F32)
        total = total.astype(BF)
        for s in range(count):
            out_ref[s, i] = total


def unpack_kernel(factor, packed_ref, first_ref, second_ref, flat_ref):
    count, _, rows, _ = packed_ref.shape
    for i, out_ref in enumerate((first_ref, second_ref)):
        for s in range(count):
            flat_ref[s * rows : (s + 1) * rows, :] = packed_ref[s, i].astype(F32)
        unpack_taps(factor, flat_ref, out_ref)


def unpack_taps(factor, packed_ref, out_ref):
    channels = out_ref.shape[1]
    lane = lax.broadcasted_iota(jnp.int32, (channels, LANES), 1)
    for g in range(7):
        v = []
        for i in range(3):
            start = (3 * g + i) * channels
            v.append(packed_ref[start : start + channels, :] * factor)
        taps = (
            v[0],
            pltpu.roll(jnp.where(lane < 64, v[1], v[0]), 32, 1),
            pltpu.roll(jnp.where(lane < 32, v[2], v[1]), 64, 1),
            pltpu.roll(v[2], 96, 1),
        )
        for u in range(4):
            if 4 * g + u < 27:
                out_ref[4 * g + u] = taps[u][:, 0:channels]


def permutation(channels, depth):
    perm = np.zeros((depth // 2, channels * depth, PAIR), np.float32)
    for c in range(channels):
        for z in range(depth):
            perm[z // 2, c * depth + z, (z % 2) * LANES + c] = 1.0
    return perm


def exchange(field, faces, ny):
    axis = field.ndim - 2
    count = lax.axis_size("rx")
    ahead = [(i, i + 1) for i in range(count - 1)]
    behind = [(t, s) for s, t in ahead]
    size = field.shape[axis]

    def cut(value, start, stop):
        return lax.slice_in_dim(value, start, stop, axis=axis)

    xlo = lax.ppermute(cut(field, size - ny, size), "rx", ahead)
    xhi = lax.ppermute(cut(field, 0, ny), "rx", behind)
    nx = faces.shape[axis] // 2
    low = jnp.concatenate([cut(xlo, 0, 1), cut(faces, 0, nx), cut(xhi, 0, 1)], axis=axis)
    high = jnp.concatenate([cut(xlo, ny - 1, ny), cut(faces, nx, 2 * nx), cut(xhi, ny - 1, ny)], axis=axis)
    count = lax.axis_size("ry")
    ahead = [(i, i + 1) for i in range(count - 1)]
    behind = [(t, s) for s, t in ahead]
    ylo = lax.ppermute(high, "ry", ahead)
    yhi = lax.ppermute(low, "ry", behind)
    return xlo, xhi, ylo, yhi


def on_device(column_features, column_route, cotangent, first_weight, second_weight):
    count_x = lax.axis_size("rx")
    count_y = lax.axis_size("ry")
    count_all = count_x * count_y
    shard_rows, row_width = column_features.shape
    nx, ny, _ = cotangent.shape
    channels = first_weight.shape[1]
    depth = row_width // channels
    slots = nx * ny
    pairs = depth // 2
    cap = 2 * shard_rows // count_all
    buffers = count_all * cap
    me_x = lax.axis_index("rx")
    me_y = lax.axis_index("ry")
    conv_flops = 2 * slots * pairs * 36 * LANES * PAIR
    axes = ("rx", "ry")

    shape = jax.ShapeDtypeStruct
    whole = lambda *dims: pl.BlockSpec(dims, lambda k: (0,) * len(dims))
    by_pair = lambda *dims: pl.BlockSpec((1,) + dims, lambda k: (k,) + (0,) * len(dims))
    zeros_like_field = shape((pairs, slots, PAIR), BF)
    ext = pltpu.VMEM((3, pairs + 1, nx + 2, ny, PAIR), BF)

    perm = jnp.asarray(permutation(channels, depth), BF)
    face_np = np.zeros((2 * nx, slots), np.float32)
    for u in range(nx):
        face_np[u, u * ny] = 1.0
        face_np[nx + u, u * ny + ny - 1] = 1.0
    face = jnp.asarray(face_np, BF)

    def share(parts):
        return lax.all_to_all(parts, axes, split_axis=0, concat_axis=0, tiled=True)

    route_row = column_route.reshape(1, shard_rows)
    route_col = column_route.reshape(shard_rows, 1)
    route_all = share(jnp.broadcast_to(route_row, (count_all, shard_rows)))
    outgoing = call(
        functools.partial(send_kernel, cap, slots), shape((buffers, row_width), BF),
        2 * buffers * shard_rows * row_width, 3 * shard_rows * row_width * 2,
    )(route_row, route_col, column_features)
    incoming = lax.all_to_all(
        outgoing.reshape(count_all, cap, row_width), axes, split_axis=0, concat_axis=0, tiled=True
    ).reshape(buffers, row_width)

    steps, cells = [], []
    for u in range(nx):
        for v in range(ny):
            steps.append((0, 0)), cells.append(u * ny + v)
    for dx, u in ((-1, nx - 1), (1, 0)):
        for v in range(ny):
            steps.append((dx, 0)), cells.append(u * ny + v)
    for dy, v in ((-1, ny - 1), (1, 0)):
        for u in range(-1, nx + 1):
            steps.append((-1 if u < 0 else 1 if u == nx else 0, dy)), cells.append((u % nx) * ny + v)
        for _ in range(2 * ny - nx - 2):
            steps.append((0, 0)), cells.append(-(1 << 30))
    steps_np = np.asarray(steps, np.int32)
    cells_np = np.asarray(cells, np.int32)
    to_x = me_x + steps_np[:, 0]
    to_y = me_y + steps_np[:, 1]
    inside = (to_x >= 0) & (to_x < count_x) & (to_y >= 0) & (to_y < count_y) & (cells_np >= 0)
    codes = jnp.where(inside, (to_x * count_y + to_y) * slots + cells_np, -1).astype(jnp.int32)[:, None]
    spots = codes.shape[0]

    cot, cot_faces = call(
        to_pairs_kernel, (zeros_like_field, shape((pairs, 2 * nx, PAIR), BF)),
        2 * slots * row_width * PAIR * pairs, 10e6, (pairs,),
        [whole(slots, row_width), by_pair(row_width, PAIR), whole(2 * nx, slots)],
        (by_pair(slots, PAIR), by_pair(2 * nx, PAIR)),
    )(cotangent.reshape(slots, row_width), perm, face)
    cot_halo = exchange(cot, cot_faces, ny)

    band = shape((36 * LANES, PAIR), BF)
    w1, w2, f1, f2 = call(band_kernel, (band,) * 4, 1e9, 12e6)(first_weight, second_weight)

    mask, take, put = call(
        functools.partial(mask_kernel, cap, slots),
        (shape((spots, LANES), F32), shape((buffers, slots), BF), shape((slots, buffers), BF)),
        1e8, 1e6,
    )(route_all, route_all - (me_x * count_y + me_y) * slots, codes)

    halo_specs = [
        whole(pairs, slots, PAIR), whole(pairs, ny, PAIR), whole(pairs, ny, PAIR),
        whole(pairs, nx + 2, PAIR), whole(pairs, nx + 2, PAIR),
    ]
    mask_spec = whole(spots, LANES)
    band_spec = whole(36 * LANES, PAIR)
    field_spec = by_pair(slots, PAIR)

    act_grad, outer = call(
        act_grad_kernel, (shape((pairs, slots, PAIR), F32), zeros_like_field),
        conv_flops, 7e6, (pairs,),
        halo_specs + [mask_spec, band_spec], (field_spec, field_spec), (ext,),
    )(cot, *cot_halo, mask, f2)

    field, field_faces = call(
        place_kernel, (zeros_like_field, shape((pairs, 2 * nx, PAIR), BF)),
        2 * slots * row_width * PAIR * pairs, 10e6, (pairs,),
        [whole(slots, buffers), whole(buffers, row_width), by_pair(row_width, PAIR), whole(2 * nx, slots)],
        (by_pair(slots, PAIR), by_pair(2 * nx, PAIR)),
        (pltpu.VMEM((slots, row_width), BF),),
    )(put, incoming, perm, face)
    field_halo = exchange(field, field_faces, ny)

    act, hg, faces = call(
        hidden_kernel,
        (zeros_like_field, zeros_like_field, shape((2, pairs, 2 * nx, PAIR), BF)),
        conv_flops, 10e6, (pairs,),
        halo_specs + [mask_spec, band_spec, field_spec, whole(2 * nx, slots)],
        (field_spec, field_spec, pl.BlockSpec((2, 1, 2 * nx, PAIR), lambda k: (0, k, 0, 0))),
        (ext,),
    )(field, *field_halo, mask, w1, act_grad, face)
    act_halo = exchange(act, faces[0], ny)
    hg_halo = exchange(hg, faces[1], ny)

    unit = 16 * count_all
    packed_rows = -(-21 * channels // unit) * unit
    corr_scratch = (
        ext, pltpu.VMEM((PAIR, pairs * slots), BF), pltpu.VMEM((28, channels, LANES), F32),
    )
    corr = call(
        functools.partial(corr_kernel, channels), shape((packed_rows, LANES), BF), conv_flops, 5e6,
        scratch=corr_scratch,
    )

    chunk = packed_rows // count_all

    def spread(part):
        return share(part.reshape(count_all, chunk, LANES))

    first_parts = spread(corr(field, *field_halo, hg))
    second_parts = spread(corr(act, *act_halo, outer))

    rows_acc = pltpu.VMEM((slots, row_width), F32)
    back = call(
        grid_grad_kernel, shape((buffers, row_width), BF), 1.5 * conv_flops, 14e6, (pairs,),
        halo_specs + [band_spec, field_spec, by_pair(row_width, PAIR), whole(buffers, slots)],
        whole(buffers, row_width), (ext, rows_acc),
    )(hg, *hg_halo, f1, outer, perm, take)
    returned = lax.all_to_all(
        back.reshape(count_all, cap, row_width), axes, split_axis=0, concat_axis=0, tiled=True
    ).reshape(buffers, row_width)

    block_output = call(
        block_kernel, shape((slots, row_width), BF), 1.5 * conv_flops, 14e6, (pairs,),
        halo_specs + [mask_spec, band_spec, field_spec, by_pair(row_width, PAIR)],
        whole(slots, row_width), (ext, rows_acc),
    )(act, *act_halo, mask, w2, field, perm)

    feature_grads = call(
        functools.partial(collect_kernel, cap, slots), shape((shard_rows, row_width), BF),
        2 * buffers * shard_rows * row_width, 3 * shard_rows * row_width * 2,
    )(route_row, route_col, returned)

    factor = float(1.0 / np.sqrt(np.float32(count_all * shard_rows * depth)))
    sums = share(call(
        chunk_sum_kernel, shape((count_all, 2, chunk, LANES), BF), 1e6, 2e6,
    )(first_parts, second_parts))
    grads = shape(first_weight.shape, F32)
    first_grad, second_grad = call(
        functools.partial(unpack_kernel, factor), (grads, grads), 1e6, 4e6,
        scratch=(pltpu.VMEM((packed_rows, LANES), F32),),
    )(sums)
    return (
        block_output.reshape(nx, ny, row_width), feature_grads, first_grad, second_grad,
    )


def solution(mesh):
    in_specs = (P(("rx", "ry"), None), P(("rx", "ry")), P("rx", "ry", None), P(), P())
    out_specs = (P("rx", "ry", None), P(("rx", "ry"), None), P(), P())
    return jax.shard_map(
        on_device, mesh=mesh, in_specs=in_specs, out_specs=out_specs, check_vma=False
    )
```

```python
import functools

import jax
import jax.numpy as jnp
import numpy as np
from jax import lax
from jax.experimental import pallas as pl
from jax.experimental.pallas import tpu as pltpu
from jax.sharding import PartitionSpec as P

LANES = 128
PAIR = 256
MIB = 1024 * 1024
BF = jnp.bfloat16
F32 = jnp.float32


def call(body, out_shape, flops, moved, scratch=(), room=16, **extra):
    return pl.pallas_call(
        body,
        out_shape=out_shape,
        scratch_shapes=list(scratch),
        compiler_params=pltpu.CompilerParams(vmem_limit_bytes=room * MIB),
        cost_estimate=pl.CostEstimate(flops=int(flops), bytes_accessed=int(moved), transcendentals=0),
        **extra,
    )


def dot(left, right):
    return jnp.dot(left, right, preferred_element_type=F32)


def dot_nt(left, right):
    return lax.dot_general(left, right, (((1,), (1,)), ((), ())), preferred_element_type=F32)


def send_kernel(cap, slots, row_ref, col_ref, feat_ref, out_ref):
    rows = feat_ref.shape[0]
    owner_row = row_ref[...] // slots
    owner_col = col_ref[...] // slots
    first = lax.broadcasted_iota(jnp.int32, (rows, rows), 0)
    second = lax.broadcasted_iota(jnp.int32, (rows, rows), 1)
    same = jnp.where((owner_col == owner_row) & (first < second), 1.0, 0.0)
    rank = jnp.sum(same, axis=0, keepdims=True)
    pos = owner_row.astype(F32) * cap + rank
    place = lax.broadcasted_iota(jnp.int32, (out_ref.shape[0], rows), 0).astype(F32)
    hot = jnp.where(place == pos, 1.0, 0.0).astype(BF)
    out_ref[...] = dot(hot, feat_ref[...]).astype(BF)


def collect_kernel(cap, slots, row_ref, col_ref, back_ref, out_ref):
    rows = out_ref.shape[0]
    owner_row = row_ref[...] // slots
    owner_col = col_ref[...] // slots
    first = lax.broadcasted_iota(jnp.int32, (rows, rows), 0)
    second = lax.broadcasted_iota(jnp.int32, (rows, rows), 1)
    same = jnp.where((owner_col == owner_row) & (second < first), 1.0, 0.0)
    rank = jnp.sum(same, axis=1, keepdims=True)
    pos = owner_col.astype(F32) * cap + rank
    place = lax.broadcasted_iota(jnp.int32, (rows, back_ref.shape[0]), 1).astype(F32)
    hot = jnp.where(place == pos, 1.0, 0.0).astype(BF)
    out_ref[...] = dot(hot, back_ref[...]).astype(BF)


def mask_kernel(cap, slots, route_ref, rel_ref, codes_ref, mask_ref, take_ref, put_ref):
    count, rows = route_ref.shape
    total = mask_ref.shape[0]
    codes = jnp.broadcast_to(codes_ref[...], (total, rows))
    hits = jnp.zeros((total, rows), F32)
    for s in range(count):
        hits = hits + jnp.where(codes == route_ref[s : s + 1, :], 1.0, 0.0)
    mask_ref[...] = jnp.broadcast_to(jnp.sum(hits, axis=1, keepdims=True), (total, LANES))
    rel = rel_ref[...]
    mine = (rel >= 0) & (rel < slots)
    mine_f = jnp.where(mine, 1.0, 0.0)
    slot_f = jnp.where(mine, rel, 0).astype(F32)
    first = lax.broadcasted_iota(jnp.int32, (rows, rows), 0)
    second = lax.broadcasted_iota(jnp.int32, (rows, rows), 1)
    tri = jnp.where(first < second, 1.0, 0.0).astype(BF)
    rank = dot(mine_f.astype(BF), tri)
    lane = lax.broadcasted_iota(jnp.int32, (count, LANES), 1)
    held = jnp.zeros((count, LANES), F32)
    for j in range(cap):
        here = jnp.where(rank == j, mine_f, 0.0)
        number = jnp.sum(here, axis=1, keepdims=True)
        value = jnp.sum(here * slot_f, axis=1, keepdims=True)
        value = value + (1.0 - number) * slots
        held = jnp.where(lane == j, value, held)
    buffers = count * cap
    place = lax.broadcasted_iota(jnp.int32, (buffers, count), 0)
    source = lax.broadcasted_iota(jnp.int32, (buffers, count), 1)
    spread = jnp.where(place // cap == source, 1.0, 0.0).astype(BF)
    wide = dot(spread, held.astype(BF))
    place = lax.broadcasted_iota(jnp.int32, (buffers, LANES), 0)
    lane = lax.broadcasted_iota(jnp.int32, (buffers, LANES), 1)
    slot_col = jnp.sum(jnp.where(place % cap == lane, wide, 0.0), axis=1, keepdims=True)
    slot_id = lax.broadcasted_iota(jnp.int32, (buffers, slots), 1).astype(F32)
    take = jnp.where(slot_col == slot_id, 1.0, 0.0)
    take_ref[...] = take.astype(BF)
    put_ref[...] = take.T.astype(BF)


GROUP = 16
FOLD = LANES // GROUP


def permutation(channels, depth):
    perm = np.zeros((channels // GROUP, PAIR, PAIR), np.float32)
    for i in range(channels // GROUP):
        for j in range(GROUP):
            for z in range(depth):
                perm[i, depth * j + z, LANES * (z // FOLD) + GROUP * ((z + i) % FOLD) + j] = 1.0
    return perm


def lane_group(rows):
    return lax.broadcasted_iota(jnp.int32, (rows, LANES), 1) // GROUP


def spread_pairs(turned_ref, out_ref):
    chunks, rows, _ = turned_ref.shape
    step = 32
    group = lane_group(step)

    def body(t, carry):
        at = pl.ds(pl.multiple_of(t * step, step), step)
        for half in range(2):
            lanes = slice(half * LANES, (half + 1) * LANES)
            parts = [turned_ref[i, at, lanes] for i in range(chunks)]
            parts = parts + [jnp.zeros((step, LANES), F32)] * (FOLD - chunks)
            for bit in (1, 2, 4):
                odd = (group & bit) != 0
                parts = [jnp.where(odd, parts[(i + bit) % FOLD], parts[i]) for i in range(FOLD)]
            for g in range(FOLD):
                value = parts[(-g) % FOLD]
                if g:
                    value = pltpu.roll(value, LANES - GROUP * g, 1)
                z = half * FOLD + g
                out_ref[z // 2, at, (z % 2) * LANES : (z % 2 + 1) * LANES] = value.astype(BF)
        return carry

    lax.fori_loop(0, rows // step, body, 0)


def gather_pairs(in_ref, turned_ref):
    chunks, rows, _ = turned_ref.shape
    step = 32
    group = lane_group(step)

    def body(t, carry):
        at = pl.ds(pl.multiple_of(t * step, step), step)
        for half in range(2):
            turned = []
            for g in range(FOLD):
                z = half * FOLD + g
                value = in_ref[z // 2, at, (z % 2) * LANES : (z % 2 + 1) * LANES].astype(F32)
                turned.append(pltpu.roll(value, GROUP * g, 1) if g else value)
            parts = [turned[(-i) % FOLD] for i in range(FOLD)]
            for bit in (1, 2, 4):
                odd = (group & bit) != 0
                parts = [jnp.where(odd, parts[(i - bit) % FOLD], parts[i]) for i in range(FOLD)]
            for i in range(chunks):
                turned_ref[i, at, half * LANES : (half + 1) * LANES] = parts[i].astype(BF)
        return carry

    lax.fori_loop(0, rows // step, body, 0)


def to_pairs_kernel(rows_ref, perm_ref, out_ref, turned_ref):
    for i in range(perm_ref.shape[0]):
        turned_ref[i] = dot(rows_ref[:, i * PAIR : (i + 1) * PAIR], perm_ref[i])
    spread_pairs(turned_ref, out_ref)


def place_kernel(put_ref, rows_ref, perm_ref, out_ref, turned_ref):
    put = put_ref[...]
    for i in range(perm_ref.shape[0]):
        held = dot(put, rows_ref[:, i * PAIR : (i + 1) * PAIR]).astype(BF)
        turned_ref[i] = dot(held, perm_ref[i])
    spread_pairs(turned_ref, out_ref)


def message_kernel(f_ref, xlo_ref, xhi_ref, pick_ref, low_ref, high_ref):
    pick = pick_ref[...]
    half = low_ref.shape[1]
    for k in range(f_ref.shape[0]):
        rows = jnp.concatenate([xlo_ref[k], f_ref[k], xhi_ref[k]], axis=0)
        sent = dot(pick, rows).astype(BF)
        low_ref[k] = sent[0:half]
        high_ref[k] = sent[half : 2 * half]


def band_kernel(first_ref, second_ref, w1_ref, w2_ref, f1_ref, f2_ref):
    channels = first_ref.shape[1]
    for ref in (w1_ref, w2_ref, f1_ref, f2_ref):
        ref[...] = jnp.zeros_like(ref)
    for a in range(3):
        for b in range(3):
            for c in range(3):
                tap = 9 * a + 3 * b + c
                back = 26 - tap
                parts = (
                    (w1_ref, first_ref[tap].T),
                    (w2_ref, second_ref[tap].T),
                    (f1_ref, first_ref[back]),
                    (f2_ref, second_ref[back]),
                )
                for zo in range(2):
                    row = ((a * 3 + b) * 4 + zo + c) * LANES
                    for ref, value in parts:
                        ref[row : row + channels, zo * LANES : zo * LANES + channels] = value


NX = 16
NY = 16
OUT_MAIN = (NX + 2) * NY
EDGE = 24
OUT_ROWS = OUT_MAIN + 2 * EDGE
MSG = 48
M_XLO = NX * NY
M_XHI = M_XLO + 2 * NY
M_YLO = M_XHI + 2 * NY
M_YHI = M_YLO + MSG
M_LOW = M_YHI + MSG
M_HIGH = M_LOW + MSG
M_EDGE = M_HIGH + MSG
M_ROWS = M_EDGE + 2 * EDGE


def twice(value):
    return jnp.concatenate([value, value], axis=1)


def put_pair(ref, lead, k, tail, value):
    value = value.astype(BF)
    ref[lead + (k,) + tail + (slice(LANES, PAIR),)] = value[:, 0:LANES]
    ref[lead + (k + 1,) + tail + (slice(0, LANES),)] = value[:, LANES:PAIR]


def clear_ends(ref, lead):
    last = ref.shape[len(lead)] - 1
    dims = ref.shape[len(lead) + 1 : -1]
    ref[lead + (0,) + (slice(None),) * len(dims) + (slice(0, LANES),)] = jnp.zeros(dims + (LANES,), BF)
    ref[lead + (last,) + (slice(None),) * len(dims) + (slice(LANES, PAIR),)] = jnp.zeros(dims + (LANES,), BF)


def put_shifted(ext_ref, k, xp, mid, before, after, row):
    ny = mid.shape[0]
    up = jnp.where(row == 0, before, pltpu.roll(mid, 1, 0))
    down = jnp.where(row == ny - 1, after, pltpu.roll(mid, ny - 1, 0))
    for b, value in enumerate((up, mid, down)):
        put_pair(ext_ref, (b,), k, (xp, slice(None)), value)


def widen_two(ext_ref, edge_ref, f_ref, xlo_ref, xhi_ref, ylo_ref, yhi_ref, low_ref, high_ref, mask_ref=None):
    pairs = f_ref.shape[0]
    for b in range(3):
        clear_ends(ext_ref, (b,))
        for a in range(3):
            clear_ends(edge_ref, (a, b))
    row = lax.broadcasted_iota(jnp.int32, (NY, PAIR), 0)

    def read(ref, k, start, size, mask_start):
        value = ref[k, start : start + size, :].astype(F32)
        if mask_ref is None:
            return value
        return value * twice(mask_ref[mask_start + start : mask_start + start + size, :])

    def body(k, carry):
        ylo = read(ylo_ref, k, 0, MSG, M_YLO)
        yhi = read(yhi_ref, k, 0, MSG, M_YHI)
        low = read(low_ref, k, 0, MSG, M_LOW)
        high = read(high_ref, k, 0, MSG, M_HIGH)
        wide = NX + 4
        for xp in range(wide):
            if xp < 2:
                mid = read(xlo_ref, k, xp * NY, NY, M_XLO)
            elif xp >= NX + 2:
                mid = read(xhi_ref, k, (xp - NX - 2) * NY, NY, M_XHI)
            else:
                mid = read(f_ref, k, (xp - 2) * NY, NY, 0)
            put_shifted(ext_ref, k, xp, mid, ylo[wide + xp : wide + xp + 1, :], yhi[xp : xp + 1, :], row)
        first = ((ylo, 0), (ylo, wide), (low, 0))
        second = ((high, wide), (yhi, 0), (yhi, wide))
        for a in range(3):
            for b in range(3):
                sides = []
                for value, start in (first[b], second[b]):
                    turn = start + a
                    if turn:
                        value = pltpu.roll(value, MSG - turn, 0)
                    sides.append(value[0:EDGE])
                put_pair(edge_ref, (a, b), k, (slice(None),), jnp.concatenate(sides, axis=0))
        return carry

    lax.fori_loop(0, pairs, body, 0)


def widen_one(ext_ref, rows_ref):
    pairs = rows_ref.shape[0]
    for b in range(3):
        clear_ends(ext_ref, (b,))
    row = lax.broadcasted_iota(jnp.int32, (NY, PAIR), 0)

    def body(k, carry):
        edges = rows_ref[k, OUT_MAIN:OUT_ROWS, :].astype(F32)
        for xp in range(NX + 2):
            mid = rows_ref[k, xp * NY : (xp + 1) * NY, :].astype(F32)
            put_shifted(ext_ref, k, xp, mid, edges[xp : xp + 1, :], edges[EDGE + xp : EDGE + xp + 1, :], row)
        return carry

    lax.fori_loop(0, pairs, body, 0)


def conv_wide(ext_ref, edge_ref, w_ref, k):
    pieces = []
    for a in range(3):
        for b in range(3):
            for j in range(2):
                main = ext_ref[b, k + j, a : a + NX + 2].reshape(OUT_MAIN, PAIR)
                pieces.append(jnp.concatenate([main, edge_ref[a, b, k + j]], axis=0))
    return dot(jnp.concatenate(pieces, axis=1), w_ref[...])


def conv_inner(ext_ref, w_ref, k):
    pieces = []
    for a in range(3):
        for b in range(3):
            for j in range(2):
                pieces.append(ext_ref[b, k + j, a : a + NX].reshape(NX * NY, PAIR))
    return dot(jnp.concatenate(pieces, axis=1), w_ref[...])


def out_mask(mask_ref):
    return twice(jnp.concatenate([
        mask_ref[M_XLO + NY : M_XLO + 2 * NY, :], mask_ref[0 : NX * NY, :],
        mask_ref[M_XHI : M_XHI + NY, :], mask_ref[M_EDGE:M_ROWS, :],
    ], axis=0))


def outer_kernel(f_ref, xlo_ref, xhi_ref, ylo_ref, yhi_ref, low_ref, high_ref, mask_ref, w_ref,
                 out_ref, outer_ref, ext_ref, edge_ref):
    widen_two(ext_ref, edge_ref, f_ref, xlo_ref, xhi_ref, ylo_ref, yhi_ref, low_ref, high_ref, mask_ref)

    def body(k, carry):
        out_ref[k] = conv_wide(ext_ref, edge_ref, w_ref, k)
        outer_ref[k] = (f_ref[k].astype(F32) * twice(mask_ref[0 : NX * NY, :])).astype(BF)
        return carry

    lax.fori_loop(0, f_ref.shape[0], body, 0)


def correlate(gt_ref, ext_ref, first_x, taps_ref, channels):
    pairs = ext_ref.shape[1] - 1

    def body(ab, carry):
        a = ab // 3
        b = ab % 3
        left = gt_ref[...]
        near = dot(left, ext_ref[b, 0:pairs, pl.ds(a + first_x, NX)].reshape(pairs * NX * NY, PAIR))
        far = dot(left, ext_ref[b, 1 : pairs + 1, pl.ds(a + first_x, NX)].reshape(pairs * NX * NY, PAIR))
        low = slice(0, channels)
        high = slice(LANES, LANES + channels)
        taps_ref[3 * ab] = near[low, 0:LANES] + near[high, LANES:PAIR]
        taps_ref[3 * ab + 1] = near[low, LANES:PAIR] + far[high, 0:LANES]
        taps_ref[3 * ab + 2] = far[low, 0:LANES] + far[high, LANES:PAIR]
        return carry

    lax.fori_loop(0, 9, body, 0)


def pack_taps(taps_ref, packed_ref, channels):
    lane = lax.broadcasted_iota(jnp.int32, (channels, LANES), 1)
    for g in range(7):
        t1 = pltpu.roll(taps_ref[4 * g + 1], 96, 1)
        t2 = pltpu.roll(taps_ref[4 * g + 2], 64, 1)
        t3 = pltpu.roll(taps_ref[4 * g + 3], 32, 1)
        blocks = (
            jnp.where(lane < 96, taps_ref[4 * g], t1),
            jnp.where(lane < 64, t1, t2),
            jnp.where(lane < 32, t2, t3),
        )
        for i, value in enumerate(blocks):
            start = (3 * g + i) * channels
            packed_ref[start : start + channels, :] = value
    rest = packed_ref.shape[0] - 21 * channels
    if rest:
        packed_ref[21 * channels :, :] = jnp.zeros((rest, LANES), F32)


def main_kernel(channels, core_ref, f_ref, xlo_ref, xhi_ref, ylo_ref, yhi_ref, low_ref, high_ref, mask_ref, w_ref,
                grad_ref, outer_ref, hg_ref, wide_ref, keep_ref, give_ref,
                ext_ref, edge_ref, act_ref, gt_ref, taps_ref, packed_ref):
    pairs = f_ref.shape[0]
    inner = NX * NY
    widen_two(ext_ref, edge_ref, f_ref, xlo_ref, xhi_ref, ylo_ref, yhi_ref, low_ref, high_ref)

    def body(k, carry):
        m = out_mask(mask_ref)
        hidden = m * conv_wide(ext_ref, edge_ref, w_ref, k)
        sigma = jax.nn.sigmoid(hidden)
        act_ref[k] = (hidden * sigma).astype(BF)
        hg_ref[k] = (m * grad_ref[k] * sigma * (1.0 + hidden * (1.0 - sigma))).astype(BF)
        return carry

    lax.fori_loop(0, pairs, body, 0)
    half = keep_ref.shape[1]
    mine = pl.ds(pl.multiple_of(core_ref[0] * half, half), half)
    other = pl.ds(pl.multiple_of((1 - core_ref[0]) * half, half), half)
    taps_ref[27] = jnp.zeros((channels, LANES), F32)
    for k in range(pairs):
        gt_ref[:, k * inner : (k + 1) * inner] = hg_ref[k, NY : NY + inner, :].T
    correlate(gt_ref, ext_ref, 1, taps_ref, channels)
    pack_taps(taps_ref, packed_ref, channels)
    keep_ref[0] = packed_ref[mine, :]
    give_ref[0] = packed_ref[other, :]
    widen_one(wide_ref, act_ref)
    for k in range(pairs):
        gt_ref[:, k * inner : (k + 1) * inner] = outer_ref[k].T
    correlate(gt_ref, wide_ref, 0, taps_ref, channels)
    pack_taps(taps_ref, packed_ref, channels)
    keep_ref[1] = packed_ref[mine, :]
    give_ref[1] = packed_ref[other, :]


def grid_grad_kernel(hg_ref, w_ref, outer_ref, perm_ref, take_ref, out_ref, ext_ref, sum_ref, turned_ref):
    widen_one(ext_ref, hg_ref)

    def body(k, carry):
        sum_ref[k] = (outer_ref[k].astype(F32) + conv_inner(ext_ref, w_ref, k)).astype(BF)
        return carry

    lax.fori_loop(0, outer_ref.shape[0], body, 0)
    gather_pairs(sum_ref, turned_ref)
    take = take_ref[...]
    for i in range(perm_ref.shape[0]):
        rows = dot_nt(turned_ref[i], perm_ref[i]).astype(BF)
        out_ref[:, i * PAIR : (i + 1) * PAIR] = dot(take, rows).astype(BF)


def block_kernel(ext_ref, mask_ref, w_ref, field_ref, perm_ref, out_ref, sum_ref, turned_ref):
    def body(k, carry):
        m = twice(mask_ref[0 : NX * NY, :])
        sum_ref[k] = (field_ref[k].astype(F32) + m * conv_inner(ext_ref, w_ref, k)).astype(BF)
        return carry

    lax.fori_loop(0, field_ref.shape[0], body, 0)
    gather_pairs(sum_ref, turned_ref)
    for i in range(perm_ref.shape[0]):
        out_ref[:, i * PAIR : (i + 1) * PAIR] = dot_nt(turned_ref[i], perm_ref[i]).astype(BF)


def pair_sum_kernel(keep_ref, got_ref, out_ref):
    count, _, chunk, _ = out_ref.shape
    for i in range(2):
        for s in range(count):
            rows = slice(s * chunk, (s + 1) * chunk)
            out_ref[s, i] = (keep_ref[i, rows, :] + got_ref[i, rows, :]).astype(BF)


def chunk_sum_kernel(in_ref, out_ref):
    count = in_ref.shape[0]
    for i in range(2):
        total = in_ref[0, i].astype(F32)
        for s in range(1, count):
            total = total + in_ref[s, i].astype(F32)
        total = total.astype(BF)
        for s in range(count):
            out_ref[s, i] = total


def unpack_kernel(factor, core_ref, mine_ref, other_ref, first_ref, second_ref, flat_ref):
    count, _, chunk, _ = mine_ref.shape
    half = count * chunk
    for i, out_ref in enumerate((first_ref, second_ref)):
        for s in range(count):
            start = core_ref[0] * half + s * chunk
            flat_ref[pl.ds(pl.multiple_of(start, chunk), chunk), :] = mine_ref[s, i].astype(F32)
            start = (1 - core_ref[0]) * half + s * chunk
            flat_ref[pl.ds(pl.multiple_of(start, chunk), chunk), :] = other_ref[s, i].astype(F32)
        unpack_taps(factor, flat_ref, out_ref)


def unpack_taps(factor, packed_ref, out_ref):
    channels = out_ref.shape[1]
    lane = lax.broadcasted_iota(jnp.int32, (channels, LANES), 1)
    for g in range(7):
        v = []
        for i in range(3):
            start = (3 * g + i) * channels
            v.append(packed_ref[start : start + channels, :] * factor)
        taps = (
            v[0],
            pltpu.roll(jnp.where(lane < 64, v[1], v[0]), 32, 1),
            pltpu.roll(jnp.where(lane < 32, v[2], v[1]), 64, 1),
            pltpu.roll(v[2], 96, 1),
        )
        for u in range(4):
            if 4 * g + u < 27:
                out_ref[4 * g + u] = taps[u][:, 0:channels]


RX = ("cx", "core")
ALL = ("cx", "core", "ry")
SAME_CORE = ("cx", "ry")


def size_of(axes):
    return int(np.prod([lax.axis_size(a) for a in ((axes,) if isinstance(axes, str) else axes)]))


def share(parts, axes):
    return lax.all_to_all(parts, axes, split_axis=0, concat_axis=0, tiled=True)


def neighbours(axes, upper, lower):
    count = size_of(axes)
    ahead = [(i, i + 1) for i in range(count - 1)]
    behind = [(t, s) for s, t in ahead]
    return lax.ppermute(upper, axes, ahead), lax.ppermute(lower, axes, behind)


def swap_cores(value):
    count = size_of(RX)
    return lax.ppermute(value, RX, [(i, i ^ 1) for i in range(count)])


def message_rows():
    cells = []
    for ys in ((0, 1), (NY - 2, NY - 1)):
        for y in ys:
            cells += [(x, y) for x in range(-2, NX + 2)]
        cells += [None] * (MSG - 2 * (NX + 4))
    return cells


def exchange(field, pick):
    pairs = field.shape[0]
    xlo, xhi = neighbours(RX, field[:, (NX - 2) * NY :, :], field[:, : 2 * NY, :])
    message = jax.ShapeDtypeStruct((pairs, MSG, PAIR), BF)
    low, high = call(message_kernel, (message, message), 5e8, 3e6)(field, xlo, xhi, pick)
    ylo, yhi = neighbours("ry", high, low)
    return xlo, xhi, ylo, yhi, low, high


def mask_cells():
    cells = [(x, y) for x in range(NX) for y in range(NY)]
    cells += [(x, y) for x in (-2, -1) for y in range(NY)]
    cells += [(x, y) for x in (NX, NX + 1) for y in range(NY)]
    for ys in ((-2, -1), (NY, NY + 1), (0, 1), (NY - 2, NY - 1)):
        for y in ys:
            cells += [(x, y) for x in range(-2, NX + 2)]
        cells += [None] * (MSG - 2 * (NX + 4))
    for y in (-1, NY):
        cells += [(x, y) for x in range(-1, NX + 1)]
        cells += [None] * (EDGE - NX - 2)
    return cells


def on_device(column_features, column_route, cotangent, first_weight, second_weight):
    count_x = size_of(RX)
    count_y = size_of("ry")
    count_all = count_x * count_y
    shard_rows, row_width = column_features.shape
    channels = first_weight.shape[1]
    depth = row_width // channels
    slots = NX * NY
    pairs = depth // 2
    chunks = channels // GROUP
    cap = 2 * shard_rows // count_all
    buffers = count_all * cap
    me_x = lax.axis_index(RX)
    me_y = lax.axis_index("ry")
    core = lax.axis_index("core").astype(jnp.int32).reshape(1)
    conv_flops = 2 * slots * pairs * 36 * LANES * PAIR

    shape = jax.ShapeDtypeStruct
    field_shape = shape((pairs, slots, PAIR), BF)
    wide_shape = shape((pairs, OUT_ROWS, PAIR), BF)
    ext = pltpu.VMEM((3, pairs + 1, NX + 4, NY, PAIR), BF)
    edge = pltpu.VMEM((3, 3, pairs + 1, 2 * EDGE, PAIR), BF)
    turned = pltpu.VMEM((chunks, slots, PAIR), F32)
    turned_low = pltpu.VMEM((chunks, slots, PAIR), BF)
    sums = pltpu.VMEM((pairs, slots, PAIR), BF)

    perm = jnp.asarray(permutation(channels, depth), BF)
    pick_np = np.zeros((2 * MSG, (NX + 4) * NY), np.float32)
    for r, cell in enumerate(message_rows()):
        if cell is not None:
            pick_np[r, (cell[0] + 2) * NY + cell[1]] = 1.0
    pick = jnp.asarray(pick_np, BF)

    route_row = column_route.reshape(1, shard_rows)
    route_col = column_route.reshape(shard_rows, 1)
    route_all = share(jnp.broadcast_to(route_row, (count_all, shard_rows)), ALL)
    outgoing = call(
        functools.partial(send_kernel, cap, slots), shape((buffers, row_width), BF),
        2 * buffers * shard_rows * row_width, 3 * shard_rows * row_width * 2,
    )(route_row, route_col, column_features)
    incoming = share(outgoing.reshape(count_all, cap, row_width), ALL).reshape(buffers, row_width)

    cells = mask_cells()
    steps = np.asarray([(0, 0) if c is None else (c[0] // NX, c[1] // NY) for c in cells], np.int32)
    local = np.asarray([-1 if c is None else (c[0] % NX) * NY + c[1] % NY for c in cells], np.int32)
    to_x = me_x + steps[:, 0]
    to_y = me_y + steps[:, 1]
    inside = (to_x >= 0) & (to_x < count_x) & (to_y >= 0) & (to_y < count_y) & (local >= 0)
    codes = jnp.where(inside, (to_x * count_y + to_y) * slots + local, -1).astype(jnp.int32)[:, None]

    cot = call(
        to_pairs_kernel, field_shape, 1e9, 3e6, (turned,),
    )(cotangent.reshape(slots, row_width), perm)
    cot_halo = exchange(cot, pick)

    band = shape((36 * LANES, PAIR), BF)
    w1, w2, f1, f2 = call(band_kernel, (band,) * 4, 1e9, 3e6)(first_weight, second_weight)

    mask, take, put = call(
        functools.partial(mask_kernel, cap, slots),
        (shape((M_ROWS, LANES), F32), shape((buffers, slots), BF), shape((slots, buffers), BF)),
        1e8, 1e6,
    )(route_all, route_all - (me_x * count_y + me_y) * slots, codes)

    act_grad, outer = call(
        outer_kernel, (shape((pairs, OUT_ROWS, PAIR), F32), field_shape),
        1.3 * conv_flops, 7e6, (ext, edge), 20,
    )(cot, *cot_halo, mask, f2)

    field = call(
        place_kernel, field_shape, 1e9, 3e6, (turned,),
    )(put, incoming, perm)
    field_halo = exchange(field, pick)

    unit = 16 * count_all
    packed_rows = -(-21 * channels // unit) * unit
    half = packed_rows // 2
    chunk = packed_rows // count_all
    smem = pl.BlockSpec(memory_space=pltpu.SMEM)
    vmem = pl.BlockSpec(memory_space=pltpu.VMEM)
    half_shape = shape((2, half, LANES), F32)
    hg, act_wide, keep, give = call(
        functools.partial(main_kernel, channels),
        (wide_shape, shape((3, pairs + 1, NX + 2, NY, PAIR), BF), half_shape, half_shape),
        3.3 * conv_flops, 10e6,
        (
            ext, edge, pltpu.VMEM((pairs, OUT_ROWS, PAIR), BF), pltpu.VMEM((PAIR, pairs * slots), BF),
            pltpu.VMEM((28, channels, LANES), F32), pltpu.VMEM((packed_rows, LANES), F32),
        ),
        28, in_specs=[smem] + [vmem] * 11,
    )(core, field, *field_halo, mask, w1, act_grad, outer)

    got = swap_cores(give)
    back = call(
        grid_grad_kernel, shape((buffers, row_width), BF), 1.2 * conv_flops, 6e6,
        (pltpu.VMEM((3, pairs + 1, NX + 2, NY, PAIR), BF), sums, turned_low),
    )(hg, f1, outer, perm, take)
    parts = share(call(
        pair_sum_kernel, shape((count_all // 2, 2, chunk, LANES), BF), 1e6, 2e6,
    )(keep, got), SAME_CORE)
    returned = share(back.reshape(count_all, cap, row_width), ALL).reshape(buffers, row_width)

    totals = share(call(
        chunk_sum_kernel, shape((count_all // 2, 2, chunk, LANES), BF), 1e6, 1e6,
    )(parts), SAME_CORE)
    block_output = call(
        block_kernel, shape((slots, row_width), BF), 1.2 * conv_flops, 8e6, (sums, turned_low),
    )(act_wide, mask, w2, field, perm)

    feature_grads = call(
        functools.partial(collect_kernel, cap, slots), shape((shard_rows, row_width), BF),
        2 * buffers * shard_rows * row_width, 3 * shard_rows * row_width * 2,
    )(route_row, route_col, returned)

    factor = float(1.0 / np.sqrt(np.float32(count_all * shard_rows * depth)))
    grads = shape(first_weight.shape, F32)
    first_grad, second_grad = call(
        functools.partial(unpack_kernel, factor), (grads, grads), 1e6, 4e6,
        (pltpu.VMEM((packed_rows, LANES), F32),), in_specs=[smem, vmem, vmem],
    )(core, totals, swap_cores(totals))
    return (block_output.reshape(cotangent.shape), feature_grads, first_grad, second_grad)


def solution(mesh):
    count_x = mesh.shape["rx"]
    fine = jax.sharding.Mesh(mesh.devices.reshape(count_x // 2, 2, mesh.shape["ry"]), ALL)
    in_specs = (P(ALL, None), P(ALL), P(RX, "ry", None), P(), P())
    out_specs = (P(RX, "ry", None), P(ALL, None), P(), P())
    return jax.shard_map(
        on_device, mesh=fine, in_specs=in_specs, out_specs=out_specs, check_vma=False
    )
```

```python
import functools

import jax
import jax.numpy as jnp
import numpy as np
from jax import lax
from jax.experimental import pallas as pl
from jax.experimental.pallas import tpu as pltpu
from jax.sharding import PartitionSpec as P

LANES = 128
PAIR = 256
MIB = 1024 * 1024
ROOM_WIDE, ROOM_NEAR, ROOM_CORR, ROOM_SMALL = 16, 12, 14, 5
BF = jnp.bfloat16
F32 = jnp.float32


def call(body, out_shape, flops, moved, scratch=(), room=ROOM_SMALL, **extra):
    return pl.pallas_call(
        body,
        out_shape=out_shape,
        scratch_shapes=list(scratch),
        compiler_params=pltpu.CompilerParams(vmem_limit_bytes=room * MIB),
        cost_estimate=pl.CostEstimate(flops=int(flops), bytes_accessed=int(moved), transcendentals=0),
        **extra,
    )


def dot(left, right):
    return jnp.dot(left, right, preferred_element_type=F32)


def dot_nt(left, right):
    return lax.dot_general(left, right, (((1,), (1,)), ((), ())), preferred_element_type=F32)


def send_kernel(cap, slots, row_ref, col_ref, feat_ref, out_ref):
    rows = feat_ref.shape[0]
    owner_row = row_ref[...] // slots
    owner_col = col_ref[...] // slots
    first = lax.broadcasted_iota(jnp.int32, (rows, rows), 0)
    second = lax.broadcasted_iota(jnp.int32, (rows, rows), 1)
    same = jnp.where((owner_col == owner_row) & (first < second), 1.0, 0.0)
    rank = jnp.sum(same, axis=0, keepdims=True)
    pos = owner_row.astype(F32) * cap + rank
    place = lax.broadcasted_iota(jnp.int32, (out_ref.shape[0], rows), 0).astype(F32)
    hot = jnp.where(place == pos, 1.0, 0.0).astype(BF)
    out_ref[...] = dot(hot, feat_ref[...]).astype(BF)


def collect_kernel(cap, slots, row_ref, col_ref, back_ref, out_ref):
    rows = out_ref.shape[0]
    owner_row = row_ref[...] // slots
    owner_col = col_ref[...] // slots
    first = lax.broadcasted_iota(jnp.int32, (rows, rows), 0)
    second = lax.broadcasted_iota(jnp.int32, (rows, rows), 1)
    same = jnp.where((owner_col == owner_row) & (second < first), 1.0, 0.0)
    rank = jnp.sum(same, axis=1, keepdims=True)
    pos = owner_col.astype(F32) * cap + rank
    place = lax.broadcasted_iota(jnp.int32, (rows, back_ref.shape[0]), 1).astype(F32)
    hot = jnp.where(place == pos, 1.0, 0.0).astype(BF)
    out_ref[...] = dot(hot, back_ref[...]).astype(BF)


def mask_kernel(cap, slots, route_ref, rel_ref, codes_ref, mask_ref, take_ref, put_ref):
    count, rows = route_ref.shape
    total = mask_ref.shape[0]
    codes = jnp.broadcast_to(codes_ref[...], (total, rows))
    hits = jnp.zeros((total, rows), F32)
    for s in range(count):
        hits = hits + jnp.where(codes == route_ref[s : s + 1, :], 1.0, 0.0)
    mask_ref[...] = jnp.broadcast_to(jnp.sum(hits, axis=1, keepdims=True), (total, LANES))
    rel = rel_ref[...]
    mine = (rel >= 0) & (rel < slots)
    mine_f = jnp.where(mine, 1.0, 0.0)
    slot_f = jnp.where(mine, rel, 0).astype(F32)
    first = lax.broadcasted_iota(jnp.int32, (rows, rows), 0)
    second = lax.broadcasted_iota(jnp.int32, (rows, rows), 1)
    tri = jnp.where(first < second, 1.0, 0.0).astype(BF)
    rank = dot(mine_f.astype(BF), tri)
    lane = lax.broadcasted_iota(jnp.int32, (count, LANES), 1)
    held = jnp.zeros((count, LANES), F32)
    for j in range(cap):
        here = jnp.where(rank == j, mine_f, 0.0)
        number = jnp.sum(here, axis=1, keepdims=True)
        value = jnp.sum(here * slot_f, axis=1, keepdims=True)
        value = value + (1.0 - number) * slots
        held = jnp.where(lane == j, value, held)
    buffers = count * cap
    place = lax.broadcasted_iota(jnp.int32, (buffers, count), 0)
    source = lax.broadcasted_iota(jnp.int32, (buffers, count), 1)
    spread = jnp.where(place // cap == source, 1.0, 0.0).astype(BF)
    wide = dot(spread, held.astype(BF))
    place = lax.broadcasted_iota(jnp.int32, (buffers, LANES), 0)
    lane = lax.broadcasted_iota(jnp.int32, (buffers, LANES), 1)
    slot_col = jnp.sum(jnp.where(place % cap == lane, wide, 0.0), axis=1, keepdims=True)
    slot_id = lax.broadcasted_iota(jnp.int32, (buffers, slots), 1).astype(F32)
    take = jnp.where(slot_col == slot_id, 1.0, 0.0)
    take_ref[...] = take.astype(BF)
    put_ref[...] = take.T.astype(BF)


GROUP = 16
FOLD = LANES // GROUP


def permutation(channels, depth):
    perm = np.zeros((channels // GROUP, PAIR, PAIR), np.float32)
    for i in range(channels // GROUP):
        for j in range(GROUP):
            for z in range(depth):
                perm[i, depth * j + z, LANES * (z // FOLD) + GROUP * ((z + i) % FOLD) + j] = 1.0
    return perm


def lane_group(rows):
    return lax.broadcasted_iota(jnp.int32, (rows, LANES), 1) // GROUP


def spread_pairs(turned_ref, out_ref):
    chunks, rows, _ = turned_ref.shape
    step = 32
    group = lane_group(step)

    def body(t, carry):
        at = pl.ds(pl.multiple_of(t * step, step), step)
        for half in range(2):
            lanes = slice(half * LANES, (half + 1) * LANES)
            parts = [turned_ref[i, at, lanes] for i in range(chunks)]
            parts = parts + [jnp.zeros((step, LANES), F32)] * (FOLD - chunks)
            for bit in (1, 2, 4):
                odd = (group & bit) != 0
                parts = [jnp.where(odd, parts[(i + bit) % FOLD], parts[i]) for i in range(FOLD)]
            for g in range(FOLD):
                value = parts[(-g) % FOLD]
                if g:
                    value = pltpu.roll(value, LANES - GROUP * g, 1)
                z = half * FOLD + g
                out_ref[z // 2, at, (z % 2) * LANES : (z % 2 + 1) * LANES] = value.astype(BF)
        return carry

    lax.fori_loop(0, rows // step, body, 0)


def gather_pairs(in_ref, turned_ref):
    chunks, rows, _ = turned_ref.shape
    step = 32
    group = lane_group(step)

    def body(t, carry):
        at = pl.ds(pl.multiple_of(t * step, step), step)
        for half in range(2):
            turned = []
            for g in range(FOLD):
                z = half * FOLD + g
                value = in_ref[z // 2, at, (z % 2) * LANES : (z % 2 + 1) * LANES].astype(F32)
                turned.append(pltpu.roll(value, GROUP * g, 1) if g else value)
            parts = [turned[(-i) % FOLD] for i in range(FOLD)]
            for bit in (1, 2, 4):
                odd = (group & bit) != 0
                parts = [jnp.where(odd, parts[(i - bit) % FOLD], parts[i]) for i in range(FOLD)]
            for i in range(chunks):
                turned_ref[i, at, half * LANES : (half + 1) * LANES] = parts[i].astype(BF)
        return carry

    lax.fori_loop(0, rows // step, body, 0)


def to_pairs_kernel(rows_ref, perm_ref, out_ref, turned_ref):
    for i in range(perm_ref.shape[0]):
        turned_ref[i] = dot(rows_ref[:, i * PAIR : (i + 1) * PAIR], perm_ref[i])
    spread_pairs(turned_ref, out_ref)


def place_kernel(put_ref, rows_ref, perm_ref, out_ref, turned_ref):
    put = put_ref[...]
    for i in range(perm_ref.shape[0]):
        held = dot(put, rows_ref[:, i * PAIR : (i + 1) * PAIR]).astype(BF)
        turned_ref[i] = dot(held, perm_ref[i])
    spread_pairs(turned_ref, out_ref)


def message_kernel(f_ref, xlo_ref, xhi_ref, pick_ref, low_ref, high_ref):
    pick = pick_ref[...]
    half = low_ref.shape[1]
    for k in range(f_ref.shape[0]):
        rows = jnp.concatenate([xlo_ref[k], f_ref[k], xhi_ref[k]], axis=0)
        sent = dot(pick, rows).astype(BF)
        low_ref[k] = sent[0:half]
        high_ref[k] = sent[half : 2 * half]


def build_band(band_ref, raw_ref, backward):
    channels = raw_ref.shape[1]
    band_ref[...] = jnp.zeros_like(band_ref)
    for tap in range(27):
        value = raw_ref[26 - tap] if backward else raw_ref[tap].T
        for zo in range(2):
            row = ((tap // 3) * 4 + zo + tap % 3) * LANES
            band_ref[row : row + channels, zo * LANES : zo * LANES + channels] = value


NX = 16
NY = 16
OUT_MAIN = (NX + 2) * NY
EDGE = 24
OUT_ROWS = OUT_MAIN + 2 * EDGE
MSG = 48
M_XLO = NX * NY
M_XHI = M_XLO + 2 * NY
M_YLO = M_XHI + 2 * NY
M_YHI = M_YLO + MSG
M_LOW = M_YHI + MSG
M_HIGH = M_LOW + MSG
M_EDGE = M_HIGH + MSG
M_ROWS = M_EDGE + 2 * EDGE


def twice(value):
    return jnp.concatenate([value, value], axis=1)


def put_pair(ref, lead, k, tail, value):
    value = value.astype(BF)
    ref[lead + (k,) + tail + (slice(LANES, PAIR),)] = value[:, 0:LANES]
    ref[lead + (k + 1,) + tail + (slice(0, LANES),)] = value[:, LANES:PAIR]


def clear_ends(ref, lead):
    last = ref.shape[len(lead)] - 1
    dims = ref.shape[len(lead) + 1 : -1]
    ref[lead + (0,) + (slice(None),) * len(dims) + (slice(0, LANES),)] = jnp.zeros(dims + (LANES,), BF)
    ref[lead + (last,) + (slice(None),) * len(dims) + (slice(LANES, PAIR),)] = jnp.zeros(dims + (LANES,), BF)


def put_shifted(ext_ref, k, xp, mid, before, after, row):
    ny = mid.shape[0]
    up = jnp.where(row == 0, before, pltpu.roll(mid, 1, 0))
    down = jnp.where(row == ny - 1, after, pltpu.roll(mid, ny - 1, 0))
    for b, value in enumerate((up, mid, down)):
        put_pair(ext_ref, (b,), k, (xp, slice(None)), value)


def widen_two(ext_ref, edge_ref, f_ref, xlo_ref, xhi_ref, ylo_ref, yhi_ref, low_ref, high_ref, mask_ref=None):
    pairs = f_ref.shape[0]
    for b in range(3):
        clear_ends(ext_ref, (b,))
        for a in range(3):
            clear_ends(edge_ref, (a, b))
    row = lax.broadcasted_iota(jnp.int32, (NY, PAIR), 0)

    def read(ref, k, start, size, mask_start):
        value = ref[k, start : start + size, :].astype(F32)
        if mask_ref is None:
            return value
        return value * twice(mask_ref[mask_start + start : mask_start + start + size, :])

    def body(k, carry):
        ylo = read(ylo_ref, k, 0, MSG, M_YLO)
        yhi = read(yhi_ref, k, 0, MSG, M_YHI)
        low = read(low_ref, k, 0, MSG, M_LOW)
        high = read(high_ref, k, 0, MSG, M_HIGH)
        wide = NX + 4
        for xp in range(wide):
            if xp < 2:
                mid = read(xlo_ref, k, xp * NY, NY, M_XLO)
            elif xp >= NX + 2:
                mid = read(xhi_ref, k, (xp - NX - 2) * NY, NY, M_XHI)
            else:
                mid = read(f_ref, k, (xp - 2) * NY, NY, 0)
            put_shifted(ext_ref, k, xp, mid, ylo[wide + xp : wide + xp + 1, :], yhi[xp : xp + 1, :], row)
        first = ((ylo, 0), (ylo, wide), (low, 0))
        second = ((high, wide), (yhi, 0), (yhi, wide))
        for a in range(3):
            for b in range(3):
                sides = []
                for value, start in (first[b], second[b]):
                    turn = start + a
                    if turn:
                        value = pltpu.roll(value, MSG - turn, 0)
                    sides.append(value[0:EDGE])
                put_pair(edge_ref, (a, b), k, (slice(None),), jnp.concatenate(sides, axis=0))
        return carry

    lax.fori_loop(0, pairs, body, 0)


def widen_near(ext_ref, f_ref, xlo_ref, xhi_ref, ylo_ref, yhi_ref):
    for b in range(3):
        clear_ends(ext_ref, (b,))
    row = lax.broadcasted_iota(jnp.int32, (NY, PAIR), 0)
    wide = NX + 4

    def body(k, carry):
        ylo = ylo_ref[k].astype(F32)
        yhi = yhi_ref[k].astype(F32)
        for xp in range(NX + 2):
            if xp == 0:
                mid = xlo_ref[k, NY : 2 * NY, :].astype(F32)
            elif xp == NX + 1:
                mid = xhi_ref[k, 0:NY, :].astype(F32)
            else:
                mid = f_ref[k, (xp - 1) * NY : xp * NY, :].astype(F32)
            put_shifted(ext_ref, k, xp, mid, ylo[wide + xp + 1 : wide + xp + 2, :], yhi[xp + 1 : xp + 2, :], row)
        return carry

    lax.fori_loop(0, f_ref.shape[0], body, 0)


def widen_one(ext_ref, rows_ref):
    pairs = rows_ref.shape[0]
    for b in range(3):
        clear_ends(ext_ref, (b,))
    row = lax.broadcasted_iota(jnp.int32, (NY, PAIR), 0)

    def body(k, carry):
        edges = rows_ref[k, OUT_MAIN:OUT_ROWS, :].astype(F32)
        for xp in range(NX + 2):
            mid = rows_ref[k, xp * NY : (xp + 1) * NY, :].astype(F32)
            put_shifted(ext_ref, k, xp, mid, edges[xp : xp + 1, :], edges[EDGE + xp : EDGE + xp + 1, :], row)
        return carry

    lax.fori_loop(0, pairs, body, 0)


def conv_wide(ext_ref, edge_ref, w_ref, k):
    pieces = []
    for a in range(3):
        for b in range(3):
            for j in range(2):
                main = ext_ref[b, k + j, a : a + NX + 2].reshape(OUT_MAIN, PAIR)
                pieces.append(jnp.concatenate([main, edge_ref[a, b, k + j]], axis=0))
    return dot(jnp.concatenate(pieces, axis=1), w_ref[...])


def conv_inner(ext_ref, w_ref, k):
    pieces = []
    for a in range(3):
        for b in range(3):
            for j in range(2):
                pieces.append(ext_ref[b, k + j, a : a + NX].reshape(NX * NY, PAIR))
    return dot(jnp.concatenate(pieces, axis=1), w_ref[...])


def out_mask(mask_ref):
    return twice(jnp.concatenate([
        mask_ref[M_XLO + NY : M_XLO + 2 * NY, :], mask_ref[0 : NX * NY, :],
        mask_ref[M_XHI : M_XHI + NY, :], mask_ref[M_EDGE:M_ROWS, :],
    ], axis=0))


def outer_kernel(f_ref, xlo_ref, xhi_ref, ylo_ref, yhi_ref, low_ref, high_ref, mask_ref, raw_ref,
                 out_ref, outer_ref, ext_ref, edge_ref, w_ref):
    build_band(w_ref, raw_ref, True)
    widen_two(ext_ref, edge_ref, f_ref, xlo_ref, xhi_ref, ylo_ref, yhi_ref, low_ref, high_ref, mask_ref)

    def body(k, carry):
        out_ref[k] = conv_wide(ext_ref, edge_ref, w_ref, k)
        outer_ref[k] = (f_ref[k].astype(F32) * twice(mask_ref[0 : NX * NY, :])).astype(BF)
        return carry

    lax.fori_loop(0, f_ref.shape[0], body, 0)


def correlate(gt_ref, ext_ref, first_x, taps_ref, channels):
    pairs = ext_ref.shape[1] - 1

    def body(ab, carry):
        a = ab // 3
        b = ab % 3
        left = gt_ref[...]
        near = dot(left, ext_ref[b, 0:pairs, pl.ds(a + first_x, NX)].reshape(pairs * NX * NY, PAIR))
        far = dot(left, ext_ref[b, 1 : pairs + 1, pl.ds(a + first_x, NX)].reshape(pairs * NX * NY, PAIR))
        low = slice(0, channels)
        high = slice(channels, 2 * channels)
        taps_ref[3 * ab] = near[low, 0:LANES] + near[high, LANES:PAIR]
        taps_ref[3 * ab + 1] = near[low, LANES:PAIR] + far[high, 0:LANES]
        taps_ref[3 * ab + 2] = far[low, 0:LANES] + far[high, LANES:PAIR]
        return carry

    lax.fori_loop(0, 9, body, 0)


def pack_taps(taps_ref, packed_ref, channels):
    lane = lax.broadcasted_iota(jnp.int32, (channels, LANES), 1)
    for g in range(7):
        t1 = pltpu.roll(taps_ref[4 * g + 1], 96, 1)
        t2 = pltpu.roll(taps_ref[4 * g + 2], 64, 1)
        t3 = pltpu.roll(taps_ref[4 * g + 3], 32, 1)
        blocks = (
            jnp.where(lane < 96, taps_ref[4 * g], t1),
            jnp.where(lane < 64, t1, t2),
            jnp.where(lane < 32, t2, t3),
        )
        for i, value in enumerate(blocks):
            start = (3 * g + i) * channels
            packed_ref[start : start + channels, :] = value
    rest = packed_ref.shape[0] - 21 * channels
    if rest:
        packed_ref[21 * channels :, :] = jnp.zeros((rest, LANES), F32)


def hidden_kernel(f_ref, xlo_ref, xhi_ref, ylo_ref, yhi_ref, low_ref, high_ref, mask_ref, raw_ref, grad_ref,
                  act_ref, hg_ref, ext_ref, edge_ref, w_ref):
    build_band(w_ref, raw_ref, False)
    widen_two(ext_ref, edge_ref, f_ref, xlo_ref, xhi_ref, ylo_ref, yhi_ref, low_ref, high_ref)

    def body(k, carry):
        m = out_mask(mask_ref)
        hidden = m * conv_wide(ext_ref, edge_ref, w_ref, k)
        sigma = jax.nn.sigmoid(hidden)
        act_ref[k] = (hidden * sigma).astype(BF)
        hg_ref[k] = (m * grad_ref[k] * sigma * (1.0 + hidden * (1.0 - sigma))).astype(BF)
        return carry

    lax.fori_loop(0, f_ref.shape[0], body, 0)


def turn(gt_ref, g_ref, start, channels):
    inner = NX * NY
    for k in range(g_ref.shape[0]):
        value = g_ref[k, start : start + inner, :].T
        gt_ref[0:channels, k * inner : (k + 1) * inner] = value[0:channels]
        gt_ref[channels : 2 * channels, k * inner : (k + 1) * inner] = value[LANES : LANES + channels]


def corr_kernel(channels, core_ref, f_ref, xlo_ref, xhi_ref, ylo_ref, yhi_ref, hg_ref, act_ref, outer_ref,
                keep_ref, give_ref, ext_ref, gt_ref, taps_ref, packed_ref):
    half = keep_ref.shape[1]
    mine = pl.ds(pl.multiple_of(core_ref[0] * half, half), half)
    other = pl.ds(pl.multiple_of((1 - core_ref[0]) * half, half), half)
    taps_ref[27] = jnp.zeros((channels, LANES), F32)
    for i in range(2):
        if i == 0:
            widen_near(ext_ref, f_ref, xlo_ref, xhi_ref, ylo_ref, yhi_ref)
            turn(gt_ref, hg_ref, NY, channels)
        else:
            widen_one(ext_ref, act_ref)
            turn(gt_ref, outer_ref, 0, channels)
        correlate(gt_ref, ext_ref, 0, taps_ref, channels)
        pack_taps(taps_ref, packed_ref, channels)
        keep_ref[i] = packed_ref[mine, :]
        give_ref[i] = packed_ref[other, :]


def grid_grad_kernel(hg_ref, raw_ref, outer_ref, perm_ref, take_ref, out_ref, ext_ref, sum_ref, turned_ref, w_ref):
    build_band(w_ref, raw_ref, True)
    widen_one(ext_ref, hg_ref)

    def body(k, carry):
        sum_ref[k] = (outer_ref[k].astype(F32) + conv_inner(ext_ref, w_ref, k)).astype(BF)
        return carry

    lax.fori_loop(0, outer_ref.shape[0], body, 0)
    gather_pairs(sum_ref, turned_ref)
    take = take_ref[...]
    for i in range(perm_ref.shape[0]):
        rows = dot_nt(turned_ref[i], perm_ref[i]).astype(BF)
        out_ref[:, i * PAIR : (i + 1) * PAIR] = dot(take, rows).astype(BF)


def block_kernel(act_ref, mask_ref, raw_ref, field_ref, perm_ref, out_ref, ext_ref, sum_ref, turned_ref, w_ref):
    build_band(w_ref, raw_ref, False)
    widen_one(ext_ref, act_ref)

    def body(k, carry):
        m = twice(mask_ref[0 : NX * NY, :])
        sum_ref[k] = (field_ref[k].astype(F32) + m * conv_inner(ext_ref, w_ref, k)).astype(BF)
        return carry

    lax.fori_loop(0, field_ref.shape[0], body, 0)
    gather_pairs(sum_ref, turned_ref)
    for i in range(perm_ref.shape[0]):
        out_ref[:, i * PAIR : (i + 1) * PAIR] = dot_nt(turned_ref[i], perm_ref[i]).astype(BF)


def pair_sum_kernel(keep_ref, got_ref, out_ref):
    count, _, chunk, _ = out_ref.shape
    for i in range(2):
        for s in range(count):
            rows = slice(s * chunk, (s + 1) * chunk)
            out_ref[s, i] = (keep_ref[i, rows, :] + got_ref[i, rows, :]).astype(BF)


def chunk_sum_kernel(in_ref, out_ref):
    count = in_ref.shape[0]
    for i in range(2):
        total = in_ref[0, i].astype(F32)
        for s in range(1, count):
            total = total + in_ref[s, i].astype(F32)
        total = total.astype(BF)
        for s in range(count):
            out_ref[s, i] = total


def unpack_kernel(factor, core_ref, mine_ref, other_ref, first_ref, second_ref, flat_ref):
    count, _, chunk, _ = mine_ref.shape
    half = count * chunk
    for i, out_ref in enumerate((first_ref, second_ref)):
        for s in range(count):
            start = core_ref[0] * half + s * chunk
            flat_ref[pl.ds(pl.multiple_of(start, chunk), chunk), :] = mine_ref[s, i].astype(F32)
            start = (1 - core_ref[0]) * half + s * chunk
            flat_ref[pl.ds(pl.multiple_of(start, chunk), chunk), :] = other_ref[s, i].astype(F32)
        unpack_taps(factor, flat_ref, out_ref)


def unpack_taps(factor, packed_ref, out_ref):
    channels = out_ref.shape[1]
    lane = lax.broadcasted_iota(jnp.int32, (channels, LANES), 1)
    for g in range(7):
        v = []
        for i in range(3):
            start = (3 * g + i) * channels
            v.append(packed_ref[start : start + channels, :] * factor)
        taps = (
            v[0],
            pltpu.roll(jnp.where(lane < 64, v[1], v[0]), 32, 1),
            pltpu.roll(jnp.where(lane < 32, v[2], v[1]), 64, 1),
            pltpu.roll(v[2], 96, 1),
        )
        for u in range(4):
            if 4 * g + u < 27:
                out_ref[4 * g + u] = taps[u][:, 0:channels]


RX = ("cx", "core")
ALL = ("cx", "core", "ry")
SAME_CORE = ("cx", "ry")


def size_of(axes):
    return int(np.prod([lax.axis_size(a) for a in ((axes,) if isinstance(axes, str) else axes)]))


def share(parts, axes):
    return lax.all_to_all(parts, axes, split_axis=0, concat_axis=0, tiled=True)


def neighbours(axes, upper, lower):
    count = size_of(axes)
    ahead = [(i, i + 1) for i in range(count - 1)]
    behind = [(t, s) for s, t in ahead]
    return lax.ppermute(upper, axes, ahead), lax.ppermute(lower, axes, behind)


def swap_cores(value):
    count = size_of(RX)
    return lax.ppermute(value, RX, [(i, i ^ 1) for i in range(count)])


def message_rows():
    cells = []
    for ys in ((0, 1), (NY - 2, NY - 1)):
        for y in ys:
            cells += [(x, y) for x in range(-2, NX + 2)]
        cells += [None] * (MSG - 2 * (NX + 4))
    return cells


def exchange(field, pick):
    pairs = field.shape[0]
    xlo, xhi = neighbours(RX, field[:, (NX - 2) * NY :, :], field[:, : 2 * NY, :])
    message = jax.ShapeDtypeStruct((pairs, MSG, PAIR), BF)
    low, high = call(message_kernel, (message, message), 5e8, 3e6)(field, xlo, xhi, pick)
    ylo, yhi = neighbours("ry", high, low)
    return xlo, xhi, ylo, yhi, low, high


def mask_cells():
    cells = [(x, y) for x in range(NX) for y in range(NY)]
    cells += [(x, y) for x in (-2, -1) for y in range(NY)]
    cells += [(x, y) for x in (NX, NX + 1) for y in range(NY)]
    for ys in ((-2, -1), (NY, NY + 1), (0, 1), (NY - 2, NY - 1)):
        for y in ys:
            cells += [(x, y) for x in range(-2, NX + 2)]
        cells += [None] * (MSG - 2 * (NX + 4))
    for y in (-1, NY):
        cells += [(x, y) for x in range(-1, NX + 1)]
        cells += [None] * (EDGE - NX - 2)
    return cells


def on_device(column_features, column_route, cotangent, first_weight, second_weight):
    count_x = size_of(RX)
    count_y = size_of("ry")
    count_all = count_x * count_y
    shard_rows, row_width = column_features.shape
    channels = first_weight.shape[1]
    depth = row_width // channels
    slots = NX * NY
    pairs = depth // 2
    chunks = channels // GROUP
    cap = 2 * shard_rows // count_all
    buffers = count_all * cap
    me_x = lax.axis_index(RX)
    me_y = lax.axis_index("ry")
    core = lax.axis_index("core").astype(jnp.int32).reshape(1)
    conv_flops = 2 * slots * pairs * 36 * LANES * PAIR

    shape = jax.ShapeDtypeStruct
    field_shape = shape((pairs, slots, PAIR), BF)
    wide_shape = shape((pairs, OUT_ROWS, PAIR), BF)
    ext = pltpu.VMEM((3, pairs + 1, NX + 4, NY, PAIR), BF)
    edge = pltpu.VMEM((3, 3, pairs + 1, 2 * EDGE, PAIR), BF)
    turned = pltpu.VMEM((chunks, slots, PAIR), F32)
    turned_low = pltpu.VMEM((chunks, slots, PAIR), BF)
    sums = pltpu.VMEM((pairs, slots, PAIR), BF)

    perm = jnp.asarray(permutation(channels, depth), BF)
    pick_np = np.zeros((2 * MSG, (NX + 4) * NY), np.float32)
    for r, cell in enumerate(message_rows()):
        if cell is not None:
            pick_np[r, (cell[0] + 2) * NY + cell[1]] = 1.0
    pick = jnp.asarray(pick_np, BF)

    route_row = column_route.reshape(1, shard_rows)
    route_col = column_route.reshape(shard_rows, 1)
    route_all = share(jnp.broadcast_to(route_row, (count_all, shard_rows)), ALL)
    outgoing = call(
        functools.partial(send_kernel, cap, slots), shape((buffers, row_width), BF),
        2 * buffers * shard_rows * row_width, 3 * shard_rows * row_width * 2,
    )(route_row, route_col, column_features)
    incoming = share(outgoing.reshape(count_all, cap, row_width), ALL).reshape(buffers, row_width)

    cells = mask_cells()
    steps = np.asarray([(0, 0) if c is None else (c[0] // NX, c[1] // NY) for c in cells], np.int32)
    local = np.asarray([-1 if c is None else (c[0] % NX) * NY + c[1] % NY for c in cells], np.int32)
    to_x = me_x + steps[:, 0]
    to_y = me_y + steps[:, 1]
    inside = (to_x >= 0) & (to_x < count_x) & (to_y >= 0) & (to_y < count_y) & (local >= 0)
    codes = jnp.where(inside, (to_x * count_y + to_y) * slots + local, -1).astype(jnp.int32)[:, None]

    cot = call(
        to_pairs_kernel, field_shape, 1e9, 3e6, (turned,),
    )(cotangent.reshape(slots, row_width), perm)
    cot_halo = exchange(cot, pick)

    mask, take, put = call(
        functools.partial(mask_kernel, cap, slots),
        (shape((M_ROWS, LANES), F32), shape((buffers, slots), BF), shape((slots, buffers), BF)),
        1e8, 1e6,
    )(route_all, route_all - (me_x * count_y + me_y) * slots, codes)

    band = pltpu.VMEM((36 * LANES, PAIR), BF)
    ext_near = pltpu.VMEM((3, pairs + 1, NX + 2, NY, PAIR), BF)
    act_grad, outer = call(
        outer_kernel, (shape((pairs, OUT_ROWS, PAIR), F32), field_shape),
        1.3 * conv_flops, 7e6, (ext, edge, band), ROOM_WIDE,
    )(cot, *cot_halo, mask, second_weight)

    incoming, act_grad = lax.optimization_barrier((incoming, act_grad))
    field = call(
        place_kernel, field_shape, 1e9, 3e6, (turned,),
    )(put, incoming, perm)
    field_halo = exchange(field, pick)

    unit = 16 * count_all
    packed_rows = -(-21 * channels // unit) * unit
    half = packed_rows // 2
    chunk = packed_rows // count_all
    smem = pl.BlockSpec(memory_space=pltpu.SMEM)
    vmem = pl.BlockSpec(memory_space=pltpu.VMEM)
    half_shape = shape((2, half, LANES), F32)
    act, hg = call(
        hidden_kernel, (wide_shape, wide_shape), 1.3 * conv_flops, 8e6, (ext, edge, band), ROOM_WIDE,
    )(field, *field_halo, mask, first_weight, act_grad)

    back = call(
        grid_grad_kernel, shape((buffers, row_width), BF), 1.2 * conv_flops, 6e6,
        (ext_near, sums, turned_low, band), ROOM_NEAR,
    )(hg, first_weight, outer, perm, take)
    returned = share(back.reshape(count_all, cap, row_width), ALL).reshape(buffers, row_width)

    act, back = lax.optimization_barrier((act, back))
    keep, give = call(
        functools.partial(corr_kernel, channels), (half_shape, half_shape), 2 * conv_flops, 10e6,
        (
            ext_near, pltpu.VMEM((2 * channels, pairs * slots), BF),
            pltpu.VMEM((28, channels, LANES), F32), pltpu.VMEM((packed_rows, LANES), F32),
        ),
        ROOM_CORR, in_specs=[smem] + [vmem] * 8,
    )(core, field, *field_halo[:4], hg, act, outer)
    got = swap_cores(give)
    got, returned = lax.optimization_barrier((got, returned))
    sent = call(
        pair_sum_kernel, shape((count_all // 2, 2, chunk, LANES), BF), 1e6, 2e6,
    )(keep, got)
    parts = share(sent, SAME_CORE)
    act, sent = lax.optimization_barrier((act, sent))
    block_output = call(
        block_kernel, shape((slots, row_width), BF), 1.2 * conv_flops, 8e6,
        (ext_near, sums, turned_low, band), ROOM_NEAR,
    )(act, mask, second_weight, field, perm)

    parts, block_output = lax.optimization_barrier((parts, block_output))
    totals = share(call(
        chunk_sum_kernel, shape((count_all // 2, 2, chunk, LANES), BF), 1e6, 1e6,
    )(parts), SAME_CORE)

    feature_grads = call(
        functools.partial(collect_kernel, cap, slots), shape((shard_rows, row_width), BF),
        2 * buffers * shard_rows * row_width, 3 * shard_rows * row_width * 2,
    )(route_row, route_col, returned)

    factor = float(1.0 / np.sqrt(np.float32(count_all * shard_rows * depth)))
    grads = shape(first_weight.shape, F32)
    first_grad, second_grad = call(
        functools.partial(unpack_kernel, factor), (grads, grads), 1e6, 4e6,
        (pltpu.VMEM((packed_rows, LANES), F32),), in_specs=[smem, vmem, vmem],
    )(core, totals, swap_cores(totals))
    return (block_output.reshape(cotangent.shape), feature_grads, first_grad, second_grad)


def solution(mesh):
    count_x = mesh.shape["rx"]
    fine = jax.sharding.Mesh(mesh.devices.reshape(count_x // 2, 2, mesh.shape["ry"]), ALL)
    in_specs = (P(ALL, None), P(ALL), P(RX, "ry", None), P(), P())
    out_specs = (P(RX, "ry", None), P(ALL, None), P(), P())
    return jax.shard_map(
        on_device, mesh=fine, in_specs=in_specs, out_specs=out_specs, check_vma=False
    )
```

```python
import functools

import jax
import jax.numpy as jnp
import numpy as np
from jax import lax
from jax.experimental import pallas as pl
from jax.experimental.pallas import tpu as pltpu
from jax.sharding import PartitionSpec as P

LANES = 128
PAIR = 256
MIB = 1024 * 1024
ROOM_WIDE, ROOM_NEAR, ROOM_CORR, ROOM_SMALL = 16, 12, 14, 5
BF = jnp.bfloat16
F32 = jnp.float32


def call(body, out_shape, flops, moved, scratch=(), room=ROOM_SMALL, **extra):
    return pl.pallas_call(
        body,
        out_shape=out_shape,
        scratch_shapes=list(scratch),
        compiler_params=pltpu.CompilerParams(vmem_limit_bytes=room * MIB),
        cost_estimate=pl.CostEstimate(flops=int(flops), bytes_accessed=int(moved), transcendentals=0),
        **extra,
    )


def dot(left, right):
    return jnp.dot(left, right, preferred_element_type=F32)


def dot_nt(left, right):
    return lax.dot_general(left, right, (((1,), (1,)), ((), ())), preferred_element_type=F32)


def send_kernel(cap, slots, row_ref, col_ref, feat_ref, out_ref):
    rows, width = feat_ref.shape
    buffers = out_ref.shape[0]
    owner_row = row_ref[...] // slots
    owner_col = col_ref[...] // slots
    first = lax.broadcasted_iota(jnp.int32, (rows, rows), 0)
    second = lax.broadcasted_iota(jnp.int32, (rows, rows), 1)
    same = jnp.where((owner_col == owner_row) & (first < second), 1.0, 0.0)
    rank = jnp.sum(same, axis=0, keepdims=True)
    pos = owner_row.astype(F32) * cap + rank
    place = lax.broadcasted_iota(jnp.int32, (buffers, rows), 0)
    hot = jnp.where(place.astype(F32) == pos, 1.0, 0.0).astype(BF)
    out_ref[:, 0:width] = dot(hot, feat_ref[...]).astype(BF)
    slot_row = (row_ref[...] % slots).astype(F32)
    kind = place % cap
    told = jnp.where(kind == 0, owner_row.astype(F32), jnp.where(kind == 1, slot_row, 0.0))
    out_ref[:, width : width + rows] = told.astype(BF)


def told_rows(cap, in_ref, which):
    buffers, width = in_ref.shape
    count = buffers // cap
    source = lax.broadcasted_iota(jnp.int32, (count, buffers), 0)
    place = lax.broadcasted_iota(jnp.int32, (count, buffers), 1)
    pick = jnp.where(place == source * cap + which, 1.0, 0.0).astype(BF)
    return dot(pick, in_ref[:, width - LANES : width])


def collect_kernel(cap, slots, row_ref, col_ref, back_ref, out_ref):
    rows = out_ref.shape[0]
    owner_row = row_ref[...] // slots
    owner_col = col_ref[...] // slots
    first = lax.broadcasted_iota(jnp.int32, (rows, rows), 0)
    second = lax.broadcasted_iota(jnp.int32, (rows, rows), 1)
    same = jnp.where((owner_col == owner_row) & (second < first), 1.0, 0.0)
    rank = jnp.sum(same, axis=1, keepdims=True)
    pos = owner_col.astype(F32) * cap + rank
    place = lax.broadcasted_iota(jnp.int32, (rows, back_ref.shape[0]), 1).astype(F32)
    hot = jnp.where(place == pos, 1.0, 0.0).astype(BF)
    out_ref[...] = dot(hot, back_ref[...]).astype(BF)


def mask_kernel(cap, slots, in_ref, codes_ref, mask_ref, route_ref):
    total = mask_ref.shape[0]
    route_ref[...] = told_rows(cap, in_ref, 0) * slots + told_rows(cap, in_ref, 1)
    codes = jnp.broadcast_to(codes_ref[...], (total, LANES))
    hits = jnp.zeros((total, LANES), F32)
    for s in range(route_ref.shape[0]):
        hits = hits + jnp.where(codes == route_ref[s : s + 1, :], 1.0, 0.0)
    mask_ref[...] = jnp.broadcast_to(jnp.sum(hits, axis=1, keepdims=True), (total, LANES))


def slot_table(cap, slots, me, in_ref):
    buffers = in_ref.shape[0]
    count = buffers // cap
    mine_f = jnp.where(told_rows(cap, in_ref, 0) == me.astype(F32), 1.0, 0.0)
    slot_f = told_rows(cap, in_ref, 1)
    first = lax.broadcasted_iota(jnp.int32, (LANES, LANES), 0)
    second = lax.broadcasted_iota(jnp.int32, (LANES, LANES), 1)
    tri = jnp.where(first < second, 1.0, 0.0).astype(BF)
    rank = dot(mine_f.astype(BF), tri)
    lane = lax.broadcasted_iota(jnp.int32, (count, LANES), 1)
    held = jnp.zeros((count, LANES), F32)
    for j in range(cap):
        here = jnp.where(rank == j, mine_f, 0.0)
        number = jnp.sum(here, axis=1, keepdims=True)
        value = jnp.sum(here * slot_f, axis=1, keepdims=True)
        value = value + (1.0 - number) * slots
        held = jnp.where(lane == j, value, held)
    place = lax.broadcasted_iota(jnp.int32, (buffers, count), 0)
    source = lax.broadcasted_iota(jnp.int32, (buffers, count), 1)
    spread = jnp.where(place // cap == source, 1.0, 0.0).astype(BF)
    wide = dot(spread, held.astype(BF))
    place = lax.broadcasted_iota(jnp.int32, (buffers, LANES), 0)
    lane = lax.broadcasted_iota(jnp.int32, (buffers, LANES), 1)
    slot_col = jnp.sum(jnp.where(place % cap == lane, wide, 0.0), axis=1, keepdims=True)
    slot_id = lax.broadcasted_iota(jnp.int32, (buffers, slots), 1).astype(F32)
    return jnp.where(slot_col == slot_id, 1.0, 0.0)


GROUP = 16
FOLD = LANES // GROUP


def permutation(channels, depth):
    perm = np.zeros((channels // GROUP, PAIR, PAIR), np.float32)
    for i in range(channels // GROUP):
        for j in range(GROUP):
            for z in range(depth):
                perm[i, depth * j + z, LANES * (z // FOLD) + GROUP * ((z + i) % FOLD) + j] = 1.0
    return perm


def lane_group(rows):
    return lax.broadcasted_iota(jnp.int32, (rows, LANES), 1) // GROUP


def spread_pairs(turned_ref, out_ref):
    chunks, rows, _ = turned_ref.shape
    step = 32
    group = lane_group(step)

    def body(t, carry):
        at = pl.ds(pl.multiple_of(t * step, step), step)
        for half in range(2):
            lanes = slice(half * LANES, (half + 1) * LANES)
            parts = [turned_ref[i, at, lanes] for i in range(chunks)]
            parts = parts + [jnp.zeros((step, LANES), F32)] * (FOLD - chunks)
            for bit in (1, 2, 4):
                odd = (group & bit) != 0
                parts = [jnp.where(odd, parts[(i + bit) % FOLD], parts[i]) for i in range(FOLD)]
            for g in range(FOLD):
                value = parts[(-g) % FOLD]
                if g:
                    value = pltpu.roll(value, LANES - GROUP * g, 1)
                z = half * FOLD + g
                out_ref[z // 2, at, (z % 2) * LANES : (z % 2 + 1) * LANES] = value.astype(BF)
        return carry

    lax.fori_loop(0, rows // step, body, 0)


def gather_pairs(in_ref, turned_ref):
    chunks, rows, _ = turned_ref.shape
    step = 32
    group = lane_group(step)

    def body(t, carry):
        at = pl.ds(pl.multiple_of(t * step, step), step)
        for half in range(2):
            turned = []
            for g in range(FOLD):
                z = half * FOLD + g
                value = in_ref[z // 2, at, (z % 2) * LANES : (z % 2 + 1) * LANES].astype(F32)
                turned.append(pltpu.roll(value, GROUP * g, 1) if g else value)
            parts = [turned[(-i) % FOLD] for i in range(FOLD)]
            for bit in (1, 2, 4):
                odd = (group & bit) != 0
                parts = [jnp.where(odd, parts[(i - bit) % FOLD], parts[i]) for i in range(FOLD)]
            for i in range(chunks):
                turned_ref[i, at, half * LANES : (half + 1) * LANES] = parts[i].astype(BF)
        return carry

    lax.fori_loop(0, rows // step, body, 0)


def to_pairs_kernel(rows_ref, perm_ref, out_ref, turned_ref):
    for i in range(perm_ref.shape[0]):
        turned_ref[i] = dot(rows_ref[:, i * PAIR : (i + 1) * PAIR], perm_ref[i])
    spread_pairs(turned_ref, out_ref)


def place_kernel(cap, slots, me_ref, rows_ref, perm_ref, out_ref, take_ref, turned_ref):
    take = slot_table(cap, slots, me_ref[0], rows_ref)
    take_ref[...] = take.astype(BF)
    put = take.T.astype(BF)
    for i in range(perm_ref.shape[0]):
        held = dot(put, rows_ref[:, i * PAIR : (i + 1) * PAIR]).astype(BF)
        turned_ref[i] = dot(held, perm_ref[i])
    spread_pairs(turned_ref, out_ref)


def message_kernel(f_ref, xlo_ref, xhi_ref, pick_ref, low_ref, high_ref):
    pick = pick_ref[...]
    half = low_ref.shape[1]
    for k in range(f_ref.shape[0]):
        rows = jnp.concatenate([xlo_ref[k], f_ref[k], xhi_ref[k]], axis=0)
        sent = dot(pick, rows).astype(BF)
        low_ref[k] = sent[0:half]
        high_ref[k] = sent[half : 2 * half]


def build_band(band_ref, raw_ref, backward):
    channels = raw_ref.shape[1]
    band_ref[...] = jnp.zeros_like(band_ref)
    for tap in range(27):
        value = raw_ref[26 - tap] if backward else raw_ref[tap].T
        for zo in range(2):
            row = ((tap // 3) * 4 + zo + tap % 3) * LANES
            band_ref[row : row + channels, zo * LANES : zo * LANES + channels] = value


NX = 16
NY = 16
OUT_MAIN = (NX + 2) * NY
EDGE = 24
OUT_ROWS = OUT_MAIN + 2 * EDGE
MSG = 48
M_XLO = NX * NY
M_XHI = M_XLO + 2 * NY
M_YLO = M_XHI + 2 * NY
M_YHI = M_YLO + MSG
M_LOW = M_YHI + MSG
M_HIGH = M_LOW + MSG
M_EDGE = M_HIGH + MSG
M_ROWS = M_EDGE + 2 * EDGE


def twice(value):
    return jnp.concatenate([value, value], axis=1)


def put_pair(ref, lead, k, tail, value):
    value = value.astype(BF)
    ref[lead + (k,) + tail + (slice(LANES, PAIR),)] = value[:, 0:LANES]
    ref[lead + (k + 1,) + tail + (slice(0, LANES),)] = value[:, LANES:PAIR]


def clear_ends(ref, lead):
    last = ref.shape[len(lead)] - 1
    dims = ref.shape[len(lead) + 1 : -1]
    ref[lead + (0,) + (slice(None),) * len(dims) + (slice(0, LANES),)] = jnp.zeros(dims + (LANES,), BF)
    ref[lead + (last,) + (slice(None),) * len(dims) + (slice(LANES, PAIR),)] = jnp.zeros(dims + (LANES,), BF)


def put_shifted(ext_ref, k, xp, mid, before, after, row):
    ny = mid.shape[0]
    up = jnp.where(row == 0, before, pltpu.roll(mid, 1, 0))
    down = jnp.where(row == ny - 1, after, pltpu.roll(mid, ny - 1, 0))
    for b, value in enumerate((up, mid, down)):
        put_pair(ext_ref, (b,), k, (xp, slice(None)), value)


def widen_two(ext_ref, edge_ref, f_ref, xlo_ref, xhi_ref, ylo_ref, yhi_ref, low_ref, high_ref, mask_ref=None):
    pairs = f_ref.shape[0]
    for b in range(3):
        clear_ends(ext_ref, (b,))
        for a in range(3):
            clear_ends(edge_ref, (a, b))
    row = lax.broadcasted_iota(jnp.int32, (NY, PAIR), 0)

    def read(ref, k, start, size, mask_start):
        value = ref[k, start : start + size, :].astype(F32)
        if mask_ref is None:
            return value
        return value * twice(mask_ref[mask_start + start : mask_start + start + size, :])

    def body(k, carry):
        ylo = read(ylo_ref, k, 0, MSG, M_YLO)
        yhi = read(yhi_ref, k, 0, MSG, M_YHI)
        low = read(low_ref, k, 0, MSG, M_LOW)
        high = read(high_ref, k, 0, MSG, M_HIGH)
        wide = NX + 4
        for xp in range(wide):
            if xp < 2:
                mid = read(xlo_ref, k, xp * NY, NY, M_XLO)
            elif xp >= NX + 2:
                mid = read(xhi_ref, k, (xp - NX - 2) * NY, NY, M_XHI)
            else:
                mid = read(f_ref, k, (xp - 2) * NY, NY, 0)
            put_shifted(ext_ref, k, xp, mid, ylo[wide + xp : wide + xp + 1, :], yhi[xp : xp + 1, :], row)
        first = ((ylo, 0), (ylo, wide), (low, 0))
        second = ((high, wide), (yhi, 0), (yhi, wide))
        for a in range(3):
            for b in range(3):
                sides = []
                for value, start in (first[b], second[b]):
                    turn = start + a
                    if turn:
                        value = pltpu.roll(value, MSG - turn, 0)
                    sides.append(value[0:EDGE])
                put_pair(edge_ref, (a, b), k, (slice(None),), jnp.concatenate(sides, axis=0))
        return carry

    lax.fori_loop(0, pairs, body, 0)


def widen_near(ext_ref, f_ref, xlo_ref, xhi_ref, ylo_ref, yhi_ref):
    for b in range(3):
        clear_ends(ext_ref, (b,))
    row = lax.broadcasted_iota(jnp.int32, (NY, PAIR), 0)
    wide = NX + 4

    def body(k, carry):
        ylo = ylo_ref[k].astype(F32)
        yhi = yhi_ref[k].astype(F32)
        for xp in range(NX + 2):
            if xp == 0:
                mid = xlo_ref[k, NY : 2 * NY, :].astype(F32)
            elif xp == NX + 1:
                mid = xhi_ref[k, 0:NY, :].astype(F32)
            else:
                mid = f_ref[k, (xp - 1) * NY : xp * NY, :].astype(F32)
            put_shifted(ext_ref, k, xp, mid, ylo[wide + xp + 1 : wide + xp + 2, :], yhi[xp + 1 : xp + 2, :], row)
        return carry

    lax.fori_loop(0, f_ref.shape[0], body, 0)


def widen_one(ext_ref, rows_ref):
    pairs = rows_ref.shape[0]
    for b in range(3):
        clear_ends(ext_ref, (b,))
    row = lax.broadcasted_iota(jnp.int32, (NY, PAIR), 0)

    def body(k, carry):
        edges = rows_ref[k, OUT_MAIN:OUT_ROWS, :].astype(F32)
        for xp in range(NX + 2):
            mid = rows_ref[k, xp * NY : (xp + 1) * NY, :].astype(F32)
            put_shifted(ext_ref, k, xp, mid, edges[xp : xp + 1, :], edges[EDGE + xp : EDGE + xp + 1, :], row)
        return carry

    lax.fori_loop(0, pairs, body, 0)


def conv_wide(ext_ref, edge_ref, w_ref, k):
    pieces = []
    for a in range(3):
        for b in range(3):
            for j in range(2):
                main = ext_ref[b, k + j, a : a + NX + 2].reshape(OUT_MAIN, PAIR)
                pieces.append(jnp.concatenate([main, edge_ref[a, b, k + j]], axis=0))
    return dot(jnp.concatenate(pieces, axis=1), w_ref[...])


def conv_inner(ext_ref, w_ref, k):
    pieces = []
    for a in range(3):
        for b in range(3):
            for j in range(2):
                pieces.append(ext_ref[b, k + j, a : a + NX].reshape(NX * NY, PAIR))
    return dot(jnp.concatenate(pieces, axis=1), w_ref[...])


def out_mask(mask_ref):
    return twice(jnp.concatenate([
        mask_ref[M_XLO + NY : M_XLO + 2 * NY, :], mask_ref[0 : NX * NY, :],
        mask_ref[M_XHI : M_XHI + NY, :], mask_ref[M_EDGE:M_ROWS, :],
    ], axis=0))


def outer_kernel(f_ref, xlo_ref, xhi_ref, ylo_ref, yhi_ref, low_ref, high_ref, mask_ref, raw_ref,
                 out_ref, outer_ref, ext_ref, edge_ref, w_ref):
    build_band(w_ref, raw_ref, True)
    widen_two(ext_ref, edge_ref, f_ref, xlo_ref, xhi_ref, ylo_ref, yhi_ref, low_ref, high_ref, mask_ref)

    def body(k, carry):
        out_ref[k] = conv_wide(ext_ref, edge_ref, w_ref, k)
        outer_ref[k] = (f_ref[k].astype(F32) * twice(mask_ref[0 : NX * NY, :])).astype(BF)
        return carry

    lax.fori_loop(0, f_ref.shape[0], body, 0)


def correlate(gt_ref, ext_ref, first_x, taps_ref, channels):
    pairs = ext_ref.shape[1] - 1

    def body(ab, carry):
        a = ab // 3
        b = ab % 3
        left = gt_ref[...]
        near = dot(left, ext_ref[b, 0:pairs, pl.ds(a + first_x, NX)].reshape(pairs * NX * NY, PAIR))
        far = dot(left, ext_ref[b, 1 : pairs + 1, pl.ds(a + first_x, NX)].reshape(pairs * NX * NY, PAIR))
        low = slice(0, channels)
        high = slice(channels, 2 * channels)
        taps_ref[3 * ab] = near[low, 0:LANES] + near[high, LANES:PAIR]
        taps_ref[3 * ab + 1] = near[low, LANES:PAIR] + far[high, 0:LANES]
        taps_ref[3 * ab + 2] = far[low, 0:LANES] + far[high, LANES:PAIR]
        return carry

    lax.fori_loop(0, 9, body, 0)


def pack_taps(taps_ref, packed_ref, channels):
    lane = lax.broadcasted_iota(jnp.int32, (channels, LANES), 1)
    for g in range(7):
        t1 = pltpu.roll(taps_ref[4 * g + 1], 96, 1)
        t2 = pltpu.roll(taps_ref[4 * g + 2], 64, 1)
        t3 = pltpu.roll(taps_ref[4 * g + 3], 32, 1)
        blocks = (
            jnp.where(lane < 96, taps_ref[4 * g], t1),
            jnp.where(lane < 64, t1, t2),
            jnp.where(lane < 32, t2, t3),
        )
        for i, value in enumerate(blocks):
            start = (3 * g + i) * channels
            packed_ref[start : start + channels, :] = value
    rest = packed_ref.shape[0] - 21 * channels
    if rest:
        packed_ref[21 * channels :, :] = jnp.zeros((rest, LANES), F32)


def hidden_kernel(f_ref, xlo_ref, xhi_ref, ylo_ref, yhi_ref, low_ref, high_ref, mask_ref, raw_ref, grad_ref,
                  act_ref, hg_ref, ext_ref, edge_ref, w_ref):
    build_band(w_ref, raw_ref, False)
    widen_two(ext_ref, edge_ref, f_ref, xlo_ref, xhi_ref, ylo_ref, yhi_ref, low_ref, high_ref)

    def body(k, carry):
        m = out_mask(mask_ref)
        hidden = m * conv_wide(ext_ref, edge_ref, w_ref, k)
        sigma = jax.nn.sigmoid(hidden)
        act_ref[k] = (hidden * sigma).astype(BF)
        hg_ref[k] = (m * grad_ref[k] * sigma * (1.0 + hidden * (1.0 - sigma))).astype(BF)
        return carry

    lax.fori_loop(0, f_ref.shape[0], body, 0)


def turn(gt_ref, g_ref, start, channels):
    inner = NX * NY
    for k in range(g_ref.shape[0]):
        value = g_ref[k, start : start + inner, :].T
        gt_ref[0:channels, k * inner : (k + 1) * inner] = value[0:channels]
        gt_ref[channels : 2 * channels, k * inner : (k + 1) * inner] = value[LANES : LANES + channels]


def corr_kernel(channels, core_ref, f_ref, xlo_ref, xhi_ref, ylo_ref, yhi_ref, hg_ref, act_ref, outer_ref,
                keep_ref, give_ref, ext_ref, gt_ref, taps_ref, packed_ref):
    half = keep_ref.shape[1]
    mine = pl.ds(pl.multiple_of(core_ref[0] * half, half), half)
    other = pl.ds(pl.multiple_of((1 - core_ref[0]) * half, half), half)
    taps_ref[27] = jnp.zeros((channels, LANES), F32)
    for i in range(2):
        if i == 0:
            widen_near(ext_ref, f_ref, xlo_ref, xhi_ref, ylo_ref, yhi_ref)
            turn(gt_ref, hg_ref, NY, channels)
        else:
            widen_one(ext_ref, act_ref)
            turn(gt_ref, outer_ref, 0, channels)
        correlate(gt_ref, ext_ref, 0, taps_ref, channels)
        pack_taps(taps_ref, packed_ref, channels)
        keep_ref[i] = packed_ref[mine, :]
        give_ref[i] = packed_ref[other, :]


def grid_grad_kernel(hg_ref, raw_ref, outer_ref, perm_ref, take_ref, out_ref, ext_ref, sum_ref, turned_ref, w_ref):
    build_band(w_ref, raw_ref, True)
    widen_one(ext_ref, hg_ref)

    def body(k, carry):
        sum_ref[k] = (outer_ref[k].astype(F32) + conv_inner(ext_ref, w_ref, k)).astype(BF)
        return carry

    lax.fori_loop(0, outer_ref.shape[0], body, 0)
    gather_pairs(sum_ref, turned_ref)
    take = take_ref[...]
    for i in range(perm_ref.shape[0]):
        rows = dot_nt(turned_ref[i], perm_ref[i]).astype(BF)
        out_ref[:, i * PAIR : (i + 1) * PAIR] = dot(take, rows).astype(BF)


def block_kernel(act_ref, mask_ref, raw_ref, field_ref, perm_ref, out_ref, ext_ref, sum_ref, turned_ref, w_ref):
    build_band(w_ref, raw_ref, False)
    widen_one(ext_ref, act_ref)

    def body(k, carry):
        m = twice(mask_ref[0 : NX * NY, :])
        sum_ref[k] = (field_ref[k].astype(F32) + m * conv_inner(ext_ref, w_ref, k)).astype(BF)
        return carry

    lax.fori_loop(0, field_ref.shape[0], body, 0)
    gather_pairs(sum_ref, turned_ref)
    for i in range(perm_ref.shape[0]):
        out_ref[:, i * PAIR : (i + 1) * PAIR] = dot_nt(turned_ref[i], perm_ref[i]).astype(BF)


def pair_sum_kernel(keep_ref, got_ref, out_ref):
    count, _, chunk, _ = out_ref.shape
    for i in range(2):
        for s in range(count):
            rows = slice(s * chunk, (s + 1) * chunk)
            out_ref[s, i] = (keep_ref[i, rows, :] + got_ref[i, rows, :]).astype(BF)


def chunk_sum_kernel(in_ref, out_ref):
    count = in_ref.shape[0]
    for i in range(2):
        total = in_ref[0, i].astype(F32)
        for s in range(1, count):
            total = total + in_ref[s, i].astype(F32)
        total = total.astype(BF)
        for s in range(count):
            out_ref[s, i] = total


def unpack_kernel(factor, core_ref, mine_ref, other_ref, first_ref, second_ref, flat_ref):
    count, _, chunk, _ = mine_ref.shape
    half = count * chunk
    for i, out_ref in enumerate((first_ref, second_ref)):
        for s in range(count):
            start = core_ref[0] * half + s * chunk
            flat_ref[pl.ds(pl.multiple_of(start, chunk), chunk), :] = mine_ref[s, i].astype(F32)
            start = (1 - core_ref[0]) * half + s * chunk
            flat_ref[pl.ds(pl.multiple_of(start, chunk), chunk), :] = other_ref[s, i].astype(F32)
        unpack_taps(factor, flat_ref, out_ref)


def unpack_taps(factor, packed_ref, out_ref):
    channels = out_ref.shape[1]
    lane = lax.broadcasted_iota(jnp.int32, (channels, LANES), 1)
    for g in range(7):
        v = []
        for i in range(3):
            start = (3 * g + i) * channels
            v.append(packed_ref[start : start + channels, :] * factor)
        taps = (
            v[0],
            pltpu.roll(jnp.where(lane < 64, v[1], v[0]), 32, 1),
            pltpu.roll(jnp.where(lane < 32, v[2], v[1]), 64, 1),
            pltpu.roll(v[2], 96, 1),
        )
        for u in range(4):
            if 4 * g + u < 27:
                out_ref[4 * g + u] = taps[u][:, 0:channels]


RX = ("cx", "core")
ALL = ("cx", "core", "ry")
SAME_CORE = ("cx", "ry")


def size_of(axes):
    return int(np.prod([lax.axis_size(a) for a in ((axes,) if isinstance(axes, str) else axes)]))


def share(parts, axes):
    return lax.all_to_all(parts, axes, split_axis=0, concat_axis=0, tiled=True)


def neighbours(axes, upper, lower):
    count = size_of(axes)
    ahead = [(i, i + 1) for i in range(count - 1)]
    behind = [(t, s) for s, t in ahead]
    return lax.ppermute(upper, axes, ahead), lax.ppermute(lower, axes, behind)


def swap_cores(value):
    count = size_of(RX)
    return lax.ppermute(value, RX, [(i, i ^ 1) for i in range(count)])


def message_rows():
    cells = []
    for ys in ((0, 1), (NY - 2, NY - 1)):
        for y in ys:
            cells += [(x, y) for x in range(-2, NX + 2)]
        cells += [None] * (MSG - 2 * (NX + 4))
    return cells


def exchange(field, pick):
    pairs = field.shape[0]
    xlo, xhi = neighbours(RX, field[:, (NX - 2) * NY :, :], field[:, : 2 * NY, :])
    message = jax.ShapeDtypeStruct((pairs, MSG, PAIR), BF)
    low, high = call(message_kernel, (message, message), 5e8, 3e6)(field, xlo, xhi, pick)
    ylo, yhi = neighbours("ry", high, low)
    return xlo, xhi, ylo, yhi, low, high


def mask_cells():
    cells = [(x, y) for x in range(NX) for y in range(NY)]
    cells += [(x, y) for x in (-2, -1) for y in range(NY)]
    cells += [(x, y) for x in (NX, NX + 1) for y in range(NY)]
    for ys in ((-2, -1), (NY, NY + 1), (0, 1), (NY - 2, NY - 1)):
        for y in ys:
            cells += [(x, y) for x in range(-2, NX + 2)]
        cells += [None] * (MSG - 2 * (NX + 4))
    for y in (-1, NY):
        cells += [(x, y) for x in range(-1, NX + 1)]
        cells += [None] * (EDGE - NX - 2)
    return cells


def on_device(column_features, column_route, cotangent, first_weight, second_weight):
    count_x = size_of(RX)
    count_y = size_of("ry")
    count_all = count_x * count_y
    shard_rows, row_width = column_features.shape
    channels = first_weight.shape[1]
    depth = row_width // channels
    slots = NX * NY
    pairs = depth // 2
    chunks = channels // GROUP
    cap = 2 * shard_rows // count_all
    buffers = count_all * cap
    me_x = lax.axis_index(RX)
    me_y = lax.axis_index("ry")
    core = lax.axis_index("core").astype(jnp.int32).reshape(1)
    conv_flops = 2 * slots * pairs * 36 * LANES * PAIR

    shape = jax.ShapeDtypeStruct
    field_shape = shape((pairs, slots, PAIR), BF)
    wide_shape = shape((pairs, OUT_ROWS, PAIR), BF)
    ext = pltpu.VMEM((3, pairs + 1, NX + 4, NY, PAIR), BF)
    edge = pltpu.VMEM((3, 3, pairs + 1, 2 * EDGE, PAIR), BF)
    turned = pltpu.VMEM((chunks, slots, PAIR), F32)
    turned_low = pltpu.VMEM((chunks, slots, PAIR), BF)
    sums = pltpu.VMEM((pairs, slots, PAIR), BF)

    perm = jnp.asarray(permutation(channels, depth), BF)
    pick_np = np.zeros((2 * MSG, (NX + 4) * NY), np.float32)
    for r, cell in enumerate(message_rows()):
        if cell is not None:
            pick_np[r, (cell[0] + 2) * NY + cell[1]] = 1.0
    pick = jnp.asarray(pick_np, BF)

    route_row = column_route.reshape(1, shard_rows)
    route_col = column_route.reshape(shard_rows, 1)
    told_width = row_width + LANES
    outgoing = call(
        functools.partial(send_kernel, cap, slots), shape((buffers, told_width), BF),
        2 * buffers * shard_rows * row_width, 3 * shard_rows * row_width * 2,
    )(route_row, route_col, column_features)
    incoming = share(outgoing.reshape(count_all, cap, told_width), ALL).reshape(buffers, told_width)

    cells = mask_cells()
    steps = np.asarray([(0, 0) if c is None else (c[0] // NX, c[1] // NY) for c in cells], np.int32)
    local = np.asarray([-1 if c is None else (c[0] % NX) * NY + c[1] % NY for c in cells], np.int32)
    to_x = me_x + steps[:, 0]
    to_y = me_y + steps[:, 1]
    inside = (to_x >= 0) & (to_x < count_x) & (to_y >= 0) & (to_y < count_y) & (local >= 0)
    codes = jnp.where(inside, (to_x * count_y + to_y) * slots + local, -1).astype(F32)[:, None]
    me = (me_x * count_y + me_y).astype(jnp.int32).reshape(1)

    cot = call(
        to_pairs_kernel, field_shape, 1e9, 3e6, (turned,),
    )(cotangent.reshape(slots, row_width), perm)
    cot_halo = exchange(cot, pick)

    smem = pl.BlockSpec(memory_space=pltpu.SMEM)
    vmem = pl.BlockSpec(memory_space=pltpu.VMEM)
    field, take = call(
        functools.partial(place_kernel, cap, slots), (field_shape, shape((buffers, slots), BF)), 1e9, 3e6,
        (turned,), in_specs=[smem, vmem, vmem],
    )(me, incoming, perm)
    field_halo = exchange(field, pick)

    mask = call(
        functools.partial(mask_kernel, cap, slots), shape((M_ROWS, LANES), F32), 1e8, 1e6,
        (pltpu.VMEM((count_all, LANES), F32),),
    )(incoming, codes)
    band = pltpu.VMEM((36 * LANES, PAIR), BF)
    ext_near = pltpu.VMEM((3, pairs + 1, NX + 2, NY, PAIR), BF)
    act_grad, outer = call(
        outer_kernel, (shape((pairs, OUT_ROWS, PAIR), F32), field_shape),
        1.3 * conv_flops, 7e6, (ext, edge, band), ROOM_WIDE,
    )(cot, *cot_halo, mask, second_weight)

    unit = 16 * count_all
    packed_rows = -(-21 * channels // unit) * unit
    half = packed_rows // 2
    chunk = packed_rows // count_all
    half_shape = shape((2, half, LANES), F32)
    act, hg = call(
        hidden_kernel, (wide_shape, wide_shape), 1.3 * conv_flops, 8e6, (ext, edge, band), ROOM_WIDE,
    )(field, *field_halo, mask, first_weight, act_grad)

    back = call(
        grid_grad_kernel, shape((buffers, row_width), BF), 1.2 * conv_flops, 6e6,
        (ext_near, sums, turned_low, band), ROOM_NEAR,
    )(hg, first_weight, outer, perm, take)
    returned = share(back.reshape(count_all, cap, row_width), ALL).reshape(buffers, row_width)

    act, back = lax.optimization_barrier((act, back))
    keep, give = call(
        functools.partial(corr_kernel, channels), (half_shape, half_shape), 2 * conv_flops, 10e6,
        (
            ext_near, pltpu.VMEM((2 * channels, pairs * slots), BF),
            pltpu.VMEM((28, channels, LANES), F32), pltpu.VMEM((packed_rows, LANES), F32),
        ),
        ROOM_CORR, in_specs=[smem] + [vmem] * 8,
    )(core, field, *field_halo[:4], hg, act, outer)
    got = swap_cores(give)
    got, returned = lax.optimization_barrier((got, returned))
    sent = call(
        pair_sum_kernel, shape((count_all // 2, 2, chunk, LANES), BF), 1e6, 2e6,
    )(keep, got)
    parts = share(sent, SAME_CORE)
    act, sent = lax.optimization_barrier((act, sent))
    block_output = call(
        block_kernel, shape((slots, row_width), BF), 1.2 * conv_flops, 8e6,
        (ext_near, sums, turned_low, band), ROOM_NEAR,
    )(act, mask, second_weight, field, perm)

    parts, block_output = lax.optimization_barrier((parts, block_output))
    totals = share(call(
        chunk_sum_kernel, shape((count_all // 2, 2, chunk, LANES), BF), 1e6, 1e6,
    )(parts), SAME_CORE)

    feature_grads = call(
        functools.partial(collect_kernel, cap, slots), shape((shard_rows, row_width), BF),
        2 * buffers * shard_rows * row_width, 3 * shard_rows * row_width * 2,
    )(route_row, route_col, returned)

    factor = float(1.0 / np.sqrt(np.float32(count_all * shard_rows * depth)))
    grads = shape(first_weight.shape, F32)
    first_grad, second_grad = call(
        functools.partial(unpack_kernel, factor), (grads, grads), 1e6, 4e6,
        (pltpu.VMEM((packed_rows, LANES), F32),), in_specs=[smem, vmem, vmem],
    )(core, totals, swap_cores(totals))
    return (block_output.reshape(cotangent.shape), feature_grads, first_grad, second_grad)


def solution(mesh):
    count_x = mesh.shape["rx"]
    fine = jax.sharding.Mesh(mesh.devices.reshape(count_x // 2, 2, mesh.shape["ry"]), ALL)
    in_specs = (P(ALL, None), P(ALL), P(RX, "ry", None), P(), P())
    out_specs = (P(RX, "ry", None), P(ALL, None), P(), P())
    return jax.shard_map(
        on_device, mesh=fine, in_specs=in_specs, out_specs=out_specs, check_vma=False
    )
```

```python
import functools

import jax
import jax.numpy as jnp
import numpy as np
from jax import lax
from jax.experimental import pallas as pl
from jax.experimental.pallas import tpu as pltpu
from jax.sharding import PartitionSpec as P

LANES = 128
PAIR = 256
MIB = 1024 * 1024
ROOM_WIDE, ROOM_NEAR, ROOM_CORR, ROOM_SMALL = 20, 14, 16, 5
BF = jnp.bfloat16
F32 = jnp.float32


def call(body, out_shape, flops, moved, scratch=(), room=ROOM_SMALL, **extra):
    return pl.pallas_call(
        body,
        out_shape=out_shape,
        scratch_shapes=list(scratch),
        compiler_params=pltpu.CompilerParams(vmem_limit_bytes=room * MIB),
        cost_estimate=pl.CostEstimate(flops=int(flops), bytes_accessed=int(moved), transcendentals=0),
        **extra,
    )


def dot(left, right):
    return jnp.dot(left, right, preferred_element_type=F32)


def dot_nt(left, right):
    return lax.dot_general(left, right, (((1,), (1,)), ((), ())), preferred_element_type=F32)


def send_kernel(cap, slots, row_ref, col_ref, feat_ref, out_ref):
    rows, width = feat_ref.shape
    buffers = out_ref.shape[0]
    owner_row = row_ref[...] // slots
    owner_col = col_ref[...] // slots
    first = lax.broadcasted_iota(jnp.int32, (rows, rows), 0)
    second = lax.broadcasted_iota(jnp.int32, (rows, rows), 1)
    same = jnp.where((owner_col == owner_row) & (first < second), 1.0, 0.0)
    rank = jnp.sum(same, axis=0, keepdims=True)
    pos = owner_row.astype(F32) * cap + rank
    place = lax.broadcasted_iota(jnp.int32, (buffers, rows), 0)
    hot = jnp.where(place.astype(F32) == pos, 1.0, 0.0).astype(BF)
    out_ref[:, 0:width] = dot(hot, feat_ref[...]).astype(BF)
    slot_row = (row_ref[...] % slots).astype(F32)
    kind = place % cap
    told = jnp.where(kind == 0, owner_row.astype(F32), jnp.where(kind == 1, slot_row, 0.0))
    out_ref[:, width : width + rows] = told.astype(BF)


def told_rows(cap, in_ref, which):
    buffers, width = in_ref.shape
    count = buffers // cap
    source = lax.broadcasted_iota(jnp.int32, (count, buffers), 0)
    place = lax.broadcasted_iota(jnp.int32, (count, buffers), 1)
    pick = jnp.where(place == source * cap + which, 1.0, 0.0).astype(BF)
    return dot(pick, in_ref[:, width - LANES : width])


def collect_kernel(cap, slots, row_ref, col_ref, back_ref, out_ref):
    rows = out_ref.shape[0]
    owner_row = row_ref[...] // slots
    owner_col = col_ref[...] // slots
    first = lax.broadcasted_iota(jnp.int32, (rows, rows), 0)
    second = lax.broadcasted_iota(jnp.int32, (rows, rows), 1)
    same = jnp.where((owner_col == owner_row) & (second < first), 1.0, 0.0)
    rank = jnp.sum(same, axis=1, keepdims=True)
    pos = owner_col.astype(F32) * cap + rank
    place = lax.broadcasted_iota(jnp.int32, (rows, back_ref.shape[0]), 1).astype(F32)
    hot = jnp.where(place == pos, 1.0, 0.0).astype(BF)
    out_ref[...] = dot(hot, back_ref[...]).astype(BF)


def mask_kernel(cap, slots, in_ref, codes_ref, mask_ref, route_ref):
    total = mask_ref.shape[0]
    route_ref[...] = told_rows(cap, in_ref, 0) * slots + told_rows(cap, in_ref, 1)
    codes = jnp.broadcast_to(codes_ref[...], (total, LANES))
    hits = jnp.zeros((total, LANES), F32)
    for s in range(route_ref.shape[0]):
        hits = hits + jnp.where(codes == route_ref[s : s + 1, :], 1.0, 0.0)
    mask_ref[...] = jnp.broadcast_to(jnp.sum(hits, axis=1, keepdims=True), (total, LANES))


def slot_table(cap, slots, me, in_ref):
    buffers = in_ref.shape[0]
    count = buffers // cap
    mine_f = jnp.where(told_rows(cap, in_ref, 0) == me.astype(F32), 1.0, 0.0)
    slot_f = told_rows(cap, in_ref, 1)
    first = lax.broadcasted_iota(jnp.int32, (LANES, LANES), 0)
    second = lax.broadcasted_iota(jnp.int32, (LANES, LANES), 1)
    tri = jnp.where(first < second, 1.0, 0.0).astype(BF)
    rank = dot(mine_f.astype(BF), tri)
    lane = lax.broadcasted_iota(jnp.int32, (count, LANES), 1)
    held = jnp.zeros((count, LANES), F32)
    for j in range(cap):
        here = jnp.where(rank == j, mine_f, 0.0)
        number = jnp.sum(here, axis=1, keepdims=True)
        value = jnp.sum(here * slot_f, axis=1, keepdims=True)
        value = value + (1.0 - number) * slots
        held = jnp.where(lane == j, value, held)
    place = lax.broadcasted_iota(jnp.int32, (buffers, count), 0)
    source = lax.broadcasted_iota(jnp.int32, (buffers, count), 1)
    spread = jnp.where(place // cap == source, 1.0, 0.0).astype(BF)
    wide = dot(spread, held.astype(BF))
    place = lax.broadcasted_iota(jnp.int32, (buffers, LANES), 0)
    lane = lax.broadcasted_iota(jnp.int32, (buffers, LANES), 1)
    slot_col = jnp.sum(jnp.where(place % cap == lane, wide, 0.0), axis=1, keepdims=True)
    slot_id = lax.broadcasted_iota(jnp.int32, (buffers, slots), 1).astype(F32)
    return jnp.where(slot_col == slot_id, 1.0, 0.0)


GROUP = 16
FOLD = LANES // GROUP


def permutation(channels, depth):
    perm = np.zeros((channels // GROUP, PAIR, PAIR), np.float32)
    for i in range(channels // GROUP):
        for j in range(GROUP):
            for z in range(depth):
                perm[i, depth * j + z, LANES * (z // FOLD) + GROUP * ((z + i) % FOLD) + j] = 1.0
    return perm


def lane_group(rows):
    return lax.broadcasted_iota(jnp.int32, (rows, LANES), 1) // GROUP


def spread_pairs(turned_ref, out_ref):
    chunks, rows, _ = turned_ref.shape
    step = 32
    group = lane_group(step)

    def body(t, carry):
        at = pl.ds(pl.multiple_of(t * step, step), step)
        for half in range(2):
            lanes = slice(half * LANES, (half + 1) * LANES)
            parts = [turned_ref[i, at, lanes] for i in range(chunks)]
            parts = parts + [jnp.zeros((step, LANES), F32)] * (FOLD - chunks)
            for bit in (1, 2, 4):
                odd = (group & bit) != 0
                parts = [jnp.where(odd, parts[(i + bit) % FOLD], parts[i]) for i in range(FOLD)]
            for g in range(FOLD):
                value = parts[(-g) % FOLD]
                if g:
                    value = pltpu.roll(value, LANES - GROUP * g, 1)
                z = half * FOLD + g
                out_ref[z // 2, at, (z % 2) * LANES : (z % 2 + 1) * LANES] = value.astype(BF)
        return carry

    lax.fori_loop(0, rows // step, body, 0)


def gather_pairs(in_ref, turned_ref):
    chunks, rows, _ = turned_ref.shape
    step = 32
    group = lane_group(step)

    def body(t, carry):
        at = pl.ds(pl.multiple_of(t * step, step), step)
        for half in range(2):
            turned = []
            for g in range(FOLD):
                z = half * FOLD + g
                value = in_ref[z // 2, at, (z % 2) * LANES : (z % 2 + 1) * LANES].astype(F32)
                turned.append(pltpu.roll(value, GROUP * g, 1) if g else value)
            parts = [turned[(-i) % FOLD] for i in range(FOLD)]
            for bit in (1, 2, 4):
                odd = (group & bit) != 0
                parts = [jnp.where(odd, parts[(i - bit) % FOLD], parts[i]) for i in range(FOLD)]
            for i in range(chunks):
                turned_ref[i, at, half * LANES : (half + 1) * LANES] = parts[i].astype(BF)
        return carry

    lax.fori_loop(0, rows // step, body, 0)


def to_pairs_kernel(rows_ref, perm_ref, out_ref, turned_ref):
    for i in range(perm_ref.shape[0]):
        turned_ref[i] = dot(rows_ref[:, i * PAIR : (i + 1) * PAIR], perm_ref[i])
    spread_pairs(turned_ref, out_ref)


def place_kernel(cap, slots, me_ref, rows_ref, perm_ref, out_ref, take_ref, turned_ref):
    take = slot_table(cap, slots, me_ref[0], rows_ref)
    take_ref[...] = take.astype(BF)
    put = take.T.astype(BF)
    for i in range(perm_ref.shape[0]):
        held = dot(put, rows_ref[:, i * PAIR : (i + 1) * PAIR]).astype(BF)
        turned_ref[i] = dot(held, perm_ref[i])
    spread_pairs(turned_ref, out_ref)


def message_kernel(f_ref, xlo_ref, xhi_ref, pick_ref, low_ref, high_ref):
    pick = pick_ref[...]
    half = low_ref.shape[1]
    for k in range(f_ref.shape[0]):
        rows = jnp.concatenate([xlo_ref[k], f_ref[k], xhi_ref[k]], axis=0)
        sent = dot(pick, rows).astype(BF)
        low_ref[k] = sent[0:half]
        high_ref[k] = sent[half : 2 * half]


def build_band(band_ref, raw_ref, backward):
    channels = raw_ref.shape[1]
    band_ref[...] = jnp.zeros_like(band_ref)
    for tap in range(27):
        value = raw_ref[26 - tap] if backward else raw_ref[tap].T
        for zo in range(2):
            row = ((tap // 3) * 4 + zo + tap % 3) * LANES
            band_ref[row : row + channels, zo * LANES : zo * LANES + channels] = value


NX = 16
NY = 16
OUT_MAIN = (NX + 2) * NY
EDGE = 24
OUT_ROWS = OUT_MAIN + 2 * EDGE
MSG = 48
M_XLO = NX * NY
M_XHI = M_XLO + 2 * NY
M_YLO = M_XHI + 2 * NY
M_YHI = M_YLO + MSG
M_LOW = M_YHI + MSG
M_HIGH = M_LOW + MSG
M_EDGE = M_HIGH + MSG
M_ROWS = M_EDGE + 2 * EDGE


def twice(value):
    return jnp.concatenate([value, value], axis=1)


def put_pair(ref, lead, k, tail, value):
    value = value.astype(BF)
    ref[lead + (k,) + tail + (slice(LANES, PAIR),)] = value[:, 0:LANES]
    ref[lead + (k + 1,) + tail + (slice(0, LANES),)] = value[:, LANES:PAIR]


def clear_ends(ref, lead):
    last = ref.shape[len(lead)] - 1
    dims = ref.shape[len(lead) + 1 : -1]
    ref[lead + (0,) + (slice(None),) * len(dims) + (slice(0, LANES),)] = jnp.zeros(dims + (LANES,), BF)
    ref[lead + (last,) + (slice(None),) * len(dims) + (slice(LANES, PAIR),)] = jnp.zeros(dims + (LANES,), BF)


def put_shifted(ext_ref, k, xp, mid, before, after, row):
    ny = mid.shape[0]
    up = jnp.where(row == 0, before, pltpu.roll(mid, 1, 0))
    down = jnp.where(row == ny - 1, after, pltpu.roll(mid, ny - 1, 0))
    for b, value in enumerate((up, mid, down)):
        put_pair(ext_ref, (b,), k, (xp, slice(None)), value)


def widen_two(ext_ref, edge_ref, f_ref, xlo_ref, xhi_ref, ylo_ref, yhi_ref, low_ref, high_ref, mask_ref=None):
    pairs = f_ref.shape[0]
    for b in range(3):
        clear_ends(ext_ref, (b,))
        for a in range(3):
            clear_ends(edge_ref, (a, b))
    row = lax.broadcasted_iota(jnp.int32, (NY, PAIR), 0)

    def read(ref, k, start, size, mask_start):
        value = ref[k, start : start + size, :].astype(F32)
        if mask_ref is None:
            return value
        return value * twice(mask_ref[mask_start + start : mask_start + start + size, :])

    def body(k, carry):
        ylo = read(ylo_ref, k, 0, MSG, M_YLO)
        yhi = read(yhi_ref, k, 0, MSG, M_YHI)
        low = read(low_ref, k, 0, MSG, M_LOW)
        high = read(high_ref, k, 0, MSG, M_HIGH)
        wide = NX + 4
        for xp in range(wide):
            if xp < 2:
                mid = read(xlo_ref, k, xp * NY, NY, M_XLO)
            elif xp >= NX + 2:
                mid = read(xhi_ref, k, (xp - NX - 2) * NY, NY, M_XHI)
            else:
                mid = read(f_ref, k, (xp - 2) * NY, NY, 0)
            put_shifted(ext_ref, k, xp, mid, ylo[wide + xp : wide + xp + 1, :], yhi[xp : xp + 1, :], row)
        first = ((ylo, 0), (ylo, wide), (low, 0))
        second = ((high, wide), (yhi, 0), (yhi, wide))
        for a in range(3):
            for b in range(3):
                sides = []
                for value, start in (first[b], second[b]):
                    turn = start + a
                    if turn:
                        value = pltpu.roll(value, MSG - turn, 0)
                    sides.append(value[0:EDGE])
                put_pair(edge_ref, (a, b), k, (slice(None),), jnp.concatenate(sides, axis=0))
        return carry

    lax.fori_loop(0, pairs, body, 0)


def widen_near(ext_ref, f_ref, xlo_ref, xhi_ref, ylo_ref, yhi_ref):
    for b in range(3):
        clear_ends(ext_ref, (b,))
    row = lax.broadcasted_iota(jnp.int32, (NY, PAIR), 0)
    wide = NX + 4

    def body(k, carry):
        ylo = ylo_ref[k].astype(F32)
        yhi = yhi_ref[k].astype(F32)
        for xp in range(NX + 2):
            if xp == 0:
                mid = xlo_ref[k, NY : 2 * NY, :].astype(F32)
            elif xp == NX + 1:
                mid = xhi_ref[k, 0:NY, :].astype(F32)
            else:
                mid = f_ref[k, (xp - 1) * NY : xp * NY, :].astype(F32)
            put_shifted(ext_ref, k, xp, mid, ylo[wide + xp + 1 : wide + xp + 2, :], yhi[xp + 1 : xp + 2, :], row)
        return carry

    lax.fori_loop(0, f_ref.shape[0], body, 0)


def widen_one(ext_ref, rows_ref):
    pairs = rows_ref.shape[0]
    for b in range(3):
        clear_ends(ext_ref, (b,))
    row = lax.broadcasted_iota(jnp.int32, (NY, PAIR), 0)

    def body(k, carry):
        edges = rows_ref[k, OUT_MAIN:OUT_ROWS, :].astype(F32)
        for xp in range(NX + 2):
            mid = rows_ref[k, xp * NY : (xp + 1) * NY, :].astype(F32)
            put_shifted(ext_ref, k, xp, mid, edges[xp : xp + 1, :], edges[EDGE + xp : EDGE + xp + 1, :], row)
        return carry

    lax.fori_loop(0, pairs, body, 0)


STEP = 2


def conv_wide(ext_ref, edge_ref, w_ref, k):
    pieces = []
    for a in range(3):
        for b in range(3):
            for j in range(2):
                parts = []
                for i in range(STEP):
                    parts.append(ext_ref[b, k + i + j, a : a + NX + 2].reshape(OUT_MAIN, PAIR))
                    parts.append(edge_ref[a, b, k + i + j])
                pieces.append(jnp.concatenate(parts, axis=0))
    return dot(jnp.concatenate(pieces, axis=1), w_ref[...])


def conv_inner(ext_ref, w_ref, k):
    pieces = []
    for a in range(3):
        for b in range(3):
            for j in range(2):
                pieces.append(ext_ref[b, pl.ds(k + j, STEP), a : a + NX].reshape(STEP * NX * NY, PAIR))
    return dot(jnp.concatenate(pieces, axis=1), w_ref[...])


def each_step(pairs, body):
    def step(t, carry):
        body(t * STEP)
        return carry

    lax.fori_loop(0, pairs // STEP, step, 0)


def out_mask(mask_ref):
    return twice(jnp.concatenate([
        mask_ref[M_XLO + NY : M_XLO + 2 * NY, :], mask_ref[0 : NX * NY, :],
        mask_ref[M_XHI : M_XHI + NY, :], mask_ref[M_EDGE:M_ROWS, :],
    ], axis=0))


def outer_kernel(f_ref, xlo_ref, xhi_ref, ylo_ref, yhi_ref, low_ref, high_ref, mask_ref, raw_ref,
                 out_ref, outer_ref, ext_ref, edge_ref, w_ref):
    build_band(w_ref, raw_ref, True)
    widen_two(ext_ref, edge_ref, f_ref, xlo_ref, xhi_ref, ylo_ref, yhi_ref, low_ref, high_ref, mask_ref)

    def body(k):
        total = conv_wide(ext_ref, edge_ref, w_ref, k)
        for i in range(STEP):
            out_ref[k + i] = total[i * OUT_ROWS : (i + 1) * OUT_ROWS]
            outer_ref[k + i] = (f_ref[k + i].astype(F32) * twice(mask_ref[0 : NX * NY, :])).astype(BF)

    each_step(f_ref.shape[0], body)


def correlate(gt_ref, ext_ref, taps_ref, channels):
    blocks = ext_ref.shape[1]

    def body(ab, carry):
        a = ab // 3
        b = ab % 3
        both = dot(gt_ref[...], ext_ref[b, :, pl.ds(a, NX)].reshape(blocks * NX * NY, PAIR))
        near = both[0 : 2 * channels]
        far = both[2 * channels : 4 * channels]
        low = slice(0, channels)
        high = slice(channels, 2 * channels)
        taps_ref[3 * ab] = near[low, 0:LANES] + near[high, LANES:PAIR]
        taps_ref[3 * ab + 1] = near[low, LANES:PAIR] + far[high, 0:LANES]
        taps_ref[3 * ab + 2] = far[low, 0:LANES] + far[high, LANES:PAIR]
        return carry

    lax.fori_loop(0, 9, body, 0)


def pack_taps(taps_ref, packed_ref, channels):
    lane = lax.broadcasted_iota(jnp.int32, (channels, LANES), 1)
    for g in range(7):
        t1 = pltpu.roll(taps_ref[4 * g + 1], 96, 1)
        t2 = pltpu.roll(taps_ref[4 * g + 2], 64, 1)
        t3 = pltpu.roll(taps_ref[4 * g + 3], 32, 1)
        blocks = (
            jnp.where(lane < 96, taps_ref[4 * g], t1),
            jnp.where(lane < 64, t1, t2),
            jnp.where(lane < 32, t2, t3),
        )
        for i, value in enumerate(blocks):
            start = (3 * g + i) * channels
            packed_ref[start : start + channels, :] = value
    rest = packed_ref.shape[0] - 21 * channels
    if rest:
        packed_ref[21 * channels :, :] = jnp.zeros((rest, LANES), F32)


def hidden_kernel(f_ref, xlo_ref, xhi_ref, ylo_ref, yhi_ref, low_ref, high_ref, mask_ref, raw_ref, grad_ref,
                  act_ref, hg_ref, ext_ref, edge_ref, w_ref):
    build_band(w_ref, raw_ref, False)
    widen_two(ext_ref, edge_ref, f_ref, xlo_ref, xhi_ref, ylo_ref, yhi_ref, low_ref, high_ref)

    def body(k):
        total = conv_wide(ext_ref, edge_ref, w_ref, k)
        m = out_mask(mask_ref)
        for i in range(STEP):
            hidden = m * total[i * OUT_ROWS : (i + 1) * OUT_ROWS]
            sigma = jax.nn.sigmoid(hidden)
            act_ref[k + i] = (hidden * sigma).astype(BF)
            hg_ref[k + i] = (m * grad_ref[k + i] * sigma * (1.0 + hidden * (1.0 - sigma))).astype(BF)

    each_step(f_ref.shape[0], body)


def turn(gt_ref, g_ref, start, channels):
    inner = NX * NY
    pairs = g_ref.shape[0]
    two = 2 * channels
    gt_ref[0:two, pairs * inner :] = jnp.zeros((two, inner), BF)
    gt_ref[two : 2 * two, 0:inner] = jnp.zeros((two, inner), BF)
    for k in range(pairs):
        value = g_ref[k, start : start + inner, :].T
        for i in range(2):
            half = value[i * LANES : i * LANES + channels]
            at = i * channels
            gt_ref[at : at + channels, k * inner : (k + 1) * inner] = half
            gt_ref[two + at : two + at + channels, (k + 1) * inner : (k + 2) * inner] = half


def corr_kernel(channels, core_ref, f_ref, xlo_ref, xhi_ref, ylo_ref, yhi_ref, hg_ref, act_ref, outer_ref,
                keep_ref, give_ref, ext_ref, gt_ref, taps_ref, packed_ref):
    half = keep_ref.shape[1]
    mine = pl.ds(pl.multiple_of(core_ref[0] * half, half), half)
    other = pl.ds(pl.multiple_of((1 - core_ref[0]) * half, half), half)
    taps_ref[27] = jnp.zeros((channels, LANES), F32)
    for i in range(2):
        if i == 0:
            widen_near(ext_ref, f_ref, xlo_ref, xhi_ref, ylo_ref, yhi_ref)
            turn(gt_ref, hg_ref, NY, channels)
        else:
            widen_one(ext_ref, act_ref)
            turn(gt_ref, outer_ref, 0, channels)
        correlate(gt_ref, ext_ref, taps_ref, channels)
        pack_taps(taps_ref, packed_ref, channels)
        keep_ref[i] = packed_ref[mine, :]
        give_ref[i] = packed_ref[other, :]


def grid_grad_kernel(hg_ref, raw_ref, outer_ref, perm_ref, take_ref, out_ref, ext_ref, sum_ref, turned_ref, w_ref):
    build_band(w_ref, raw_ref, True)
    widen_one(ext_ref, hg_ref)

    def body(k):
        total = conv_inner(ext_ref, w_ref, k)
        rows = NX * NY
        for i in range(STEP):
            sum_ref[k + i] = (outer_ref[k + i].astype(F32) + total[i * rows : (i + 1) * rows]).astype(BF)

    each_step(outer_ref.shape[0], body)
    gather_pairs(sum_ref, turned_ref)
    take = take_ref[...]
    for i in range(perm_ref.shape[0]):
        rows = dot_nt(turned_ref[i], perm_ref[i]).astype(BF)
        out_ref[:, i * PAIR : (i + 1) * PAIR] = dot(take, rows).astype(BF)


def block_kernel(act_ref, mask_ref, raw_ref, field_ref, perm_ref, out_ref, ext_ref, sum_ref, turned_ref, w_ref):
    build_band(w_ref, raw_ref, False)
    widen_one(ext_ref, act_ref)

    def body(k):
        total = conv_inner(ext_ref, w_ref, k)
        m = twice(mask_ref[0 : NX * NY, :])
        rows = NX * NY
        for i in range(STEP):
            sum_ref[k + i] = (field_ref[k + i].astype(F32) + m * total[i * rows : (i + 1) * rows]).astype(BF)

    each_step(field_ref.shape[0], body)
    gather_pairs(sum_ref, turned_ref)
    for i in range(perm_ref.shape[0]):
        out_ref[:, i * PAIR : (i + 1) * PAIR] = dot_nt(turned_ref[i], perm_ref[i]).astype(BF)


def pair_sum_kernel(keep_ref, got_ref, out_ref):
    count, _, chunk, _ = out_ref.shape
    for i in range(2):
        for s in range(count):
            rows = slice(s * chunk, (s + 1) * chunk)
            out_ref[s, i] = (keep_ref[i, rows, :] + got_ref[i, rows, :]).astype(BF)


def chunk_sum_kernel(in_ref, out_ref):
    count = in_ref.shape[0]
    for i in range(2):
        total = in_ref[0, i].astype(F32)
        for s in range(1, count):
            total = total + in_ref[s, i].astype(F32)
        total = total.astype(BF)
        for s in range(count):
            out_ref[s, i] = total


def unpack_kernel(factor, core_ref, mine_ref, other_ref, first_ref, second_ref, flat_ref):
    count, _, chunk, _ = mine_ref.shape
    half = count * chunk
    for i, out_ref in enumerate((first_ref, second_ref)):
        for s in range(count):
            start = core_ref[0] * half + s * chunk
            flat_ref[pl.ds(pl.multiple_of(start, chunk), chunk), :] = mine_ref[s, i].astype(F32)
            start = (1 - core_ref[0]) * half + s * chunk
            flat_ref[pl.ds(pl.multiple_of(start, chunk), chunk), :] = other_ref[s, i].astype(F32)
        unpack_taps(factor, flat_ref, out_ref)


def unpack_taps(factor, packed_ref, out_ref):
    channels = out_ref.shape[1]
    lane = lax.broadcasted_iota(jnp.int32, (channels, LANES), 1)
    for g in range(7):
        v = []
        for i in range(3):
            start = (3 * g + i) * channels
            v.append(packed_ref[start : start + channels, :] * factor)
        taps = (
            v[0],
            pltpu.roll(jnp.where(lane < 64, v[1], v[0]), 32, 1),
            pltpu.roll(jnp.where(lane < 32, v[2], v[1]), 64, 1),
            pltpu.roll(v[2], 96, 1),
        )
        for u in range(4):
            if 4 * g + u < 27:
                out_ref[4 * g + u] = taps[u][:, 0:channels]


RX = ("cx", "core")
ALL = ("cx", "core", "ry")
SAME_CORE = ("cx", "ry")


def size_of(axes):
    return int(np.prod([lax.axis_size(a) for a in ((axes,) if isinstance(axes, str) else axes)]))


def share(parts, axes):
    return lax.all_to_all(parts, axes, split_axis=0, concat_axis=0, tiled=True)


def neighbours(axes, upper, lower):
    count = size_of(axes)
    ahead = [(i, i + 1) for i in range(count - 1)]
    behind = [(t, s) for s, t in ahead]
    return lax.ppermute(upper, axes, ahead), lax.ppermute(lower, axes, behind)


def swap_cores(value):
    count = size_of(RX)
    return lax.ppermute(value, RX, [(i, i ^ 1) for i in range(count)])


def message_rows():
    cells = []
    for ys in ((0, 1), (NY - 2, NY - 1)):
        for y in ys:
            cells += [(x, y) for x in range(-2, NX + 2)]
        cells += [None] * (MSG - 2 * (NX + 4))
    return cells


def exchange(field, pick):
    pairs = field.shape[0]
    xlo, xhi = neighbours(RX, field[:, (NX - 2) * NY :, :], field[:, : 2 * NY, :])
    message = jax.ShapeDtypeStruct((pairs, MSG, PAIR), BF)
    low, high = call(message_kernel, (message, message), 5e8, 3e6)(field, xlo, xhi, pick)
    ylo, yhi = neighbours("ry", high, low)
    return xlo, xhi, ylo, yhi, low, high


def mask_cells():
    cells = [(x, y) for x in range(NX) for y in range(NY)]
    cells += [(x, y) for x in (-2, -1) for y in range(NY)]
    cells += [(x, y) for x in (NX, NX + 1) for y in range(NY)]
    for ys in ((-2, -1), (NY, NY + 1), (0, 1), (NY - 2, NY - 1)):
        for y in ys:
            cells += [(x, y) for x in range(-2, NX + 2)]
        cells += [None] * (MSG - 2 * (NX + 4))
    for y in (-1, NY):
        cells += [(x, y) for x in range(-1, NX + 1)]
        cells += [None] * (EDGE - NX - 2)
    return cells


def on_device(column_features, column_route, cotangent, first_weight, second_weight):
    count_x = size_of(RX)
    count_y = size_of("ry")
    count_all = count_x * count_y
    shard_rows, row_width = column_features.shape
    channels = first_weight.shape[1]
    depth = row_width // channels
    slots = NX * NY
    pairs = depth // 2
    chunks = channels // GROUP
    cap = 2 * shard_rows // count_all
    buffers = count_all * cap
    me_x = lax.axis_index(RX)
    me_y = lax.axis_index("ry")
    core = lax.axis_index("core").astype(jnp.int32).reshape(1)
    conv_flops = 2 * slots * pairs * 36 * LANES * PAIR

    shape = jax.ShapeDtypeStruct
    field_shape = shape((pairs, slots, PAIR), BF)
    wide_shape = shape((pairs, OUT_ROWS, PAIR), BF)
    ext = pltpu.VMEM((3, pairs + 1, NX + 4, NY, PAIR), BF)
    edge = pltpu.VMEM((3, 3, pairs + 1, 2 * EDGE, PAIR), BF)
    turned = pltpu.VMEM((chunks, slots, PAIR), F32)
    turned_low = pltpu.VMEM((chunks, slots, PAIR), BF)
    sums = pltpu.VMEM((pairs, slots, PAIR), BF)

    perm = jnp.asarray(permutation(channels, depth), BF)
    pick_np = np.zeros((2 * MSG, (NX + 4) * NY), np.float32)
    for r, cell in enumerate(message_rows()):
        if cell is not None:
            pick_np[r, (cell[0] + 2) * NY + cell[1]] = 1.0
    pick = jnp.asarray(pick_np, BF)

    route_row = column_route.reshape(1, shard_rows)
    route_col = column_route.reshape(shard_rows, 1)
    told_width = row_width + LANES
    outgoing = call(
        functools.partial(send_kernel, cap, slots), shape((buffers, told_width), BF),
        2 * buffers * shard_rows * row_width, 3 * shard_rows * row_width * 2,
    )(route_row, route_col, column_features)
    incoming = share(outgoing.reshape(count_all, cap, told_width), ALL).reshape(buffers, told_width)

    cells = mask_cells()
    steps = np.asarray([(0, 0) if c is None else (c[0] // NX, c[1] // NY) for c in cells], np.int32)
    local = np.asarray([-1 if c is None else (c[0] % NX) * NY + c[1] % NY for c in cells], np.int32)
    to_x = me_x + steps[:, 0]
    to_y = me_y + steps[:, 1]
    inside = (to_x >= 0) & (to_x < count_x) & (to_y >= 0) & (to_y < count_y) & (local >= 0)
    codes = jnp.where(inside, (to_x * count_y + to_y) * slots + local, -1).astype(F32)[:, None]
    me = (me_x * count_y + me_y).astype(jnp.int32).reshape(1)

    cot = call(
        to_pairs_kernel, field_shape, 1e9, 3e6, (turned,),
    )(cotangent.reshape(slots, row_width), perm)
    cot_halo = exchange(cot, pick)

    smem = pl.BlockSpec(memory_space=pltpu.SMEM)
    vmem = pl.BlockSpec(memory_space=pltpu.VMEM)
    field, take = call(
        functools.partial(place_kernel, cap, slots), (field_shape, shape((buffers, slots), BF)), 1e9, 3e6,
        (turned,), in_specs=[smem, vmem, vmem],
    )(me, incoming, perm)
    field_halo = exchange(field, pick)

    mask = call(
        functools.partial(mask_kernel, cap, slots), shape((M_ROWS, LANES), F32), 1e8, 1e6,
        (pltpu.VMEM((count_all, LANES), F32),),
    )(incoming, codes)
    band = pltpu.VMEM((36 * LANES, PAIR), BF)
    ext_near = pltpu.VMEM((3, pairs + 1, NX + 2, NY, PAIR), BF)
    act_grad, outer = call(
        outer_kernel, (shape((pairs, OUT_ROWS, PAIR), F32), field_shape),
        1.3 * conv_flops, 7e6, (ext, edge, band), ROOM_WIDE,
    )(cot, *cot_halo, mask, second_weight)

    unit = 16 * count_all
    packed_rows = -(-21 * channels // unit) * unit
    half = packed_rows // 2
    chunk = packed_rows // count_all
    half_shape = shape((2, half, LANES), F32)
    act, hg = call(
        hidden_kernel, (wide_shape, wide_shape), 1.3 * conv_flops, 8e6, (ext, edge, band), ROOM_WIDE,
    )(field, *field_halo, mask, first_weight, act_grad)

    back = call(
        grid_grad_kernel, shape((buffers, row_width), BF), 1.2 * conv_flops, 6e6,
        (ext_near, sums, turned_low, band), ROOM_NEAR,
    )(hg, first_weight, outer, perm, take)
    returned = share(back.reshape(count_all, cap, row_width), ALL).reshape(buffers, row_width)

    act, back = lax.optimization_barrier((act, back))
    keep, give = call(
        functools.partial(corr_kernel, channels), (half_shape, half_shape), 2 * conv_flops, 10e6,
        (
            ext_near, pltpu.VMEM((4 * channels, (pairs + 1) * slots), BF),
            pltpu.VMEM((28, channels, LANES), F32), pltpu.VMEM((packed_rows, LANES), F32),
        ),
        ROOM_CORR, in_specs=[smem] + [vmem] * 8,
    )(core, field, *field_halo[:4], hg, act, outer)
    got = swap_cores(give)
    got, returned = lax.optimization_barrier((got, returned))
    sent = call(
        pair_sum_kernel, shape((count_all // 2, 2, chunk, LANES), BF), 1e6, 2e6,
    )(keep, got)
    parts = share(sent, SAME_CORE)
    act, sent = lax.optimization_barrier((act, sent))
    block_output = call(
        block_kernel, shape((slots, row_width), BF), 1.2 * conv_flops, 8e6,
        (ext_near, sums, turned_low, band), ROOM_NEAR,
    )(act, mask, second_weight, field, perm)

    parts, block_output = lax.optimization_barrier((parts, block_output))
    totals = share(call(
        chunk_sum_kernel, shape((count_all // 2, 2, chunk, LANES), BF), 1e6, 1e6,
    )(parts), SAME_CORE)

    feature_grads = call(
        functools.partial(collect_kernel, cap, slots), shape((shard_rows, row_width), BF),
        2 * buffers * shard_rows * row_width, 3 * shard_rows * row_width * 2,
    )(route_row, route_col, returned)

    factor = float(1.0 / np.sqrt(np.float32(count_all * shard_rows * depth)))
    grads = shape(first_weight.shape, F32)
    first_grad, second_grad = call(
        functools.partial(unpack_kernel, factor), (grads, grads), 1e6, 4e6,
        (pltpu.VMEM((packed_rows, LANES), F32),), in_specs=[smem, vmem, vmem],
    )(core, totals, swap_cores(totals))
    return (block_output.reshape(cotangent.shape), feature_grads, first_grad, second_grad)


def solution(mesh):
    count_x = mesh.shape["rx"]
    fine = jax.sharding.Mesh(mesh.devices.reshape(count_x // 2, 2, mesh.shape["ry"]), ALL)
    in_specs = (P(ALL, None), P(ALL), P(RX, "ry", None), P(), P())
    out_specs = (P(RX, "ry", None), P(ALL, None), P(), P())
    return jax.shard_map(
        on_device, mesh=fine, in_specs=in_specs, out_specs=out_specs, check_vma=False
    )
```

```python
import functools

import jax
import jax.numpy as jnp
import numpy as np
from jax import lax
from jax.experimental import pallas as pl
from jax.experimental.pallas import tpu as pltpu
from jax.sharding import PartitionSpec as P

LANES = 128
PAIR = 256
MIB = 1024 * 1024
ROOM_WIDE, ROOM_NEAR, ROOM_CORR, ROOM_SMALL = 20, 14, 16, 5
BF = jnp.bfloat16
F32 = jnp.float32


def call(body, out_shape, flops, moved, scratch=(), room=ROOM_SMALL, **extra):
    return pl.pallas_call(
        body,
        out_shape=out_shape,
        scratch_shapes=list(scratch),
        compiler_params=pltpu.CompilerParams(vmem_limit_bytes=room * MIB),
        cost_estimate=pl.CostEstimate(flops=int(flops), bytes_accessed=int(moved), transcendentals=0),
        **extra,
    )


def dot(left, right):
    return jnp.dot(left, right, preferred_element_type=F32)


def dot_nt(left, right):
    return lax.dot_general(left, right, (((1,), (1,)), ((), ())), preferred_element_type=F32)


def send_kernel(cap, slots, row_ref, col_ref, feat_ref, out_ref):
    rows, width = feat_ref.shape
    buffers = out_ref.shape[0]
    owner_row = row_ref[...] // slots
    owner_col = col_ref[...] // slots
    first = lax.broadcasted_iota(jnp.int32, (rows, rows), 0)
    second = lax.broadcasted_iota(jnp.int32, (rows, rows), 1)
    same = jnp.where((owner_col == owner_row) & (first < second), 1.0, 0.0)
    rank = jnp.sum(same, axis=0, keepdims=True)
    pos = owner_row.astype(F32) * cap + rank
    place = lax.broadcasted_iota(jnp.int32, (buffers, rows), 0)
    hot = jnp.where(place.astype(F32) == pos, 1.0, 0.0).astype(BF)
    out_ref[:, 0:width] = dot(hot, feat_ref[...]).astype(BF)
    slot_row = (row_ref[...] % slots).astype(F32)
    kind = place % cap
    told = jnp.where(kind == 0, owner_row.astype(F32), jnp.where(kind == 1, slot_row, 0.0))
    out_ref[:, width : width + rows] = told.astype(BF)


def told_rows(cap, in_ref, which):
    buffers, width = in_ref.shape
    count = buffers // cap
    source = lax.broadcasted_iota(jnp.int32, (count, buffers), 0)
    place = lax.broadcasted_iota(jnp.int32, (count, buffers), 1)
    pick = jnp.where(place == source * cap + which, 1.0, 0.0).astype(BF)
    return dot(pick, in_ref[:, width - LANES : width])


def collect_kernel(cap, slots, row_ref, col_ref, back_ref, out_ref):
    rows = out_ref.shape[0]
    owner_row = row_ref[...] // slots
    owner_col = col_ref[...] // slots
    first = lax.broadcasted_iota(jnp.int32, (rows, rows), 0)
    second = lax.broadcasted_iota(jnp.int32, (rows, rows), 1)
    same = jnp.where((owner_col == owner_row) & (second < first), 1.0, 0.0)
    rank = jnp.sum(same, axis=1, keepdims=True)
    pos = owner_col.astype(F32) * cap + rank
    place = lax.broadcasted_iota(jnp.int32, (rows, back_ref.shape[0]), 1).astype(F32)
    hot = jnp.where(place == pos, 1.0, 0.0).astype(BF)
    out_ref[...] = dot(hot, back_ref[:, 0 : out_ref.shape[1]]).astype(BF)


def mask_kernel(cap, slots, in_ref, codes_ref, mask_ref, route_ref):
    total = mask_ref.shape[0]
    route_ref[...] = told_rows(cap, in_ref, 0) * slots + told_rows(cap, in_ref, 1)
    codes = jnp.broadcast_to(codes_ref[...], (total, LANES))
    hits = jnp.zeros((total, LANES), F32)
    for s in range(route_ref.shape[0]):
        hits = hits + jnp.where(codes == route_ref[s : s + 1, :], 1.0, 0.0)
    mask_ref[...] = jnp.broadcast_to(jnp.sum(hits, axis=1, keepdims=True), (total, LANES))


def slot_table(cap, slots, me, in_ref):
    buffers = in_ref.shape[0]
    count = buffers // cap
    mine_f = jnp.where(told_rows(cap, in_ref, 0) == me.astype(F32), 1.0, 0.0)
    slot_f = told_rows(cap, in_ref, 1)
    first = lax.broadcasted_iota(jnp.int32, (LANES, LANES), 0)
    second = lax.broadcasted_iota(jnp.int32, (LANES, LANES), 1)
    tri = jnp.where(first < second, 1.0, 0.0).astype(BF)
    rank = dot(mine_f.astype(BF), tri)
    lane = lax.broadcasted_iota(jnp.int32, (count, LANES), 1)
    held = jnp.zeros((count, LANES), F32)
    for j in range(cap):
        here = jnp.where(rank == j, mine_f, 0.0)
        number = jnp.sum(here, axis=1, keepdims=True)
        value = jnp.sum(here * slot_f, axis=1, keepdims=True)
        value = value + (1.0 - number) * slots
        held = jnp.where(lane == j, value, held)
    place = lax.broadcasted_iota(jnp.int32, (buffers, count), 0)
    source = lax.broadcasted_iota(jnp.int32, (buffers, count), 1)
    spread = jnp.where(place // cap == source, 1.0, 0.0).astype(BF)
    wide = dot(spread, held.astype(BF))
    place = lax.broadcasted_iota(jnp.int32, (buffers, LANES), 0)
    lane = lax.broadcasted_iota(jnp.int32, (buffers, LANES), 1)
    slot_col = jnp.sum(jnp.where(place % cap == lane, wide, 0.0), axis=1, keepdims=True)
    slot_id = lax.broadcasted_iota(jnp.int32, (buffers, slots), 1).astype(F32)
    return jnp.where(slot_col == slot_id, 1.0, 0.0)


GROUP = 16
FOLD = LANES // GROUP


def permutation(channels, depth):
    perm = np.zeros((channels // GROUP, PAIR, PAIR), np.float32)
    for i in range(channels // GROUP):
        for j in range(GROUP):
            for z in range(depth):
                perm[i, depth * j + z, LANES * (z // FOLD) + GROUP * ((z + i) % FOLD) + j] = 1.0
    return perm


def lane_group(rows):
    return lax.broadcasted_iota(jnp.int32, (rows, LANES), 1) // GROUP


def spread_pairs(turned_ref, out_ref):
    chunks, rows, _ = turned_ref.shape
    step = 32
    group = lane_group(step)

    def body(t, carry):
        at = pl.ds(pl.multiple_of(t * step, step), step)
        for half in range(2):
            lanes = slice(half * LANES, (half + 1) * LANES)
            parts = [turned_ref[i, at, lanes] for i in range(chunks)]
            parts = parts + [jnp.zeros((step, LANES), F32)] * (FOLD - chunks)
            for bit in (1, 2, 4):
                odd = (group & bit) != 0
                parts = [jnp.where(odd, parts[(i + bit) % FOLD], parts[i]) for i in range(FOLD)]
            for g in range(FOLD):
                value = parts[(-g) % FOLD]
                if g:
                    value = pltpu.roll(value, LANES - GROUP * g, 1)
                z = half * FOLD + g
                out_ref[z // 2, at, (z % 2) * LANES : (z % 2 + 1) * LANES] = value.astype(BF)
        return carry

    lax.fori_loop(0, rows // step, body, 0)


def gather_pairs(in_ref, turned_ref):
    chunks, rows, _ = turned_ref.shape
    step = 32
    group = lane_group(step)

    def body(t, carry):
        at = pl.ds(pl.multiple_of(t * step, step), step)
        for half in range(2):
            turned = []
            for g in range(FOLD):
                z = half * FOLD + g
                value = in_ref[z // 2, at, (z % 2) * LANES : (z % 2 + 1) * LANES].astype(F32)
                turned.append(pltpu.roll(value, GROUP * g, 1) if g else value)
            parts = [turned[(-i) % FOLD] for i in range(FOLD)]
            for bit in (1, 2, 4):
                odd = (group & bit) != 0
                parts = [jnp.where(odd, parts[(i - bit) % FOLD], parts[i]) for i in range(FOLD)]
            for i in range(chunks):
                turned_ref[i, at, half * LANES : (half + 1) * LANES] = parts[i].astype(BF)
        return carry

    lax.fori_loop(0, rows // step, body, 0)


def to_pairs_kernel(rows_ref, perm_ref, out_ref, turned_ref):
    for i in range(perm_ref.shape[0]):
        turned_ref[i] = dot(rows_ref[:, i * PAIR : (i + 1) * PAIR], perm_ref[i])
    spread_pairs(turned_ref, out_ref)


def place_kernel(cap, slots, me_ref, rows_ref, perm_ref, out_ref, take_ref, turned_ref):
    take = slot_table(cap, slots, me_ref[0], rows_ref)
    take_ref[...] = take.astype(BF)
    put = take.T.astype(BF)
    for i in range(perm_ref.shape[0]):
        held = dot(put, rows_ref[:, i * PAIR : (i + 1) * PAIR]).astype(BF)
        turned_ref[i] = dot(held, perm_ref[i])
    spread_pairs(turned_ref, out_ref)


def message_kernel(f_ref, xlo_ref, xhi_ref, pick_ref, low_ref, high_ref):
    pick = pick_ref[...]
    half = low_ref.shape[1]
    for k in range(f_ref.shape[0]):
        rows = jnp.concatenate([xlo_ref[k], f_ref[k], xhi_ref[k]], axis=0)
        sent = dot(pick, rows).astype(BF)
        low_ref[k] = sent[0:half]
        high_ref[k] = sent[half : 2 * half]


def build_band(band_ref, raw_ref, backward):
    channels = raw_ref.shape[1]
    band_ref[...] = jnp.zeros_like(band_ref)
    for tap in range(27):
        value = raw_ref[26 - tap] if backward else raw_ref[tap].T
        for zo in range(2):
            row = ((tap // 3) * 4 + zo + tap % 3) * LANES
            band_ref[row : row + channels, zo * LANES : zo * LANES + channels] = value


NX = 16
NY = 16
OUT_MAIN = (NX + 2) * NY
EDGE = 24
OUT_ROWS = OUT_MAIN + 2 * EDGE
MSG = 48
M_XLO = NX * NY
M_XHI = M_XLO + 2 * NY
M_YLO = M_XHI + 2 * NY
M_YHI = M_YLO + MSG
M_LOW = M_YHI + MSG
M_HIGH = M_LOW + MSG
M_EDGE = M_HIGH + MSG
M_ROWS = M_EDGE + 2 * EDGE


def twice(value):
    return jnp.concatenate([value, value], axis=1)


def put_pair(ref, lead, k, tail, value):
    value = value.astype(BF)
    ref[lead + (k,) + tail + (slice(LANES, PAIR),)] = value[:, 0:LANES]
    ref[lead + (k + 1,) + tail + (slice(0, LANES),)] = value[:, LANES:PAIR]


def clear_ends(ref, lead):
    last = ref.shape[len(lead)] - 1
    dims = ref.shape[len(lead) + 1 : -1]
    ref[lead + (0,) + (slice(None),) * len(dims) + (slice(0, LANES),)] = jnp.zeros(dims + (LANES,), BF)
    ref[lead + (last,) + (slice(None),) * len(dims) + (slice(LANES, PAIR),)] = jnp.zeros(dims + (LANES,), BF)


def put_shifted(ext_ref, k, xp, mid, before, after, row):
    ny = mid.shape[0]
    up = jnp.where(row == 0, before, pltpu.roll(mid, 1, 0))
    down = jnp.where(row == ny - 1, after, pltpu.roll(mid, ny - 1, 0))
    for b, value in enumerate((up, mid, down)):
        put_pair(ext_ref, (b,), k, (xp, slice(None)), value)


def widen_two(ext_ref, edge_ref, f_ref, xlo_ref, xhi_ref, ylo_ref, yhi_ref, low_ref, high_ref, mask_ref=None):
    pairs = f_ref.shape[0]
    for b in range(3):
        clear_ends(ext_ref, (b,))
        for a in range(3):
            clear_ends(edge_ref, (a, b))
    row = lax.broadcasted_iota(jnp.int32, (NY, PAIR), 0)

    def read(ref, k, start, size, mask_start):
        value = ref[k, start : start + size, :].astype(F32)
        if mask_ref is None:
            return value
        return value * twice(mask_ref[mask_start + start : mask_start + start + size, :])

    def body(k, carry):
        ylo = read(ylo_ref, k, 0, MSG, M_YLO)
        yhi = read(yhi_ref, k, 0, MSG, M_YHI)
        low = read(low_ref, k, 0, MSG, M_LOW)
        high = read(high_ref, k, 0, MSG, M_HIGH)
        wide = NX + 4
        for xp in range(wide):
            if xp < 2:
                mid = read(xlo_ref, k, xp * NY, NY, M_XLO)
            elif xp >= NX + 2:
                mid = read(xhi_ref, k, (xp - NX - 2) * NY, NY, M_XHI)
            else:
                mid = read(f_ref, k, (xp - 2) * NY, NY, 0)
            put_shifted(ext_ref, k, xp, mid, ylo[wide + xp : wide + xp + 1, :], yhi[xp : xp + 1, :], row)
        first = ((ylo, 0), (ylo, wide), (low, 0))
        second = ((high, wide), (yhi, 0), (yhi, wide))
        for a in range(3):
            for b in range(3):
                sides = []
                for value, start in (first[b], second[b]):
                    turn = start + a
                    if turn:
                        value = pltpu.roll(value, MSG - turn, 0)
                    sides.append(value[0:EDGE])
                put_pair(edge_ref, (a, b), k, (slice(None),), jnp.concatenate(sides, axis=0))
        return carry

    lax.fori_loop(0, pairs, body, 0)


def widen_near(ext_ref, f_ref, xlo_ref, xhi_ref, ylo_ref, yhi_ref):
    for b in range(3):
        clear_ends(ext_ref, (b,))
    row = lax.broadcasted_iota(jnp.int32, (NY, PAIR), 0)
    wide = NX + 4

    def body(k, carry):
        ylo = ylo_ref[k].astype(F32)
        yhi = yhi_ref[k].astype(F32)
        for xp in range(NX + 2):
            if xp == 0:
                mid = xlo_ref[k, NY : 2 * NY, :].astype(F32)
            elif xp == NX + 1:
                mid = xhi_ref[k, 0:NY, :].astype(F32)
            else:
                mid = f_ref[k, (xp - 1) * NY : xp * NY, :].astype(F32)
            put_shifted(ext_ref, k, xp, mid, ylo[wide + xp + 1 : wide + xp + 2, :], yhi[xp + 1 : xp + 2, :], row)
        return carry

    lax.fori_loop(0, f_ref.shape[0], body, 0)


def widen_one(ext_ref, rows_ref):
    pairs = rows_ref.shape[0]
    for b in range(3):
        clear_ends(ext_ref, (b,))
    row = lax.broadcasted_iota(jnp.int32, (NY, PAIR), 0)

    def body(k, carry):
        edges = rows_ref[k, OUT_MAIN:OUT_ROWS, :].astype(F32)
        for xp in range(NX + 2):
            mid = rows_ref[k, xp * NY : (xp + 1) * NY, :].astype(F32)
            put_shifted(ext_ref, k, xp, mid, edges[xp : xp + 1, :], edges[EDGE + xp : EDGE + xp + 1, :], row)
        return carry

    lax.fori_loop(0, pairs, body, 0)


STEP = 2


def conv_wide(ext_ref, edge_ref, w_ref, k):
    pieces = []
    for a in range(3):
        for b in range(3):
            for j in range(2):
                parts = []
                for i in range(STEP):
                    parts.append(ext_ref[b, k + i + j, a : a + NX + 2].reshape(OUT_MAIN, PAIR))
                    parts.append(edge_ref[a, b, k + i + j])
                pieces.append(jnp.concatenate(parts, axis=0))
    return dot(jnp.concatenate(pieces, axis=1), w_ref[...])


def conv_inner(ext_ref, w_ref, k):
    pieces = []
    for a in range(3):
        for b in range(3):
            for j in range(2):
                pieces.append(ext_ref[b, pl.ds(k + j, STEP), a : a + NX].reshape(STEP * NX * NY, PAIR))
    return dot(jnp.concatenate(pieces, axis=1), w_ref[...])


def each_step(pairs, body):
    def step(t, carry):
        body(t * STEP)
        return carry

    lax.fori_loop(0, pairs // STEP, step, 0)


def out_mask(mask_ref):
    return twice(jnp.concatenate([
        mask_ref[M_XLO + NY : M_XLO + 2 * NY, :], mask_ref[0 : NX * NY, :],
        mask_ref[M_XHI : M_XHI + NY, :], mask_ref[M_EDGE:M_ROWS, :],
    ], axis=0))


def outer_kernel(f_ref, xlo_ref, xhi_ref, ylo_ref, yhi_ref, low_ref, high_ref, mask_ref, raw_ref,
                 out_ref, outer_ref, ext_ref, edge_ref, w_ref):
    build_band(w_ref, raw_ref, True)
    widen_two(ext_ref, edge_ref, f_ref, xlo_ref, xhi_ref, ylo_ref, yhi_ref, low_ref, high_ref, mask_ref)

    def body(k):
        total = conv_wide(ext_ref, edge_ref, w_ref, k)
        for i in range(STEP):
            out_ref[k + i] = total[i * OUT_ROWS : (i + 1) * OUT_ROWS]
            outer_ref[k + i] = (f_ref[k + i].astype(F32) * twice(mask_ref[0 : NX * NY, :])).astype(BF)

    each_step(f_ref.shape[0], body)


def correlate(gt_ref, ext_ref, first_x, taps_ref, channels):
    pairs = ext_ref.shape[1] - 1

    def body(ab, carry):
        a = ab // 3
        b = ab % 3
        left = gt_ref[...]
        near = dot(left, ext_ref[b, 0:pairs, pl.ds(a + first_x, NX)].reshape(pairs * NX * NY, PAIR))
        far = dot(left, ext_ref[b, 1 : pairs + 1, pl.ds(a + first_x, NX)].reshape(pairs * NX * NY, PAIR))
        low = slice(0, channels)
        high = slice(channels, 2 * channels)
        taps_ref[3 * ab] = near[low, 0:LANES] + near[high, LANES:PAIR]
        taps_ref[3 * ab + 1] = near[low, LANES:PAIR] + far[high, 0:LANES]
        taps_ref[3 * ab + 2] = far[low, 0:LANES] + far[high, LANES:PAIR]
        return carry

    lax.fori_loop(0, 9, body, 0)


def pack_taps(taps_ref, packed_ref, channels):
    lane = lax.broadcasted_iota(jnp.int32, (channels, LANES), 1)
    for g in range(7):
        t1 = pltpu.roll(taps_ref[4 * g + 1], 96, 1)
        t2 = pltpu.roll(taps_ref[4 * g + 2], 64, 1)
        t3 = pltpu.roll(taps_ref[4 * g + 3], 32, 1)
        blocks = (
            jnp.where(lane < 96, taps_ref[4 * g], t1),
            jnp.where(lane < 64, t1, t2),
            jnp.where(lane < 32, t2, t3),
        )
        for i, value in enumerate(blocks):
            start = (3 * g + i) * channels
            packed_ref[start : start + channels, :] = value
    rest = packed_ref.shape[0] - 21 * channels
    if rest:
        packed_ref[21 * channels :, :] = jnp.zeros((rest, LANES), F32)


def hidden_kernel(f_ref, xlo_ref, xhi_ref, ylo_ref, yhi_ref, low_ref, high_ref, mask_ref, raw_ref, grad_ref,
                  act_ref, hg_ref, ext_ref, edge_ref, w_ref):
    build_band(w_ref, raw_ref, False)
    widen_two(ext_ref, edge_ref, f_ref, xlo_ref, xhi_ref, ylo_ref, yhi_ref, low_ref, high_ref)

    def body(k):
        total = conv_wide(ext_ref, edge_ref, w_ref, k)
        m = out_mask(mask_ref)
        for i in range(STEP):
            hidden = m * total[i * OUT_ROWS : (i + 1) * OUT_ROWS]
            sigma = jax.nn.sigmoid(hidden)
            act_ref[k + i] = (hidden * sigma).astype(BF)
            hg_ref[k + i] = (m * grad_ref[k + i] * sigma * (1.0 + hidden * (1.0 - sigma))).astype(BF)

    each_step(f_ref.shape[0], body)


def turn(gt_ref, g_ref, start, channels):
    inner = NX * NY
    for k in range(g_ref.shape[0]):
        value = g_ref[k, start : start + inner, :].T
        gt_ref[0:channels, k * inner : (k + 1) * inner] = value[0:channels]
        gt_ref[channels : 2 * channels, k * inner : (k + 1) * inner] = value[LANES : LANES + channels]


def corr_kernel(channels, run, core_ref, f_ref, xlo_ref, xhi_ref, ylo_ref, yhi_ref, hg_ref, act_ref, outer_ref,
                keep_ref, give_ref, ext_ref, gt_ref, taps_ref, packed_ref):
    runs = keep_ref.shape[0] // run
    block = 2 * runs * run
    blocks = packed_ref.shape[0] // block
    taps_ref[27] = jnp.zeros((channels, LANES), F32)
    for i in range(2):
        if i == 0:
            widen_near(ext_ref, f_ref, xlo_ref, xhi_ref, ylo_ref, yhi_ref)
            turn(gt_ref, hg_ref, NY, channels)
        else:
            widen_one(ext_ref, act_ref)
            turn(gt_ref, outer_ref, 0, channels)
        correlate(gt_ref, ext_ref, 0, taps_ref, channels)
        pack_taps(taps_ref, packed_ref, channels)
        for l in range(blocks):
            lanes = slice((i * blocks + l) * LANES, (i * blocks + l + 1) * LANES)
            for x in range(runs):
                base = l * block + 2 * x * run
                rows = slice(x * run, (x + 1) * run)
                mine = pl.multiple_of(base + core_ref[0] * run, run)
                other = pl.multiple_of(base + (1 - core_ref[0]) * run, run)
                keep_ref[rows, lanes] = packed_ref[pl.ds(mine, run), :]
                give_ref[rows, lanes] = packed_ref[pl.ds(other, run), :]


def grid_grad_kernel(hg_ref, raw_ref, outer_ref, perm_ref, take_ref, out_ref, ext_ref, sum_ref, turned_ref, w_ref):
    build_band(w_ref, raw_ref, True)
    widen_one(ext_ref, hg_ref)

    def body(k):
        total = conv_inner(ext_ref, w_ref, k)
        rows = NX * NY
        for i in range(STEP):
            sum_ref[k + i] = (outer_ref[k + i].astype(F32) + total[i * rows : (i + 1) * rows]).astype(BF)

    each_step(outer_ref.shape[0], body)
    gather_pairs(sum_ref, turned_ref)
    take = take_ref[...]
    for i in range(perm_ref.shape[0]):
        rows = dot_nt(turned_ref[i], perm_ref[i]).astype(BF)
        out_ref[:, i * PAIR : (i + 1) * PAIR] = dot(take, rows).astype(BF)


def block_kernel(act_ref, mask_ref, raw_ref, field_ref, perm_ref, out_ref, ext_ref, sum_ref, turned_ref, w_ref):
    build_band(w_ref, raw_ref, False)
    widen_one(ext_ref, act_ref)

    def body(k):
        total = conv_inner(ext_ref, w_ref, k)
        m = twice(mask_ref[0 : NX * NY, :])
        rows = NX * NY
        for i in range(STEP):
            sum_ref[k + i] = (field_ref[k + i].astype(F32) + m * total[i * rows : (i + 1) * rows]).astype(BF)

    each_step(field_ref.shape[0], body)
    gather_pairs(sum_ref, turned_ref)
    for i in range(perm_ref.shape[0]):
        out_ref[:, i * PAIR : (i + 1) * PAIR] = dot_nt(turned_ref[i], perm_ref[i]).astype(BF)


def pair_sum_kernel(keep_ref, got_ref, out_ref):
    out_ref[...] = (keep_ref[...] + got_ref[...]).astype(BF)


def assemble_kernel(cap, run, back_ref, parts_ref, out_ref):
    buffers, width = back_ref.shape
    senders, lanes = parts_ref.shape
    half = lanes // 2
    out_ref[:, 0:width] = back_ref[...]
    row = lax.broadcasted_iota(jnp.int32, (buffers, senders), 0)
    col = lax.broadcasted_iota(jnp.int32, (buffers, senders), 1)
    same = row % cap == col % cap
    core = (row // run) % 2
    total = jnp.zeros((buffers, half), F32)
    for i in range(2):
        add = jnp.where(same & (core == i), 1.0, 0.0).astype(BF)
        total = total + dot(add, parts_ref[:, i * half : (i + 1) * half])
    out_ref[:, width : width + half] = total.astype(BF)


def unpack_kernel(factor, core_ref, mine_ref, other_ref, first_ref, second_ref, flat_ref):
    rows, lanes = mine_ref.shape
    for i, out_ref in enumerate((first_ref, second_ref)):
        own = core_ref[0] == i
        for l in range(lanes // LANES):
            at = slice(l * LANES, (l + 1) * LANES)
            value = jnp.where(own, mine_ref[:, at].astype(F32), other_ref[:, at].astype(F32))
            flat_ref[l * rows : (l + 1) * rows, :] = value
        unpack_taps(factor, flat_ref, out_ref)


def unpack_taps(factor, packed_ref, out_ref):
    channels = out_ref.shape[1]
    lane = lax.broadcasted_iota(jnp.int32, (channels, LANES), 1)
    for g in range(7):
        v = []
        for i in range(3):
            start = (3 * g + i) * channels
            v.append(packed_ref[start : start + channels, :] * factor)
        taps = (
            v[0],
            pltpu.roll(jnp.where(lane < 64, v[1], v[0]), 32, 1),
            pltpu.roll(jnp.where(lane < 32, v[2], v[1]), 64, 1),
            pltpu.roll(v[2], 96, 1),
        )
        for u in range(4):
            if 4 * g + u < 27:
                out_ref[4 * g + u] = taps[u][:, 0:channels]


RX = ("cx", "core")
ALL = ("cx", "core", "ry")
SAME_CORE = ("cx", "ry")


def size_of(axes):
    return int(np.prod([lax.axis_size(a) for a in ((axes,) if isinstance(axes, str) else axes)]))


def share(parts, axes):
    return lax.all_to_all(parts, axes, split_axis=0, concat_axis=0, tiled=True)


def neighbours(axes, upper, lower):
    count = size_of(axes)
    ahead = [(i, i + 1) for i in range(count - 1)]
    behind = [(t, s) for s, t in ahead]
    return lax.ppermute(upper, axes, ahead), lax.ppermute(lower, axes, behind)


def swap_cores(value):
    count = size_of(RX)
    return lax.ppermute(value, RX, [(i, i ^ 1) for i in range(count)])


def message_rows():
    cells = []
    for ys in ((0, 1), (NY - 2, NY - 1)):
        for y in ys:
            cells += [(x, y) for x in range(-2, NX + 2)]
        cells += [None] * (MSG - 2 * (NX + 4))
    return cells


def exchange(field, pick):
    pairs = field.shape[0]
    xlo, xhi = neighbours(RX, field[:, (NX - 2) * NY :, :], field[:, : 2 * NY, :])
    message = jax.ShapeDtypeStruct((pairs, MSG, PAIR), BF)
    low, high = call(message_kernel, (message, message), 5e8, 3e6)(field, xlo, xhi, pick)
    ylo, yhi = neighbours("ry", high, low)
    return xlo, xhi, ylo, yhi, low, high


def mask_cells():
    cells = [(x, y) for x in range(NX) for y in range(NY)]
    cells += [(x, y) for x in (-2, -1) for y in range(NY)]
    cells += [(x, y) for x in (NX, NX + 1) for y in range(NY)]
    for ys in ((-2, -1), (NY, NY + 1), (0, 1), (NY - 2, NY - 1)):
        for y in ys:
            cells += [(x, y) for x in range(-2, NX + 2)]
        cells += [None] * (MSG - 2 * (NX + 4))
    for y in (-1, NY):
        cells += [(x, y) for x in range(-1, NX + 1)]
        cells += [None] * (EDGE - NX - 2)
    return cells


def on_device(column_features, column_route, cotangent, first_weight, second_weight):
    count_x = size_of(RX)
    count_y = size_of("ry")
    count_all = count_x * count_y
    shard_rows, row_width = column_features.shape
    channels = first_weight.shape[1]
    depth = row_width // channels
    slots = NX * NY
    pairs = depth // 2
    chunks = channels // GROUP
    cap = 2 * shard_rows // count_all
    buffers = count_all * cap
    me_x = lax.axis_index(RX)
    me_y = lax.axis_index("ry")
    core = lax.axis_index("core").astype(jnp.int32).reshape(1)
    conv_flops = 2 * slots * pairs * 36 * LANES * PAIR

    shape = jax.ShapeDtypeStruct
    field_shape = shape((pairs, slots, PAIR), BF)
    wide_shape = shape((pairs, OUT_ROWS, PAIR), BF)
    ext = pltpu.VMEM((3, pairs + 1, NX + 4, NY, PAIR), BF)
    edge = pltpu.VMEM((3, 3, pairs + 1, 2 * EDGE, PAIR), BF)
    turned = pltpu.VMEM((chunks, slots, PAIR), F32)
    turned_low = pltpu.VMEM((chunks, slots, PAIR), BF)
    sums = pltpu.VMEM((pairs, slots, PAIR), BF)

    perm = jnp.asarray(permutation(channels, depth), BF)
    pick_np = np.zeros((2 * MSG, (NX + 4) * NY), np.float32)
    for r, cell in enumerate(message_rows()):
        if cell is not None:
            pick_np[r, (cell[0] + 2) * NY + cell[1]] = 1.0
    pick = jnp.asarray(pick_np, BF)

    route_row = column_route.reshape(1, shard_rows)
    route_col = column_route.reshape(shard_rows, 1)
    told_width = row_width + LANES
    outgoing = call(
        functools.partial(send_kernel, cap, slots), shape((buffers, told_width), BF),
        2 * buffers * shard_rows * row_width, 3 * shard_rows * row_width * 2,
    )(route_row, route_col, column_features)
    incoming = share(outgoing.reshape(count_all, cap, told_width), ALL).reshape(buffers, told_width)

    cells = mask_cells()
    steps = np.asarray([(0, 0) if c is None else (c[0] // NX, c[1] // NY) for c in cells], np.int32)
    local = np.asarray([-1 if c is None else (c[0] % NX) * NY + c[1] % NY for c in cells], np.int32)
    to_x = me_x + steps[:, 0]
    to_y = me_y + steps[:, 1]
    inside = (to_x >= 0) & (to_x < count_x) & (to_y >= 0) & (to_y < count_y) & (local >= 0)
    codes = jnp.where(inside, (to_x * count_y + to_y) * slots + local, -1).astype(F32)[:, None]
    me = (me_x * count_y + me_y).astype(jnp.int32).reshape(1)

    cot = call(
        to_pairs_kernel, field_shape, 1e9, 3e6, (turned,),
    )(cotangent.reshape(slots, row_width), perm)
    cot_halo = exchange(cot, pick)

    smem = pl.BlockSpec(memory_space=pltpu.SMEM)
    vmem = pl.BlockSpec(memory_space=pltpu.VMEM)
    field, take = call(
        functools.partial(place_kernel, cap, slots), (field_shape, shape((buffers, slots), BF)), 1e9, 3e6,
        (turned,), in_specs=[smem, vmem, vmem],
    )(me, incoming, perm)
    field_halo = exchange(field, pick)

    mask = call(
        functools.partial(mask_kernel, cap, slots), shape((M_ROWS, LANES), F32), 1e8, 1e6,
        (pltpu.VMEM((count_all, LANES), F32),),
    )(incoming, codes)
    band = pltpu.VMEM((36 * LANES, PAIR), BF)
    ext_near = pltpu.VMEM((3, pairs + 1, NX + 2, NY, PAIR), BF)
    act_grad, outer = call(
        outer_kernel, (shape((pairs, OUT_ROWS, PAIR), F32), field_shape),
        1.3 * conv_flops, 7e6, (ext, edge, band), ROOM_WIDE,
    )(cot, *cot_halo, mask, second_weight)

    act, hg = call(
        hidden_kernel, (wide_shape, wide_shape), 1.3 * conv_flops, 8e6, (ext, edge, band), ROOM_WIDE,
    )(field, *field_halo, mask, first_weight, act_grad)

    packed_rows = -(-21 * channels // buffers) * buffers
    run = count_y * cap
    grad_lanes = 2 * packed_rows // buffers * LANES
    half_shape = shape((buffers // 2, grad_lanes), F32)
    keep, give = call(
        functools.partial(corr_kernel, channels, run), (half_shape, half_shape), 2 * conv_flops, 10e6,
        (
            ext_near, pltpu.VMEM((2 * channels, pairs * slots), BF),
            pltpu.VMEM((28, channels, LANES), F32), pltpu.VMEM((packed_rows, LANES), F32),
        ),
        ROOM_CORR, in_specs=[smem] + [vmem] * 8,
    )(core, field, *field_halo[:4], hg, act, outer)
    got = swap_cores(give)
    sent = call(
        pair_sum_kernel, shape((buffers // 2, grad_lanes), BF), 1e6, 2e6,
    )(keep, got)
    parts = share(sent.reshape(count_all // 2, cap, grad_lanes), SAME_CORE).reshape(buffers // 2, grad_lanes)

    hg, sent = lax.optimization_barrier((hg, sent))
    back = call(
        grid_grad_kernel, shape((buffers, row_width), BF), 1.2 * conv_flops, 6e6,
        (ext_near, sums, turned_low, band), ROOM_NEAR,
    )(hg, first_weight, outer, perm, take)
    back_width = row_width + grad_lanes // 2
    mixed = call(
        functools.partial(assemble_kernel, cap, run), shape((buffers, back_width), BF), 2e8, 3e6,
    )(back, parts)
    returned = share(mixed.reshape(count_all, cap, back_width), ALL).reshape(buffers, back_width)

    act, mixed = lax.optimization_barrier((act, mixed))
    block_output = call(
        block_kernel, shape((slots, row_width), BF), 1.2 * conv_flops, 8e6,
        (ext_near, sums, turned_low, band), ROOM_NEAR,
    )(act, mask, second_weight, field, perm)

    mine = returned[:, row_width:]
    feature_grads = call(
        functools.partial(collect_kernel, cap, slots), shape((shard_rows, row_width), BF),
        2 * buffers * shard_rows * row_width, 3 * shard_rows * row_width * 2,
    )(route_row, route_col, returned)

    factor = float(1.0 / np.sqrt(np.float32(count_all * shard_rows * depth)))
    grads = shape(first_weight.shape, F32)
    first_grad, second_grad = call(
        functools.partial(unpack_kernel, factor), (grads, grads), 1e6, 4e6,
        (pltpu.VMEM((packed_rows, LANES), F32),), in_specs=[smem, vmem, vmem],
    )(core, mine, swap_cores(mine))
    return (block_output.reshape(cotangent.shape), feature_grads, first_grad, second_grad)


def solution(mesh):
    count_x = mesh.shape["rx"]
    fine = jax.sharding.Mesh(mesh.devices.reshape(count_x // 2, 2, mesh.shape["ry"]), ALL)
    in_specs = (P(ALL, None), P(ALL), P(RX, "ry", None), P(), P())
    out_specs = (P(RX, "ry", None), P(ALL, None), P(), P())
    return jax.shard_map(
        on_device, mesh=fine, in_specs=in_specs, out_specs=out_specs, check_vma=False
    )
```

```python
import functools

import jax
import jax.numpy as jnp
import numpy as np
from jax import lax
from jax.experimental import pallas as pl
from jax.experimental.pallas import tpu as pltpu
from jax.sharding import PartitionSpec as P

LANES = 128
PAIR = 256
MIB = 1024 * 1024
ROOM_WIDE, ROOM_NEAR, ROOM_CORR, ROOM_SMALL = 20, 14, 16, 5
BF = jnp.bfloat16
F32 = jnp.float32


def call(body, out_shape, flops, moved, scratch=(), room=ROOM_SMALL, **extra):
    return pl.pallas_call(
        body,
        out_shape=out_shape,
        scratch_shapes=list(scratch),
        compiler_params=pltpu.CompilerParams(vmem_limit_bytes=room * MIB),
        cost_estimate=pl.CostEstimate(flops=int(flops), bytes_accessed=int(moved), transcendentals=0),
        **extra,
    )


def dot(left, right):
    return jnp.dot(left, right, preferred_element_type=F32)


def dot_nt(left, right):
    return lax.dot_general(left, right, (((1,), (1,)), ((), ())), preferred_element_type=F32)


def send_kernel(cap, slots, row_ref, col_ref, feat_ref, out_ref):
    rows, width = feat_ref.shape
    buffers = out_ref.shape[0]
    owner_row = row_ref[...] // slots
    owner_col = col_ref[...] // slots
    first = lax.broadcasted_iota(jnp.int32, (rows, rows), 0)
    second = lax.broadcasted_iota(jnp.int32, (rows, rows), 1)
    same = jnp.where((owner_col == owner_row) & (first < second), 1.0, 0.0)
    rank = jnp.sum(same, axis=0, keepdims=True)
    pos = owner_row.astype(F32) * cap + rank
    place = lax.broadcasted_iota(jnp.int32, (buffers, rows), 0)
    hot = jnp.where(place.astype(F32) == pos, 1.0, 0.0).astype(BF)
    out_ref[:, 0:width] = dot(hot, feat_ref[...]).astype(BF)
    slot_row = (row_ref[...] % slots).astype(F32)
    kind = place % cap
    told = jnp.where(kind == 0, owner_row.astype(F32), jnp.where(kind == 1, slot_row, 0.0))
    out_ref[:, width : width + rows] = told.astype(BF)


def told_rows(cap, in_ref, which):
    buffers, width = in_ref.shape
    count = buffers // cap
    source = lax.broadcasted_iota(jnp.int32, (count, buffers), 0)
    place = lax.broadcasted_iota(jnp.int32, (count, buffers), 1)
    pick = jnp.where(place == source * cap + which, 1.0, 0.0).astype(BF)
    return dot(pick, in_ref[:, width - LANES : width])


def collect_kernel(cap, slots, row_ref, col_ref, back_ref, out_ref):
    rows = out_ref.shape[0]
    owner_row = row_ref[...] // slots
    owner_col = col_ref[...] // slots
    first = lax.broadcasted_iota(jnp.int32, (rows, rows), 0)
    second = lax.broadcasted_iota(jnp.int32, (rows, rows), 1)
    same = jnp.where((owner_col == owner_row) & (second < first), 1.0, 0.0)
    rank = jnp.sum(same, axis=1, keepdims=True)
    pos = owner_col.astype(F32) * cap + rank
    place = lax.broadcasted_iota(jnp.int32, (rows, back_ref.shape[0]), 1).astype(F32)
    hot = jnp.where(place == pos, 1.0, 0.0).astype(BF)
    out_ref[...] = dot(hot, back_ref[:, 0 : out_ref.shape[1]]).astype(BF)


def mask_kernel(cap, slots, in_ref, codes_ref, mask_ref, route_ref):
    total = mask_ref.shape[0]
    route_ref[...] = told_rows(cap, in_ref, 0) * slots + told_rows(cap, in_ref, 1)
    codes = jnp.broadcast_to(codes_ref[...], (total, LANES))
    hits = jnp.zeros((total, LANES), F32)
    for s in range(route_ref.shape[0]):
        hits = hits + jnp.where(codes == route_ref[s : s + 1, :], 1.0, 0.0)
    mask_ref[...] = jnp.broadcast_to(jnp.sum(hits, axis=1, keepdims=True), (total, LANES))


def slot_table(cap, slots, me, in_ref):
    buffers = in_ref.shape[0]
    count = buffers // cap
    mine_f = jnp.where(told_rows(cap, in_ref, 0) == me.astype(F32), 1.0, 0.0)
    slot_f = told_rows(cap, in_ref, 1)
    first = lax.broadcasted_iota(jnp.int32, (LANES, LANES), 0)
    second = lax.broadcasted_iota(jnp.int32, (LANES, LANES), 1)
    tri = jnp.where(first < second, 1.0, 0.0).astype(BF)
    rank = dot(mine_f.astype(BF), tri)
    lane = lax.broadcasted_iota(jnp.int32, (count, LANES), 1)
    held = jnp.zeros((count, LANES), F32)
    for j in range(cap):
        here = jnp.where(rank == j, mine_f, 0.0)
        number = jnp.sum(here, axis=1, keepdims=True)
        value = jnp.sum(here * slot_f, axis=1, keepdims=True)
        value = value + (1.0 - number) * slots
        held = jnp.where(lane == j, value, held)
    place = lax.broadcasted_iota(jnp.int32, (buffers, count), 0)
    source = lax.broadcasted_iota(jnp.int32, (buffers, count), 1)
    spread = jnp.where(place // cap == source, 1.0, 0.0).astype(BF)
    wide = dot(spread, held.astype(BF))
    place = lax.broadcasted_iota(jnp.int32, (buffers, LANES), 0)
    lane = lax.broadcasted_iota(jnp.int32, (buffers, LANES), 1)
    slot_col = jnp.sum(jnp.where(place % cap == lane, wide, 0.0), axis=1, keepdims=True)
    slot_id = lax.broadcasted_iota(jnp.int32, (buffers, slots), 1).astype(F32)
    return jnp.where(slot_col == slot_id, 1.0, 0.0)


GROUP = 16
FOLD = LANES // GROUP


def permutation(channels, depth):
    perm = np.zeros((channels // GROUP, PAIR, PAIR), np.float32)
    for i in range(channels // GROUP):
        for j in range(GROUP):
            for z in range(depth):
                perm[i, depth * j + z, LANES * (z // FOLD) + GROUP * ((z + i) % FOLD) + j] = 1.0
    return perm


def lane_group(rows):
    return lax.broadcasted_iota(jnp.int32, (rows, LANES), 1) // GROUP


def spread_pairs(turned_ref, out_ref):
    chunks, rows, _ = turned_ref.shape
    step = 32
    group = lane_group(step)

    def body(t, carry):
        at = pl.ds(pl.multiple_of(t * step, step), step)
        for half in range(2):
            lanes = slice(half * LANES, (half + 1) * LANES)
            parts = [turned_ref[i, at, lanes] for i in range(chunks)]
            parts = parts + [jnp.zeros((step, LANES), F32)] * (FOLD - chunks)
            for bit in (1, 2, 4):
                odd = (group & bit) != 0
                parts = [jnp.where(odd, parts[(i + bit) % FOLD], parts[i]) for i in range(FOLD)]
            for g in range(FOLD):
                value = parts[(-g) % FOLD]
                if g:
                    value = pltpu.roll(value, LANES - GROUP * g, 1)
                z = half * FOLD + g
                out_ref[z // 2, at, (z % 2) * LANES : (z % 2 + 1) * LANES] = value.astype(BF)
        return carry

    lax.fori_loop(0, rows // step, body, 0)


def gather_pairs(in_ref, turned_ref):
    chunks, rows, _ = turned_ref.shape
    step = 32
    group = lane_group(step)

    def body(t, carry):
        at = pl.ds(pl.multiple_of(t * step, step), step)
        for half in range(2):
            turned = []
            for g in range(FOLD):
                z = half * FOLD + g
                value = in_ref[z // 2, at, (z % 2) * LANES : (z % 2 + 1) * LANES].astype(F32)
                turned.append(pltpu.roll(value, GROUP * g, 1) if g else value)
            parts = [turned[(-i) % FOLD] for i in range(FOLD)]
            for bit in (1, 2, 4):
                odd = (group & bit) != 0
                parts = [jnp.where(odd, parts[(i - bit) % FOLD], parts[i]) for i in range(FOLD)]
            for i in range(chunks):
                turned_ref[i, at, half * LANES : (half + 1) * LANES] = parts[i].astype(BF)
        return carry

    lax.fori_loop(0, rows // step, body, 0)


def to_pairs_kernel(rows_ref, perm_ref, out_ref, turned_ref):
    for i in range(perm_ref.shape[0]):
        turned_ref[i] = dot(rows_ref[:, i * PAIR : (i + 1) * PAIR], perm_ref[i])
    spread_pairs(turned_ref, out_ref)


def place_kernel(cap, slots, me_ref, rows_ref, perm_ref, out_ref, take_ref, turned_ref):
    take = slot_table(cap, slots, me_ref[0], rows_ref)
    take_ref[...] = take.astype(BF)
    put = take.T.astype(BF)
    for i in range(perm_ref.shape[0]):
        held = dot(put, rows_ref[:, i * PAIR : (i + 1) * PAIR]).astype(BF)
        turned_ref[i] = dot(held, perm_ref[i])
    spread_pairs(turned_ref, out_ref)


def message_kernel(f_ref, xlo_ref, xhi_ref, pick_ref, low_ref, high_ref):
    pick = pick_ref[...]
    half = low_ref.shape[1]
    for k in range(f_ref.shape[0]):
        rows = jnp.concatenate([xlo_ref[k], f_ref[k], xhi_ref[k]], axis=0)
        sent = dot(pick, rows).astype(BF)
        low_ref[k] = sent[0:half]
        high_ref[k] = sent[half : 2 * half]


def build_band(band_ref, raw_ref, backward):
    channels = raw_ref.shape[1]
    band_ref[...] = jnp.zeros_like(band_ref)
    for tap in range(27):
        value = raw_ref[26 - tap] if backward else raw_ref[tap].T
        for zo in range(2):
            row = ((tap // 3) * 4 + zo + tap % 3) * LANES
            band_ref[row : row + channels, zo * LANES : zo * LANES + channels] = value


NX = 16
NY = 16
OUT_MAIN = (NX + 2) * NY
EDGE = 24
OUT_ROWS = OUT_MAIN + 2 * EDGE
MSG = 48
M_XLO = NX * NY
M_XHI = M_XLO + 2 * NY
M_YLO = M_XHI + 2 * NY
M_YHI = M_YLO + MSG
M_LOW = M_YHI + MSG
M_HIGH = M_LOW + MSG
M_EDGE = M_HIGH + MSG
M_ROWS = M_EDGE + 2 * EDGE


def twice(value):
    return jnp.concatenate([value, value], axis=1)


def put_pair(ref, lead, k, tail, value):
    value = value.astype(BF)
    ref[lead + (k,) + tail + (slice(LANES, PAIR),)] = value[:, 0:LANES]
    ref[lead + (k + 1,) + tail + (slice(0, LANES),)] = value[:, LANES:PAIR]


def clear_ends(ref, lead):
    last = ref.shape[len(lead)] - 1
    dims = ref.shape[len(lead) + 1 : -1]
    ref[lead + (0,) + (slice(None),) * len(dims) + (slice(0, LANES),)] = jnp.zeros(dims + (LANES,), BF)
    ref[lead + (last,) + (slice(None),) * len(dims) + (slice(LANES, PAIR),)] = jnp.zeros(dims + (LANES,), BF)


def put_shifted(ext_ref, k, xp, mid, before, after, row):
    ny = mid.shape[0]
    up = jnp.where(row == 0, before, pltpu.roll(mid, 1, 0))
    down = jnp.where(row == ny - 1, after, pltpu.roll(mid, ny - 1, 0))
    for b, value in enumerate((up, mid, down)):
        put_pair(ext_ref, (b,), k, (xp, slice(None)), value)


def widen_two(ext_ref, edge_ref, f_ref, xlo_ref, xhi_ref, ylo_ref, yhi_ref, low_ref, high_ref, mask_ref=None):
    pairs = f_ref.shape[0]
    for b in range(3):
        clear_ends(ext_ref, (b,))
        for a in range(3):
            clear_ends(edge_ref, (a, b))
    row = lax.broadcasted_iota(jnp.int32, (NY, PAIR), 0)

    def read(ref, k, start, size, mask_start):
        value = ref[k, start : start + size, :].astype(F32)
        if mask_ref is None:
            return value
        return value * twice(mask_ref[mask_start + start : mask_start + start + size, :])

    def body(k, carry):
        ylo = read(ylo_ref, k, 0, MSG, M_YLO)
        yhi = read(yhi_ref, k, 0, MSG, M_YHI)
        low = read(low_ref, k, 0, MSG, M_LOW)
        high = read(high_ref, k, 0, MSG, M_HIGH)
        wide = NX + 4
        for xp in range(wide):
            if xp < 2:
                mid = read(xlo_ref, k, xp * NY, NY, M_XLO)
            elif xp >= NX + 2:
                mid = read(xhi_ref, k, (xp - NX - 2) * NY, NY, M_XHI)
            else:
                mid = read(f_ref, k, (xp - 2) * NY, NY, 0)
            put_shifted(ext_ref, k, xp, mid, ylo[wide + xp : wide + xp + 1, :], yhi[xp : xp + 1, :], row)
        first = ((ylo, 0), (ylo, wide), (low, 0))
        second = ((high, wide), (yhi, 0), (yhi, wide))
        for a in range(3):
            for b in range(3):
                sides = []
                for value, start in (first[b], second[b]):
                    turn = start + a
                    if turn:
                        value = pltpu.roll(value, MSG - turn, 0)
                    sides.append(value[0:EDGE])
                put_pair(edge_ref, (a, b), k, (slice(None),), jnp.concatenate(sides, axis=0))
        return carry

    lax.fori_loop(0, pairs, body, 0)


def widen_near(ext_ref, f_ref, xlo_ref, xhi_ref, ylo_ref, yhi_ref):
    for b in range(3):
        clear_ends(ext_ref, (b,))
    row = lax.broadcasted_iota(jnp.int32, (NY, PAIR), 0)
    wide = NX + 4

    def body(k, carry):
        ylo = ylo_ref[k].astype(F32)
        yhi = yhi_ref[k].astype(F32)
        for xp in range(NX + 2):
            if xp == 0:
                mid = xlo_ref[k, NY : 2 * NY, :].astype(F32)
            elif xp == NX + 1:
                mid = xhi_ref[k, 0:NY, :].astype(F32)
            else:
                mid = f_ref[k, (xp - 1) * NY : xp * NY, :].astype(F32)
            put_shifted(ext_ref, k, xp, mid, ylo[wide + xp + 1 : wide + xp + 2, :], yhi[xp + 1 : xp + 2, :], row)
        return carry

    lax.fori_loop(0, f_ref.shape[0], body, 0)


def widen_one(ext_ref, rows_ref):
    pairs = rows_ref.shape[0]
    for b in range(3):
        clear_ends(ext_ref, (b,))
    row = lax.broadcasted_iota(jnp.int32, (NY, PAIR), 0)

    def body(k, carry):
        edges = rows_ref[k, OUT_MAIN:OUT_ROWS, :].astype(F32)
        for xp in range(NX + 2):
            mid = rows_ref[k, xp * NY : (xp + 1) * NY, :].astype(F32)
            put_shifted(ext_ref, k, xp, mid, edges[xp : xp + 1, :], edges[EDGE + xp : EDGE + xp + 1, :], row)
        return carry

    lax.fori_loop(0, pairs, body, 0)


STEP = 2


def conv_wide(ext_ref, edge_ref, w_ref, k):
    pieces = []
    for a in range(3):
        for b in range(3):
            for j in range(2):
                parts = []
                for i in range(STEP):
                    parts.append(ext_ref[b, k + i + j, a : a + NX + 2].reshape(OUT_MAIN, PAIR))
                    parts.append(edge_ref[a, b, k + i + j])
                pieces.append(jnp.concatenate(parts, axis=0))
    return dot(jnp.concatenate(pieces, axis=1), w_ref[...])


def conv_inner(ext_ref, w_ref, k):
    pieces = []
    for a in range(3):
        for b in range(3):
            for j in range(2):
                pieces.append(ext_ref[b, pl.ds(k + j, STEP), a : a + NX].reshape(STEP * NX * NY, PAIR))
    return dot(jnp.concatenate(pieces, axis=1), w_ref[...])


def each_step(pairs, body):
    def step(t, carry):
        body(t * STEP)
        return carry

    lax.fori_loop(0, pairs // STEP, step, 0)


def out_mask(mask_ref):
    return twice(jnp.concatenate([
        mask_ref[M_XLO + NY : M_XLO + 2 * NY, :], mask_ref[0 : NX * NY, :],
        mask_ref[M_XHI : M_XHI + NY, :], mask_ref[M_EDGE:M_ROWS, :],
    ], axis=0))


def outer_kernel(f_ref, xlo_ref, xhi_ref, ylo_ref, yhi_ref, low_ref, high_ref, mask_ref, raw_ref,
                 out_ref, outer_ref, ext_ref, edge_ref, w_ref):
    build_band(w_ref, raw_ref, True)
    widen_two(ext_ref, edge_ref, f_ref, xlo_ref, xhi_ref, ylo_ref, yhi_ref, low_ref, high_ref, mask_ref)

    def body(k):
        total = conv_wide(ext_ref, edge_ref, w_ref, k)
        for i in range(STEP):
            out_ref[k + i] = total[i * OUT_ROWS : (i + 1) * OUT_ROWS]
            outer_ref[k + i] = (f_ref[k + i].astype(F32) * twice(mask_ref[0 : NX * NY, :])).astype(BF)

    each_step(f_ref.shape[0], body)


def correlate(gt_ref, ext_ref, taps_ref):
    depth = 2 * (ext_ref.shape[1] - 1)

    def body(b, carry):
        rows = []
        for z in range(depth):
            parts = []
            for a in range(3):
                for c in range(3):
                    half = (z + c) % 2 * LANES
                    part = ext_ref[b, (z + c) // 2, a : a + NX, :, half : half + LANES]
                    parts.append(part.reshape(NX * NY, LANES))
            rows.append(jnp.concatenate(parts, axis=1))
        sums = dot(gt_ref[...], jnp.concatenate(rows, axis=0))
        for a in range(3):
            for c in range(3):
                taps_ref[9 * a + 3 * b + c] = sums[:, (3 * a + c) * LANES : (3 * a + c + 1) * LANES]
        return carry

    lax.fori_loop(0, 3, body, 0)


def pack_taps(taps_ref, packed_ref, channels):
    lane = lax.broadcasted_iota(jnp.int32, (channels, LANES), 1)
    for g in range(7):
        t1 = pltpu.roll(taps_ref[4 * g + 1], 96, 1)
        t2 = pltpu.roll(taps_ref[4 * g + 2], 64, 1)
        t3 = pltpu.roll(taps_ref[4 * g + 3], 32, 1)
        blocks = (
            jnp.where(lane < 96, taps_ref[4 * g], t1),
            jnp.where(lane < 64, t1, t2),
            jnp.where(lane < 32, t2, t3),
        )
        for i, value in enumerate(blocks):
            start = (3 * g + i) * channels
            packed_ref[start : start + channels, :] = value
    rest = packed_ref.shape[0] - 21 * channels
    if rest:
        packed_ref[21 * channels :, :] = jnp.zeros((rest, LANES), F32)


def hidden_kernel(f_ref, xlo_ref, xhi_ref, ylo_ref, yhi_ref, low_ref, high_ref, mask_ref, raw_ref, grad_ref,
                  act_ref, hg_ref, ext_ref, edge_ref, w_ref):
    build_band(w_ref, raw_ref, False)
    widen_two(ext_ref, edge_ref, f_ref, xlo_ref, xhi_ref, ylo_ref, yhi_ref, low_ref, high_ref)

    def body(k):
        total = conv_wide(ext_ref, edge_ref, w_ref, k)
        m = out_mask(mask_ref)
        for i in range(STEP):
            hidden = m * total[i * OUT_ROWS : (i + 1) * OUT_ROWS]
            sigma = jax.nn.sigmoid(hidden)
            act_ref[k + i] = (hidden * sigma).astype(BF)
            hg_ref[k + i] = (m * grad_ref[k + i] * sigma * (1.0 + hidden * (1.0 - sigma))).astype(BF)

    each_step(f_ref.shape[0], body)


def turn(gt_ref, g_ref, start, channels):
    inner = NX * NY
    for k in range(g_ref.shape[0]):
        value = g_ref[k, start : start + inner, :].T
        for i in range(2):
            z = 2 * k + i
            gt_ref[:, z * inner : (z + 1) * inner] = value[i * LANES : i * LANES + channels]


def corr_kernel(channels, run, core_ref, f_ref, xlo_ref, xhi_ref, ylo_ref, yhi_ref, hg_ref, act_ref, outer_ref,
                keep_ref, give_ref, ext_ref, gt_ref, taps_ref, packed_ref):
    runs = keep_ref.shape[0] // run
    block = 2 * runs * run
    blocks = packed_ref.shape[0] // block
    taps_ref[27] = jnp.zeros((channels, LANES), F32)
    for i in range(2):
        if i == 0:
            widen_near(ext_ref, f_ref, xlo_ref, xhi_ref, ylo_ref, yhi_ref)
            turn(gt_ref, hg_ref, NY, channels)
        else:
            widen_one(ext_ref, act_ref)
            turn(gt_ref, outer_ref, 0, channels)
        correlate(gt_ref, ext_ref, taps_ref)
        pack_taps(taps_ref, packed_ref, channels)
        for l in range(blocks):
            lanes = slice((i * blocks + l) * LANES, (i * blocks + l + 1) * LANES)
            for x in range(runs):
                base = l * block + 2 * x * run
                rows = slice(x * run, (x + 1) * run)
                mine = pl.multiple_of(base + core_ref[0] * run, run)
                other = pl.multiple_of(base + (1 - core_ref[0]) * run, run)
                keep_ref[rows, lanes] = packed_ref[pl.ds(mine, run), :]
                give_ref[rows, lanes] = packed_ref[pl.ds(other, run), :]


def grid_grad_kernel(hg_ref, raw_ref, outer_ref, perm_ref, take_ref, out_ref, ext_ref, sum_ref, turned_ref, w_ref):
    build_band(w_ref, raw_ref, True)
    widen_one(ext_ref, hg_ref)

    def body(k):
        total = conv_inner(ext_ref, w_ref, k)
        rows = NX * NY
        for i in range(STEP):
            sum_ref[k + i] = (outer_ref[k + i].astype(F32) + total[i * rows : (i + 1) * rows]).astype(BF)

    each_step(outer_ref.shape[0], body)
    gather_pairs(sum_ref, turned_ref)
    take = take_ref[...]
    for i in range(perm_ref.shape[0]):
        rows = dot_nt(turned_ref[i], perm_ref[i]).astype(BF)
        out_ref[:, i * PAIR : (i + 1) * PAIR] = dot(take, rows).astype(BF)


def block_kernel(act_ref, mask_ref, raw_ref, field_ref, perm_ref, out_ref, ext_ref, sum_ref, turned_ref, w_ref):
    build_band(w_ref, raw_ref, False)
    widen_one(ext_ref, act_ref)

    def body(k):
        total = conv_inner(ext_ref, w_ref, k)
        m = twice(mask_ref[0 : NX * NY, :])
        rows = NX * NY
        for i in range(STEP):
            sum_ref[k + i] = (field_ref[k + i].astype(F32) + m * total[i * rows : (i + 1) * rows]).astype(BF)

    each_step(field_ref.shape[0], body)
    gather_pairs(sum_ref, turned_ref)
    for i in range(perm_ref.shape[0]):
        out_ref[:, i * PAIR : (i + 1) * PAIR] = dot_nt(turned_ref[i], perm_ref[i]).astype(BF)


def pair_sum_kernel(keep_ref, got_ref, out_ref):
    out_ref[...] = (keep_ref[...] + got_ref[...]).astype(BF)


def assemble_kernel(cap, run, back_ref, parts_ref, out_ref):
    buffers, width = back_ref.shape
    senders, lanes = parts_ref.shape
    half = lanes // 2
    out_ref[:, 0:width] = back_ref[...]
    row = lax.broadcasted_iota(jnp.int32, (buffers, senders), 0)
    col = lax.broadcasted_iota(jnp.int32, (buffers, senders), 1)
    same = row % cap == col % cap
    core = (row // run) % 2
    total = jnp.zeros((buffers, half), F32)
    for i in range(2):
        add = jnp.where(same & (core == i), 1.0, 0.0).astype(BF)
        total = total + dot(add, parts_ref[:, i * half : (i + 1) * half])
    out_ref[:, width : width + half] = total.astype(BF)


def unpack_kernel(factor, core_ref, mine_ref, other_ref, first_ref, second_ref, flat_ref):
    rows, lanes = mine_ref.shape
    for i, out_ref in enumerate((first_ref, second_ref)):
        own = core_ref[0] == i
        for l in range(lanes // LANES):
            at = slice(l * LANES, (l + 1) * LANES)
            value = jnp.where(own, mine_ref[:, at].astype(F32), other_ref[:, at].astype(F32))
            flat_ref[l * rows : (l + 1) * rows, :] = value
        unpack_taps(factor, flat_ref, out_ref)


def unpack_taps(factor, packed_ref, out_ref):
    channels = out_ref.shape[1]
    lane = lax.broadcasted_iota(jnp.int32, (channels, LANES), 1)
    for g in range(7):
        v = []
        for i in range(3):
            start = (3 * g + i) * channels
            v.append(packed_ref[start : start + channels, :] * factor)
        taps = (
            v[0],
            pltpu.roll(jnp.where(lane < 64, v[1], v[0]), 32, 1),
            pltpu.roll(jnp.where(lane < 32, v[2], v[1]), 64, 1),
            pltpu.roll(v[2], 96, 1),
        )
        for u in range(4):
            if 4 * g + u < 27:
                out_ref[4 * g + u] = taps[u][:, 0:channels]


RX = ("cx", "core")
ALL = ("cx", "core", "ry")
SAME_CORE = ("cx", "ry")


def size_of(axes):
    return int(np.prod([lax.axis_size(a) for a in ((axes,) if isinstance(axes, str) else axes)]))


def share(parts, axes):
    return lax.all_to_all(parts, axes, split_axis=0, concat_axis=0, tiled=True)


def neighbours(axes, upper, lower):
    count = size_of(axes)
    ahead = [(i, i + 1) for i in range(count - 1)]
    behind = [(t, s) for s, t in ahead]
    return lax.ppermute(upper, axes, ahead), lax.ppermute(lower, axes, behind)


def swap_cores(value):
    count = size_of(RX)
    return lax.ppermute(value, RX, [(i, i ^ 1) for i in range(count)])


def message_rows():
    cells = []
    for ys in ((0, 1), (NY - 2, NY - 1)):
        for y in ys:
            cells += [(x, y) for x in range(-2, NX + 2)]
        cells += [None] * (MSG - 2 * (NX + 4))
    return cells


def exchange(field, pick):
    pairs = field.shape[0]
    xlo, xhi = neighbours(RX, field[:, (NX - 2) * NY :, :], field[:, : 2 * NY, :])
    message = jax.ShapeDtypeStruct((pairs, MSG, PAIR), BF)
    low, high = call(message_kernel, (message, message), 5e8, 3e6)(field, xlo, xhi, pick)
    ylo, yhi = neighbours("ry", high, low)
    return xlo, xhi, ylo, yhi, low, high


def mask_cells():
    cells = [(x, y) for x in range(NX) for y in range(NY)]
    cells += [(x, y) for x in (-2, -1) for y in range(NY)]
    cells += [(x, y) for x in (NX, NX + 1) for y in range(NY)]
    for ys in ((-2, -1), (NY, NY + 1), (0, 1), (NY - 2, NY - 1)):
        for y in ys:
            cells += [(x, y) for x in range(-2, NX + 2)]
        cells += [None] * (MSG - 2 * (NX + 4))
    for y in (-1, NY):
        cells += [(x, y) for x in range(-1, NX + 1)]
        cells += [None] * (EDGE - NX - 2)
    return cells


def on_device(column_features, column_route, cotangent, first_weight, second_weight):
    count_x = size_of(RX)
    count_y = size_of("ry")
    count_all = count_x * count_y
    shard_rows, row_width = column_features.shape
    channels = first_weight.shape[1]
    depth = row_width // channels
    slots = NX * NY
    pairs = depth // 2
    chunks = channels // GROUP
    cap = 2 * shard_rows // count_all
    buffers = count_all * cap
    me_x = lax.axis_index(RX)
    me_y = lax.axis_index("ry")
    core = lax.axis_index("core").astype(jnp.int32).reshape(1)
    conv_flops = 2 * slots * pairs * 36 * LANES * PAIR

    shape = jax.ShapeDtypeStruct
    field_shape = shape((pairs, slots, PAIR), BF)
    wide_shape = shape((pairs, OUT_ROWS, PAIR), BF)
    ext = pltpu.VMEM((3, pairs + 1, NX + 4, NY, PAIR), BF)
    edge = pltpu.VMEM((3, 3, pairs + 1, 2 * EDGE, PAIR), BF)
    turned = pltpu.VMEM((chunks, slots, PAIR), F32)
    turned_low = pltpu.VMEM((chunks, slots, PAIR), BF)
    sums = pltpu.VMEM((pairs, slots, PAIR), BF)

    perm = jnp.asarray(permutation(channels, depth), BF)
    pick_np = np.zeros((2 * MSG, (NX + 4) * NY), np.float32)
    for r, cell in enumerate(message_rows()):
        if cell is not None:
            pick_np[r, (cell[0] + 2) * NY + cell[1]] = 1.0
    pick = jnp.asarray(pick_np, BF)

    route_row = column_route.reshape(1, shard_rows)
    route_col = column_route.reshape(shard_rows, 1)
    told_width = row_width + LANES
    outgoing = call(
        functools.partial(send_kernel, cap, slots), shape((buffers, told_width), BF),
        2 * buffers * shard_rows * row_width, 3 * shard_rows * row_width * 2,
    )(route_row, route_col, column_features)
    incoming = share(outgoing.reshape(count_all, cap, told_width), ALL).reshape(buffers, told_width)

    cells = mask_cells()
    steps = np.asarray([(0, 0) if c is None else (c[0] // NX, c[1] // NY) for c in cells], np.int32)
    local = np.asarray([-1 if c is None else (c[0] % NX) * NY + c[1] % NY for c in cells], np.int32)
    to_x = me_x + steps[:, 0]
    to_y = me_y + steps[:, 1]
    inside = (to_x >= 0) & (to_x < count_x) & (to_y >= 0) & (to_y < count_y) & (local >= 0)
    codes = jnp.where(inside, (to_x * count_y + to_y) * slots + local, -1).astype(F32)[:, None]
    me = (me_x * count_y + me_y).astype(jnp.int32).reshape(1)

    cot = call(
        to_pairs_kernel, field_shape, 1e9, 3e6, (turned,),
    )(cotangent.reshape(slots, row_width), perm)
    cot_halo = exchange(cot, pick)

    smem = pl.BlockSpec(memory_space=pltpu.SMEM)
    vmem = pl.BlockSpec(memory_space=pltpu.VMEM)
    field, take = call(
        functools.partial(place_kernel, cap, slots), (field_shape, shape((buffers, slots), BF)), 1e9, 3e6,
        (turned,), in_specs=[smem, vmem, vmem],
    )(me, incoming, perm)
    field_halo = exchange(field, pick)

    mask = call(
        functools.partial(mask_kernel, cap, slots), shape((M_ROWS, LANES), F32), 1e8, 1e6,
        (pltpu.VMEM((count_all, LANES), F32),),
    )(incoming, codes)
    band = pltpu.VMEM((36 * LANES, PAIR), BF)
    ext_near = pltpu.VMEM((3, pairs + 1, NX + 2, NY, PAIR), BF)
    act_grad, outer = call(
        outer_kernel, (shape((pairs, OUT_ROWS, PAIR), F32), field_shape),
        1.3 * conv_flops, 7e6, (ext, edge, band), ROOM_WIDE,
    )(cot, *cot_halo, mask, second_weight)

    act, hg = call(
        hidden_kernel, (wide_shape, wide_shape), 1.3 * conv_flops, 8e6, (ext, edge, band), ROOM_WIDE,
    )(field, *field_halo, mask, first_weight, act_grad)

    packed_rows = -(-21 * channels // buffers) * buffers
    run = count_y * cap
    grad_lanes = 2 * packed_rows // buffers * LANES
    half_shape = shape((buffers // 2, grad_lanes), F32)
    keep, give = call(
        functools.partial(corr_kernel, channels, run), (half_shape, half_shape), 2 * conv_flops, 10e6,
        (
            ext_near, pltpu.VMEM((channels, depth * slots), BF),
            pltpu.VMEM((28, channels, LANES), F32), pltpu.VMEM((packed_rows, LANES), F32),
        ),
        ROOM_CORR, in_specs=[smem] + [vmem] * 8,
    )(core, field, *field_halo[:4], hg, act, outer)
    got = swap_cores(give)
    sent = call(
        pair_sum_kernel, shape((buffers // 2, grad_lanes), BF), 1e6, 2e6,
    )(keep, got)
    parts = share(sent.reshape(count_all // 2, cap, grad_lanes), SAME_CORE).reshape(buffers // 2, grad_lanes)

    hg, sent = lax.optimization_barrier((hg, sent))
    back = call(
        grid_grad_kernel, shape((buffers, row_width), BF), 1.2 * conv_flops, 6e6,
        (ext_near, sums, turned_low, band), ROOM_NEAR,
    )(hg, first_weight, outer, perm, take)
    back_width = row_width + grad_lanes // 2
    mixed = call(
        functools.partial(assemble_kernel, cap, run), shape((buffers, back_width), BF), 2e8, 3e6,
    )(back, parts)
    returned = share(mixed.reshape(count_all, cap, back_width), ALL).reshape(buffers, back_width)

    act, mixed = lax.optimization_barrier((act, mixed))
    block_output = call(
        block_kernel, shape((slots, row_width), BF), 1.2 * conv_flops, 8e6,
        (ext_near, sums, turned_low, band), ROOM_NEAR,
    )(act, mask, second_weight, field, perm)

    returned, block_output = lax.optimization_barrier((returned, block_output))
    mine = returned[:, row_width:]
    feature_grads = call(
        functools.partial(collect_kernel, cap, slots), shape((shard_rows, row_width), BF),
        2 * buffers * shard_rows * row_width, 3 * shard_rows * row_width * 2,
    )(route_row, route_col, returned)

    factor = float(1.0 / np.sqrt(np.float32(count_all * shard_rows * depth)))
    grads = shape(first_weight.shape, F32)
    first_grad, second_grad = call(
        functools.partial(unpack_kernel, factor), (grads, grads), 1e6, 4e6,
        (pltpu.VMEM((packed_rows, LANES), F32),), in_specs=[smem, vmem, vmem],
    )(core, mine, swap_cores(mine))
    return (block_output.reshape(cotangent.shape), feature_grads, first_grad, second_grad)


def solution(mesh):
    count_x = mesh.shape["rx"]
    fine = jax.sharding.Mesh(mesh.devices.reshape(count_x // 2, 2, mesh.shape["ry"]), ALL)
    in_specs = (P(ALL, None), P(ALL), P(RX, "ry", None), P(), P())
    out_specs = (P(RX, "ry", None), P(ALL, None), P(), P())
    return jax.shard_map(
        on_device, mesh=fine, in_specs=in_specs, out_specs=out_specs, check_vma=False
    )
```

```python
import functools

import jax
import jax.numpy as jnp
import numpy as np
from jax import lax
from jax.experimental import pallas as pl
from jax.experimental.pallas import tpu as pltpu
from jax.sharding import PartitionSpec as P

LANES = 128
PAIR = 256
MIB = 1024 * 1024
ROOM_WIDE, ROOM_NEAR, ROOM_CORR, ROOM_SMALL = 22, 14, 14, 5
BF = jnp.bfloat16
F32 = jnp.float32


def call(body, out_shape, flops, moved, scratch=(), room=ROOM_SMALL, **extra):
    return pl.pallas_call(
        body,
        out_shape=out_shape,
        scratch_shapes=list(scratch),
        compiler_params=pltpu.CompilerParams(vmem_limit_bytes=room * MIB),
        cost_estimate=pl.CostEstimate(flops=int(flops), bytes_accessed=int(moved), transcendentals=0),
        **extra,
    )


def dot(left, right):
    return jnp.dot(left, right, preferred_element_type=F32)


def dot_nt(left, right):
    return lax.dot_general(left, right, (((1,), (1,)), ((), ())), preferred_element_type=F32)


def as_column(row):
    return jnp.broadcast_to(row, (row.shape[1], row.shape[1])).T


def send_kernel(cap, slots, row_ref, feat_hbm, out_ref, feat_ref, sem):
    fetch = pltpu.make_async_copy(feat_hbm, feat_ref, sem)
    fetch.start()
    rows, width = feat_ref.shape
    buffers = out_ref.shape[0]
    owner_row = (row_ref[...] // slots).astype(F32)
    owner_col = as_column(owner_row)
    first = lax.broadcasted_iota(jnp.int32, (rows, rows), 0)
    second = lax.broadcasted_iota(jnp.int32, (rows, rows), 1)
    same = jnp.where((owner_col == owner_row) & (first < second), 1.0, 0.0)
    rank = jnp.sum(same, axis=0, keepdims=True)
    pos = owner_row * cap + rank
    place = lax.broadcasted_iota(jnp.int32, (buffers, rows), 0)
    hot = jnp.where(place.astype(F32) == pos, 1.0, 0.0).astype(BF)
    slot_row = (row_ref[...] % slots).astype(F32)
    kind = place % cap
    told = jnp.where(kind == 0, owner_row, jnp.where(kind == 1, slot_row, 0.0))
    out_ref[:, width : width + rows] = told.astype(BF)
    fetch.wait()
    out_ref[:, 0:width] = dot(hot, feat_ref[...]).astype(BF)


def collect_kernel(cap, slots, row_ref, back_ref, out_ref):
    rows, width = out_ref.shape
    owner_row = (row_ref[...] // slots).astype(F32)
    owner_col = as_column(owner_row)
    first = lax.broadcasted_iota(jnp.int32, (rows, rows), 0)
    second = lax.broadcasted_iota(jnp.int32, (rows, rows), 1)
    same = jnp.where((owner_col == owner_row) & (second < first), 1.0, 0.0)
    pos = owner_col[:, 0:1] * cap + jnp.sum(same, axis=1, keepdims=True)
    place = lax.broadcasted_iota(jnp.int32, (rows, back_ref.shape[0]), 1).astype(F32)
    hot = jnp.where(place == pos, 1.0, 0.0).astype(BF)
    out_ref[...] = dot(hot, back_ref[:, 0:width]).astype(BF)


def told_rows(cap, in_ref, which):
    buffers, width = in_ref.shape
    count = buffers // cap
    source = lax.broadcasted_iota(jnp.int32, (count, buffers), 0)
    place = lax.broadcasted_iota(jnp.int32, (count, buffers), 1)
    pick = jnp.where(place == source * cap + which, 1.0, 0.0).astype(BF)
    return dot(pick, in_ref[:, width - LANES : width])


def mask_kernel(cap, slots, in_ref, codes_ref, mask_ref, route_ref):
    total = mask_ref.shape[0]
    route_ref[...] = told_rows(cap, in_ref, 0) * slots + told_rows(cap, in_ref, 1)
    codes = jnp.broadcast_to(codes_ref[...], (total, LANES))
    hits = jnp.zeros((total, LANES), F32)
    for s in range(route_ref.shape[0]):
        hits = hits + jnp.where(codes == route_ref[s : s + 1, :], 1.0, 0.0)
    mask_ref[...] = jnp.broadcast_to(jnp.sum(hits, axis=1, keepdims=True), (total, LANES))


def slot_table(cap, slots, me, in_ref):
    buffers = in_ref.shape[0]
    count = buffers // cap
    mine_f = jnp.where(told_rows(cap, in_ref, 0) == me.astype(F32), 1.0, 0.0)
    slot_f = told_rows(cap, in_ref, 1)
    first = lax.broadcasted_iota(jnp.int32, (LANES, LANES), 0)
    second = lax.broadcasted_iota(jnp.int32, (LANES, LANES), 1)
    tri = jnp.where(first < second, 1.0, 0.0).astype(BF)
    rank = dot(mine_f.astype(BF), tri)
    lane = lax.broadcasted_iota(jnp.int32, (count, LANES), 1)
    held = jnp.zeros((count, LANES), F32)
    for j in range(cap):
        here = jnp.where(rank == j, mine_f, 0.0)
        number = jnp.sum(here, axis=1, keepdims=True)
        value = jnp.sum(here * slot_f, axis=1, keepdims=True)
        value = value + (1.0 - number) * slots
        held = jnp.where(lane == j, value, held)
    place = lax.broadcasted_iota(jnp.int32, (buffers, count), 0)
    source = lax.broadcasted_iota(jnp.int32, (buffers, count), 1)
    spread = jnp.where(place // cap == source, 1.0, 0.0).astype(BF)
    wide = dot(spread, held.astype(BF))
    place = lax.broadcasted_iota(jnp.int32, (buffers, LANES), 0)
    lane = lax.broadcasted_iota(jnp.int32, (buffers, LANES), 1)
    slot_col = jnp.sum(jnp.where(place % cap == lane, wide, 0.0), axis=1, keepdims=True)
    slot_id = lax.broadcasted_iota(jnp.int32, (buffers, slots), 1).astype(F32)
    return jnp.where(slot_col == slot_id, 1.0, 0.0)


GROUP = 16
FOLD = LANES // GROUP


def permutation(channels, depth):
    perm = np.zeros((channels // GROUP, PAIR, PAIR), np.float32)
    for i in range(channels // GROUP):
        for j in range(GROUP):
            for z in range(depth):
                perm[i, depth * j + z, LANES * (z // FOLD) + GROUP * ((z + i) % FOLD) + j] = 1.0
    return perm


def lane_group(rows):
    return lax.broadcasted_iota(jnp.int32, (rows, LANES), 1) // GROUP


def spread_pairs(turned_ref, out_ref):
    chunks, rows, _ = turned_ref.shape
    step = 32
    group = lane_group(step)

    def body(t, carry):
        at = pl.ds(pl.multiple_of(t * step, step), step)
        for half in range(2):
            lanes = slice(half * LANES, (half + 1) * LANES)
            parts = [turned_ref[i, at, lanes] for i in range(chunks)]
            parts = parts + [jnp.zeros((step, LANES), F32)] * (FOLD - chunks)
            for bit in (1, 2, 4):
                odd = (group & bit) != 0
                parts = [jnp.where(odd, parts[(i + bit) % FOLD], parts[i]) for i in range(FOLD)]
            for g in range(FOLD):
                value = parts[(-g) % FOLD]
                if g:
                    value = pltpu.roll(value, LANES - GROUP * g, 1)
                z = half * FOLD + g
                out_ref[z // 2, at, (z % 2) * LANES : (z % 2 + 1) * LANES] = value.astype(BF)
        return carry

    lax.fori_loop(0, rows // step, body, 0)


def gather_pairs(in_ref, turned_ref):
    chunks, rows, _ = turned_ref.shape
    step = 32
    group = lane_group(step)

    def body(t, carry):
        at = pl.ds(pl.multiple_of(t * step, step), step)
        for half in range(2):
            turned = []
            for g in range(FOLD):
                z = half * FOLD + g
                value = in_ref[z // 2, at, (z % 2) * LANES : (z % 2 + 1) * LANES].astype(F32)
                turned.append(pltpu.roll(value, GROUP * g, 1) if g else value)
            parts = [turned[(-i) % FOLD] for i in range(FOLD)]
            for bit in (1, 2, 4):
                odd = (group & bit) != 0
                parts = [jnp.where(odd, parts[(i - bit) % FOLD], parts[i]) for i in range(FOLD)]
            for i in range(chunks):
                turned_ref[i, at, half * LANES : (half + 1) * LANES] = parts[i].astype(BF)
        return carry

    lax.fori_loop(0, rows // step, body, 0)


def to_pairs_kernel(rows_ref, perm_ref, out_ref, turned_ref):
    for i in range(perm_ref.shape[0]):
        turned_ref[i] = dot(rows_ref[:, i * PAIR : (i + 1) * PAIR], perm_ref[i])
    spread_pairs(turned_ref, out_ref)


def place_kernel(cap, slots, me_ref, rows_ref, perm_hbm, out_ref, take_ref, turned_ref, perm_ref, sem):
    fetch = pltpu.make_async_copy(perm_hbm, perm_ref, sem)
    fetch.start()
    take = slot_table(cap, slots, me_ref[0], rows_ref)
    take_ref[...] = take.astype(BF)
    put = take.T.astype(BF)
    fetch.wait()
    for i in range(perm_ref.shape[0]):
        held = dot(put, rows_ref[:, i * PAIR : (i + 1) * PAIR]).astype(BF)
        turned_ref[i] = dot(held, perm_ref[i])
    spread_pairs(turned_ref, out_ref)


def message_kernel(f_ref, xlo_ref, xhi_ref, pick_ref, low_ref, high_ref):
    pick = pick_ref[...]
    half = low_ref.shape[1]
    for k in range(f_ref.shape[0]):
        rows = jnp.concatenate([xlo_ref[k], f_ref[k], xhi_ref[k]], axis=0)
        sent = dot(pick, rows).astype(BF)
        low_ref[k] = sent[0:half]
        high_ref[k] = sent[half : 2 * half]


def build_band(band_ref, raw_ref, backward):
    channels = raw_ref.shape[1]
    band_ref[...] = jnp.zeros_like(band_ref)
    for tap in range(27):
        value = raw_ref[26 - tap] if backward else raw_ref[tap].T
        for zo in range(2):
            row = ((tap // 3) * 4 + zo + tap % 3) * LANES
            band_ref[row : row + channels, zo * LANES : zo * LANES + channels] = value


NX = 16
NY = 16
OUT_MAIN = (NX + 2) * NY
EDGE = 24
OUT_ROWS = OUT_MAIN + 2 * EDGE
MSG = 48
M_XLO = NX * NY
M_XHI = M_XLO + 2 * NY
M_YLO = M_XHI + 2 * NY
M_YHI = M_YLO + MSG
M_LOW = M_YHI + MSG
M_HIGH = M_LOW + MSG
M_EDGE = M_HIGH + MSG
M_ROWS = M_EDGE + 2 * EDGE


def twice(value):
    return jnp.concatenate([value, value], axis=1)


def put_pair(ref, lead, k, tail, value):
    value = value.astype(BF)
    ref[lead + (k,) + tail + (slice(LANES, PAIR),)] = value[:, 0:LANES]
    ref[lead + (k + 1,) + tail + (slice(0, LANES),)] = value[:, LANES:PAIR]


def clear_ends(ref, lead):
    last = ref.shape[len(lead)] - 1
    dims = ref.shape[len(lead) + 1 : -1]
    ref[lead + (0,) + (slice(None),) * len(dims) + (slice(0, LANES),)] = jnp.zeros(dims + (LANES,), BF)
    ref[lead + (last,) + (slice(None),) * len(dims) + (slice(LANES, PAIR),)] = jnp.zeros(dims + (LANES,), BF)


def put_shifted(ext_ref, k, xp, mid, before, after, row):
    ny = mid.shape[0]
    up = jnp.where(row == 0, before, pltpu.roll(mid, 1, 0))
    down = jnp.where(row == ny - 1, after, pltpu.roll(mid, ny - 1, 0))
    for b, value in enumerate((up, mid, down)):
        put_pair(ext_ref, (b,), k, (xp, slice(None)), value)


def widen_two(ext_ref, edge_ref, f_ref, xlo_ref, xhi_ref, ylo_ref, yhi_ref, low_ref, high_ref, mask_ref=None):
    pairs = f_ref.shape[0]
    for b in range(3):
        clear_ends(ext_ref, (b,))
        for a in range(3):
            clear_ends(edge_ref, (a, b))
    row = lax.broadcasted_iota(jnp.int32, (NY, PAIR), 0)

    def read(ref, k, start, size, mask_start):
        value = ref[k, start : start + size, :].astype(F32)
        if mask_ref is None:
            return value
        return value * twice(mask_ref[mask_start + start : mask_start + start + size, :])

    def body(k, carry):
        ylo = read(ylo_ref, k, 0, MSG, M_YLO)
        yhi = read(yhi_ref, k, 0, MSG, M_YHI)
        low = read(low_ref, k, 0, MSG, M_LOW)
        high = read(high_ref, k, 0, MSG, M_HIGH)
        wide = NX + 4
        for xp in range(wide):
            if xp < 2:
                mid = read(xlo_ref, k, xp * NY, NY, M_XLO)
            elif xp >= NX + 2:
                mid = read(xhi_ref, k, (xp - NX - 2) * NY, NY, M_XHI)
            else:
                mid = read(f_ref, k, (xp - 2) * NY, NY, 0)
            put_shifted(ext_ref, k, xp, mid, ylo[wide + xp : wide + xp + 1, :], yhi[xp : xp + 1, :], row)
        first = ((ylo, 0), (ylo, wide), (low, 0))
        second = ((high, wide), (yhi, 0), (yhi, wide))
        for a in range(3):
            for b in range(3):
                sides = []
                for value, start in (first[b], second[b]):
                    turn = start + a
                    if turn:
                        value = pltpu.roll(value, MSG - turn, 0)
                    sides.append(value[0:EDGE])
                put_pair(edge_ref, (a, b), k, (slice(None),), jnp.concatenate(sides, axis=0))
        return carry

    lax.fori_loop(0, pairs, body, 0)


def widen_one(ext_ref, rows_ref):
    pairs = rows_ref.shape[0]
    for b in range(3):
        clear_ends(ext_ref, (b,))
    row = lax.broadcasted_iota(jnp.int32, (NY, PAIR), 0)

    def body(k, carry):
        edges = rows_ref[k, OUT_MAIN:OUT_ROWS, :].astype(F32)
        for xp in range(NX + 2):
            mid = rows_ref[k, xp * NY : (xp + 1) * NY, :].astype(F32)
            put_shifted(ext_ref, k, xp, mid, edges[xp : xp + 1, :], edges[EDGE + xp : EDGE + xp + 1, :], row)
        return carry

    lax.fori_loop(0, pairs, body, 0)


STEP = 2


def conv_wide(ext_ref, edge_ref, w_ref, k):
    pieces = []
    for a in range(3):
        for b in range(3):
            for j in range(2):
                parts = []
                for i in range(STEP):
                    parts.append(ext_ref[b, k + i + j, a : a + NX + 2].reshape(OUT_MAIN, PAIR))
                    parts.append(edge_ref[a, b, k + i + j])
                pieces.append(jnp.concatenate(parts, axis=0))
    return dot(jnp.concatenate(pieces, axis=1), w_ref[...])


def conv_inner(ext_ref, w_ref, k):
    pieces = []
    for a in range(3):
        for b in range(3):
            for j in range(2):
                pieces.append(ext_ref[b, pl.ds(k + j, STEP), a : a + NX].reshape(STEP * NX * NY, PAIR))
    return dot(jnp.concatenate(pieces, axis=1), w_ref[...])


def each_step(pairs, body):
    def step(t, carry):
        body(t * STEP)
        return carry

    lax.fori_loop(0, pairs // STEP, step, 0)


def out_mask(mask_ref):
    return twice(jnp.concatenate([
        mask_ref[M_XLO + NY : M_XLO + 2 * NY, :], mask_ref[0 : NX * NY, :],
        mask_ref[M_XHI : M_XHI + NY, :], mask_ref[M_EDGE:M_ROWS, :],
    ], axis=0))


def outer_kernel(f_ref, xlo_ref, xhi_ref, ylo_ref, yhi_ref, low_ref, high_ref, mask_ref, raw_ref,
                 out_ref, outer_ref, ext_ref, edge_ref, w_ref):
    build_band(w_ref, raw_ref, True)
    widen_two(ext_ref, edge_ref, f_ref, xlo_ref, xhi_ref, ylo_ref, yhi_ref, low_ref, high_ref, mask_ref)

    def body(k):
        total = conv_wide(ext_ref, edge_ref, w_ref, k)
        for i in range(STEP):
            out_ref[k + i] = total[i * OUT_ROWS : (i + 1) * OUT_ROWS]
            outer_ref[k + i] = (f_ref[k + i].astype(F32) * twice(mask_ref[0 : NX * NY, :])).astype(BF)

    each_step(f_ref.shape[0], body)


def correlate(gt_ref, ext_ref, first_x, taps_ref):
    depth = 2 * (ext_ref.shape[1] - 1)

    def body(b, carry):
        rows = []
        for z in range(depth):
            parts = []
            for a in range(3):
                for c in range(3):
                    half = (z + c) % 2 * LANES
                    part = ext_ref[b, (z + c) // 2, first_x + a : first_x + a + NX, :, half : half + LANES]
                    parts.append(part.reshape(NX * NY, LANES))
            rows.append(jnp.concatenate(parts, axis=1))
        sums = dot(gt_ref[...], jnp.concatenate(rows, axis=0))
        for a in range(3):
            for c in range(3):
                taps_ref[9 * a + 3 * b + c] = sums[:, (3 * a + c) * LANES : (3 * a + c + 1) * LANES]
        return carry

    lax.fori_loop(0, 3, body, 0)


def pack_taps(taps_ref, packed_ref, channels):
    lane = lax.broadcasted_iota(jnp.int32, (channels, LANES), 1)
    for g in range(7):
        t1 = pltpu.roll(taps_ref[4 * g + 1], 96, 1)
        t2 = pltpu.roll(taps_ref[4 * g + 2], 64, 1)
        t3 = pltpu.roll(taps_ref[4 * g + 3], 32, 1)
        blocks = (
            jnp.where(lane < 96, taps_ref[4 * g], t1),
            jnp.where(lane < 64, t1, t2),
            jnp.where(lane < 32, t2, t3),
        )
        for i, value in enumerate(blocks):
            start = (3 * g + i) * channels
            packed_ref[start : start + channels, :] = value
    rest = packed_ref.shape[0] - 21 * channels
    if rest:
        packed_ref[21 * channels :, :] = jnp.zeros((rest, LANES), F32)


def hidden_kernel(channels, run, core_ref, f_ref, xlo_ref, xhi_ref, ylo_ref, yhi_ref, low_ref, high_ref, mask_ref,
                  raw_ref, grad_ref, act_ref, hg_ref, keep_ref, give_ref,
                  ext_ref, edge_ref, w_ref, gt_ref, taps_ref, packed_ref):
    build_band(w_ref, raw_ref, False)
    widen_two(ext_ref, edge_ref, f_ref, xlo_ref, xhi_ref, ylo_ref, yhi_ref, low_ref, high_ref)

    def body(k):
        total = conv_wide(ext_ref, edge_ref, w_ref, k)
        m = out_mask(mask_ref)
        for i in range(STEP):
            hidden = m * total[i * OUT_ROWS : (i + 1) * OUT_ROWS]
            sigma = jax.nn.sigmoid(hidden)
            act_ref[k + i] = (hidden * sigma).astype(BF)
            hg_ref[k + i] = (m * grad_ref[k + i] * sigma * (1.0 + hidden * (1.0 - sigma))).astype(BF)

    each_step(f_ref.shape[0], body)
    turn(gt_ref, hg_ref, NY, channels)
    correlate(gt_ref, ext_ref, 1, taps_ref)
    hand_out(channels, run, core_ref, taps_ref, packed_ref, keep_ref, give_ref)


def turn(gt_ref, g_ref, start, channels):
    inner = NX * NY
    for k in range(g_ref.shape[0]):
        value = g_ref[k, start : start + inner, :].T
        for i in range(2):
            z = 2 * k + i
            gt_ref[:, z * inner : (z + 1) * inner] = value[i * LANES : i * LANES + channels]


def hand_out(channels, run, core_ref, taps_ref, packed_ref, keep_ref, give_ref):
    runs = keep_ref.shape[0] // run
    block = 2 * runs * run
    taps_ref[27] = jnp.zeros((channels, LANES), F32)
    pack_taps(taps_ref, packed_ref, channels)
    for l in range(packed_ref.shape[0] // block):
        lanes = slice(l * LANES, (l + 1) * LANES)
        for x in range(runs):
            base = l * block + 2 * x * run
            rows = slice(x * run, (x + 1) * run)
            mine = pl.multiple_of(base + core_ref[0] * run, run)
            other = pl.multiple_of(base + (1 - core_ref[0]) * run, run)
            keep_ref[rows, lanes] = packed_ref[pl.ds(mine, run), :]
            give_ref[rows, lanes] = packed_ref[pl.ds(other, run), :]


def corr_kernel(channels, run, core_ref, act_ref, outer_ref, keep_ref, give_ref, ext_ref, gt_ref, taps_ref, packed_ref):
    widen_one(ext_ref, act_ref)
    turn(gt_ref, outer_ref, 0, channels)
    correlate(gt_ref, ext_ref, 0, taps_ref)
    hand_out(channels, run, core_ref, taps_ref, packed_ref, keep_ref, give_ref)


def grid_grad_kernel(hg_ref, raw_ref, outer_ref, perm_ref, take_ref, out_ref, ext_ref, sum_ref, turned_ref, w_ref):
    build_band(w_ref, raw_ref, True)
    widen_one(ext_ref, hg_ref)

    def body(k):
        total = conv_inner(ext_ref, w_ref, k)
        rows = NX * NY
        for i in range(STEP):
            sum_ref[k + i] = (outer_ref[k + i].astype(F32) + total[i * rows : (i + 1) * rows]).astype(BF)

    each_step(outer_ref.shape[0], body)
    gather_pairs(sum_ref, turned_ref)
    take = take_ref[...]
    for i in range(perm_ref.shape[0]):
        rows = dot_nt(turned_ref[i], perm_ref[i]).astype(BF)
        out_ref[:, i * PAIR : (i + 1) * PAIR] = dot(take, rows).astype(BF)


def block_kernel(act_ref, mask_ref, raw_ref, field_ref, perm_ref, out_ref, ext_ref, sum_ref, turned_ref, w_ref):
    build_band(w_ref, raw_ref, False)
    widen_one(ext_ref, act_ref)

    def body(k):
        total = conv_inner(ext_ref, w_ref, k)
        m = twice(mask_ref[0 : NX * NY, :])
        rows = NX * NY
        for i in range(STEP):
            sum_ref[k + i] = (field_ref[k + i].astype(F32) + m * total[i * rows : (i + 1) * rows]).astype(BF)

    each_step(field_ref.shape[0], body)
    gather_pairs(sum_ref, turned_ref)
    for i in range(perm_ref.shape[0]):
        out_ref[:, i * PAIR : (i + 1) * PAIR] = dot_nt(turned_ref[i], perm_ref[i]).astype(BF)


def pair_sum_kernel(keep0_ref, got0_ref, keep1_ref, got1_ref, out_ref):
    half = keep0_ref.shape[1]
    out_ref[:, 0:half] = (keep0_ref[...] + got0_ref[...]).astype(BF)
    out_ref[:, half : 2 * half] = (keep1_ref[...] + got1_ref[...]).astype(BF)


def assemble_kernel(cap, run, back_hbm, parts_ref, out_hbm, total_ref, sem):
    buffers, half = total_ref.shape
    senders = parts_ref.shape[0]
    row = lax.broadcasted_iota(jnp.int32, (buffers, senders), 0)
    col = lax.broadcasted_iota(jnp.int32, (buffers, senders), 1)
    same = row % cap == col % cap
    core = (row // run) % 2
    total = jnp.zeros((buffers, half), F32)
    for i in range(2):
        add = jnp.where(same & (core == i), 1.0, 0.0).astype(BF)
        total = total + dot(add, parts_ref[:, i * half : (i + 1) * half])
    total_ref[...] = total.astype(BF)
    width = out_hbm.shape[1] - half
    store = pltpu.make_async_copy(total_ref, out_hbm.at[:, width : width + half], sem)
    store.start()
    store.wait()


def unpack_kernel(factor, core_ref, mine_ref, other_ref, first_ref, second_ref, flat_ref):
    rows, lanes = mine_ref.shape
    for i, out_ref in enumerate((first_ref, second_ref)):
        own = core_ref[0] == i
        for l in range(lanes // LANES):
            at = slice(l * LANES, (l + 1) * LANES)
            value = jnp.where(own, mine_ref[:, at].astype(F32), other_ref[:, at].astype(F32))
            flat_ref[l * rows : (l + 1) * rows, :] = value
        unpack_taps(factor, flat_ref, out_ref)


def unpack_taps(factor, packed_ref, out_ref):
    channels = out_ref.shape[1]
    lane = lax.broadcasted_iota(jnp.int32, (channels, LANES), 1)
    for g in range(7):
        v = []
        for i in range(3):
            start = (3 * g + i) * channels
            v.append(packed_ref[start : start + channels, :] * factor)
        taps = (
            v[0],
            pltpu.roll(jnp.where(lane < 64, v[1], v[0]), 32, 1),
            pltpu.roll(jnp.where(lane < 32, v[2], v[1]), 64, 1),
            pltpu.roll(v[2], 96, 1),
        )
        for u in range(4):
            if 4 * g + u < 27:
                out_ref[4 * g + u] = taps[u][:, 0:channels]


RX = ("cx", "core")
ALL = ("cx", "core", "ry")
SAME_CORE = ("cx", "ry")


def size_of(axes):
    return int(np.prod([lax.axis_size(a) for a in ((axes,) if isinstance(axes, str) else axes)]))


def share(parts, axes):
    return lax.all_to_all(parts, axes, split_axis=0, concat_axis=0, tiled=True)


def neighbours(axes, upper, lower):
    count = size_of(axes)
    ahead = [(i, i + 1) for i in range(count - 1)]
    behind = [(t, s) for s, t in ahead]
    return lax.ppermute(upper, axes, ahead), lax.ppermute(lower, axes, behind)


def swap_cores(value):
    count = size_of(RX)
    return lax.ppermute(value, RX, [(i, i ^ 1) for i in range(count)])


def message_rows():
    cells = []
    for ys in ((0, 1), (NY - 2, NY - 1)):
        for y in ys:
            cells += [(x, y) for x in range(-2, NX + 2)]
        cells += [None] * (MSG - 2 * (NX + 4))
    return cells


def exchange(field, pick):
    pairs = field.shape[0]
    xlo, xhi = neighbours(RX, field[:, (NX - 2) * NY :, :], field[:, : 2 * NY, :])
    message = jax.ShapeDtypeStruct((pairs, MSG, PAIR), BF)
    low, high = call(message_kernel, (message, message), 5e8, 3e6)(field, xlo, xhi, pick)
    ylo, yhi = neighbours("ry", high, low)
    return xlo, xhi, ylo, yhi, low, high


def mask_cells():
    cells = [(x, y) for x in range(NX) for y in range(NY)]
    cells += [(x, y) for x in (-2, -1) for y in range(NY)]
    cells += [(x, y) for x in (NX, NX + 1) for y in range(NY)]
    for ys in ((-2, -1), (NY, NY + 1), (0, 1), (NY - 2, NY - 1)):
        for y in ys:
            cells += [(x, y) for x in range(-2, NX + 2)]
        cells += [None] * (MSG - 2 * (NX + 4))
    for y in (-1, NY):
        cells += [(x, y) for x in range(-1, NX + 1)]
        cells += [None] * (EDGE - NX - 2)
    return cells


def on_device(column_features, column_route, cotangent, first_weight, second_weight):
    count_x = size_of(RX)
    count_y = size_of("ry")
    count_all = count_x * count_y
    shard_rows, row_width = column_features.shape
    channels = first_weight.shape[1]
    depth = row_width // channels
    slots = NX * NY
    pairs = depth // 2
    chunks = channels // GROUP
    cap = 2 * shard_rows // count_all
    buffers = count_all * cap
    me_x = lax.axis_index(RX)
    me_y = lax.axis_index("ry")
    core = lax.axis_index("core").astype(jnp.int32).reshape(1)
    conv_flops = 2 * slots * pairs * 36 * LANES * PAIR

    smem = pl.BlockSpec(memory_space=pltpu.SMEM)
    vmem = pl.BlockSpec(memory_space=pltpu.VMEM)
    hbm = pl.BlockSpec(memory_space=pltpu.HBM)
    shape = jax.ShapeDtypeStruct
    field_shape = shape((pairs, slots, PAIR), BF)
    wide_shape = shape((pairs, OUT_ROWS, PAIR), BF)
    ext = pltpu.VMEM((3, pairs + 1, NX + 4, NY, PAIR), BF)
    edge = pltpu.VMEM((3, 3, pairs + 1, 2 * EDGE, PAIR), BF)
    turned = pltpu.VMEM((chunks, slots, PAIR), F32)
    turned_low = pltpu.VMEM((chunks, slots, PAIR), BF)
    sums = pltpu.VMEM((pairs, slots, PAIR), BF)

    perm = jnp.asarray(permutation(channels, depth), BF)
    pick_np = np.zeros((2 * MSG, (NX + 4) * NY), np.float32)
    for r, cell in enumerate(message_rows()):
        if cell is not None:
            pick_np[r, (cell[0] + 2) * NY + cell[1]] = 1.0
    pick = jnp.asarray(pick_np, BF)

    route_row = column_route.reshape(1, shard_rows)
    told_width = row_width + LANES
    outgoing = call(
        functools.partial(send_kernel, cap, slots), shape((buffers, told_width), BF),
        2 * buffers * shard_rows * row_width, 3 * shard_rows * row_width * 2,
        (pltpu.VMEM((shard_rows, row_width), BF), pltpu.SemaphoreType.DMA), in_specs=[vmem, hbm],
    )(route_row, column_features)
    incoming = share(outgoing.reshape(count_all, cap, told_width), ALL).reshape(buffers, told_width)

    cells = mask_cells()
    steps = np.asarray([(0, 0) if c is None else (c[0] // NX, c[1] // NY) for c in cells], np.int32)
    local = np.asarray([-1 if c is None else (c[0] % NX) * NY + c[1] % NY for c in cells], np.int32)
    to_x = me_x + steps[:, 0]
    to_y = me_y + steps[:, 1]
    inside = (to_x >= 0) & (to_x < count_x) & (to_y >= 0) & (to_y < count_y) & (local >= 0)
    codes = jnp.where(inside, (to_x * count_y + to_y) * slots + local, -1).astype(F32)[:, None]
    me = (me_x * count_y + me_y).astype(jnp.int32).reshape(1)

    cot = call(
        to_pairs_kernel, field_shape, 1e9, 3e6, (turned,),
    )(cotangent.reshape(slots, row_width), perm)
    cot_halo = exchange(cot, pick)

    field, take = call(
        functools.partial(place_kernel, cap, slots), (field_shape, shape((buffers, slots), BF)), 1e9, 3e6,
        (turned, pltpu.VMEM(perm.shape, BF), pltpu.SemaphoreType.DMA), in_specs=[smem, vmem, hbm],
    )(me, incoming, perm)
    field_halo = exchange(field, pick)

    mask = call(
        functools.partial(mask_kernel, cap, slots), shape((M_ROWS, LANES), F32), 1e8, 1e6,
        (pltpu.VMEM((count_all, LANES), F32),),
    )(incoming, codes)
    band = pltpu.VMEM((36 * LANES, PAIR), BF)
    ext_near = pltpu.VMEM((3, pairs + 1, NX + 2, NY, PAIR), BF)
    act_grad, outer = call(
        outer_kernel, (shape((pairs, OUT_ROWS, PAIR), F32), field_shape),
        1.3 * conv_flops, 7e6, (ext, edge, band), ROOM_WIDE,
    )(cot, *cot_halo, mask, second_weight)

    packed_rows = -(-21 * channels // buffers) * buffers
    run = count_y * cap
    grad_lanes = 2 * packed_rows // buffers * LANES
    half_shape = shape((buffers // 2, grad_lanes // 2), F32)
    corr_scratch = (
        pltpu.VMEM((channels, depth * slots), BF),
        pltpu.VMEM((28, channels, LANES), F32), pltpu.VMEM((packed_rows, LANES), F32),
    )
    act, hg, keep0, give0 = call(
        functools.partial(hidden_kernel, channels, run), (wide_shape, wide_shape, half_shape, half_shape),
        2.3 * conv_flops, 9e6, (ext, edge, band) + corr_scratch, ROOM_WIDE, in_specs=[smem] + [vmem] * 10,
    )(core, field, *field_halo, mask, first_weight, act_grad)
    got0 = swap_cores(give0)
    keep1, give1 = call(
        functools.partial(corr_kernel, channels, run), (half_shape, half_shape), conv_flops, 5e6,
        (ext_near,) + corr_scratch, ROOM_CORR, in_specs=[smem, vmem, vmem],
    )(core, act, outer)
    sent = call(
        pair_sum_kernel, shape((buffers // 2, grad_lanes), BF), 1e6, 2e6,
    )(keep0, got0, keep1, swap_cores(give1))
    parts = share(sent.reshape(count_all // 2, cap, grad_lanes), SAME_CORE).reshape(buffers // 2, grad_lanes)

    hg, sent = lax.optimization_barrier((hg, sent))
    back_width = row_width + grad_lanes // 2
    back = call(
        grid_grad_kernel, shape((buffers, back_width), BF), 1.2 * conv_flops, 6e6,
        (ext_near, sums, turned_low, band), ROOM_NEAR,
    )(hg, first_weight, outer, perm, take)
    mixed = call(
        functools.partial(assemble_kernel, cap, run), shape((buffers, back_width), BF), 2e8, 3e6,
        (pltpu.VMEM((buffers, grad_lanes // 2), BF), pltpu.SemaphoreType.DMA),
        in_specs=[hbm, vmem], out_specs=hbm, input_output_aliases={0: 0},
    )(back, parts)
    returned = share(mixed.reshape(count_all, cap, back_width), ALL).reshape(buffers, back_width)

    act, mixed = lax.optimization_barrier((act, mixed))
    block_output = call(
        block_kernel, shape((slots, row_width), BF), 1.2 * conv_flops, 8e6,
        (ext_near, sums, turned_low, band), ROOM_NEAR,
    )(act, mask, second_weight, field, perm)

    returned, block_output = lax.optimization_barrier((returned, block_output))
    mine = returned[:, row_width:]
    feature_grads = call(
        functools.partial(collect_kernel, cap, slots), shape((shard_rows, row_width), BF),
        2 * buffers * shard_rows * row_width, 3 * shard_rows * row_width * 2,
    )(route_row, returned)

    factor = float(1.0 / np.sqrt(np.float32(count_all * shard_rows * depth)))
    grads = shape(first_weight.shape, F32)
    first_grad, second_grad = call(
        functools.partial(unpack_kernel, factor), (grads, grads), 1e6, 4e6,
        (pltpu.VMEM((packed_rows, LANES), F32),), in_specs=[smem, vmem, vmem],
    )(core, mine, swap_cores(mine))
    return (block_output.reshape(cotangent.shape), feature_grads, first_grad, second_grad)


def solution(mesh):
    count_x = mesh.shape["rx"]
    fine = jax.sharding.Mesh(mesh.devices.reshape(count_x // 2, 2, mesh.shape["ry"]), ALL)
    in_specs = (P(ALL, None), P(ALL), P(RX, "ry", None), P(), P())
    out_specs = (P(RX, "ry", None), P(ALL, None), P(), P())
    return jax.shard_map(
        on_device, mesh=fine, in_specs=in_specs, out_specs=out_specs, check_vma=False
    )
```

```python
import functools

import jax
import jax.numpy as jnp
import numpy as np
from jax import lax
from jax.experimental import pallas as pl
from jax.experimental.pallas import tpu as pltpu
from jax.sharding import PartitionSpec as P

LANES = 128
PAIR = 256
MIB = 1024 * 1024
ROOM_WIDE, ROOM_NEAR, ROOM_CORR, ROOM_SMALL = 26, 18, 14, 5
BF = jnp.bfloat16
F32 = jnp.float32


def call(body, out_shape, flops, moved, scratch=(), room=ROOM_SMALL, **extra):
    return pl.pallas_call(
        body,
        out_shape=out_shape,
        scratch_shapes=list(scratch),
        compiler_params=pltpu.CompilerParams(vmem_limit_bytes=room * MIB),
        cost_estimate=pl.CostEstimate(flops=int(flops), bytes_accessed=int(moved), transcendentals=0),
        **extra,
    )


def dot(left, right):
    return jnp.dot(left, right, preferred_element_type=F32)


def dot_nt(left, right):
    return lax.dot_general(left, right, (((1,), (1,)), ((), ())), preferred_element_type=F32)


def as_column(row):
    return jnp.broadcast_to(row, (row.shape[1], row.shape[1])).T


def send_kernel(cap, slots, row_ref, feat_hbm, out_ref, feat_ref, sem):
    fetch = pltpu.make_async_copy(feat_hbm, feat_ref, sem)
    fetch.start()
    rows, width = feat_ref.shape
    buffers = out_ref.shape[0]
    owner_row = (row_ref[...] // slots).astype(F32)
    owner_col = as_column(owner_row)
    first = lax.broadcasted_iota(jnp.int32, (rows, rows), 0)
    second = lax.broadcasted_iota(jnp.int32, (rows, rows), 1)
    same = jnp.where((owner_col == owner_row) & (first < second), 1.0, 0.0)
    rank = jnp.sum(same, axis=0, keepdims=True)
    pos = owner_row * cap + rank
    place = lax.broadcasted_iota(jnp.int32, (buffers, rows), 0)
    hot = jnp.where(place.astype(F32) == pos, 1.0, 0.0).astype(BF)
    slot_row = (row_ref[...] % slots).astype(F32)
    kind = place % cap
    told = jnp.where(kind == 0, owner_row, jnp.where(kind == 1, slot_row, 0.0))
    out_ref[:, width : width + rows] = told.astype(BF)
    fetch.wait()
    out_ref[:, 0:width] = dot(hot, feat_ref[...]).astype(BF)


def collect_kernel(cap, slots, row_ref, back_ref, out_ref):
    rows, width = out_ref.shape
    owner_row = (row_ref[...] // slots).astype(F32)
    owner_col = as_column(owner_row)
    first = lax.broadcasted_iota(jnp.int32, (rows, rows), 0)
    second = lax.broadcasted_iota(jnp.int32, (rows, rows), 1)
    same = jnp.where((owner_col == owner_row) & (second < first), 1.0, 0.0)
    pos = owner_col[:, 0:1] * cap + jnp.sum(same, axis=1, keepdims=True)
    place = lax.broadcasted_iota(jnp.int32, (rows, back_ref.shape[0]), 1).astype(F32)
    hot = jnp.where(place == pos, 1.0, 0.0).astype(BF)
    out_ref[...] = dot(hot, back_ref[:, 0:width]).astype(BF)


def told_rows(cap, in_ref, which):
    buffers, width = in_ref.shape
    count = buffers // cap
    source = lax.broadcasted_iota(jnp.int32, (count, buffers), 0)
    place = lax.broadcasted_iota(jnp.int32, (count, buffers), 1)
    pick = jnp.where(place == source * cap + which, 1.0, 0.0).astype(BF)
    return dot(pick, in_ref[:, width - LANES : width])


def mask_kernel(cap, slots, in_ref, codes_ref, mask_ref, route_ref):
    total = mask_ref.shape[0]
    route_ref[...] = told_rows(cap, in_ref, 0) * slots + told_rows(cap, in_ref, 1)
    codes = jnp.broadcast_to(codes_ref[...], (total, LANES))
    hits = jnp.zeros((total, LANES), F32)
    for s in range(route_ref.shape[0]):
        hits = hits + jnp.where(codes == route_ref[s : s + 1, :], 1.0, 0.0)
    mask_ref[...] = jnp.broadcast_to(jnp.sum(hits, axis=1, keepdims=True), (total, LANES))


def slot_table(cap, slots, me, in_ref):
    buffers = in_ref.shape[0]
    count = buffers // cap
    mine_f = jnp.where(told_rows(cap, in_ref, 0) == me.astype(F32), 1.0, 0.0)
    slot_f = told_rows(cap, in_ref, 1)
    first = lax.broadcasted_iota(jnp.int32, (LANES, LANES), 0)
    second = lax.broadcasted_iota(jnp.int32, (LANES, LANES), 1)
    tri = jnp.where(first < second, 1.0, 0.0).astype(BF)
    rank = dot(mine_f.astype(BF), tri)
    lane = lax.broadcasted_iota(jnp.int32, (count, LANES), 1)
    held = jnp.zeros((count, LANES), F32)
    for j in range(cap):
        here = jnp.where(rank == j, mine_f, 0.0)
        number = jnp.sum(here, axis=1, keepdims=True)
        value = jnp.sum(here * slot_f, axis=1, keepdims=True)
        value = value + (1.0 - number) * slots
        held = jnp.where(lane == j, value, held)
    place = lax.broadcasted_iota(jnp.int32, (buffers, count), 0)
    source = lax.broadcasted_iota(jnp.int32, (buffers, count), 1)
    spread = jnp.where(place // cap == source, 1.0, 0.0).astype(BF)
    wide = dot(spread, held.astype(BF))
    place = lax.broadcasted_iota(jnp.int32, (buffers, LANES), 0)
    lane = lax.broadcasted_iota(jnp.int32, (buffers, LANES), 1)
    slot_col = jnp.sum(jnp.where(place % cap == lane, wide, 0.0), axis=1, keepdims=True)
    slot_id = lax.broadcasted_iota(jnp.int32, (buffers, slots), 1).astype(F32)
    return jnp.where(slot_col == slot_id, 1.0, 0.0)


GROUP = 16
FOLD = LANES // GROUP


def permutation(channels, depth):
    perm = np.zeros((channels // GROUP, PAIR, PAIR), np.float32)
    for i in range(channels // GROUP):
        for j in range(GROUP):
            for z in range(depth):
                perm[i, depth * j + z, LANES * (z // FOLD) + GROUP * ((z + i) % FOLD) + j] = 1.0
    return perm


def lane_group(rows):
    return lax.broadcasted_iota(jnp.int32, (rows, LANES), 1) // GROUP


def spread_pairs(turned_ref, out_ref):
    chunks, rows, _ = turned_ref.shape
    step = 32
    group = lane_group(step)

    def body(t, carry):
        at = pl.ds(pl.multiple_of(t * step, step), step)
        for half in range(2):
            lanes = slice(half * LANES, (half + 1) * LANES)
            parts = [turned_ref[i, at, lanes] for i in range(chunks)]
            parts = parts + [jnp.zeros((step, LANES), F32)] * (FOLD - chunks)
            for bit in (1, 2, 4):
                odd = (group & bit) != 0
                parts = [jnp.where(odd, parts[(i + bit) % FOLD], parts[i]) for i in range(FOLD)]
            for g in range(FOLD):
                value = parts[(-g) % FOLD]
                if g:
                    value = pltpu.roll(value, LANES - GROUP * g, 1)
                z = half * FOLD + g
                out_ref[z // 2, at, (z % 2) * LANES : (z % 2 + 1) * LANES] = value.astype(BF)
        return carry

    lax.fori_loop(0, rows // step, body, 0)


def gather_pairs(in_ref, turned_ref):
    chunks, rows, _ = turned_ref.shape
    step = 32
    group = lane_group(step)

    def body(t, carry):
        at = pl.ds(pl.multiple_of(t * step, step), step)
        for half in range(2):
            turned = []
            for g in range(FOLD):
                z = half * FOLD + g
                value = in_ref[z // 2, at, (z % 2) * LANES : (z % 2 + 1) * LANES].astype(F32)
                turned.append(pltpu.roll(value, GROUP * g, 1) if g else value)
            parts = [turned[(-i) % FOLD] for i in range(FOLD)]
            for bit in (1, 2, 4):
                odd = (group & bit) != 0
                parts = [jnp.where(odd, parts[(i - bit) % FOLD], parts[i]) for i in range(FOLD)]
            for i in range(chunks):
                turned_ref[i, at, half * LANES : (half + 1) * LANES] = parts[i].astype(BF)
        return carry

    lax.fori_loop(0, rows // step, body, 0)


def to_pairs_kernel(rows_ref, perm_ref, out_ref, turned_ref):
    for i in range(perm_ref.shape[0]):
        turned_ref[i] = dot(rows_ref[:, i * PAIR : (i + 1) * PAIR], perm_ref[i])
    spread_pairs(turned_ref, out_ref)


def place_kernel(cap, slots, me_ref, rows_ref, perm_hbm, out_ref, take_ref, turned_ref, perm_ref, sem):
    fetch = pltpu.make_async_copy(perm_hbm, perm_ref, sem)
    fetch.start()
    take = slot_table(cap, slots, me_ref[0], rows_ref)
    take_ref[...] = take.astype(BF)
    put = take.T.astype(BF)
    fetch.wait()
    for i in range(perm_ref.shape[0]):
        held = dot(put, rows_ref[:, i * PAIR : (i + 1) * PAIR]).astype(BF)
        turned_ref[i] = dot(held, perm_ref[i])
    spread_pairs(turned_ref, out_ref)


def message_kernel(f_ref, xlo_ref, xhi_ref, pick_ref, low_ref, high_ref):
    pick = pick_ref[...]
    half = low_ref.shape[1]
    for k in range(f_ref.shape[0]):
        rows = jnp.concatenate([xlo_ref[k], f_ref[k], xhi_ref[k]], axis=0)
        sent = dot(pick, rows).astype(BF)
        low_ref[k] = sent[0:half]
        high_ref[k] = sent[half : 2 * half]


def build_band(band_ref, raw_ref, backward):
    channels = raw_ref.shape[1]
    band_ref[...] = jnp.zeros_like(band_ref)
    for tap in range(27):
        value = raw_ref[26 - tap] if backward else raw_ref[tap].T
        for zo in range(2):
            row = ((tap // 3) * 4 + zo + tap % 3) * LANES
            band_ref[row : row + channels, zo * LANES : zo * LANES + channels] = value


NX = 16
NY = 16
OUT_MAIN = (NX + 2) * NY
EDGE = 24
OUT_ROWS = OUT_MAIN + 2 * EDGE
MSG = 48
M_XLO = NX * NY
M_XHI = M_XLO + 2 * NY
M_YLO = M_XHI + 2 * NY
M_YHI = M_YLO + MSG
M_LOW = M_YHI + MSG
M_HIGH = M_LOW + MSG
M_EDGE = M_HIGH + MSG
M_ROWS = M_EDGE + 2 * EDGE


def twice(value):
    return jnp.concatenate([value, value], axis=1)


def put_pair(ref, lead, k, tail, value):
    value = value.astype(BF)
    ref[lead + (k,) + tail + (slice(LANES, PAIR),)] = value[:, 0:LANES]
    ref[lead + (k + 1,) + tail + (slice(0, LANES),)] = value[:, LANES:PAIR]


def clear_ends(ref, lead):
    last = ref.shape[len(lead)] - 1
    dims = ref.shape[len(lead) + 1 : -1]
    ref[lead + (0,) + (slice(None),) * len(dims) + (slice(0, LANES),)] = jnp.zeros(dims + (LANES,), BF)
    ref[lead + (last,) + (slice(None),) * len(dims) + (slice(LANES, PAIR),)] = jnp.zeros(dims + (LANES,), BF)


def put_shifted(ext_ref, k, xp, mid, before, after, row):
    ny = mid.shape[0]
    up = jnp.where(row == 0, before, pltpu.roll(mid, 1, 0))
    down = jnp.where(row == ny - 1, after, pltpu.roll(mid, ny - 1, 0))
    for b, value in enumerate((up, mid, down)):
        put_pair(ext_ref, (b,), k, (xp, slice(None)), value)


def widen_two(ext_ref, edge_ref, f_ref, xlo_ref, xhi_ref, ylo_ref, yhi_ref, low_ref, high_ref, mask_ref=None):
    for b in range(3):
        clear_ends(ext_ref, (b,))
        for a in range(3):
            clear_ends(edge_ref, (a, b))
    row = lax.broadcasted_iota(jnp.int32, (NY, PAIR), 0)

    def read(ref, k, start, size, mask_start):
        value = ref[k, start : start + size, :].astype(F32)
        if mask_ref is None:
            return value
        return value * twice(mask_ref[mask_start + start : mask_start + start + size, :])

    def fill(k):
        ylo = read(ylo_ref, k, 0, MSG, M_YLO)
        yhi = read(yhi_ref, k, 0, MSG, M_YHI)
        low = read(low_ref, k, 0, MSG, M_LOW)
        high = read(high_ref, k, 0, MSG, M_HIGH)
        wide = NX + 4
        for xp in range(wide):
            if xp < 2:
                mid = read(xlo_ref, k, xp * NY, NY, M_XLO)
            elif xp >= NX + 2:
                mid = read(xhi_ref, k, (xp - NX - 2) * NY, NY, M_XHI)
            else:
                mid = read(f_ref, k, (xp - 2) * NY, NY, 0)
            put_shifted(ext_ref, k, xp, mid, ylo[wide + xp : wide + xp + 1, :], yhi[xp : xp + 1, :], row)
        first = ((ylo, 0), (ylo, wide), (low, 0))
        second = ((high, wide), (yhi, 0), (yhi, wide))
        for a in range(3):
            for b in range(3):
                sides = []
                for value, start in (first[b], second[b]):
                    turn = start + a
                    if turn:
                        value = pltpu.roll(value, MSG - turn, 0)
                    sides.append(value[0:EDGE])
                put_pair(edge_ref, (a, b), k, (slice(None),), jnp.concatenate(sides, axis=0))

    return fill


def widen_one(ext_ref, rows_ref):
    for b in range(3):
        clear_ends(ext_ref, (b,))
    row = lax.broadcasted_iota(jnp.int32, (NY, PAIR), 0)

    def fill(k):
        edges = rows_ref[k, OUT_MAIN:OUT_ROWS, :].astype(F32)
        for xp in range(NX + 2):
            mid = rows_ref[k, xp * NY : (xp + 1) * NY, :].astype(F32)
            put_shifted(ext_ref, k, xp, mid, edges[xp : xp + 1, :], edges[EDGE + xp : EDGE + xp + 1, :], row)

    return fill


def fill_all(fill, pairs):
    def body(k, carry):
        fill(k)
        return carry

    lax.fori_loop(0, pairs, body, 0)


STEP = 2


def conv_wide(ext_ref, edge_ref, w_ref, k):
    pieces = []
    for a in range(3):
        for b in range(3):
            for j in range(2):
                parts = []
                for i in range(STEP):
                    parts.append(ext_ref[b, k + i + j, a : a + NX + 2].reshape(OUT_MAIN, PAIR))
                    parts.append(edge_ref[a, b, k + i + j])
                pieces.append(jnp.concatenate(parts, axis=0))
    return dot(jnp.concatenate(pieces, axis=1), w_ref[...])


def conv_inner(ext_ref, w_ref, k):
    pieces = []
    for a in range(3):
        for b in range(3):
            for j in range(2):
                pieces.append(ext_ref[b, k + j : k + j + STEP, a : a + NX].reshape(STEP * NX * NY, PAIR))
    return dot(jnp.concatenate(pieces, axis=1), w_ref[...])


def each_step(pairs, fill, conv, finish):
    for k in range(STEP + 1):
        fill(k)
    last = None
    for k in range(0, pairs, STEP):
        for ahead in range(k + STEP + 1, min(k + 2 * STEP + 1, pairs)):
            fill(ahead)
        total = conv(k)
        if last is not None:
            finish(*last)
        last = (k, total)
    finish(*last)


def out_mask(mask_ref):
    return twice(jnp.concatenate([
        mask_ref[M_XLO + NY : M_XLO + 2 * NY, :], mask_ref[0 : NX * NY, :],
        mask_ref[M_XHI : M_XHI + NY, :], mask_ref[M_EDGE:M_ROWS, :],
    ], axis=0))


def outer_kernel(f_ref, xlo_ref, xhi_ref, ylo_ref, yhi_ref, low_ref, high_ref, mask_ref, raw_ref,
                 out_ref, outer_ref, ext_ref, edge_ref, w_ref):
    build_band(w_ref, raw_ref, True)
    fill = widen_two(ext_ref, edge_ref, f_ref, xlo_ref, xhi_ref, ylo_ref, yhi_ref, low_ref, high_ref, mask_ref)

    def finish(k, total):
        for i in range(STEP):
            out_ref[k + i] = total[i * OUT_ROWS : (i + 1) * OUT_ROWS]
            outer_ref[k + i] = (f_ref[k + i].astype(F32) * twice(mask_ref[0 : NX * NY, :])).astype(BF)

    each_step(f_ref.shape[0], fill, lambda k: conv_wide(ext_ref, edge_ref, w_ref, k), finish)


def correlate(gt_ref, ext_ref, first_x, taps_ref):
    depth = 2 * (ext_ref.shape[1] - 1)

    def body(b, carry):
        rows = []
        for z in range(depth):
            parts = []
            for a in range(3):
                for c in range(3):
                    half = (z + c) % 2 * LANES
                    part = ext_ref[b, (z + c) // 2, first_x + a : first_x + a + NX, :, half : half + LANES]
                    parts.append(part.reshape(NX * NY, LANES))
            rows.append(jnp.concatenate(parts, axis=1))
        sums = dot(gt_ref[...], jnp.concatenate(rows, axis=0))
        for a in range(3):
            for c in range(3):
                taps_ref[9 * a + 3 * b + c] = sums[:, (3 * a + c) * LANES : (3 * a + c + 1) * LANES]
        return carry

    lax.fori_loop(0, 3, body, 0)


def pack_taps(taps_ref, packed_ref, channels):
    lane = lax.broadcasted_iota(jnp.int32, (channels, LANES), 1)
    for g in range(7):
        t1 = pltpu.roll(taps_ref[4 * g + 1], 96, 1)
        t2 = pltpu.roll(taps_ref[4 * g + 2], 64, 1)
        t3 = pltpu.roll(taps_ref[4 * g + 3], 32, 1)
        blocks = (
            jnp.where(lane < 96, taps_ref[4 * g], t1),
            jnp.where(lane < 64, t1, t2),
            jnp.where(lane < 32, t2, t3),
        )
        for i, value in enumerate(blocks):
            start = (3 * g + i) * channels
            packed_ref[start : start + channels, :] = value
    rest = packed_ref.shape[0] - 21 * channels
    if rest:
        packed_ref[21 * channels :, :] = jnp.zeros((rest, LANES), F32)


def hidden_kernel(channels, run, core_ref, f_ref, xlo_ref, xhi_ref, ylo_ref, yhi_ref, low_ref, high_ref, mask_ref,
                  raw_ref, grad_ref, act_ref, hg_ref, keep_ref, give_ref,
                  ext_ref, edge_ref, w_ref, gt_ref, taps_ref, packed_ref):
    build_band(w_ref, raw_ref, False)
    fill = widen_two(ext_ref, edge_ref, f_ref, xlo_ref, xhi_ref, ylo_ref, yhi_ref, low_ref, high_ref)

    def finish(k, total):
        m = out_mask(mask_ref)
        for i in range(STEP):
            hidden = m * total[i * OUT_ROWS : (i + 1) * OUT_ROWS]
            sigma = jax.nn.sigmoid(hidden)
            act_ref[k + i] = (hidden * sigma).astype(BF)
            hg_ref[k + i] = (m * grad_ref[k + i] * sigma * (1.0 + hidden * (1.0 - sigma))).astype(BF)

    each_step(f_ref.shape[0], fill, lambda k: conv_wide(ext_ref, edge_ref, w_ref, k), finish)
    turn(gt_ref, hg_ref, NY, channels)
    correlate(gt_ref, ext_ref, 1, taps_ref)
    hand_out(channels, run, core_ref, taps_ref, packed_ref, keep_ref, give_ref)


def turn(gt_ref, g_ref, start, channels):
    inner = NX * NY
    for k in range(g_ref.shape[0]):
        value = g_ref[k, start : start + inner, :].T
        for i in range(2):
            z = 2 * k + i
            gt_ref[:, z * inner : (z + 1) * inner] = value[i * LANES : i * LANES + channels]


def hand_out(channels, run, core_ref, taps_ref, packed_ref, keep_ref, give_ref):
    runs = keep_ref.shape[0] // run
    block = 2 * runs * run
    taps_ref[27] = jnp.zeros((channels, LANES), F32)
    pack_taps(taps_ref, packed_ref, channels)
    for l in range(packed_ref.shape[0] // block):
        lanes = slice(l * LANES, (l + 1) * LANES)
        for x in range(runs):
            base = l * block + 2 * x * run
            rows = slice(x * run, (x + 1) * run)
            mine = pl.multiple_of(base + core_ref[0] * run, run)
            other = pl.multiple_of(base + (1 - core_ref[0]) * run, run)
            keep_ref[rows, lanes] = packed_ref[pl.ds(mine, run), :]
            give_ref[rows, lanes] = packed_ref[pl.ds(other, run), :]


def corr_kernel(channels, run, core_ref, act_ref, outer_ref, keep_ref, give_ref, ext_ref, gt_ref, taps_ref, packed_ref):
    fill_all(widen_one(ext_ref, act_ref), act_ref.shape[0])
    turn(gt_ref, outer_ref, 0, channels)
    correlate(gt_ref, ext_ref, 0, taps_ref)
    hand_out(channels, run, core_ref, taps_ref, packed_ref, keep_ref, give_ref)


def grid_grad_kernel(hg_ref, raw_ref, outer_ref, perm_ref, take_ref, out_ref, ext_ref, sum_ref, turned_ref, w_ref):
    build_band(w_ref, raw_ref, True)
    fill = widen_one(ext_ref, hg_ref)

    def finish(k, total):
        rows = NX * NY
        for i in range(STEP):
            sum_ref[k + i] = (outer_ref[k + i].astype(F32) + total[i * rows : (i + 1) * rows]).astype(BF)

    each_step(outer_ref.shape[0], fill, lambda k: conv_inner(ext_ref, w_ref, k), finish)
    gather_pairs(sum_ref, turned_ref)
    take = take_ref[...]
    for i in range(perm_ref.shape[0]):
        rows = dot_nt(turned_ref[i], perm_ref[i]).astype(BF)
        out_ref[:, i * PAIR : (i + 1) * PAIR] = dot(take, rows).astype(BF)


def block_kernel(act_ref, mask_ref, raw_ref, field_ref, perm_ref, out_ref, ext_ref, sum_ref, turned_ref, w_ref):
    build_band(w_ref, raw_ref, False)
    fill = widen_one(ext_ref, act_ref)

    def finish(k, total):
        m = twice(mask_ref[0 : NX * NY, :])
        rows = NX * NY
        for i in range(STEP):
            sum_ref[k + i] = (field_ref[k + i].astype(F32) + m * total[i * rows : (i + 1) * rows]).astype(BF)

    each_step(field_ref.shape[0], fill, lambda k: conv_inner(ext_ref, w_ref, k), finish)
    gather_pairs(sum_ref, turned_ref)
    for i in range(perm_ref.shape[0]):
        out_ref[:, i * PAIR : (i + 1) * PAIR] = dot_nt(turned_ref[i], perm_ref[i]).astype(BF)


def pair_sum_kernel(keep0_ref, got0_ref, keep1_ref, got1_ref, out_ref):
    half = keep0_ref.shape[1]
    out_ref[:, 0:half] = (keep0_ref[...] + got0_ref[...]).astype(BF)
    out_ref[:, half : 2 * half] = (keep1_ref[...] + got1_ref[...]).astype(BF)


def assemble_kernel(cap, run, back_hbm, parts_ref, out_hbm, total_ref, sem):
    buffers, half = total_ref.shape
    senders = parts_ref.shape[0]
    row = lax.broadcasted_iota(jnp.int32, (buffers, senders), 0)
    col = lax.broadcasted_iota(jnp.int32, (buffers, senders), 1)
    same = row % cap == col % cap
    core = (row // run) % 2
    total = jnp.zeros((buffers, half), F32)
    for i in range(2):
        add = jnp.where(same & (core == i), 1.0, 0.0).astype(BF)
        total = total + dot(add, parts_ref[:, i * half : (i + 1) * half])
    total_ref[...] = total.astype(BF)
    width = out_hbm.shape[1] - half
    store = pltpu.make_async_copy(total_ref, out_hbm.at[:, width : width + half], sem)
    store.start()
    store.wait()


def unpack_kernel(factor, core_ref, mine_ref, other_ref, first_ref, second_ref, flat_ref):
    rows, lanes = mine_ref.shape
    for i, out_ref in enumerate((first_ref, second_ref)):
        own = core_ref[0] == i
        for l in range(lanes // LANES):
            at = slice(l * LANES, (l + 1) * LANES)
            value = jnp.where(own, mine_ref[:, at].astype(F32), other_ref[:, at].astype(F32))
            flat_ref[l * rows : (l + 1) * rows, :] = value
        unpack_taps(factor, flat_ref, out_ref)


def unpack_taps(factor, packed_ref, out_ref):
    channels = out_ref.shape[1]
    lane = lax.broadcasted_iota(jnp.int32, (channels, LANES), 1)
    for g in range(7):
        v = []
        for i in range(3):
            start = (3 * g + i) * channels
            v.append(packed_ref[start : start + channels, :] * factor)
        taps = (
            v[0],
            pltpu.roll(jnp.where(lane < 64, v[1], v[0]), 32, 1),
            pltpu.roll(jnp.where(lane < 32, v[2], v[1]), 64, 1),
            pltpu.roll(v[2], 96, 1),
        )
        for u in range(4):
            if 4 * g + u < 27:
                out_ref[4 * g + u] = taps[u][:, 0:channels]


RX = ("cx", "core")
ALL = ("cx", "core", "ry")
SAME_CORE = ("cx", "ry")


def size_of(axes):
    return int(np.prod([lax.axis_size(a) for a in ((axes,) if isinstance(axes, str) else axes)]))


def share(parts, axes):
    return lax.all_to_all(parts, axes, split_axis=0, concat_axis=0, tiled=True)


def neighbours(axes, upper, lower):
    count = size_of(axes)
    ahead = [(i, i + 1) for i in range(count - 1)]
    behind = [(t, s) for s, t in ahead]
    return lax.ppermute(upper, axes, ahead), lax.ppermute(lower, axes, behind)


def swap_cores(value):
    count = size_of(RX)
    return lax.ppermute(value, RX, [(i, i ^ 1) for i in range(count)])


def message_rows():
    cells = []
    for ys in ((0, 1), (NY - 2, NY - 1)):
        for y in ys:
            cells += [(x, y) for x in range(-2, NX + 2)]
        cells += [None] * (MSG - 2 * (NX + 4))
    return cells


def exchange(field, pick):
    pairs = field.shape[0]
    xlo, xhi = neighbours(RX, field[:, (NX - 2) * NY :, :], field[:, : 2 * NY, :])
    message = jax.ShapeDtypeStruct((pairs, MSG, PAIR), BF)
    low, high = call(message_kernel, (message, message), 5e8, 3e6)(field, xlo, xhi, pick)
    ylo, yhi = neighbours("ry", high, low)
    return xlo, xhi, ylo, yhi, low, high


def mask_cells():
    cells = [(x, y) for x in range(NX) for y in range(NY)]
    cells += [(x, y) for x in (-2, -1) for y in range(NY)]
    cells += [(x, y) for x in (NX, NX + 1) for y in range(NY)]
    for ys in ((-2, -1), (NY, NY + 1), (0, 1), (NY - 2, NY - 1)):
        for y in ys:
            cells += [(x, y) for x in range(-2, NX + 2)]
        cells += [None] * (MSG - 2 * (NX + 4))
    for y in (-1, NY):
        cells += [(x, y) for x in range(-1, NX + 1)]
        cells += [None] * (EDGE - NX - 2)
    return cells


def on_device(column_features, column_route, cotangent, first_weight, second_weight):
    count_x = size_of(RX)
    count_y = size_of("ry")
    count_all = count_x * count_y
    shard_rows, row_width = column_features.shape
    channels = first_weight.shape[1]
    depth = row_width // channels
    slots = NX * NY
    pairs = depth // 2
    chunks = channels // GROUP
    cap = 2 * shard_rows // count_all
    buffers = count_all * cap
    me_x = lax.axis_index(RX)
    me_y = lax.axis_index("ry")
    core = lax.axis_index("core").astype(jnp.int32).reshape(1)
    conv_flops = 2 * slots * pairs * 36 * LANES * PAIR

    smem = pl.BlockSpec(memory_space=pltpu.SMEM)
    vmem = pl.BlockSpec(memory_space=pltpu.VMEM)
    hbm = pl.BlockSpec(memory_space=pltpu.HBM)
    shape = jax.ShapeDtypeStruct
    field_shape = shape((pairs, slots, PAIR), BF)
    wide_shape = shape((pairs, OUT_ROWS, PAIR), BF)
    ext = pltpu.VMEM((3, pairs + 1, NX + 4, NY, PAIR), BF)
    edge = pltpu.VMEM((3, 3, pairs + 1, 2 * EDGE, PAIR), BF)
    turned = pltpu.VMEM((chunks, slots, PAIR), F32)
    turned_low = pltpu.VMEM((chunks, slots, PAIR), BF)
    sums = pltpu.VMEM((pairs, slots, PAIR), BF)

    perm = jnp.asarray(permutation(channels, depth), BF)
    pick_np = np.zeros((2 * MSG, (NX + 4) * NY), np.float32)
    for r, cell in enumerate(message_rows()):
        if cell is not None:
            pick_np[r, (cell[0] + 2) * NY + cell[1]] = 1.0
    pick = jnp.asarray(pick_np, BF)

    route_row = column_route.reshape(1, shard_rows)
    told_width = row_width + LANES
    outgoing = call(
        functools.partial(send_kernel, cap, slots), shape((buffers, told_width), BF),
        2 * buffers * shard_rows * row_width, 3 * shard_rows * row_width * 2,
        (pltpu.VMEM((shard_rows, row_width), BF), pltpu.SemaphoreType.DMA), in_specs=[vmem, hbm],
    )(route_row, column_features)
    incoming = share(outgoing.reshape(count_all, cap, told_width), ALL).reshape(buffers, told_width)

    cells = mask_cells()
    steps = np.asarray([(0, 0) if c is None else (c[0] // NX, c[1] // NY) for c in cells], np.int32)
    local = np.asarray([-1 if c is None else (c[0] % NX) * NY + c[1] % NY for c in cells], np.int32)
    to_x = me_x + steps[:, 0]
    to_y = me_y + steps[:, 1]
    inside = (to_x >= 0) & (to_x < count_x) & (to_y >= 0) & (to_y < count_y) & (local >= 0)
    codes = jnp.where(inside, (to_x * count_y + to_y) * slots + local, -1).astype(F32)[:, None]
    me = (me_x * count_y + me_y).astype(jnp.int32).reshape(1)

    cot = call(
        to_pairs_kernel, field_shape, 1e9, 3e6, (turned,),
    )(cotangent.reshape(slots, row_width), perm)
    cot_halo = exchange(cot, pick)

    field, take = call(
        functools.partial(place_kernel, cap, slots), (field_shape, shape((buffers, slots), BF)), 1e9, 3e6,
        (turned, pltpu.VMEM(perm.shape, BF), pltpu.SemaphoreType.DMA), in_specs=[smem, vmem, hbm],
    )(me, incoming, perm)
    field_halo = exchange(field, pick)

    mask = call(
        functools.partial(mask_kernel, cap, slots), shape((M_ROWS, LANES), F32), 1e8, 1e6,
        (pltpu.VMEM((count_all, LANES), F32),),
    )(incoming, codes)
    band = pltpu.VMEM((36 * LANES, PAIR), BF)
    ext_near = pltpu.VMEM((3, pairs + 1, NX + 2, NY, PAIR), BF)
    act_grad, outer = call(
        outer_kernel, (shape((pairs, OUT_ROWS, PAIR), F32), field_shape),
        1.3 * conv_flops, 7e6, (ext, edge, band), ROOM_WIDE,
    )(cot, *cot_halo, mask, second_weight)

    packed_rows = -(-21 * channels // buffers) * buffers
    run = count_y * cap
    grad_lanes = 2 * packed_rows // buffers * LANES
    half_shape = shape((buffers // 2, grad_lanes // 2), F32)
    corr_scratch = (
        pltpu.VMEM((channels, depth * slots), BF),
        pltpu.VMEM((28, channels, LANES), F32), pltpu.VMEM((packed_rows, LANES), F32),
    )
    act, hg, keep0, give0 = call(
        functools.partial(hidden_kernel, channels, run), (wide_shape, wide_shape, half_shape, half_shape),
        2.3 * conv_flops, 9e6, (ext, edge, band) + corr_scratch, ROOM_WIDE, in_specs=[smem] + [vmem] * 10,
    )(core, field, *field_halo, mask, first_weight, act_grad)
    got0 = swap_cores(give0)
    keep1, give1 = call(
        functools.partial(corr_kernel, channels, run), (half_shape, half_shape), conv_flops, 5e6,
        (ext_near,) + corr_scratch, ROOM_CORR, in_specs=[smem, vmem, vmem],
    )(core, act, outer)
    sent = call(
        pair_sum_kernel, shape((buffers // 2, grad_lanes), BF), 1e6, 2e6,
    )(keep0, got0, keep1, swap_cores(give1))
    parts = share(sent.reshape(count_all // 2, cap, grad_lanes), SAME_CORE).reshape(buffers // 2, grad_lanes)

    hg, sent = lax.optimization_barrier((hg, sent))
    back_width = row_width + grad_lanes // 2
    back = call(
        grid_grad_kernel, shape((buffers, back_width), BF), 1.2 * conv_flops, 6e6,
        (ext_near, sums, turned_low, band), ROOM_NEAR,
    )(hg, first_weight, outer, perm, take)
    mixed = call(
        functools.partial(assemble_kernel, cap, run), shape((buffers, back_width), BF), 2e8, 3e6,
        (pltpu.VMEM((buffers, grad_lanes // 2), BF), pltpu.SemaphoreType.DMA),
        in_specs=[hbm, vmem], out_specs=hbm, input_output_aliases={0: 0},
    )(back, parts)
    returned = share(mixed.reshape(count_all, cap, back_width), ALL).reshape(buffers, back_width)

    act, mixed = lax.optimization_barrier((act, mixed))
    block_output = call(
        block_kernel, shape((slots, row_width), BF), 1.2 * conv_flops, 8e6,
        (ext_near, sums, turned_low, band), ROOM_NEAR,
    )(act, mask, second_weight, field, perm)

    returned, block_output = lax.optimization_barrier((returned, block_output))
    mine = returned[:, row_width:]
    feature_grads = call(
        functools.partial(collect_kernel, cap, slots), shape((shard_rows, row_width), BF),
        2 * buffers * shard_rows * row_width, 3 * shard_rows * row_width * 2,
    )(route_row, returned)

    factor = float(1.0 / np.sqrt(np.float32(count_all * shard_rows * depth)))
    grads = shape(first_weight.shape, F32)
    first_grad, second_grad = call(
        functools.partial(unpack_kernel, factor), (grads, grads), 1e6, 4e6,
        (pltpu.VMEM((packed_rows, LANES), F32),), in_specs=[smem, vmem, vmem],
    )(core, mine, swap_cores(mine))
    return (block_output.reshape(cotangent.shape), feature_grads, first_grad, second_grad)


def solution(mesh):
    count_x = mesh.shape["rx"]
    fine = jax.sharding.Mesh(mesh.devices.reshape(count_x // 2, 2, mesh.shape["ry"]), ALL)
    in_specs = (P(ALL, None), P(ALL), P(RX, "ry", None), P(), P())
    out_specs = (P(RX, "ry", None), P(ALL, None), P(), P())
    return jax.shard_map(
        on_device, mesh=fine, in_specs=in_specs, out_specs=out_specs, check_vma=False
    )
```

```python
import functools

import jax
import jax.numpy as jnp
import numpy as np
from jax import lax
from jax.experimental import pallas as pl
from jax.experimental.pallas import tpu as pltpu
from jax.sharding import PartitionSpec as P

LANES = 128
PAIR = 256
MIB = 1024 * 1024
ROOM_WIDE, ROOM_NEAR, ROOM_CORR, ROOM_SMALL = 26, 18, 14, 5
BF = jnp.bfloat16
F32 = jnp.float32


def call(body, out_shape, flops, moved, scratch=(), room=ROOM_SMALL, **extra):
    return pl.pallas_call(
        body,
        out_shape=out_shape,
        scratch_shapes=list(scratch),
        compiler_params=pltpu.CompilerParams(vmem_limit_bytes=room * MIB),
        cost_estimate=pl.CostEstimate(flops=int(flops), bytes_accessed=int(moved), transcendentals=0),
        **extra,
    )


def dot(left, right):
    return jnp.dot(left, right, preferred_element_type=F32)


def dot_nt(left, right):
    return lax.dot_general(left, right, (((1,), (1,)), ((), ())), preferred_element_type=F32)


def as_column(row):
    return jnp.broadcast_to(row, (row.shape[1], row.shape[1])).T


def send_kernel(cap, slots, row_ref, feat_hbm, out_ref, feat_ref, sem):
    fetch = pltpu.make_async_copy(feat_hbm, feat_ref, sem)
    fetch.start()
    rows, width = feat_ref.shape
    buffers = out_ref.shape[0]
    owner_row = (row_ref[...] // slots).astype(F32)
    owner_col = as_column(owner_row)
    first = lax.broadcasted_iota(jnp.int32, (rows, rows), 0)
    second = lax.broadcasted_iota(jnp.int32, (rows, rows), 1)
    same = jnp.where((owner_col == owner_row) & (first < second), 1.0, 0.0)
    rank = jnp.sum(same, axis=0, keepdims=True)
    pos = owner_row * cap + rank
    place = lax.broadcasted_iota(jnp.int32, (buffers, rows), 0)
    hot = jnp.where(place.astype(F32) == pos, 1.0, 0.0).astype(BF)
    slot_row = (row_ref[...] % slots).astype(F32)
    kind = place % cap
    told = jnp.where(kind == 0, owner_row, jnp.where(kind == 1, slot_row, 0.0))
    out_ref[:, width : width + rows] = told.astype(BF)
    fetch.wait()
    out_ref[:, 0:width] = dot(hot, feat_ref[...]).astype(BF)


def collect_kernel(cap, slots, row_ref, back_ref, out_ref):
    rows, width = out_ref.shape
    owner_row = (row_ref[...] // slots).astype(F32)
    owner_col = as_column(owner_row)
    first = lax.broadcasted_iota(jnp.int32, (rows, rows), 0)
    second = lax.broadcasted_iota(jnp.int32, (rows, rows), 1)
    same = jnp.where((owner_col == owner_row) & (second < first), 1.0, 0.0)
    pos = owner_col[:, 0:1] * cap + jnp.sum(same, axis=1, keepdims=True)
    place = lax.broadcasted_iota(jnp.int32, (rows, back_ref.shape[0]), 1).astype(F32)
    hot = jnp.where(place == pos, 1.0, 0.0).astype(BF)
    out_ref[...] = dot(hot, back_ref[:, 0:width]).astype(BF)


def told_rows(cap, in_ref, which):
    buffers, width = in_ref.shape
    count = buffers // cap
    source = lax.broadcasted_iota(jnp.int32, (count, buffers), 0)
    place = lax.broadcasted_iota(jnp.int32, (count, buffers), 1)
    pick = jnp.where(place == source * cap + which, 1.0, 0.0).astype(BF)
    return dot(pick, in_ref[:, width - LANES : width])


def mask_kernel(cap, slots, in_ref, codes_ref, mask_ref, route_ref):
    total = mask_ref.shape[0]
    route_ref[...] = told_rows(cap, in_ref, 0) * slots + told_rows(cap, in_ref, 1)
    codes = jnp.broadcast_to(codes_ref[...], (total, LANES))
    hits = jnp.zeros((total, LANES), F32)
    for s in range(route_ref.shape[0]):
        hits = hits + jnp.where(codes == route_ref[s : s + 1, :], 1.0, 0.0)
    mask_ref[...] = jnp.broadcast_to(jnp.sum(hits, axis=1, keepdims=True), (total, LANES))


def slot_table(cap, slots, me, in_ref):
    buffers = in_ref.shape[0]
    count = buffers // cap
    mine_f = jnp.where(told_rows(cap, in_ref, 0) == me.astype(F32), 1.0, 0.0)
    slot_f = told_rows(cap, in_ref, 1)
    first = lax.broadcasted_iota(jnp.int32, (LANES, LANES), 0)
    second = lax.broadcasted_iota(jnp.int32, (LANES, LANES), 1)
    tri = jnp.where(first < second, 1.0, 0.0).astype(BF)
    rank = dot(mine_f.astype(BF), tri)
    lane = lax.broadcasted_iota(jnp.int32, (count, LANES), 1)
    held = jnp.zeros((count, LANES), F32)
    for j in range(cap):
        here = jnp.where(rank == j, mine_f, 0.0)
        number = jnp.sum(here, axis=1, keepdims=True)
        value = jnp.sum(here * slot_f, axis=1, keepdims=True)
        value = value + (1.0 - number) * slots
        held = jnp.where(lane == j, value, held)
    place = lax.broadcasted_iota(jnp.int32, (buffers, count), 0)
    source = lax.broadcasted_iota(jnp.int32, (buffers, count), 1)
    spread = jnp.where(place // cap == source, 1.0, 0.0).astype(BF)
    wide = dot(spread, held.astype(BF))
    place = lax.broadcasted_iota(jnp.int32, (buffers, LANES), 0)
    lane = lax.broadcasted_iota(jnp.int32, (buffers, LANES), 1)
    slot_col = jnp.sum(jnp.where(place % cap == lane, wide, 0.0), axis=1, keepdims=True)
    slot_id = lax.broadcasted_iota(jnp.int32, (buffers, slots), 1).astype(F32)
    return jnp.where(slot_col == slot_id, 1.0, 0.0)


GROUP = 16
FOLD = LANES // GROUP


def permutation(channels, depth):
    perm = np.zeros((channels // GROUP, PAIR, PAIR), np.float32)
    for i in range(channels // GROUP):
        for j in range(GROUP):
            for z in range(depth):
                perm[i, depth * j + z, LANES * (z // FOLD) + GROUP * ((z + i) % FOLD) + j] = 1.0
    return perm


def lane_group(rows):
    return lax.broadcasted_iota(jnp.int32, (rows, LANES), 1) // GROUP


def spread_pairs(turned_ref, out_ref):
    chunks, rows, _ = turned_ref.shape
    step = 32
    group = lane_group(step)

    def body(t, carry):
        at = pl.ds(pl.multiple_of(t * step, step), step)
        for half in range(2):
            lanes = slice(half * LANES, (half + 1) * LANES)
            parts = [turned_ref[i, at, lanes] for i in range(chunks)]
            parts = parts + [jnp.zeros((step, LANES), F32)] * (FOLD - chunks)
            for bit in (1, 2, 4):
                odd = (group & bit) != 0
                parts = [jnp.where(odd, parts[(i + bit) % FOLD], parts[i]) for i in range(FOLD)]
            for g in range(FOLD):
                value = parts[(-g) % FOLD]
                if g:
                    value = pltpu.roll(value, LANES - GROUP * g, 1)
                z = half * FOLD + g
                out_ref[z // 2, at, (z % 2) * LANES : (z % 2 + 1) * LANES] = value.astype(BF)
        return carry

    lax.fori_loop(0, rows // step, body, 0)


def gather_pairs(in_ref, turned_ref):
    chunks, rows, _ = turned_ref.shape
    step = 32
    group = lane_group(step)

    def body(t, carry):
        at = pl.ds(pl.multiple_of(t * step, step), step)
        for half in range(2):
            turned = []
            for g in range(FOLD):
                z = half * FOLD + g
                value = in_ref[z // 2, at, (z % 2) * LANES : (z % 2 + 1) * LANES].astype(F32)
                turned.append(pltpu.roll(value, GROUP * g, 1) if g else value)
            parts = [turned[(-i) % FOLD] for i in range(FOLD)]
            for bit in (1, 2, 4):
                odd = (group & bit) != 0
                parts = [jnp.where(odd, parts[(i - bit) % FOLD], parts[i]) for i in range(FOLD)]
            for i in range(chunks):
                turned_ref[i, at, half * LANES : (half + 1) * LANES] = parts[i].astype(BF)
        return carry

    lax.fori_loop(0, rows // step, body, 0)


def to_pairs_kernel(rows_ref, perm_ref, out_ref, turned_ref):
    for i in range(perm_ref.shape[0]):
        turned_ref[i] = dot(rows_ref[:, i * PAIR : (i + 1) * PAIR], perm_ref[i])
    spread_pairs(turned_ref, out_ref)


def place_kernel(cap, slots, me_ref, rows_ref, perm_hbm, out_ref, take_ref, turned_ref, perm_ref, sem):
    fetch = pltpu.make_async_copy(perm_hbm, perm_ref, sem)
    fetch.start()
    take = slot_table(cap, slots, me_ref[0], rows_ref)
    take_ref[...] = take.astype(BF)
    put = take.T.astype(BF)
    fetch.wait()
    for i in range(perm_ref.shape[0]):
        held = dot(put, rows_ref[:, i * PAIR : (i + 1) * PAIR]).astype(BF)
        turned_ref[i] = dot(held, perm_ref[i])
    spread_pairs(turned_ref, out_ref)


def message_kernel(f_ref, xlo_ref, xhi_ref, pick_ref, low_ref, high_ref):
    pick = pick_ref[...]
    half = low_ref.shape[1]
    for k in range(f_ref.shape[0]):
        rows = jnp.concatenate([xlo_ref[k], f_ref[k], xhi_ref[k]], axis=0)
        sent = dot(pick, rows).astype(BF)
        low_ref[k] = sent[0:half]
        high_ref[k] = sent[half : 2 * half]


def build_band(band_ref, raw_ref, backward):
    channels = raw_ref.shape[1]
    band_ref[...] = jnp.zeros_like(band_ref)
    for tap in range(27):
        value = raw_ref[26 - tap] if backward else raw_ref[tap].T
        for zo in range(2):
            row = ((tap // 3) * 4 + zo + tap % 3) * LANES
            band_ref[row : row + channels, zo * LANES : zo * LANES + channels] = value


NX = 16
NY = 16
OUT_MAIN = (NX + 2) * NY
EDGE = 24
OUT_ROWS = OUT_MAIN + 2 * EDGE
MSG = 48
M_XLO = NX * NY
M_XHI = M_XLO + 2 * NY
M_YLO = M_XHI + 2 * NY
M_YHI = M_YLO + MSG
M_LOW = M_YHI + MSG
M_HIGH = M_LOW + MSG
M_EDGE = M_HIGH + MSG
M_ROWS = M_EDGE + 2 * EDGE


def twice(value):
    return jnp.concatenate([value, value], axis=1)


def put_pair(ref, lead, k, tail, value):
    value = value.astype(BF)
    ref[lead + (k,) + tail + (slice(LANES, PAIR),)] = value[:, 0:LANES]
    ref[lead + (k + 1,) + tail + (slice(0, LANES),)] = value[:, LANES:PAIR]


def clear_ends(ref, lead):
    last = ref.shape[len(lead)] - 1
    dims = ref.shape[len(lead) + 1 : -1]
    ref[lead + (0,) + (slice(None),) * len(dims) + (slice(0, LANES),)] = jnp.zeros(dims + (LANES,), BF)
    ref[lead + (last,) + (slice(None),) * len(dims) + (slice(LANES, PAIR),)] = jnp.zeros(dims + (LANES,), BF)


def put_shifted(ext_ref, k, xp, mid, before, after, row):
    ny = mid.shape[0]
    up = jnp.where(row == 0, before, pltpu.roll(mid, 1, 0))
    down = jnp.where(row == ny - 1, after, pltpu.roll(mid, ny - 1, 0))
    for b, value in enumerate((up, mid, down)):
        put_pair(ext_ref, (b,), k, (xp, slice(None)), value)


def widen_two(ext_ref, edge_ref, f_ref, xlo_ref, xhi_ref, ylo_ref, yhi_ref, low_ref, high_ref, mask_ref=None):
    for b in range(3):
        clear_ends(ext_ref, (b,))
        for a in range(3):
            clear_ends(edge_ref, (a, b))
    row = lax.broadcasted_iota(jnp.int32, (NY, PAIR), 0)

    def read(ref, k, start, size, mask_start):
        value = ref[k, start : start + size, :].astype(F32)
        if mask_ref is None:
            return value
        return value * twice(mask_ref[mask_start + start : mask_start + start + size, :])

    def fill(k):
        ylo = read(ylo_ref, k, 0, MSG, M_YLO)
        yhi = read(yhi_ref, k, 0, MSG, M_YHI)
        low = read(low_ref, k, 0, MSG, M_LOW)
        high = read(high_ref, k, 0, MSG, M_HIGH)
        wide = NX + 4
        for xp in range(wide):
            if xp < 2:
                mid = read(xlo_ref, k, xp * NY, NY, M_XLO)
            elif xp >= NX + 2:
                mid = read(xhi_ref, k, (xp - NX - 2) * NY, NY, M_XHI)
            else:
                mid = read(f_ref, k, (xp - 2) * NY, NY, 0)
            put_shifted(ext_ref, k, xp, mid, ylo[wide + xp : wide + xp + 1, :], yhi[xp : xp + 1, :], row)
        first = ((ylo, 0), (ylo, wide), (low, 0))
        second = ((high, wide), (yhi, 0), (yhi, wide))
        for a in range(3):
            for b in range(3):
                sides = []
                for value, start in (first[b], second[b]):
                    turn = start + a
                    if turn:
                        value = pltpu.roll(value, MSG - turn, 0)
                    sides.append(value[0:EDGE])
                put_pair(edge_ref, (a, b), k, (slice(None),), jnp.concatenate(sides, axis=0))

    return fill


def widen_one(ext_ref, rows_ref):
    for b in range(3):
        clear_ends(ext_ref, (b,))
    row = lax.broadcasted_iota(jnp.int32, (NY, PAIR), 0)

    return lambda k: fill_rows(ext_ref, k, rows_ref[k].astype(F32), row)


def fill_rows(ext_ref, k, value, row):
    edges = value[OUT_MAIN:OUT_ROWS]
    for xp in range(NX + 2):
        mid = value[xp * NY : (xp + 1) * NY]
        put_shifted(ext_ref, k, xp, mid, edges[xp : xp + 1, :], edges[EDGE + xp : EDGE + xp + 1, :], row)


STEP = 2


def conv_wide(ext_ref, edge_ref, w_ref, k):
    pieces = []
    for a in range(3):
        for b in range(3):
            for j in range(2):
                parts = []
                for i in range(STEP):
                    parts.append(ext_ref[b, k + i + j, a : a + NX + 2].reshape(OUT_MAIN, PAIR))
                    parts.append(edge_ref[a, b, k + i + j])
                pieces.append(jnp.concatenate(parts, axis=0))
    return dot(jnp.concatenate(pieces, axis=1), w_ref[...])


def conv_inner(ext_ref, w_ref, k):
    pieces = []
    for a in range(3):
        for b in range(3):
            for j in range(2):
                pieces.append(ext_ref[b, k + j : k + j + STEP, a : a + NX].reshape(STEP * NX * NY, PAIR))
    return dot(jnp.concatenate(pieces, axis=1), w_ref[...])


def each_step(pairs, fill, conv, finish):
    for k in range(STEP + 1):
        fill(k)
    last = None
    for k in range(0, pairs, STEP):
        for ahead in range(k + STEP + 1, min(k + 2 * STEP + 1, pairs)):
            fill(ahead)
        total = conv(k)
        if last is not None:
            finish(*last)
        last = (k, total)
    finish(*last)


def out_mask(mask_ref):
    return twice(jnp.concatenate([
        mask_ref[M_XLO + NY : M_XLO + 2 * NY, :], mask_ref[0 : NX * NY, :],
        mask_ref[M_XHI : M_XHI + NY, :], mask_ref[M_EDGE:M_ROWS, :],
    ], axis=0))


def outer_kernel(f_ref, xlo_ref, xhi_ref, ylo_ref, yhi_ref, low_ref, high_ref, mask_ref, raw_ref,
                 out_ref, outer_ref, gt_ref, ext_ref, edge_ref, w_ref):
    build_band(w_ref, raw_ref, True)
    fill = widen_two(ext_ref, edge_ref, f_ref, xlo_ref, xhi_ref, ylo_ref, yhi_ref, low_ref, high_ref, mask_ref)

    def finish(k, total):
        for i in range(STEP):
            out_ref[k + i] = total[i * OUT_ROWS : (i + 1) * OUT_ROWS]
            outer = (f_ref[k + i].astype(F32) * twice(mask_ref[0 : NX * NY, :])).astype(BF)
            outer_ref[k + i] = outer
            turn(gt_ref, k + i, outer)

    each_step(f_ref.shape[0], fill, lambda k: conv_wide(ext_ref, edge_ref, w_ref, k), finish)


def correlate(gt_ref, ext_ref, first_x, taps_ref):
    depth = 2 * (ext_ref.shape[1] - 1)
    for b in range(3):
        rows = []
        for z in range(depth):
            parts = []
            for a in range(3):
                for c in range(3):
                    half = (z + c) % 2 * LANES
                    part = ext_ref[b, (z + c) // 2, first_x + a : first_x + a + NX, :, half : half + LANES]
                    parts.append(part.reshape(NX * NY, LANES))
            rows.append(jnp.concatenate(parts, axis=1))
        sums = dot(gt_ref[...], jnp.concatenate(rows, axis=0))
        for a in range(3):
            for c in range(3):
                taps_ref[9 * a + 3 * b + c] = sums[:, (3 * a + c) * LANES : (3 * a + c + 1) * LANES]


def pack_taps(taps_ref, packed_ref, channels):
    lane = lax.broadcasted_iota(jnp.int32, (channels, LANES), 1)
    for g in range(7):
        t1 = pltpu.roll(taps_ref[4 * g + 1], 96, 1)
        t2 = pltpu.roll(taps_ref[4 * g + 2], 64, 1)
        t3 = pltpu.roll(taps_ref[4 * g + 3], 32, 1)
        blocks = (
            jnp.where(lane < 96, taps_ref[4 * g], t1),
            jnp.where(lane < 64, t1, t2),
            jnp.where(lane < 32, t2, t3),
        )
        for i, value in enumerate(blocks):
            start = (3 * g + i) * channels
            packed_ref[start : start + channels, :] = value
    rest = packed_ref.shape[0] - 21 * channels
    if rest:
        packed_ref[21 * channels :, :] = jnp.zeros((rest, LANES), F32)


def hidden_kernel(channels, run, core_ref, f_ref, xlo_ref, xhi_ref, ylo_ref, yhi_ref, low_ref, high_ref, mask_ref,
                  raw_ref, grad_ref, act_ref, hg_ref, wide_ref, keep_ref, give_ref,
                  ext_ref, edge_ref, w_ref, gt_ref, taps_ref, packed_ref):
    build_band(w_ref, raw_ref, False)
    fill = widen_two(ext_ref, edge_ref, f_ref, xlo_ref, xhi_ref, ylo_ref, yhi_ref, low_ref, high_ref)

    for b in range(3):
        clear_ends(wide_ref, (b,))
    row = lax.broadcasted_iota(jnp.int32, (NY, PAIR), 0)

    def finish(k, total):
        m = out_mask(mask_ref)
        for i in range(STEP):
            hidden = m * total[i * OUT_ROWS : (i + 1) * OUT_ROWS]
            sigma = jax.nn.sigmoid(hidden)
            act = (hidden * sigma).astype(BF)
            act_ref[k + i] = act
            fill_rows(wide_ref, k + i, act.astype(F32), row)
            hg = (m * grad_ref[k + i] * sigma * (1.0 + hidden * (1.0 - sigma))).astype(BF)
            hg_ref[k + i] = hg
            turn(gt_ref, k + i, hg[NY : NY + NX * NY])

    each_step(f_ref.shape[0], fill, lambda k: conv_wide(ext_ref, edge_ref, w_ref, k), finish)
    correlate(gt_ref, ext_ref, 1, taps_ref)
    hand_out(channels, run, core_ref, taps_ref, packed_ref, keep_ref, give_ref)


def turn(gt_ref, k, value):
    channels = gt_ref.shape[0]
    inner = value.shape[0]
    value = value.T
    for i in range(2):
        z = 2 * k + i
        gt_ref[:, z * inner : (z + 1) * inner] = value[i * LANES : i * LANES + channels]


def hand_out(channels, run, core_ref, taps_ref, packed_ref, keep_ref, give_ref):
    runs = keep_ref.shape[0] // run
    block = 2 * runs * run
    taps_ref[27] = jnp.zeros((channels, LANES), F32)
    pack_taps(taps_ref, packed_ref, channels)
    for l in range(packed_ref.shape[0] // block):
        lanes = slice(l * LANES, (l + 1) * LANES)
        for x in range(runs):
            base = l * block + 2 * x * run
            rows = slice(x * run, (x + 1) * run)
            mine = pl.multiple_of(base + core_ref[0] * run, run)
            other = pl.multiple_of(base + (1 - core_ref[0]) * run, run)
            keep_ref[rows, lanes] = packed_ref[pl.ds(mine, run), :]
            give_ref[rows, lanes] = packed_ref[pl.ds(other, run), :]


def corr_kernel(channels, run, core_ref, ext_ref, gt_ref, keep_ref, give_ref, taps_ref, packed_ref):
    correlate(gt_ref, ext_ref, 0, taps_ref)
    hand_out(channels, run, core_ref, taps_ref, packed_ref, keep_ref, give_ref)


def grid_grad_kernel(hg_ref, raw_ref, outer_ref, perm_ref, take_ref, out_ref, ext_ref, sum_ref, turned_ref, w_ref):
    build_band(w_ref, raw_ref, True)
    fill = widen_one(ext_ref, hg_ref)

    def finish(k, total):
        rows = NX * NY
        for i in range(STEP):
            sum_ref[k + i] = (outer_ref[k + i].astype(F32) + total[i * rows : (i + 1) * rows]).astype(BF)

    each_step(outer_ref.shape[0], fill, lambda k: conv_inner(ext_ref, w_ref, k), finish)
    gather_pairs(sum_ref, turned_ref)
    take = take_ref[...]
    for i in range(perm_ref.shape[0]):
        rows = dot_nt(turned_ref[i], perm_ref[i]).astype(BF)
        out_ref[:, i * PAIR : (i + 1) * PAIR] = dot(take, rows).astype(BF)


def block_kernel(act_ref, mask_ref, raw_ref, field_ref, perm_ref, out_ref, ext_ref, sum_ref, turned_ref, w_ref):
    build_band(w_ref, raw_ref, False)
    fill = widen_one(ext_ref, act_ref)

    def finish(k, total):
        m = twice(mask_ref[0 : NX * NY, :])
        rows = NX * NY
        for i in range(STEP):
            sum_ref[k + i] = (field_ref[k + i].astype(F32) + m * total[i * rows : (i + 1) * rows]).astype(BF)

    each_step(field_ref.shape[0], fill, lambda k: conv_inner(ext_ref, w_ref, k), finish)
    gather_pairs(sum_ref, turned_ref)
    for i in range(perm_ref.shape[0]):
        out_ref[:, i * PAIR : (i + 1) * PAIR] = dot_nt(turned_ref[i], perm_ref[i]).astype(BF)


def pair_sum_kernel(keep0_ref, got0_ref, keep1_ref, got1_ref, out_ref):
    half = keep0_ref.shape[1]
    out_ref[:, 0:half] = (keep0_ref[...] + got0_ref[...]).astype(BF)
    out_ref[:, half : 2 * half] = (keep1_ref[...] + got1_ref[...]).astype(BF)


def assemble_kernel(cap, run, back_hbm, parts_ref, out_hbm, total_ref, sem):
    buffers, half = total_ref.shape
    senders = parts_ref.shape[0]
    row = lax.broadcasted_iota(jnp.int32, (buffers, senders), 0)
    col = lax.broadcasted_iota(jnp.int32, (buffers, senders), 1)
    same = row % cap == col % cap
    core = (row // run) % 2
    total = jnp.zeros((buffers, half), F32)
    for i in range(2):
        add = jnp.where(same & (core == i), 1.0, 0.0).astype(BF)
        total = total + dot(add, parts_ref[:, i * half : (i + 1) * half])
    total_ref[...] = total.astype(BF)
    width = out_hbm.shape[1] - half
    store = pltpu.make_async_copy(total_ref, out_hbm.at[:, width : width + half], sem)
    store.start()
    store.wait()


def unpack_kernel(factor, core_ref, mine_ref, other_ref, first_ref, second_ref, flat_ref):
    rows, lanes = mine_ref.shape
    for i, out_ref in enumerate((first_ref, second_ref)):
        own = core_ref[0] == i
        for l in range(lanes // LANES):
            at = slice(l * LANES, (l + 1) * LANES)
            value = jnp.where(own, mine_ref[:, at].astype(F32), other_ref[:, at].astype(F32))
            flat_ref[l * rows : (l + 1) * rows, :] = value
        unpack_taps(factor, flat_ref, out_ref)


def unpack_taps(factor, packed_ref, out_ref):
    channels = out_ref.shape[1]
    lane = lax.broadcasted_iota(jnp.int32, (channels, LANES), 1)
    for g in range(7):
        v = []
        for i in range(3):
            start = (3 * g + i) * channels
            v.append(packed_ref[start : start + channels, :] * factor)
        taps = (
            v[0],
            pltpu.roll(jnp.where(lane < 64, v[1], v[0]), 32, 1),
            pltpu.roll(jnp.where(lane < 32, v[2], v[1]), 64, 1),
            pltpu.roll(v[2], 96, 1),
        )
        for u in range(4):
            if 4 * g + u < 27:
                out_ref[4 * g + u] = taps[u][:, 0:channels]


RX = ("cx", "core")
ALL = ("cx", "core", "ry")
SAME_CORE = ("cx", "ry")


def size_of(axes):
    return int(np.prod([lax.axis_size(a) for a in ((axes,) if isinstance(axes, str) else axes)]))


def share(parts, axes):
    return lax.all_to_all(parts, axes, split_axis=0, concat_axis=0, tiled=True)


def neighbours(axes, upper, lower):
    count = size_of(axes)
    ahead = [(i, i + 1) for i in range(count - 1)]
    behind = [(t, s) for s, t in ahead]
    return lax.ppermute(upper, axes, ahead), lax.ppermute(lower, axes, behind)


def swap_cores(value):
    count = size_of(RX)
    return lax.ppermute(value, RX, [(i, i ^ 1) for i in range(count)])


def message_rows():
    cells = []
    for ys in ((0, 1), (NY - 2, NY - 1)):
        for y in ys:
            cells += [(x, y) for x in range(-2, NX + 2)]
        cells += [None] * (MSG - 2 * (NX + 4))
    return cells


def exchange(field, pick):
    pairs = field.shape[0]
    xlo, xhi = neighbours(RX, field[:, (NX - 2) * NY :, :], field[:, : 2 * NY, :])
    message = jax.ShapeDtypeStruct((pairs, MSG, PAIR), BF)
    low, high = call(message_kernel, (message, message), 5e8, 3e6)(field, xlo, xhi, pick)
    ylo, yhi = neighbours("ry", high, low)
    return xlo, xhi, ylo, yhi, low, high


def mask_cells():
    cells = [(x, y) for x in range(NX) for y in range(NY)]
    cells += [(x, y) for x in (-2, -1) for y in range(NY)]
    cells += [(x, y) for x in (NX, NX + 1) for y in range(NY)]
    for ys in ((-2, -1), (NY, NY + 1), (0, 1), (NY - 2, NY - 1)):
        for y in ys:
            cells += [(x, y) for x in range(-2, NX + 2)]
        cells += [None] * (MSG - 2 * (NX + 4))
    for y in (-1, NY):
        cells += [(x, y) for x in range(-1, NX + 1)]
        cells += [None] * (EDGE - NX - 2)
    return cells


def on_device(column_features, column_route, cotangent, first_weight, second_weight):
    count_x = size_of(RX)
    count_y = size_of("ry")
    count_all = count_x * count_y
    shard_rows, row_width = column_features.shape
    channels = first_weight.shape[1]
    depth = row_width // channels
    slots = NX * NY
    pairs = depth // 2
    chunks = channels // GROUP
    cap = 2 * shard_rows // count_all
    buffers = count_all * cap
    me_x = lax.axis_index(RX)
    me_y = lax.axis_index("ry")
    core = lax.axis_index("core").astype(jnp.int32).reshape(1)
    conv_flops = 2 * slots * pairs * 36 * LANES * PAIR

    smem = pl.BlockSpec(memory_space=pltpu.SMEM)
    vmem = pl.BlockSpec(memory_space=pltpu.VMEM)
    hbm = pl.BlockSpec(memory_space=pltpu.HBM)
    shape = jax.ShapeDtypeStruct
    field_shape = shape((pairs, slots, PAIR), BF)
    wide_shape = shape((pairs, OUT_ROWS, PAIR), BF)
    ext = pltpu.VMEM((3, pairs + 1, NX + 4, NY, PAIR), BF)
    edge = pltpu.VMEM((3, 3, pairs + 1, 2 * EDGE, PAIR), BF)
    turned = pltpu.VMEM((chunks, slots, PAIR), F32)
    turned_low = pltpu.VMEM((chunks, slots, PAIR), BF)
    sums = pltpu.VMEM((pairs, slots, PAIR), BF)

    perm = jnp.asarray(permutation(channels, depth), BF)
    pick_np = np.zeros((2 * MSG, (NX + 4) * NY), np.float32)
    for r, cell in enumerate(message_rows()):
        if cell is not None:
            pick_np[r, (cell[0] + 2) * NY + cell[1]] = 1.0
    pick = jnp.asarray(pick_np, BF)

    route_row = column_route.reshape(1, shard_rows)
    told_width = row_width + LANES
    outgoing = call(
        functools.partial(send_kernel, cap, slots), shape((buffers, told_width), BF),
        2 * buffers * shard_rows * row_width, 3 * shard_rows * row_width * 2,
        (pltpu.VMEM((shard_rows, row_width), BF), pltpu.SemaphoreType.DMA), in_specs=[vmem, hbm],
    )(route_row, column_features)
    incoming = share(outgoing.reshape(count_all, cap, told_width), ALL).reshape(buffers, told_width)

    cells = mask_cells()
    steps = np.asarray([(0, 0) if c is None else (c[0] // NX, c[1] // NY) for c in cells], np.int32)
    local = np.asarray([-1 if c is None else (c[0] % NX) * NY + c[1] % NY for c in cells], np.int32)
    to_x = me_x + steps[:, 0]
    to_y = me_y + steps[:, 1]
    inside = (to_x >= 0) & (to_x < count_x) & (to_y >= 0) & (to_y < count_y) & (local >= 0)
    codes = jnp.where(inside, (to_x * count_y + to_y) * slots + local, -1).astype(F32)[:, None]
    me = (me_x * count_y + me_y).astype(jnp.int32).reshape(1)

    cot = call(
        to_pairs_kernel, field_shape, 1e9, 3e6, (turned,),
    )(cotangent.reshape(slots, row_width), perm)
    cot_halo = exchange(cot, pick)

    field, take = call(
        functools.partial(place_kernel, cap, slots), (field_shape, shape((buffers, slots), BF)), 1e9, 3e6,
        (turned, pltpu.VMEM(perm.shape, BF), pltpu.SemaphoreType.DMA), in_specs=[smem, vmem, hbm],
    )(me, incoming, perm)
    field_halo = exchange(field, pick)

    mask = call(
        functools.partial(mask_kernel, cap, slots), shape((M_ROWS, LANES), F32), 1e8, 1e6,
        (pltpu.VMEM((count_all, LANES), F32),),
    )(incoming, codes)
    band = pltpu.VMEM((36 * LANES, PAIR), BF)
    ext_near = pltpu.VMEM((3, pairs + 1, NX + 2, NY, PAIR), BF)
    turned_shape = shape((channels, depth * slots), BF)
    act_grad, outer, outer_turned = call(
        outer_kernel, (shape((pairs, OUT_ROWS, PAIR), F32), field_shape, turned_shape),
        1.3 * conv_flops, 7e6, (ext, edge, band), ROOM_WIDE,
    )(cot, *cot_halo, mask, second_weight)

    packed_rows = -(-21 * channels // buffers) * buffers
    run = count_y * cap
    grad_lanes = 2 * packed_rows // buffers * LANES
    half_shape = shape((buffers // 2, grad_lanes // 2), F32)
    corr_scratch = (
        pltpu.VMEM((28, channels, LANES), F32), pltpu.VMEM((packed_rows, LANES), F32),
    )
    act_shape = shape(ext_near.shape, BF)
    act, hg, act_wide, keep0, give0 = call(
        functools.partial(hidden_kernel, channels, run), (wide_shape, wide_shape, act_shape, half_shape, half_shape),
        2.3 * conv_flops, 9e6, (ext, edge, band, pltpu.VMEM(turned_shape.shape, BF)) + corr_scratch, ROOM_WIDE, in_specs=[smem] + [vmem] * 10,
    )(core, field, *field_halo, mask, first_weight, act_grad)
    got0 = swap_cores(give0)
    keep1, give1 = call(
        functools.partial(corr_kernel, channels, run), (half_shape, half_shape), conv_flops, 5e6,
        corr_scratch, ROOM_CORR, in_specs=[smem, vmem, vmem],
    )(core, act_wide, outer_turned)
    sent = call(
        pair_sum_kernel, shape((buffers // 2, grad_lanes), BF), 1e6, 2e6,
    )(keep0, got0, keep1, swap_cores(give1))
    parts = share(sent.reshape(count_all // 2, cap, grad_lanes), SAME_CORE).reshape(buffers // 2, grad_lanes)

    hg, sent = lax.optimization_barrier((hg, sent))
    back_width = row_width + grad_lanes // 2
    back = call(
        grid_grad_kernel, shape((buffers, back_width), BF), 1.2 * conv_flops, 6e6,
        (ext_near, sums, turned_low, band), ROOM_NEAR,
    )(hg, first_weight, outer, perm, take)
    mixed = call(
        functools.partial(assemble_kernel, cap, run), shape((buffers, back_width), BF), 2e8, 3e6,
        (pltpu.VMEM((buffers, grad_lanes // 2), BF), pltpu.SemaphoreType.DMA),
        in_specs=[hbm, vmem], out_specs=hbm, input_output_aliases={0: 0},
    )(back, parts)
    returned = share(mixed.reshape(count_all, cap, back_width), ALL).reshape(buffers, back_width)

    act, mixed = lax.optimization_barrier((act, mixed))
    block_output = call(
        block_kernel, shape((slots, row_width), BF), 1.2 * conv_flops, 8e6,
        (ext_near, sums, turned_low, band), ROOM_NEAR,
    )(act, mask, second_weight, field, perm)

    returned, block_output = lax.optimization_barrier((returned, block_output))
    mine = returned[:, row_width:]
    feature_grads = call(
        functools.partial(collect_kernel, cap, slots), shape((shard_rows, row_width), BF),
        2 * buffers * shard_rows * row_width, 3 * shard_rows * row_width * 2,
    )(route_row, returned)

    factor = float(1.0 / np.sqrt(np.float32(count_all * shard_rows * depth)))
    grads = shape(first_weight.shape, F32)
    first_grad, second_grad = call(
        functools.partial(unpack_kernel, factor), (grads, grads), 1e6, 4e6,
        (pltpu.VMEM((packed_rows, LANES), F32),), in_specs=[smem, vmem, vmem],
    )(core, mine, swap_cores(mine))
    return (block_output.reshape(cotangent.shape), feature_grads, first_grad, second_grad)


def solution(mesh):
    count_x = mesh.shape["rx"]
    fine = jax.sharding.Mesh(mesh.devices.reshape(count_x // 2, 2, mesh.shape["ry"]), ALL)
    in_specs = (P(ALL, None), P(ALL), P(RX, "ry", None), P(), P())
    out_specs = (P(RX, "ry", None), P(ALL, None), P(), P())
    return jax.shard_map(
        on_device, mesh=fine, in_specs=in_specs, out_specs=out_specs, check_vma=False
    )
```

```python
import functools

import jax
import jax.numpy as jnp
import numpy as np
from jax import lax
from jax.experimental import pallas as pl
from jax.experimental.pallas import tpu as pltpu
from jax.sharding import PartitionSpec as P

LANES = 128
PAIR = 256
MIB = 1024 * 1024
ROOM_MAIN, ROOM_WIDE, ROOM_NEAR, ROOM_SMALL = 30, 18, 16, 5
BF = jnp.bfloat16
F32 = jnp.float32


def call(body, out_shape, flops, moved, scratch=(), room=ROOM_SMALL, **extra):
    return pl.pallas_call(
        body,
        out_shape=out_shape,
        scratch_shapes=list(scratch),
        compiler_params=pltpu.CompilerParams(vmem_limit_bytes=room * MIB),
        cost_estimate=pl.CostEstimate(flops=int(flops), bytes_accessed=int(moved), transcendentals=0),
        **extra,
    )


def dot(left, right):
    return jnp.dot(left, right, preferred_element_type=F32)


def dot_nt(left, right):
    return lax.dot_general(left, right, (((1,), (1,)), ((), ())), preferred_element_type=F32)


def as_column(row):
    return jnp.broadcast_to(row, (row.shape[1], row.shape[1])).T


def send_kernel(cap, slots, row_ref, feat_hbm, out_ref, feat_ref, sem):
    fetch = pltpu.make_async_copy(feat_hbm, feat_ref, sem)
    fetch.start()
    rows, width = feat_ref.shape
    buffers = out_ref.shape[0]
    owner_row = (row_ref[...] // slots).astype(F32)
    owner_col = as_column(owner_row)
    first = lax.broadcasted_iota(jnp.int32, (rows, rows), 0)
    second = lax.broadcasted_iota(jnp.int32, (rows, rows), 1)
    same = jnp.where((owner_col == owner_row) & (first < second), 1.0, 0.0)
    rank = jnp.sum(same, axis=0, keepdims=True)
    pos = owner_row * cap + rank
    place = lax.broadcasted_iota(jnp.int32, (buffers, rows), 0)
    hot = jnp.where(place.astype(F32) == pos, 1.0, 0.0).astype(BF)
    slot_row = (row_ref[...] % slots).astype(F32)
    kind = place % cap
    told = jnp.where(kind == 0, owner_row, jnp.where(kind == 1, slot_row, 0.0))
    out_ref[:, width : width + rows] = told.astype(BF)
    fetch.wait()
    out_ref[:, 0:width] = dot(hot, feat_ref[...]).astype(BF)


def collect_kernel(cap, slots, row_ref, back_ref, out_ref):
    rows, width = out_ref.shape
    owner_row = (row_ref[...] // slots).astype(F32)
    owner_col = as_column(owner_row)
    first = lax.broadcasted_iota(jnp.int32, (rows, rows), 0)
    second = lax.broadcasted_iota(jnp.int32, (rows, rows), 1)
    same = jnp.where((owner_col == owner_row) & (second < first), 1.0, 0.0)
    pos = owner_col[:, 0:1] * cap + jnp.sum(same, axis=1, keepdims=True)
    place = lax.broadcasted_iota(jnp.int32, (rows, back_ref.shape[0]), 1).astype(F32)
    hot = jnp.where(place == pos, 1.0, 0.0).astype(BF)
    out_ref[...] = dot(hot, back_ref[:, 0:width]).astype(BF)


def told_rows(cap, in_ref, which):
    buffers, width = in_ref.shape
    count = buffers // cap
    source = lax.broadcasted_iota(jnp.int32, (count, buffers), 0)
    place = lax.broadcasted_iota(jnp.int32, (count, buffers), 1)
    pick = jnp.where(place == source * cap + which, 1.0, 0.0).astype(BF)
    return dot(pick, in_ref[:, width - LANES : width])


def mask_kernel(cap, slots, in_ref, codes_ref, mask_ref, route_ref):
    total = mask_ref.shape[0]
    route_ref[...] = told_rows(cap, in_ref, 0) * slots + told_rows(cap, in_ref, 1)
    codes = jnp.broadcast_to(codes_ref[...], (total, LANES))
    hits = jnp.zeros((total, LANES), F32)
    for s in range(route_ref.shape[0]):
        hits = hits + jnp.where(codes == route_ref[s : s + 1, :], 1.0, 0.0)
    mask_ref[...] = jnp.broadcast_to(jnp.sum(hits, axis=1, keepdims=True), (total, LANES))


def slot_table(cap, slots, me, in_ref):
    buffers = in_ref.shape[0]
    count = buffers // cap
    mine_f = jnp.where(told_rows(cap, in_ref, 0) == me.astype(F32), 1.0, 0.0)
    slot_f = told_rows(cap, in_ref, 1)
    first = lax.broadcasted_iota(jnp.int32, (LANES, LANES), 0)
    second = lax.broadcasted_iota(jnp.int32, (LANES, LANES), 1)
    tri = jnp.where(first < second, 1.0, 0.0).astype(BF)
    rank = dot(mine_f.astype(BF), tri)
    lane = lax.broadcasted_iota(jnp.int32, (count, LANES), 1)
    held = jnp.zeros((count, LANES), F32)
    for j in range(cap):
        here = jnp.where(rank == j, mine_f, 0.0)
        number = jnp.sum(here, axis=1, keepdims=True)
        value = jnp.sum(here * slot_f, axis=1, keepdims=True)
        value = value + (1.0 - number) * slots
        held = jnp.where(lane == j, value, held)
    place = lax.broadcasted_iota(jnp.int32, (buffers, count), 0)
    source = lax.broadcasted_iota(jnp.int32, (buffers, count), 1)
    spread = jnp.where(place // cap == source, 1.0, 0.0).astype(BF)
    wide = dot(spread, held.astype(BF))
    place = lax.broadcasted_iota(jnp.int32, (buffers, LANES), 0)
    lane = lax.broadcasted_iota(jnp.int32, (buffers, LANES), 1)
    slot_col = jnp.sum(jnp.where(place % cap == lane, wide, 0.0), axis=1, keepdims=True)
    slot_id = lax.broadcasted_iota(jnp.int32, (buffers, slots), 1).astype(F32)
    return jnp.where(slot_col == slot_id, 1.0, 0.0)


GROUP = 16
FOLD = LANES // GROUP


def permutation(channels, depth):
    perm = np.zeros((channels // GROUP, PAIR, PAIR), np.float32)
    for i in range(channels // GROUP):
        for j in range(GROUP):
            for z in range(depth):
                perm[i, depth * j + z, LANES * (z // FOLD) + GROUP * ((z + i) % FOLD) + j] = 1.0
    return perm


def lane_group(rows):
    return lax.broadcasted_iota(jnp.int32, (rows, LANES), 1) // GROUP


def spread_pairs(turned_ref, out_ref):
    chunks, rows, _ = turned_ref.shape
    step = 32
    group = lane_group(step)

    def body(t, carry):
        at = pl.ds(pl.multiple_of(t * step, step), step)
        for half in range(2):
            lanes = slice(half * LANES, (half + 1) * LANES)
            parts = [turned_ref[i, at, lanes] for i in range(chunks)]
            parts = parts + [jnp.zeros((step, LANES), F32)] * (FOLD - chunks)
            for bit in (1, 2, 4):
                odd = (group & bit) != 0
                parts = [jnp.where(odd, parts[(i + bit) % FOLD], parts[i]) for i in range(FOLD)]
            for g in range(FOLD):
                value = parts[(-g) % FOLD]
                if g:
                    value = pltpu.roll(value, LANES - GROUP * g, 1)
                z = half * FOLD + g
                out_ref[z // 2, at, (z % 2) * LANES : (z % 2 + 1) * LANES] = value.astype(BF)
        return carry

    lax.fori_loop(0, rows // step, body, 0)


def gather_pairs(in_ref, turned_ref):
    chunks, rows, _ = turned_ref.shape
    step = 32
    group = lane_group(step)

    def body(t, carry):
        at = pl.ds(pl.multiple_of(t * step, step), step)
        for half in range(2):
            turned = []
            for g in range(FOLD):
                z = half * FOLD + g
                value = in_ref[z // 2, at, (z % 2) * LANES : (z % 2 + 1) * LANES].astype(F32)
                turned.append(pltpu.roll(value, GROUP * g, 1) if g else value)
            parts = [turned[(-i) % FOLD] for i in range(FOLD)]
            for bit in (1, 2, 4):
                odd = (group & bit) != 0
                parts = [jnp.where(odd, parts[(i - bit) % FOLD], parts[i]) for i in range(FOLD)]
            for i in range(chunks):
                turned_ref[i, at, half * LANES : (half + 1) * LANES] = parts[i].astype(BF)
        return carry

    lax.fori_loop(0, rows // step, body, 0)


def to_pairs_kernel(rows_ref, perm_ref, out_ref, turned_ref):
    for i in range(perm_ref.shape[0]):
        turned_ref[i] = dot(rows_ref[:, i * PAIR : (i + 1) * PAIR], perm_ref[i])
    spread_pairs(turned_ref, out_ref)


def place_kernel(cap, slots, me_ref, rows_ref, perm_hbm, out_ref, take_ref, turned_ref, perm_ref, sem):
    fetch = pltpu.make_async_copy(perm_hbm, perm_ref, sem)
    fetch.start()
    take = slot_table(cap, slots, me_ref[0], rows_ref)
    take_ref[...] = take.astype(BF)
    put = take.T.astype(BF)
    fetch.wait()
    for i in range(perm_ref.shape[0]):
        held = dot(put, rows_ref[:, i * PAIR : (i + 1) * PAIR]).astype(BF)
        turned_ref[i] = dot(held, perm_ref[i])
    spread_pairs(turned_ref, out_ref)


def message_kernel(f_ref, xlo_ref, xhi_ref, pick_ref, low_ref, high_ref):
    pick = pick_ref[...]
    half = low_ref.shape[1]
    for k in range(f_ref.shape[0]):
        rows = jnp.concatenate([xlo_ref[k], f_ref[k], xhi_ref[k]], axis=0)
        sent = dot(pick, rows).astype(BF)
        low_ref[k] = sent[0:half]
        high_ref[k] = sent[half : 2 * half]


def build_band(band_ref, raw_ref, backward):
    channels = raw_ref.shape[1]
    band_ref[...] = jnp.zeros_like(band_ref)
    for tap in range(27):
        value = raw_ref[26 - tap] if backward else raw_ref[tap].T
        for zo in range(2):
            row = ((tap // 3) * 4 + zo + tap % 3) * LANES
            band_ref[row : row + channels, zo * LANES : zo * LANES + channels] = value


NX = 16
NY = 16
OUT_MAIN = (NX + 2) * NY
EDGE = 24
OUT_ROWS = OUT_MAIN + 2 * EDGE
MSG = 48
M_XLO = NX * NY
M_XHI = M_XLO + 2 * NY
M_YLO = M_XHI + 2 * NY
M_YHI = M_YLO + MSG
M_LOW = M_YHI + MSG
M_HIGH = M_LOW + MSG
M_EDGE = M_HIGH + MSG
M_ROWS = M_EDGE + 2 * EDGE


def twice(value):
    return jnp.concatenate([value, value], axis=1)


def put_pair(ref, lead, k, tail, value):
    value = value.astype(BF)
    ref[lead + (k,) + tail + (slice(LANES, PAIR),)] = value[:, 0:LANES]
    ref[lead + (k + 1,) + tail + (slice(0, LANES),)] = value[:, LANES:PAIR]


def clear_ends(ref, lead):
    last = ref.shape[len(lead)] - 1
    dims = ref.shape[len(lead) + 1 : -1]
    ref[lead + (0,) + (slice(None),) * len(dims) + (slice(0, LANES),)] = jnp.zeros(dims + (LANES,), BF)
    ref[lead + (last,) + (slice(None),) * len(dims) + (slice(LANES, PAIR),)] = jnp.zeros(dims + (LANES,), BF)


def put_shifted(ext_ref, k, xp, mid, before, after, row):
    ny = mid.shape[0]
    up = jnp.where(row == 0, before, pltpu.roll(mid, 1, 0))
    down = jnp.where(row == ny - 1, after, pltpu.roll(mid, ny - 1, 0))
    for b, value in enumerate((up, mid, down)):
        put_pair(ext_ref, (b,), k, (xp, slice(None)), value)


def widen_two(ext_ref, edge_ref, f_ref, xlo_ref, xhi_ref, ylo_ref, yhi_ref, low_ref, high_ref, mask_ref=None):
    for b in range(3):
        clear_ends(ext_ref, (b,))
        for a in range(3):
            clear_ends(edge_ref, (a, b))
    row = lax.broadcasted_iota(jnp.int32, (NY, PAIR), 0)

    def read(ref, k, start, size, mask_start):
        value = ref[k, start : start + size, :].astype(F32)
        if mask_ref is None:
            return value
        return value * twice(mask_ref[mask_start + start : mask_start + start + size, :])

    def fill(k):
        ylo = read(ylo_ref, k, 0, MSG, M_YLO)
        yhi = read(yhi_ref, k, 0, MSG, M_YHI)
        low = read(low_ref, k, 0, MSG, M_LOW)
        high = read(high_ref, k, 0, MSG, M_HIGH)
        wide = NX + 4
        for xp in range(wide):
            if xp < 2:
                mid = read(xlo_ref, k, xp * NY, NY, M_XLO)
            elif xp >= NX + 2:
                mid = read(xhi_ref, k, (xp - NX - 2) * NY, NY, M_XHI)
            else:
                mid = read(f_ref, k, (xp - 2) * NY, NY, 0)
            put_shifted(ext_ref, k, xp, mid, ylo[wide + xp : wide + xp + 1, :], yhi[xp : xp + 1, :], row)
        first = ((ylo, 0), (ylo, wide), (low, 0))
        second = ((high, wide), (yhi, 0), (yhi, wide))
        for a in range(3):
            for b in range(3):
                sides = []
                for value, start in (first[b], second[b]):
                    turn = start + a
                    if turn:
                        value = pltpu.roll(value, MSG - turn, 0)
                    sides.append(value[0:EDGE])
                put_pair(edge_ref, (a, b), k, (slice(None),), jnp.concatenate(sides, axis=0))

    return fill


def widen_one(ext_ref, rows_ref):
    for b in range(3):
        clear_ends(ext_ref, (b,))
    row = lax.broadcasted_iota(jnp.int32, (NY, PAIR), 0)

    return lambda k: fill_rows(ext_ref, k, rows_ref[k].astype(F32), row)


def fill_rows(ext_ref, k, value, row):
    edges = value[OUT_MAIN:OUT_ROWS]
    for xp in range(NX + 2):
        mid = value[xp * NY : (xp + 1) * NY]
        put_shifted(ext_ref, k, xp, mid, edges[xp : xp + 1, :], edges[EDGE + xp : EDGE + xp + 1, :], row)


STEP = 2


def conv_wide(ext_ref, edge_ref, w_ref, k):
    pieces = []
    for a in range(3):
        for b in range(3):
            for j in range(2):
                parts = []
                for i in range(STEP):
                    parts.append(ext_ref[b, k + i + j, a : a + NX + 2].reshape(OUT_MAIN, PAIR))
                    parts.append(edge_ref[a, b, k + i + j])
                pieces.append(jnp.concatenate(parts, axis=0))
    return dot(jnp.concatenate(pieces, axis=1), w_ref[...])


def conv_inner(ext_ref, w_ref, k):
    pieces = []
    for a in range(3):
        for b in range(3):
            for j in range(2):
                pieces.append(ext_ref[b, k + j : k + j + STEP, a : a + NX].reshape(STEP * NX * NY, PAIR))
    return dot(jnp.concatenate(pieces, axis=1), w_ref[...])


def each_step(pairs, fill, conv, finish):
    for k in range(STEP + 1):
        fill(k)
    last = None
    for k in range(0, pairs, STEP):
        for ahead in range(k + STEP + 1, min(k + 2 * STEP + 1, pairs)):
            fill(ahead)
        total = conv(k)
        if last is not None:
            finish(*last)
        last = (k, total)
    finish(*last)


def out_mask(mask_ref):
    return twice(jnp.concatenate([
        mask_ref[M_XLO + NY : M_XLO + 2 * NY, :], mask_ref[0 : NX * NY, :],
        mask_ref[M_XHI : M_XHI + NY, :], mask_ref[M_EDGE:M_ROWS, :],
    ], axis=0))


def outer_kernel(f_ref, xlo_ref, xhi_ref, ylo_ref, yhi_ref, low_ref, high_ref, mask_ref, raw_ref,
                 out_ref, outer_ref, gt_ref, ext_ref, edge_ref, w_ref):
    build_band(w_ref, raw_ref, True)
    fill = widen_two(ext_ref, edge_ref, f_ref, xlo_ref, xhi_ref, ylo_ref, yhi_ref, low_ref, high_ref, mask_ref)

    def finish(k, total):
        for i in range(STEP):
            out_ref[k + i] = total[i * OUT_ROWS : (i + 1) * OUT_ROWS]
            outer = (f_ref[k + i].astype(F32) * twice(mask_ref[0 : NX * NY, :])).astype(BF)
            outer_ref[k + i] = outer
            turn(gt_ref, k + i, outer)

    each_step(f_ref.shape[0], fill, lambda k: conv_wide(ext_ref, edge_ref, w_ref, k), finish)


def correlate(gt_ref, ext_ref, first_x, taps_ref):
    depth = 2 * (ext_ref.shape[1] - 1)
    for b in range(3):
        rows = []
        for z in range(depth):
            parts = []
            for a in range(3):
                for c in range(3):
                    half = (z + c) % 2 * LANES
                    part = ext_ref[b, (z + c) // 2, first_x + a : first_x + a + NX, :, half : half + LANES]
                    parts.append(part.reshape(NX * NY, LANES))
            rows.append(jnp.concatenate(parts, axis=1))
        sums = dot(gt_ref[...], jnp.concatenate(rows, axis=0))
        for a in range(3):
            for c in range(3):
                taps_ref[9 * a + 3 * b + c] = sums[:, (3 * a + c) * LANES : (3 * a + c + 1) * LANES]


def pack_taps(taps_ref, packed_ref, channels):
    lane = lax.broadcasted_iota(jnp.int32, (channels, LANES), 1)
    for g in range(7):
        t1 = pltpu.roll(taps_ref[4 * g + 1], 96, 1)
        t2 = pltpu.roll(taps_ref[4 * g + 2], 64, 1)
        t3 = pltpu.roll(taps_ref[4 * g + 3], 32, 1)
        blocks = (
            jnp.where(lane < 96, taps_ref[4 * g], t1),
            jnp.where(lane < 64, t1, t2),
            jnp.where(lane < 32, t2, t3),
        )
        for i, value in enumerate(blocks):
            start = (3 * g + i) * channels
            packed_ref[start : start + channels, :] = value
    rest = packed_ref.shape[0] - 21 * channels
    if rest:
        packed_ref[21 * channels :, :] = jnp.zeros((rest, LANES), F32)


def hidden_kernel(channels, run, core_ref, f_ref, xlo_ref, xhi_ref, ylo_ref, yhi_ref, low_ref, high_ref, mask_ref,
                  raw_ref, grad_ref, outer_gt_ref, act_ref, hg_ref, keep_ref, give_ref,
                  ext_ref, edge_ref, w_ref, gt_ref, wide_ref, taps_ref, packed_ref, taps2_ref, packed2_ref):
    build_band(w_ref, raw_ref, False)
    fill = widen_two(ext_ref, edge_ref, f_ref, xlo_ref, xhi_ref, ylo_ref, yhi_ref, low_ref, high_ref)

    for b in range(3):
        clear_ends(wide_ref, (b,))
    row = lax.broadcasted_iota(jnp.int32, (NY, PAIR), 0)

    def finish(k, total):
        m = out_mask(mask_ref)
        for i in range(STEP):
            hidden = m * total[i * OUT_ROWS : (i + 1) * OUT_ROWS]
            sigma = jax.nn.sigmoid(hidden)
            act = (hidden * sigma).astype(BF)
            act_ref[k + i] = act
            fill_rows(wide_ref, k + i, act.astype(F32), row)
            hg = (m * grad_ref[k + i] * sigma * (1.0 + hidden * (1.0 - sigma))).astype(BF)
            hg_ref[k + i] = hg
            turn(gt_ref, k + i, hg[NY : NY + NX * NY])

    each_step(f_ref.shape[0], fill, lambda k: conv_wide(ext_ref, edge_ref, w_ref, k), finish)
    correlate(gt_ref, ext_ref, 1, taps_ref)
    hand_out(channels, run, core_ref, taps_ref, packed_ref, keep_ref, give_ref, 0)
    correlate(outer_gt_ref, wide_ref, 0, taps2_ref)
    hand_out(channels, run, core_ref, taps2_ref, packed2_ref, keep_ref, give_ref, 1)


def turn(gt_ref, k, value):
    channels = gt_ref.shape[0]
    inner = value.shape[0]
    value = value.T
    for i in range(2):
        z = 2 * k + i
        gt_ref[:, z * inner : (z + 1) * inner] = value[i * LANES : i * LANES + channels]


def hand_out(channels, run, core_ref, taps_ref, packed_ref, keep_ref, give_ref, which):
    runs = keep_ref.shape[0] // run
    block = 2 * runs * run
    taps_ref[27] = jnp.zeros((channels, LANES), F32)
    pack_taps(taps_ref, packed_ref, channels)
    blocks = packed_ref.shape[0] // block
    for l in range(blocks):
        lanes = slice((which * blocks + l) * LANES, (which * blocks + l + 1) * LANES)
        for x in range(runs):
            base = l * block + 2 * x * run
            rows = slice(x * run, (x + 1) * run)
            mine = pl.multiple_of(base + core_ref[0] * run, run)
            other = pl.multiple_of(base + (1 - core_ref[0]) * run, run)
            keep_ref[rows, lanes] = packed_ref[pl.ds(mine, run), :]
            give_ref[rows, lanes] = packed_ref[pl.ds(other, run), :]


def grid_grad_kernel(hg_ref, raw_ref, outer_ref, perm_ref, take_ref, out_ref, ext_ref, sum_ref, turned_ref, w_ref):
    build_band(w_ref, raw_ref, True)
    fill = widen_one(ext_ref, hg_ref)

    def finish(k, total):
        rows = NX * NY
        for i in range(STEP):
            sum_ref[k + i] = (outer_ref[k + i].astype(F32) + total[i * rows : (i + 1) * rows]).astype(BF)

    each_step(outer_ref.shape[0], fill, lambda k: conv_inner(ext_ref, w_ref, k), finish)
    gather_pairs(sum_ref, turned_ref)
    take = take_ref[...]
    for i in range(perm_ref.shape[0]):
        rows = dot_nt(turned_ref[i], perm_ref[i]).astype(BF)
        out_ref[:, i * PAIR : (i + 1) * PAIR] = dot(take, rows).astype(BF)


def block_kernel(act_ref, mask_ref, raw_ref, field_ref, perm_ref, out_ref, ext_ref, sum_ref, turned_ref, w_ref):
    build_band(w_ref, raw_ref, False)
    fill = widen_one(ext_ref, act_ref)

    def finish(k, total):
        m = twice(mask_ref[0 : NX * NY, :])
        rows = NX * NY
        for i in range(STEP):
            sum_ref[k + i] = (field_ref[k + i].astype(F32) + m * total[i * rows : (i + 1) * rows]).astype(BF)

    each_step(field_ref.shape[0], fill, lambda k: conv_inner(ext_ref, w_ref, k), finish)
    gather_pairs(sum_ref, turned_ref)
    for i in range(perm_ref.shape[0]):
        out_ref[:, i * PAIR : (i + 1) * PAIR] = dot_nt(turned_ref[i], perm_ref[i]).astype(BF)


def pair_sum_kernel(keep_ref, got_ref, out_ref):
    out_ref[...] = (keep_ref[...] + got_ref[...]).astype(BF)


def assemble_kernel(cap, run, back_hbm, parts_ref, out_hbm, total_ref, sem):
    buffers, half = total_ref.shape
    senders = parts_ref.shape[0]
    row = lax.broadcasted_iota(jnp.int32, (buffers, senders), 0)
    col = lax.broadcasted_iota(jnp.int32, (buffers, senders), 1)
    same = row % cap == col % cap
    core = (row // run) % 2
    total = jnp.zeros((buffers, half), F32)
    for i in range(2):
        add = jnp.where(same & (core == i), 1.0, 0.0).astype(BF)
        total = total + dot(add, parts_ref[:, i * half : (i + 1) * half])
    total_ref[...] = total.astype(BF)
    width = out_hbm.shape[1] - half
    store = pltpu.make_async_copy(total_ref, out_hbm.at[:, width : width + half], sem)
    store.start()
    store.wait()


def unpack_kernel(factor, core_ref, mine_ref, other_ref, first_ref, second_ref, flat_ref):
    rows, lanes = mine_ref.shape
    for i, out_ref in enumerate((first_ref, second_ref)):
        own = core_ref[0] == i
        for l in range(lanes // LANES):
            at = slice(l * LANES, (l + 1) * LANES)
            value = jnp.where(own, mine_ref[:, at].astype(F32), other_ref[:, at].astype(F32))
            flat_ref[l * rows : (l + 1) * rows, :] = value
        unpack_taps(factor, flat_ref, out_ref)


def unpack_taps(factor, packed_ref, out_ref):
    channels = out_ref.shape[1]
    lane = lax.broadcasted_iota(jnp.int32, (channels, LANES), 1)
    for g in range(7):
        v = []
        for i in range(3):
            start = (3 * g + i) * channels
            v.append(packed_ref[start : start + channels, :] * factor)
        taps = (
            v[0],
            pltpu.roll(jnp.where(lane < 64, v[1], v[0]), 32, 1),
            pltpu.roll(jnp.where(lane < 32, v[2], v[1]), 64, 1),
            pltpu.roll(v[2], 96, 1),
        )
        for u in range(4):
            if 4 * g + u < 27:
                out_ref[4 * g + u] = taps[u][:, 0:channels]


RX = ("cx", "core")
ALL = ("cx", "core", "ry")
SAME_CORE = ("cx", "ry")


def size_of(axes):
    return int(np.prod([lax.axis_size(a) for a in ((axes,) if isinstance(axes, str) else axes)]))


def share(parts, axes):
    return lax.all_to_all(parts, axes, split_axis=0, concat_axis=0, tiled=True)


def neighbours(axes, upper, lower):
    count = size_of(axes)
    ahead = [(i, i + 1) for i in range(count - 1)]
    behind = [(t, s) for s, t in ahead]
    return lax.ppermute(upper, axes, ahead), lax.ppermute(lower, axes, behind)


def swap_cores(value):
    count = size_of(RX)
    return lax.ppermute(value, RX, [(i, i ^ 1) for i in range(count)])


def message_rows():
    cells = []
    for ys in ((0, 1), (NY - 2, NY - 1)):
        for y in ys:
            cells += [(x, y) for x in range(-2, NX + 2)]
        cells += [None] * (MSG - 2 * (NX + 4))
    return cells


def exchange(field, pick):
    pairs = field.shape[0]
    xlo, xhi = neighbours(RX, field[:, (NX - 2) * NY :, :], field[:, : 2 * NY, :])
    message = jax.ShapeDtypeStruct((pairs, MSG, PAIR), BF)
    low, high = call(message_kernel, (message, message), 5e8, 3e6)(field, xlo, xhi, pick)
    ylo, yhi = neighbours("ry", high, low)
    return xlo, xhi, ylo, yhi, low, high


def mask_cells():
    cells = [(x, y) for x in range(NX) for y in range(NY)]
    cells += [(x, y) for x in (-2, -1) for y in range(NY)]
    cells += [(x, y) for x in (NX, NX + 1) for y in range(NY)]
    for ys in ((-2, -1), (NY, NY + 1), (0, 1), (NY - 2, NY - 1)):
        for y in ys:
            cells += [(x, y) for x in range(-2, NX + 2)]
        cells += [None] * (MSG - 2 * (NX + 4))
    for y in (-1, NY):
        cells += [(x, y) for x in range(-1, NX + 1)]
        cells += [None] * (EDGE - NX - 2)
    return cells


def on_device(column_features, column_route, cotangent, first_weight, second_weight):
    count_x = size_of(RX)
    count_y = size_of("ry")
    count_all = count_x * count_y
    shard_rows, row_width = column_features.shape
    channels = first_weight.shape[1]
    depth = row_width // channels
    slots = NX * NY
    pairs = depth // 2
    chunks = channels // GROUP
    cap = 2 * shard_rows // count_all
    buffers = count_all * cap
    me_x = lax.axis_index(RX)
    me_y = lax.axis_index("ry")
    core = lax.axis_index("core").astype(jnp.int32).reshape(1)
    conv_flops = 2 * slots * pairs * 36 * LANES * PAIR

    smem = pl.BlockSpec(memory_space=pltpu.SMEM)
    vmem = pl.BlockSpec(memory_space=pltpu.VMEM)
    hbm = pl.BlockSpec(memory_space=pltpu.HBM)
    shape = jax.ShapeDtypeStruct
    field_shape = shape((pairs, slots, PAIR), BF)
    wide_shape = shape((pairs, OUT_ROWS, PAIR), BF)
    ext = pltpu.VMEM((3, pairs + 1, NX + 4, NY, PAIR), BF)
    edge = pltpu.VMEM((3, 3, pairs + 1, 2 * EDGE, PAIR), BF)
    turned = pltpu.VMEM((chunks, slots, PAIR), F32)
    turned_low = pltpu.VMEM((chunks, slots, PAIR), BF)
    sums = pltpu.VMEM((pairs, slots, PAIR), BF)

    perm = jnp.asarray(permutation(channels, depth), BF)
    pick_np = np.zeros((2 * MSG, (NX + 4) * NY), np.float32)
    for r, cell in enumerate(message_rows()):
        if cell is not None:
            pick_np[r, (cell[0] + 2) * NY + cell[1]] = 1.0
    pick = jnp.asarray(pick_np, BF)

    route_row = column_route.reshape(1, shard_rows)
    told_width = row_width + LANES
    outgoing = call(
        functools.partial(send_kernel, cap, slots), shape((buffers, told_width), BF),
        2 * buffers * shard_rows * row_width, 3 * shard_rows * row_width * 2,
        (pltpu.VMEM((shard_rows, row_width), BF), pltpu.SemaphoreType.DMA), in_specs=[vmem, hbm],
    )(route_row, column_features)
    incoming = share(outgoing.reshape(count_all, cap, told_width), ALL).reshape(buffers, told_width)

    cells = mask_cells()
    steps = np.asarray([(0, 0) if c is None else (c[0] // NX, c[1] // NY) for c in cells], np.int32)
    local = np.asarray([-1 if c is None else (c[0] % NX) * NY + c[1] % NY for c in cells], np.int32)
    to_x = me_x + steps[:, 0]
    to_y = me_y + steps[:, 1]
    inside = (to_x >= 0) & (to_x < count_x) & (to_y >= 0) & (to_y < count_y) & (local >= 0)
    codes = jnp.where(inside, (to_x * count_y + to_y) * slots + local, -1).astype(F32)[:, None]
    me = (me_x * count_y + me_y).astype(jnp.int32).reshape(1)

    cot = call(
        to_pairs_kernel, field_shape, 1e9, 3e6, (turned,),
    )(cotangent.reshape(slots, row_width), perm)
    cot_halo = exchange(cot, pick)

    field, take = call(
        functools.partial(place_kernel, cap, slots), (field_shape, shape((buffers, slots), BF)), 1e9, 3e6,
        (turned, pltpu.VMEM(perm.shape, BF), pltpu.SemaphoreType.DMA), in_specs=[smem, vmem, hbm],
    )(me, incoming, perm)
    field_halo = exchange(field, pick)

    mask = call(
        functools.partial(mask_kernel, cap, slots), shape((M_ROWS, LANES), F32), 1e8, 1e6,
        (pltpu.VMEM((count_all, LANES), F32),),
    )(incoming, codes)
    band = pltpu.VMEM((36 * LANES, PAIR), BF)
    ext_near = pltpu.VMEM((3, pairs + 1, NX + 2, NY, PAIR), BF)
    turned_shape = shape((channels, depth * slots), BF)
    act_grad, outer, outer_turned = call(
        outer_kernel, (shape((pairs, OUT_ROWS, PAIR), F32), field_shape, turned_shape),
        1.3 * conv_flops, 7e6, (ext, edge, band), ROOM_WIDE,
    )(cot, *cot_halo, mask, second_weight)

    packed_rows = -(-21 * channels // buffers) * buffers
    run = count_y * cap
    grad_lanes = 2 * packed_rows // buffers * LANES
    half_shape = shape((buffers // 2, grad_lanes), F32)
    corr_scratch = (pltpu.VMEM((28, channels, LANES), F32), pltpu.VMEM((packed_rows, LANES), F32))
    act, hg, keep, give = call(
        functools.partial(hidden_kernel, channels, run), (wide_shape, wide_shape, half_shape, half_shape),
        3.3 * conv_flops, 9e6,
        (ext, edge, band, pltpu.VMEM(turned_shape.shape, BF), ext_near) + 2 * corr_scratch, ROOM_MAIN,
        in_specs=[smem] + [vmem] * 11,
    )(core, field, *field_halo, mask, first_weight, act_grad, outer_turned)
    sent = call(
        pair_sum_kernel, shape((buffers // 2, grad_lanes), BF), 1e6, 2e6,
    )(keep, swap_cores(give))
    parts = share(sent.reshape(count_all // 2, cap, grad_lanes), SAME_CORE).reshape(buffers // 2, grad_lanes)

    hg, sent = lax.optimization_barrier((hg, sent))
    back_width = row_width + grad_lanes // 2
    back = call(
        grid_grad_kernel, shape((buffers, back_width), BF), 1.2 * conv_flops, 6e6,
        (ext_near, sums, turned_low, band), ROOM_NEAR,
    )(hg, first_weight, outer, perm, take)
    mixed = call(
        functools.partial(assemble_kernel, cap, run), shape((buffers, back_width), BF), 2e8, 3e6,
        (pltpu.VMEM((buffers, grad_lanes // 2), BF), pltpu.SemaphoreType.DMA),
        in_specs=[hbm, vmem], out_specs=hbm, input_output_aliases={0: 0},
    )(back, parts)
    returned = share(mixed.reshape(count_all, cap, back_width), ALL).reshape(buffers, back_width)

    act, mixed = lax.optimization_barrier((act, mixed))
    block_output = call(
        block_kernel, shape((slots, row_width), BF), 1.2 * conv_flops, 8e6,
        (ext_near, sums, turned_low, band), ROOM_NEAR,
    )(act, mask, second_weight, field, perm)

    returned, block_output = lax.optimization_barrier((returned, block_output))
    mine = returned[:, row_width:]
    feature_grads = call(
        functools.partial(collect_kernel, cap, slots), shape((shard_rows, row_width), BF),
        2 * buffers * shard_rows * row_width, 3 * shard_rows * row_width * 2,
    )(route_row, returned)

    factor = float(1.0 / np.sqrt(np.float32(count_all * shard_rows * depth)))
    grads = shape(first_weight.shape, F32)
    first_grad, second_grad = call(
        functools.partial(unpack_kernel, factor), (grads, grads), 1e6, 4e6,
        (pltpu.VMEM((packed_rows, LANES), F32),), in_specs=[smem, vmem, vmem],
    )(core, mine, swap_cores(mine))
    return (block_output.reshape(cotangent.shape), feature_grads, first_grad, second_grad)


def solution(mesh):
    count_x = mesh.shape["rx"]
    fine = jax.sharding.Mesh(mesh.devices.reshape(count_x // 2, 2, mesh.shape["ry"]), ALL)
    in_specs = (P(ALL, None), P(ALL), P(RX, "ry", None), P(), P())
    out_specs = (P(RX, "ry", None), P(ALL, None), P(), P())
    return jax.shard_map(
        on_device, mesh=fine, in_specs=in_specs, out_specs=out_specs, check_vma=False
    )
```

```python
import functools

import jax
import jax.numpy as jnp
import numpy as np
from jax import lax
from jax.experimental import pallas as pl
from jax.experimental.pallas import tpu as pltpu
from jax.sharding import PartitionSpec as P

LANES = 128
PAIR = 256
MIB = 1024 * 1024
ROOM_WIDE, ROOM_NEAR, ROOM_CORR, ROOM_SMALL = 26, 18, 14, 5
BF = jnp.bfloat16
F32 = jnp.float32


def call(body, out_shape, flops, moved, scratch=(), room=ROOM_SMALL, **extra):
    return pl.pallas_call(
        body,
        out_shape=out_shape,
        scratch_shapes=list(scratch),
        compiler_params=pltpu.CompilerParams(vmem_limit_bytes=room * MIB),
        cost_estimate=pl.CostEstimate(flops=int(flops), bytes_accessed=int(moved), transcendentals=0),
        **extra,
    )


def dot(left, right):
    return jnp.dot(left, right, preferred_element_type=F32)


def dot_nt(left, right):
    return lax.dot_general(left, right, (((1,), (1,)), ((), ())), preferred_element_type=F32)


def as_column(row):
    return jnp.broadcast_to(row, (row.shape[1], row.shape[1])).T


def send_kernel(cap, slots, row_ref, feat_hbm, out_ref, feat_ref, sem):
    fetch = pltpu.make_async_copy(feat_hbm, feat_ref, sem)
    fetch.start()
    rows, width = feat_ref.shape
    buffers = out_ref.shape[0]
    owner_row = (row_ref[...] // slots).astype(F32)
    owner_col = as_column(owner_row)
    first = lax.broadcasted_iota(jnp.int32, (rows, rows), 0)
    second = lax.broadcasted_iota(jnp.int32, (rows, rows), 1)
    same = jnp.where((owner_col == owner_row) & (first < second), 1.0, 0.0)
    rank = jnp.sum(same, axis=0, keepdims=True)
    pos = owner_row * cap + rank
    place = lax.broadcasted_iota(jnp.int32, (buffers, rows), 0)
    hot = jnp.where(place.astype(F32) == pos, 1.0, 0.0).astype(BF)
    slot_row = (row_ref[...] % slots).astype(F32)
    kind = place % cap
    told = jnp.where(kind == 0, owner_row, jnp.where(kind == 1, slot_row, 0.0))
    out_ref[:, width : width + rows] = told.astype(BF)
    fetch.wait()
    out_ref[:, 0:width] = dot(hot, feat_ref[...]).astype(BF)


def collect_kernel(cap, slots, row_ref, back_ref, out_ref):
    rows, width = out_ref.shape
    owner_row = (row_ref[...] // slots).astype(F32)
    owner_col = as_column(owner_row)
    first = lax.broadcasted_iota(jnp.int32, (rows, rows), 0)
    second = lax.broadcasted_iota(jnp.int32, (rows, rows), 1)
    same = jnp.where((owner_col == owner_row) & (second < first), 1.0, 0.0)
    pos = owner_col[:, 0:1] * cap + jnp.sum(same, axis=1, keepdims=True)
    place = lax.broadcasted_iota(jnp.int32, (rows, back_ref.shape[0]), 1).astype(F32)
    hot = jnp.where(place == pos, 1.0, 0.0).astype(BF)
    out_ref[...] = dot(hot, back_ref[:, 0:width]).astype(BF)


def told_rows(cap, in_ref, which):
    buffers, width = in_ref.shape
    count = buffers // cap
    source = lax.broadcasted_iota(jnp.int32, (count, buffers), 0)
    place = lax.broadcasted_iota(jnp.int32, (count, buffers), 1)
    pick = jnp.where(place == source * cap + which, 1.0, 0.0).astype(BF)
    return dot(pick, in_ref[:, width - LANES : width])


def mask_kernel(cap, slots, in_ref, codes_ref, mask_ref, route_ref):
    total = mask_ref.shape[0]
    route_ref[...] = told_rows(cap, in_ref, 0) * slots + told_rows(cap, in_ref, 1)
    codes = jnp.broadcast_to(codes_ref[...], (total, LANES))
    hits = jnp.zeros((total, LANES), F32)
    for s in range(route_ref.shape[0]):
        hits = hits + jnp.where(codes == route_ref[s : s + 1, :], 1.0, 0.0)
    mask_ref[...] = jnp.broadcast_to(jnp.sum(hits, axis=1, keepdims=True), (total, LANES))


def slot_table(cap, slots, me, in_ref):
    buffers = in_ref.shape[0]
    count = buffers // cap
    mine_f = jnp.where(told_rows(cap, in_ref, 0) == me.astype(F32), 1.0, 0.0)
    slot_f = told_rows(cap, in_ref, 1)
    first = lax.broadcasted_iota(jnp.int32, (LANES, LANES), 0)
    second = lax.broadcasted_iota(jnp.int32, (LANES, LANES), 1)
    tri = jnp.where(first < second, 1.0, 0.0).astype(BF)
    rank = dot(mine_f.astype(BF), tri)
    lane = lax.broadcasted_iota(jnp.int32, (count, LANES), 1)
    held = jnp.zeros((count, LANES), F32)
    for j in range(cap):
        here = jnp.where(rank == j, mine_f, 0.0)
        number = jnp.sum(here, axis=1, keepdims=True)
        value = jnp.sum(here * slot_f, axis=1, keepdims=True)
        value = value + (1.0 - number) * slots
        held = jnp.where(lane == j, value, held)
    place = lax.broadcasted_iota(jnp.int32, (buffers, count), 0)
    source = lax.broadcasted_iota(jnp.int32, (buffers, count), 1)
    spread = jnp.where(place // cap == source, 1.0, 0.0).astype(BF)
    wide = dot(spread, held.astype(BF))
    place = lax.broadcasted_iota(jnp.int32, (buffers, LANES), 0)
    lane = lax.broadcasted_iota(jnp.int32, (buffers, LANES), 1)
    slot_col = jnp.sum(jnp.where(place % cap == lane, wide, 0.0), axis=1, keepdims=True)
    slot_id = lax.broadcasted_iota(jnp.int32, (buffers, slots), 1).astype(F32)
    return jnp.where(slot_col == slot_id, 1.0, 0.0)


GROUP = 16
FOLD = LANES // GROUP


def permutation(channels, depth):
    perm = np.zeros((channels // GROUP, PAIR, PAIR), np.float32)
    for i in range(channels // GROUP):
        for j in range(GROUP):
            for z in range(depth):
                perm[i, depth * j + z, LANES * (z // FOLD) + GROUP * ((z + i) % FOLD) + j] = 1.0
    return perm


def lane_group(rows):
    return lax.broadcasted_iota(jnp.int32, (rows, LANES), 1) // GROUP


def spread_pairs(turned_ref, out_ref):
    chunks, rows, _ = turned_ref.shape
    step = 32
    group = lane_group(step)

    def body(t, carry):
        at = pl.ds(pl.multiple_of(t * step, step), step)
        for half in range(2):
            lanes = slice(half * LANES, (half + 1) * LANES)
            parts = [turned_ref[i, at, lanes] for i in range(chunks)]
            parts = parts + [jnp.zeros((step, LANES), F32)] * (FOLD - chunks)
            for bit in (1, 2, 4):
                odd = (group & bit) != 0
                parts = [jnp.where(odd, parts[(i + bit) % FOLD], parts[i]) for i in range(FOLD)]
            for g in range(FOLD):
                value = parts[(-g) % FOLD]
                if g:
                    value = pltpu.roll(value, LANES - GROUP * g, 1)
                z = half * FOLD + g
                out_ref[z // 2, at, (z % 2) * LANES : (z % 2 + 1) * LANES] = value.astype(BF)
        return carry

    lax.fori_loop(0, rows // step, body, 0)


def gather_pairs(in_ref, turned_ref):
    chunks, rows, _ = turned_ref.shape
    step = 32
    group = lane_group(step)

    def body(t, carry):
        at = pl.ds(pl.multiple_of(t * step, step), step)
        for half in range(2):
            turned = []
            for g in range(FOLD):
                z = half * FOLD + g
                value = in_ref[z // 2, at, (z % 2) * LANES : (z % 2 + 1) * LANES].astype(F32)
                turned.append(pltpu.roll(value, GROUP * g, 1) if g else value)
            parts = [turned[(-i) % FOLD] for i in range(FOLD)]
            for bit in (1, 2, 4):
                odd = (group & bit) != 0
                parts = [jnp.where(odd, parts[(i - bit) % FOLD], parts[i]) for i in range(FOLD)]
            for i in range(chunks):
                turned_ref[i, at, half * LANES : (half + 1) * LANES] = parts[i].astype(BF)
        return carry

    lax.fori_loop(0, rows // step, body, 0)


def to_pairs_kernel(rows_ref, perm_ref, out_ref, turned_ref):
    for i in range(perm_ref.shape[0]):
        turned_ref[i] = dot(rows_ref[:, i * PAIR : (i + 1) * PAIR], perm_ref[i])
    spread_pairs(turned_ref, out_ref)


def place_kernel(cap, slots, me_ref, rows_ref, perm_hbm, out_ref, take_ref, turned_ref, perm_ref, sem):
    fetch = pltpu.make_async_copy(perm_hbm, perm_ref, sem)
    fetch.start()
    take = slot_table(cap, slots, me_ref[0], rows_ref)
    take_ref[...] = take.astype(BF)
    put = take.T.astype(BF)
    fetch.wait()
    for i in range(perm_ref.shape[0]):
        held = dot(put, rows_ref[:, i * PAIR : (i + 1) * PAIR]).astype(BF)
        turned_ref[i] = dot(held, perm_ref[i])
    spread_pairs(turned_ref, out_ref)


def message_kernel(f_ref, xlo_ref, xhi_ref, pick_ref, low_ref, high_ref):
    pick = pick_ref[...]
    half = low_ref.shape[1]
    for k in range(f_ref.shape[0]):
        rows = jnp.concatenate([xlo_ref[k], f_ref[k], xhi_ref[k]], axis=0)
        sent = dot(pick, rows).astype(BF)
        low_ref[k] = sent[0:half]
        high_ref[k] = sent[half : 2 * half]


def build_band(band_ref, raw_ref, backward):
    channels = raw_ref.shape[1]
    band_ref[...] = jnp.zeros_like(band_ref)
    for tap in range(27):
        value = raw_ref[26 - tap] if backward else raw_ref[tap].T
        for zo in range(2):
            row = ((tap // 3) * 4 + zo + tap % 3) * LANES
            band_ref[row : row + channels, zo * LANES : zo * LANES + channels] = value


NX = 16
NY = 16
OUT_MAIN = (NX + 2) * NY
EDGE = 24
OUT_ROWS = OUT_MAIN + 2 * EDGE
MSG = 48
M_XLO = NX * NY
M_XHI = M_XLO + 2 * NY
M_YLO = M_XHI + 2 * NY
M_YHI = M_YLO + MSG
M_LOW = M_YHI + MSG
M_HIGH = M_LOW + MSG
M_EDGE = M_HIGH + MSG
M_ROWS = M_EDGE + 2 * EDGE


def twice(value):
    return jnp.concatenate([value, value], axis=1)


def put_pair(ref, lead, k, tail, value):
    value = value.astype(BF)
    ref[lead + (k,) + tail + (slice(LANES, PAIR),)] = value[:, 0:LANES]
    ref[lead + (k + 1,) + tail + (slice(0, LANES),)] = value[:, LANES:PAIR]


def clear_ends(ref, lead):
    last = ref.shape[len(lead)] - 1
    dims = ref.shape[len(lead) + 1 : -1]
    ref[lead + (0,) + (slice(None),) * len(dims) + (slice(0, LANES),)] = jnp.zeros(dims + (LANES,), BF)
    ref[lead + (last,) + (slice(None),) * len(dims) + (slice(LANES, PAIR),)] = jnp.zeros(dims + (LANES,), BF)


def put_shifted(ext_ref, k, xp, mid, before, after, row):
    ny = mid.shape[0]
    up = jnp.where(row == 0, before, pltpu.roll(mid, 1, 0))
    down = jnp.where(row == ny - 1, after, pltpu.roll(mid, ny - 1, 0))
    for b, value in enumerate((up, mid, down)):
        put_pair(ext_ref, (b,), k, (xp, slice(None)), value)


def widen_two(ext_ref, edge_ref, f_ref, xlo_ref, xhi_ref, ylo_ref, yhi_ref, low_ref, high_ref, mask_ref=None):
    for b in range(3):
        clear_ends(ext_ref, (b,))
        for a in range(3):
            clear_ends(edge_ref, (a, b))
    row = lax.broadcasted_iota(jnp.int32, (NY, PAIR), 0)

    def read(ref, k, start, size, mask_start):
        value = ref[k, start : start + size, :].astype(F32)
        if mask_ref is None:
            return value
        return value * twice(mask_ref[mask_start + start : mask_start + start + size, :])

    def fill(k):
        ylo = read(ylo_ref, k, 0, MSG, M_YLO)
        yhi = read(yhi_ref, k, 0, MSG, M_YHI)
        low = read(low_ref, k, 0, MSG, M_LOW)
        high = read(high_ref, k, 0, MSG, M_HIGH)
        wide = NX + 4
        for xp in range(wide):
            if xp < 2:
                mid = read(xlo_ref, k, xp * NY, NY, M_XLO)
            elif xp >= NX + 2:
                mid = read(xhi_ref, k, (xp - NX - 2) * NY, NY, M_XHI)
            else:
                mid = read(f_ref, k, (xp - 2) * NY, NY, 0)
            put_shifted(ext_ref, k, xp, mid, ylo[wide + xp : wide + xp + 1, :], yhi[xp : xp + 1, :], row)
        first = ((ylo, 0), (ylo, wide), (low, 0))
        second = ((high, wide), (yhi, 0), (yhi, wide))
        for a in range(3):
            for b in range(3):
                sides = []
                for value, start in (first[b], second[b]):
                    turn = start + a
                    if turn:
                        value = pltpu.roll(value, MSG - turn, 0)
                    sides.append(value[0:EDGE])
                put_pair(edge_ref, (a, b), k, (slice(None),), jnp.concatenate(sides, axis=0))

    return fill


def widen_one(ext_ref, rows_ref):
    for b in range(3):
        clear_ends(ext_ref, (b,))
    row = lax.broadcasted_iota(jnp.int32, (NY, PAIR), 0)

    def fill(k):
        edges = rows_ref[k, OUT_MAIN:OUT_ROWS, :].astype(F32)
        for xp in range(NX + 2):
            mid = rows_ref[k, xp * NY : (xp + 1) * NY, :].astype(F32)
            put_shifted(ext_ref, k, xp, mid, edges[xp : xp + 1, :], edges[EDGE + xp : EDGE + xp + 1, :], row)

    return fill


def fill_all(fill, pairs):
    def body(k, carry):
        fill(k)
        return carry

    lax.fori_loop(0, pairs, body, 0)


STEP = 2


def conv_wide(ext_ref, edge_ref, w_ref, k):
    pieces = []
    for a in range(3):
        for b in range(3):
            for j in range(2):
                parts = []
                for i in range(STEP):
                    parts.append(ext_ref[b, k + i + j, a : a + NX + 2].reshape(OUT_MAIN, PAIR))
                    parts.append(edge_ref[a, b, k + i + j])
                pieces.append(jnp.concatenate(parts, axis=0))
    return dot(jnp.concatenate(pieces, axis=1), w_ref[...])


def conv_inner(ext_ref, w_ref, k):
    pieces = []
    for a in range(3):
        for b in range(3):
            for j in range(2):
                pieces.append(ext_ref[b, k + j : k + j + STEP, a : a + NX].reshape(STEP * NX * NY, PAIR))
    return dot(jnp.concatenate(pieces, axis=1), w_ref[...])


def each_step(pairs, fill, conv, finish):
    for k in range(STEP + 1):
        fill(k)
    last = None
    for k in range(0, pairs, STEP):
        for ahead in range(k + STEP + 1, min(k + 2 * STEP + 1, pairs)):
            fill(ahead)
        total = conv(k)
        if last is not None:
            finish(*last)
        last = (k, total)
    finish(*last)


def out_mask(mask_ref):
    return twice(jnp.concatenate([
        mask_ref[M_XLO + NY : M_XLO + 2 * NY, :], mask_ref[0 : NX * NY, :],
        mask_ref[M_XHI : M_XHI + NY, :], mask_ref[M_EDGE:M_ROWS, :],
    ], axis=0))


def outer_kernel(f_ref, xlo_ref, xhi_ref, ylo_ref, yhi_ref, low_ref, high_ref, mask_ref, raw_ref,
                 out_ref, outer_ref, ext_ref, edge_ref, w_ref):
    build_band(w_ref, raw_ref, True)
    fill = widen_two(ext_ref, edge_ref, f_ref, xlo_ref, xhi_ref, ylo_ref, yhi_ref, low_ref, high_ref, mask_ref)

    def finish(k, total):
        for i in range(STEP):
            out_ref[k + i] = total[i * OUT_ROWS : (i + 1) * OUT_ROWS]
            outer_ref[k + i] = (f_ref[k + i].astype(F32) * twice(mask_ref[0 : NX * NY, :])).astype(BF)

    each_step(f_ref.shape[0], fill, lambda k: conv_wide(ext_ref, edge_ref, w_ref, k), finish)


def correlate(gt_ref, ext_ref, first_x, taps_ref):
    depth = 2 * (ext_ref.shape[1] - 1)

    def body(b, carry):
        rows = []
        for z in range(depth):
            parts = []
            for a in range(3):
                for c in range(3):
                    half = (z + c) % 2 * LANES
                    part = ext_ref[b, (z + c) // 2, first_x + a : first_x + a + NX, :, half : half + LANES]
                    parts.append(part.reshape(NX * NY, LANES))
            rows.append(jnp.concatenate(parts, axis=1))
        sums = dot(gt_ref[...], jnp.concatenate(rows, axis=0))
        for a in range(3):
            for c in range(3):
                taps_ref[9 * a + 3 * b + c] = sums[:, (3 * a + c) * LANES : (3 * a + c + 1) * LANES]
        return carry

    lax.fori_loop(0, 3, body, 0)


def pack_taps(taps_ref, packed_ref, channels):
    lane = lax.broadcasted_iota(jnp.int32, (channels, LANES), 1)
    for g in range(7):
        t1 = pltpu.roll(taps_ref[4 * g + 1], 96, 1)
        t2 = pltpu.roll(taps_ref[4 * g + 2], 64, 1)
        t3 = pltpu.roll(taps_ref[4 * g + 3], 32, 1)
        blocks = (
            jnp.where(lane < 96, taps_ref[4 * g], t1),
            jnp.where(lane < 64, t1, t2),
            jnp.where(lane < 32, t2, t3),
        )
        for i, value in enumerate(blocks):
            start = (3 * g + i) * channels
            packed_ref[start : start + channels, :] = value
    rest = packed_ref.shape[0] - 21 * channels
    if rest:
        packed_ref[21 * channels :, :] = jnp.zeros((rest, LANES), F32)


def hidden_kernel(channels, run, core_ref, f_ref, xlo_ref, xhi_ref, ylo_ref, yhi_ref, low_ref, high_ref, mask_ref,
                  raw_ref, grad_ref, act_ref, hg_ref, keep_ref, give_ref,
                  ext_ref, edge_ref, w_ref, gt_ref, taps_ref, packed_ref):
    build_band(w_ref, raw_ref, False)
    fill = widen_two(ext_ref, edge_ref, f_ref, xlo_ref, xhi_ref, ylo_ref, yhi_ref, low_ref, high_ref)

    def finish(k, total):
        m = out_mask(mask_ref)
        for i in range(STEP):
            hidden = m * total[i * OUT_ROWS : (i + 1) * OUT_ROWS]
            sigma = jax.nn.sigmoid(hidden)
            act_ref[k + i] = (hidden * sigma).astype(BF)
            hg = (m * grad_ref[k + i] * sigma * (1.0 + hidden * (1.0 - sigma))).astype(BF)
            hg_ref[k + i] = hg
            inner = NX * NY
            value = hg[NY : NY + inner].T
            for j in range(2):
                z = 2 * (k + i) + j
                gt_ref[:, z * inner : (z + 1) * inner] = value[j * LANES : j * LANES + channels]

    each_step(f_ref.shape[0], fill, lambda k: conv_wide(ext_ref, edge_ref, w_ref, k), finish)
    correlate(gt_ref, ext_ref, 1, taps_ref)
    hand_out(channels, run, core_ref, taps_ref, packed_ref, keep_ref, give_ref)


def turn(gt_ref, g_ref, start, channels):
    inner = NX * NY
    for k in range(g_ref.shape[0]):
        value = g_ref[k, start : start + inner, :].T
        for i in range(2):
            z = 2 * k + i
            gt_ref[:, z * inner : (z + 1) * inner] = value[i * LANES : i * LANES + channels]


def hand_out(channels, run, core_ref, taps_ref, packed_ref, keep_ref, give_ref):
    runs = keep_ref.shape[0] // run
    block = 2 * runs * run
    taps_ref[27] = jnp.zeros((channels, LANES), F32)
    pack_taps(taps_ref, packed_ref, channels)
    for l in range(packed_ref.shape[0] // block):
        lanes = slice(l * LANES, (l + 1) * LANES)
        for x in range(runs):
            base = l * block + 2 * x * run
            rows = slice(x * run, (x + 1) * run)
            mine = pl.multiple_of(base + core_ref[0] * run, run)
            other = pl.multiple_of(base + (1 - core_ref[0]) * run, run)
            keep_ref[rows, lanes] = packed_ref[pl.ds(mine, run), :]
            give_ref[rows, lanes] = packed_ref[pl.ds(other, run), :]


def corr_kernel(channels, run, core_ref, act_ref, outer_ref, keep_ref, give_ref, ext_ref, gt_ref, taps_ref, packed_ref):
    fill_all(widen_one(ext_ref, act_ref), act_ref.shape[0])
    turn(gt_ref, outer_ref, 0, channels)
    correlate(gt_ref, ext_ref, 0, taps_ref)
    hand_out(channels, run, core_ref, taps_ref, packed_ref, keep_ref, give_ref)


def grid_grad_kernel(hg_ref, raw_ref, outer_ref, perm_ref, take_ref, out_ref, ext_ref, sum_ref, turned_ref, w_ref):
    build_band(w_ref, raw_ref, True)
    fill = widen_one(ext_ref, hg_ref)

    def finish(k, total):
        rows = NX * NY
        for i in range(STEP):
            sum_ref[k + i] = (outer_ref[k + i].astype(F32) + total[i * rows : (i + 1) * rows]).astype(BF)

    each_step(outer_ref.shape[0], fill, lambda k: conv_inner(ext_ref, w_ref, k), finish)
    gather_pairs(sum_ref, turned_ref)
    take = take_ref[...]
    for i in range(perm_ref.shape[0]):
        rows = dot_nt(turned_ref[i], perm_ref[i]).astype(BF)
        out_ref[:, i * PAIR : (i + 1) * PAIR] = dot(take, rows).astype(BF)


def block_kernel(act_ref, mask_ref, raw_ref, field_ref, perm_ref, out_ref, ext_ref, sum_ref, turned_ref, w_ref):
    build_band(w_ref, raw_ref, False)
    fill = widen_one(ext_ref, act_ref)

    def finish(k, total):
        m = twice(mask_ref[0 : NX * NY, :])
        rows = NX * NY
        for i in range(STEP):
            sum_ref[k + i] = (field_ref[k + i].astype(F32) + m * total[i * rows : (i + 1) * rows]).astype(BF)

    each_step(field_ref.shape[0], fill, lambda k: conv_inner(ext_ref, w_ref, k), finish)
    gather_pairs(sum_ref, turned_ref)
    for i in range(perm_ref.shape[0]):
        out_ref[:, i * PAIR : (i + 1) * PAIR] = dot_nt(turned_ref[i], perm_ref[i]).astype(BF)


def pair_sum_kernel(keep0_ref, got0_ref, keep1_ref, got1_ref, out_ref):
    half = keep0_ref.shape[1]
    out_ref[:, 0:half] = (keep0_ref[...] + got0_ref[...]).astype(BF)
    out_ref[:, half : 2 * half] = (keep1_ref[...] + got1_ref[...]).astype(BF)


def assemble_kernel(cap, run, back_hbm, parts_ref, out_hbm, total_ref, sem):
    buffers, half = total_ref.shape
    senders = parts_ref.shape[0]
    row = lax.broadcasted_iota(jnp.int32, (buffers, senders), 0)
    col = lax.broadcasted_iota(jnp.int32, (buffers, senders), 1)
    same = row % cap == col % cap
    core = (row // run) % 2
    total = jnp.zeros((buffers, half), F32)
    for i in range(2):
        add = jnp.where(same & (core == i), 1.0, 0.0).astype(BF)
        total = total + dot(add, parts_ref[:, i * half : (i + 1) * half])
    total_ref[...] = total.astype(BF)
    width = out_hbm.shape[1] - half
    store = pltpu.make_async_copy(total_ref, out_hbm.at[:, width : width + half], sem)
    store.start()
    store.wait()


def unpack_kernel(factor, core_ref, mine_ref, other_ref, first_ref, second_ref, flat_ref):
    rows, lanes = mine_ref.shape
    for i, out_ref in enumerate((first_ref, second_ref)):
        own = core_ref[0] == i
        for l in range(lanes // LANES):
            at = slice(l * LANES, (l + 1) * LANES)
            value = jnp.where(own, mine_ref[:, at].astype(F32), other_ref[:, at].astype(F32))
            flat_ref[l * rows : (l + 1) * rows, :] = value
        unpack_taps(factor, flat_ref, out_ref)


def unpack_taps(factor, packed_ref, out_ref):
    channels = out_ref.shape[1]
    lane = lax.broadcasted_iota(jnp.int32, (channels, LANES), 1)
    for g in range(7):
        v = []
        for i in range(3):
            start = (3 * g + i) * channels
            v.append(packed_ref[start : start + channels, :] * factor)
        taps = (
            v[0],
            pltpu.roll(jnp.where(lane < 64, v[1], v[0]), 32, 1),
            pltpu.roll(jnp.where(lane < 32, v[2], v[1]), 64, 1),
            pltpu.roll(v[2], 96, 1),
        )
        for u in range(4):
            if 4 * g + u < 27:
                out_ref[4 * g + u] = taps[u][:, 0:channels]


RX = ("cx", "core")
ALL = ("cx", "core", "ry")
SAME_CORE = ("cx", "ry")


def size_of(axes):
    return int(np.prod([lax.axis_size(a) for a in ((axes,) if isinstance(axes, str) else axes)]))


def share(parts, axes):
    return lax.all_to_all(parts, axes, split_axis=0, concat_axis=0, tiled=True)


def neighbours(axes, upper, lower):
    count = size_of(axes)
    ahead = [(i, i + 1) for i in range(count - 1)]
    behind = [(t, s) for s, t in ahead]
    return lax.ppermute(upper, axes, ahead), lax.ppermute(lower, axes, behind)


def swap_cores(value):
    count = size_of(RX)
    return lax.ppermute(value, RX, [(i, i ^ 1) for i in range(count)])


def message_rows():
    cells = []
    for ys in ((0, 1), (NY - 2, NY - 1)):
        for y in ys:
            cells += [(x, y) for x in range(-2, NX + 2)]
        cells += [None] * (MSG - 2 * (NX + 4))
    return cells


def exchange(field, pick):
    pairs = field.shape[0]
    xlo, xhi = neighbours(RX, field[:, (NX - 2) * NY :, :], field[:, : 2 * NY, :])
    message = jax.ShapeDtypeStruct((pairs, MSG, PAIR), BF)
    low, high = call(message_kernel, (message, message), 5e8, 3e6)(field, xlo, xhi, pick)
    ylo, yhi = neighbours("ry", high, low)
    return xlo, xhi, ylo, yhi, low, high


def mask_cells():
    cells = [(x, y) for x in range(NX) for y in range(NY)]
    cells += [(x, y) for x in (-2, -1) for y in range(NY)]
    cells += [(x, y) for x in (NX, NX + 1) for y in range(NY)]
    for ys in ((-2, -1), (NY, NY + 1), (0, 1), (NY - 2, NY - 1)):
        for y in ys:
            cells += [(x, y) for x in range(-2, NX + 2)]
        cells += [None] * (MSG - 2 * (NX + 4))
    for y in (-1, NY):
        cells += [(x, y) for x in range(-1, NX + 1)]
        cells += [None] * (EDGE - NX - 2)
    return cells


def on_device(column_features, column_route, cotangent, first_weight, second_weight):
    count_x = size_of(RX)
    count_y = size_of("ry")
    count_all = count_x * count_y
    shard_rows, row_width = column_features.shape
    channels = first_weight.shape[1]
    depth = row_width // channels
    slots = NX * NY
    pairs = depth // 2
    chunks = channels // GROUP
    cap = 2 * shard_rows // count_all
    buffers = count_all * cap
    me_x = lax.axis_index(RX)
    me_y = lax.axis_index("ry")
    core = lax.axis_index("core").astype(jnp.int32).reshape(1)
    conv_flops = 2 * slots * pairs * 36 * LANES * PAIR

    smem = pl.BlockSpec(memory_space=pltpu.SMEM)
    vmem = pl.BlockSpec(memory_space=pltpu.VMEM)
    hbm = pl.BlockSpec(memory_space=pltpu.HBM)
    shape = jax.ShapeDtypeStruct
    field_shape = shape((pairs, slots, PAIR), BF)
    wide_shape = shape((pairs, OUT_ROWS, PAIR), BF)
    ext = pltpu.VMEM((3, pairs + 1, NX + 4, NY, PAIR), BF)
    edge = pltpu.VMEM((3, 3, pairs + 1, 2 * EDGE, PAIR), BF)
    turned = pltpu.VMEM((chunks, slots, PAIR), F32)
    turned_low = pltpu.VMEM((chunks, slots, PAIR), BF)
    sums = pltpu.VMEM((pairs, slots, PAIR), BF)

    perm = jnp.asarray(permutation(channels, depth), BF)
    pick_np = np.zeros((2 * MSG, (NX + 4) * NY), np.float32)
    for r, cell in enumerate(message_rows()):
        if cell is not None:
            pick_np[r, (cell[0] + 2) * NY + cell[1]] = 1.0
    pick = jnp.asarray(pick_np, BF)

    route_row = column_route.reshape(1, shard_rows)
    told_width = row_width + LANES
    outgoing = call(
        functools.partial(send_kernel, cap, slots), shape((buffers, told_width), BF),
        2 * buffers * shard_rows * row_width, 3 * shard_rows * row_width * 2,
        (pltpu.VMEM((shard_rows, row_width), BF), pltpu.SemaphoreType.DMA), in_specs=[vmem, hbm],
    )(route_row, column_features)
    incoming = share(outgoing.reshape(count_all, cap, told_width), ALL).reshape(buffers, told_width)

    cells = mask_cells()
    steps = np.asarray([(0, 0) if c is None else (c[0] // NX, c[1] // NY) for c in cells], np.int32)
    local = np.asarray([-1 if c is None else (c[0] % NX) * NY + c[1] % NY for c in cells], np.int32)
    to_x = me_x + steps[:, 0]
    to_y = me_y + steps[:, 1]
    inside = (to_x >= 0) & (to_x < count_x) & (to_y >= 0) & (to_y < count_y) & (local >= 0)
    codes = jnp.where(inside, (to_x * count_y + to_y) * slots + local, -1).astype(F32)[:, None]
    me = (me_x * count_y + me_y).astype(jnp.int32).reshape(1)

    cot = call(
        to_pairs_kernel, field_shape, 1e9, 3e6, (turned,),
    )(cotangent.reshape(slots, row_width), perm)
    cot_halo = exchange(cot, pick)

    field, take = call(
        functools.partial(place_kernel, cap, slots), (field_shape, shape((buffers, slots), BF)), 1e9, 3e6,
        (turned, pltpu.VMEM(perm.shape, BF), pltpu.SemaphoreType.DMA), in_specs=[smem, vmem, hbm],
    )(me, incoming, perm)
    field_halo = exchange(field, pick)

    mask = call(
        functools.partial(mask_kernel, cap, slots), shape((M_ROWS, LANES), F32), 1e8, 1e6,
        (pltpu.VMEM((count_all, LANES), F32),),
    )(incoming, codes)
    band = pltpu.VMEM((36 * LANES, PAIR), BF)
    ext_near = pltpu.VMEM((3, pairs + 1, NX + 2, NY, PAIR), BF)
    act_grad, outer = call(
        outer_kernel, (shape((pairs, OUT_ROWS, PAIR), F32), field_shape),
        1.3 * conv_flops, 7e6, (ext, edge, band), ROOM_WIDE,
    )(cot, *cot_halo, mask, second_weight)

    packed_rows = -(-21 * channels // buffers) * buffers
    run = count_y * cap
    grad_lanes = 2 * packed_rows // buffers * LANES
    half_shape = shape((buffers // 2, grad_lanes // 2), F32)
    corr_scratch = (
        pltpu.VMEM((channels, depth * slots), BF),
        pltpu.VMEM((28, channels, LANES), F32), pltpu.VMEM((packed_rows, LANES), F32),
    )
    act, hg, keep0, give0 = call(
        functools.partial(hidden_kernel, channels, run), (wide_shape, wide_shape, half_shape, half_shape),
        2.3 * conv_flops, 9e6, (ext, edge, band) + corr_scratch, ROOM_WIDE, in_specs=[smem] + [vmem] * 10,
    )(core, field, *field_halo, mask, first_weight, act_grad)
    got0 = swap_cores(give0)
    keep1, give1 = call(
        functools.partial(corr_kernel, channels, run), (half_shape, half_shape), conv_flops, 5e6,
        (ext_near,) + corr_scratch, ROOM_CORR, in_specs=[smem, vmem, vmem],
    )(core, act, outer)
    sent = call(
        pair_sum_kernel, shape((buffers // 2, grad_lanes), BF), 1e6, 2e6,
    )(keep0, got0, keep1, swap_cores(give1))
    parts = share(sent.reshape(count_all // 2, cap, grad_lanes), SAME_CORE).reshape(buffers // 2, grad_lanes)

    hg, sent = lax.optimization_barrier((hg, sent))
    back_width = row_width + grad_lanes // 2
    back = call(
        grid_grad_kernel, shape((buffers, back_width), BF), 1.2 * conv_flops, 6e6,
        (ext_near, sums, turned_low, band), ROOM_NEAR,
    )(hg, first_weight, outer, perm, take)
    mixed = call(
        functools.partial(assemble_kernel, cap, run), shape((buffers, back_width), BF), 2e8, 3e6,
        (pltpu.VMEM((buffers, grad_lanes // 2), BF), pltpu.SemaphoreType.DMA),
        in_specs=[hbm, vmem], out_specs=hbm, input_output_aliases={0: 0},
    )(back, parts)
    returned = share(mixed.reshape(count_all, cap, back_width), ALL).reshape(buffers, back_width)

    act, mixed = lax.optimization_barrier((act, mixed))
    block_output = call(
        block_kernel, shape((slots, row_width), BF), 1.2 * conv_flops, 8e6,
        (ext_near, sums, turned_low, band), ROOM_NEAR,
    )(act, mask, second_weight, field, perm)

    returned, block_output = lax.optimization_barrier((returned, block_output))
    mine = returned[:, row_width:]
    feature_grads = call(
        functools.partial(collect_kernel, cap, slots), shape((shard_rows, row_width), BF),
        2 * buffers * shard_rows * row_width, 3 * shard_rows * row_width * 2,
    )(route_row, returned)

    factor = float(1.0 / np.sqrt(np.float32(count_all * shard_rows * depth)))
    grads = shape(first_weight.shape, F32)
    first_grad, second_grad = call(
        functools.partial(unpack_kernel, factor), (grads, grads), 1e6, 4e6,
        (pltpu.VMEM((packed_rows, LANES), F32),), in_specs=[smem, vmem, vmem],
    )(core, mine, swap_cores(mine))
    return (block_output.reshape(cotangent.shape), feature_grads, first_grad, second_grad)


def solution(mesh):
    count_x = mesh.shape["rx"]
    fine = jax.sharding.Mesh(mesh.devices.reshape(count_x // 2, 2, mesh.shape["ry"]), ALL)
    in_specs = (P(ALL, None), P(ALL), P(RX, "ry", None), P(), P())
    out_specs = (P(RX, "ry", None), P(ALL, None), P(), P())
    return jax.shard_map(
        on_device, mesh=fine, in_specs=in_specs, out_specs=out_specs, check_vma=False
    )
```
